32 devices in a mesh: dp: 16 (over z, x, core), tensor: 2 (over y).
Axes of the slice: x: 2, y: 2, z: 4, core: 2. Of those that a mesh axis runs over, the one named last changes fastest.
Arguments:
- layer_input: bfloat16 [23360, 1152], P(('dp', 'tensor')), may hold values from -6 to 6
- token_image: int32 [23360], P('dp'), may hold values from 0 to 2, as said below
- cotangent: bfloat16 [23360, 1152], P(('dp', 'tensor')), may hold values from -6 to 6
- ln1_gain: bfloat16 [1152], P('dp'), may hold values from 0.5 to 1.5
- ln1_bias: bfloat16 [1152], P('dp'), may hold values from -3 to 3
- w_qkv: bfloat16 [3, 1152, 1152], P(None, 'dp', 'tensor'), may hold values from -0.25 to 0.25
- qv_bias: bfloat16 [2, 1152], P(None, 'tensor'), may hold values from -3 to 3
- w_out: bfloat16 [1152, 1152], P('tensor', 'dp'), may hold values from -1 to 1
- out_bias: bfloat16 [1152], P('dp'), may hold values from -3 to 3
- ln2_gain: bfloat16 [1152], P('dp'), may hold values from 0.5 to 1.5
- ln2_bias: bfloat16 [1152], P('dp'), may hold values from -3 to 3
- w_fc1: bfloat16 [1152, 4304], P('dp', 'tensor'), may hold values from -0.1875 to 0.1875
- fc1_bias: bfloat16 [4304], P('tensor'), may hold values from -3 to 3
- w_fc2: bfloat16 [4304, 1152], P('tensor', 'dp'), may hold values from -0.09375 to 0.09375
- fc2_bias: bfloat16 [1152], P('dp'), may hold values from -3 to 3
Outputs:
- layer_output: bfloat16 [23360, 1152], P(('dp', 'tensor'))
- input_grad: float32 [23360, 1152], P(('dp', 'tensor'))
- ln1_gain_grad: float32 [1152], P('dp')
- ln1_bias_grad: float32 [1152], P('dp')
- w_qkv_grad: float32 [3, 1152, 1152], P(None, 'dp', 'tensor')
- qv_bias_grad: float32 [2, 1152], P(None, 'tensor')
- w_out_grad: float32 [1152, 1152], P('tensor', 'dp')
- out_bias_grad: float32 [1152], P('dp')
- ln2_gain_grad: float32 [1152], P('dp')
- ln2_bias_grad: float32 [1152], P('dp')
- w_fc1_grad: float32 [1152, 4304], P('dp', 'tensor')
- fc1_bias_grad: float32 [4304], P('tensor')
- w_fc2_grad: float32 [4304, 1152], P('tensor', 'dp')
- fc2_bias_grad: float32 [1152], P('dp')
The draws below stay inside these ranges and needn't reach their ends.
Inputs may be any that keep to these rules, and one draw needn't show every extreme that they name: `token_image`: in each group of 1460 consecutive positions the values 0 to 1 appear in this order, 729 positions each; every other position holds 2 (padding), at places drawn from the seed.
All inputs are finite; a program needn't handle non-finite values.
Results may differ from the reference program's by a relative error of at most 0.012.
The reference program's roundings to bfloat16 on the way count: a program that leaves them out, or rounds other values in their place, can miss the bound.
Values may be sent and summed in bfloat16 or wider, within the bound.
No kernel may reach another device: no remote copies, remote signals or barrier semaphores. Data moves between devices by JAX's collectives and lax.ppermute only.
A program may use at most 256 MiB of HBM per device.

```python
import jax
import jax.numpy as jnp
from jax import lax

D = 1152
HEADS = 16
HEAD_DIM = 72
FF = 4304
PATCHES = 729
IMAGES = 2
SLOTS = 1460
TOKENS = 23360


def draw_token_image(key, part):
    key = jax.random.fold_in(key, 11)
    groups = TOKENS // SLOTS
    padding = SLOTS - IMAGES * PATCHES

    def one_group(group_key):
        order = jax.random.permutation(group_key, SLOTS)
        marks = jnp.zeros((SLOTS,), jnp.int32).at[order[:padding]].set(1)
        ranks = jnp.cumsum(1 - marks) - 1
        return jnp.where(marks == 1, IMAGES, ranks // PATCHES).astype(jnp.int32)
    group_keys = jax.random.split(key, groups)
    return jax.vmap(one_group)(group_keys).reshape(TOKENS)


def block_scale(key, extent, cuts, least, high):
    loudness = 1.0
    for axis_at, blocks in cuts:
        heights = jax.random.uniform(jax.random.fold_in(jax.random.fold_in(key, 6), axis_at), (blocks,), jnp.float32, least / len(cuts), high / len(cuts))
        loudness = loudness * jnp.repeat(jnp.exp(heights), extent[axis_at] // blocks).reshape((-1,) + (1,) * (len(extent) - 1 - axis_at))
    return loudness


def scatter_about(key, shape, deviation, most, cuts=(), kind=jnp.bfloat16):
    values = deviation * jax.random.normal(key, shape, jnp.float32)
    if cuts:
        values = values * block_scale(key, shape, cuts, -0.22, 0.18)
    return jnp.clip(values, -most, most).astype(kind)


def setup_inputs(seed: int = 0) -> dict:
    streams_of = jax.random.split(jax.random.key(seed), 16)
    layer_input = scatter_about(streams_of[0], (TOKENS, D), 1.0, 6.0, ((0, 32),))
    token_image = draw_token_image(jax.random.fold_in(streams_of[15], 71), 0)
    cotangent = scatter_about(streams_of[2], (TOKENS, D), 1.0, 6.0, ((0, 32),))
    ln1_gain = jnp.clip(1.0 + 0.1 * jax.random.normal(streams_of[3], (D,), jnp.float32), 0.5, 1.5).astype(jnp.bfloat16)
    ln1_bias = scatter_about(streams_of[4], (D,), 0.5, 3.0, ((0, 16),))
    w_qkv = scatter_about(streams_of[5], (3, D, D), (D // 2) ** -0.5, 0.25, ((1, 16), (2, 2)))
    qv_bias = scatter_about(streams_of[6], (2, D), 0.5, 3.0, ((1, 2),))
    w_out = scatter_about(streams_of[7], (D, D), (D // 32) ** -0.5, 1.0, ((0, 2), (1, 16)))
    out_bias = scatter_about(streams_of[8], (D,), 0.5, 3.0, ((0, 16),))
    ln2_gain = jnp.clip(1.0 + 0.1 * jax.random.normal(streams_of[9], (D,), jnp.float32), 0.5, 1.5).astype(jnp.bfloat16)
    ln2_bias = scatter_about(streams_of[10], (D,), 0.5, 3.0, ((0, 16),))
    w_fc1 = scatter_about(streams_of[11], (D, FF), D ** -0.5, 0.1875, ((0, 16), (1, 2)))
    fc1_bias = scatter_about(streams_of[12], (FF,), 0.5, 3.0, ((0, 2),))
    w_fc2 = scatter_about(streams_of[13], (FF, D), FF ** -0.5, 0.09375, ((0, 2), (1, 16)))
    fc2_bias = scatter_about(streams_of[14], (D,), 0.5, 3.0, ((0, 16),))
    return dict(layer_input=layer_input, token_image=token_image, cotangent=cotangent, ln1_gain=ln1_gain, ln1_bias=ln1_bias, w_qkv=w_qkv, qv_bias=qv_bias, w_out=w_out, out_bias=out_bias, ln2_gain=ln2_gain, ln2_bias=ln2_bias, w_fc1=w_fc1, fc1_bias=fc1_bias, w_fc2=w_fc2, fc2_bias=fc2_bias)


layer_eps = 1e-06
gelu_scale = 0.7978845608028654

@jax.custom_vjp
def low(v):
    return lax.optimization_barrier(v.astype(jnp.bfloat16)).astype(jnp.float32)

@jax.custom_vjp
def low_back(v):
    return v

def low_keep(v):
    return (low(v), None)

def low_pass(kept, grad):
    return (grad,)

def back_keep(v):
    return (v, None)

def back_low(kept, grad):
    return (low(grad),)
low.defvjp(low_keep, low_pass)
low_back.defvjp(back_keep, back_low)

def round_both(values):
    return low(low_back(values))

def gelu_tanh(values):
    return 0.5 * values * (1.0 + jnp.tanh(gelu_scale * (values + 0.044715 * values * values * values)))

def norm_rows(values, gain, shift):
    centre = values - lax.optimization_barrier(jnp.mean(values, axis=1, keepdims=True))
    spread = lax.optimization_barrier(jnp.mean(centre * centre, axis=1, keepdims=True))
    return centre * lax.rsqrt(spread + layer_eps) * gain + shift

def highest(left, right):
    return jnp.dot(left, right, precision=lax.Precision.HIGHEST)

def group_forward(rows_in, image_ids, params):
    ln1_gain, ln1_bias, w_qkv, qv_bias, w_out, out_bias, ln2_gain, ln2_bias, w_fc1, fc1_bias, w_fc2, fc2_bias = params
    slot_count = rows_in.shape[0]
    normed = low(norm_rows(rows_in, ln1_gain, ln1_bias))
    query = round_both(highest(normed, w_qkv[0]) + qv_bias[0])
    key_rows = round_both(highest(normed, w_qkv[1]))
    value_rows = round_both(highest(normed, w_qkv[2]) + qv_bias[1])
    query_heads = query.reshape(slot_count, HEADS, HEAD_DIM).transpose(1, 0, 2)
    key_heads = key_rows.reshape(slot_count, HEADS, HEAD_DIM).transpose(1, 0, 2)
    value_heads = value_rows.reshape(slot_count, HEADS, HEAD_DIM).transpose(1, 0, 2)
    scores = jnp.einsum('hqd,hkd->hqk', query_heads, key_heads, precision=lax.Precision.HIGHEST)
    scores = low_back(scores * HEAD_DIM ** (-0.5))
    allowed = image_ids[:, None] == image_ids[None, :]
    scores = jnp.where(allowed[None, :, :], scores, -1e+30)
    peak = lax.optimization_barrier(jnp.max(scores, axis=2, keepdims=True))
    expo_rows = jnp.exp(scores - peak)
    prob_rows = low(expo_rows / lax.optimization_barrier(jnp.sum(expo_rows, axis=2, keepdims=True)))
    mixed = jnp.einsum('hqk,hkd->hqd', prob_rows, value_heads, precision=lax.Precision.HIGHEST)
    attn_out = round_both(mixed.transpose(1, 0, 2).reshape(slot_count, HEADS * HEAD_DIM))
    resid = rows_in + low_back(highest(attn_out, w_out) + out_bias)
    normed_two = low(norm_rows(resid, ln2_gain, ln2_bias))
    hidden = low_back(highest(normed_two, w_fc1) + fc1_bias)
    active = low(gelu_tanh(hidden))
    return resid + low_back(highest(active, w_fc2) + fc2_bias)

def reference(layer_input, token_image, cotangent, ln1_gain, ln1_bias, w_qkv, qv_bias, w_out, out_bias, ln2_gain, ln2_bias, w_fc1, fc1_bias, w_fc2, fc2_bias):
    groups = layer_input.shape[0] // SLOTS
    rows_all = layer_input.astype(jnp.float32).reshape(groups, SLOTS, D)
    image_ids = token_image.reshape(groups, SLOTS)
    valid_mask = (image_ids < IMAGES).astype(jnp.float32)
    grad_out = cotangent.astype(jnp.float32).reshape(groups, SLOTS, D) * valid_mask[:, :, None]
    params = tuple((param_value.astype(jnp.float32) for param_value in (ln1_gain, ln1_bias, w_qkv, qv_bias, w_out, out_bias, ln2_gain, ln2_bias, w_fc1, fc1_bias, w_fc2, fc2_bias)))
    checked = jax.checkpoint(group_forward)

    def whole_layer(rows_in, weights):

        def one_group(group_entry):
            return checked(group_entry[0], group_entry[1], weights)
        return lax.map(one_group, (rows_in, image_ids))
    result, pull_back = jax.vjp(whole_layer, rows_all, params)
    input_grad, weight_grads = pull_back(grad_out)
    return (result.reshape(groups * SLOTS, D).astype(jnp.bfloat16), input_grad.reshape(groups * SLOTS, D), weight_grads[0], weight_grads[1], weight_grads[2], weight_grads[3], weight_grads[4], weight_grads[5], weight_grads[6], weight_grads[7], weight_grads[8], weight_grads[9], weight_grads[10], weight_grads[11])
```

```python
import functools

import jax
import jax.numpy as jnp
from jax import lax
from jax.experimental import pallas as pl
from jax.experimental.pallas import tpu as pltpu
from jax.sharding import PartitionSpec as P

HEAD_DIM = 72
LOG2E = 1.4426950408889634
VMEM_BYTES = 60 * 1024 * 1024
IMAGES = 2


layer_eps = 1e-06
gelu_scale = 0.7978845608028654


def gelu_tanh(values):
    return (
        0.5 * values * (1.0 + jnp.tanh(gelu_scale * (values + 0.044715 * values * values * values)))
    )


def norm_rows(values, gain, shift):
    centre = values - jnp.mean(values, axis=1, keepdims=True)
    spread = jnp.mean(centre * centre, axis=1, keepdims=True)
    return centre * lax.rsqrt(spread + layer_eps) * gain + shift


def contract_rows(left, right):
    return lax.dot_general(
        left, right, (((0,), (0,)), ((), ())), preferred_element_type=jnp.float32
    )


def contract_cols(left, right):
    return lax.dot_general(
        left, right, (((1,), (1,)), ((), ())), preferred_element_type=jnp.float32
    )


def split_heads(values, head_count):
    slot_count = values.shape[0]
    return values.reshape(slot_count, head_count, -1).transpose(1, 0, 2)


def join_heads(values):
    head_count, slot_count, head_size = values.shape
    return values.transpose(1, 0, 2).reshape(slot_count, head_count * head_size)


def block_rows(slot_count):
    half_rows = slot_count // 2
    return half_rows


def masked_scores(rows_query, head_keys, rows_ids, image_ids, score_scale):
    scores = contract_cols(rows_query, head_keys) * score_scale
    return jnp.where(rows_ids[:, None] == image_ids[None, :], scores, -1e30)


def heads_forward(query_heads, key_heads, value_heads, image_ids, score_scale):
    slot_count, head_size = (query_heads.shape[1], query_heads.shape[2])
    block_size = block_rows(slot_count)
    block_count = slot_count // block_size
    id_blocks = image_ids.reshape(block_count, block_size)

    def one_head(head_inputs):
        head_query, head_keys, head_values = head_inputs

        def one_block(block_inputs):
            rows_query, rows_ids = block_inputs
            scores = masked_scores(rows_query, head_keys, rows_ids, image_ids, score_scale)
            peak = jnp.max(scores, axis=1, keepdims=True)
            expo_rows = jnp.exp(scores - peak)
            row_total = jnp.sum(expo_rows, axis=1, keepdims=True)
            prob_rows = (expo_rows / row_total).astype(jnp.bfloat16)
            mixed = jnp.dot(prob_rows, head_values, preferred_element_type=jnp.float32)
            return (mixed.astype(jnp.bfloat16), peak[:, 0] + jnp.log(row_total[:, 0]))

        mixed, logsum = lax.map(
            one_block, (head_query.reshape(block_count, block_size, head_size), id_blocks)
        )
        return (mixed.reshape(slot_count, head_size), logsum.reshape(slot_count))

    return lax.map(one_head, (query_heads, key_heads, value_heads))


def heads_backward(query_heads, key_heads, value_heads, grad_heads, logsum, image_ids, score_scale):
    slot_count, head_size = (query_heads.shape[1], query_heads.shape[2])
    block_size = block_rows(slot_count)
    block_count = slot_count // block_size
    id_blocks = image_ids.reshape(block_count, block_size)

    def one_head(head_inputs):
        head_query, head_keys, head_values, head_grad, head_logsum = head_inputs

        def one_block(carried, block_inputs):
            key_sum, value_sum = carried
            rows_query, rows_grad, rows_logsum, rows_ids = block_inputs
            scores = masked_scores(rows_query, head_keys, rows_ids, image_ids, score_scale)
            prob_rows = jnp.exp(scores - rows_logsum[:, None])
            value_sum = value_sum + contract_rows(prob_rows.astype(jnp.bfloat16), rows_grad)
            grad_probs = contract_cols(rows_grad, head_values)
            centre = jnp.sum(grad_probs * prob_rows, axis=1, keepdims=True)
            grad_scores = (prob_rows * (grad_probs - centre)).astype(jnp.bfloat16)
            rows_dq = (
                jnp.dot(grad_scores, head_keys, preferred_element_type=jnp.float32) * score_scale
            ).astype(jnp.bfloat16)
            key_sum = key_sum + contract_rows(grad_scores, rows_query) * score_scale
            return ((key_sum, value_sum), rows_dq)

        zeros_init = jnp.zeros((slot_count, head_size), jnp.float32)
        block_inputs = (
            head_query.reshape(block_count, block_size, head_size),
            head_grad.reshape(block_count, block_size, head_size),
            head_logsum.reshape(block_count, block_size),
            id_blocks,
        )
        (key_sum, value_sum), query_grad = lax.scan(
            one_block, (zeros_init, zeros_init), block_inputs
        )
        return (
            query_grad.reshape(slot_count, head_size),
            key_sum.astype(jnp.bfloat16),
            value_sum.astype(jnp.bfloat16),
        )

    return lax.map(one_head, (query_heads, key_heads, value_heads, grad_heads, logsum))


def forward_pass(inputs, full_output):
    (
        layer_input,
        token_image,
        ln1_gain,
        ln1_bias,
        w_qkv,
        qv_bias,
        w_out,
        out_bias,
        ln2_gain,
        ln2_bias,
        w_fc1,
        fc1_bias,
        w_fc2,
        fc2_bias,
    ) = inputs
    head_count = w_qkv.shape[2] // HEAD_DIM
    score_scale = HEAD_DIM ** (-0.5)
    attn_params = (
        lax.all_gather(ln1_gain, "dp", axis=0, tiled=True),
        lax.all_gather(ln1_bias, "dp", axis=0, tiled=True),
        lax.all_gather(w_qkv, "dp", axis=1, tiled=True),
        lax.all_gather(w_out, "dp", axis=1, tiled=True),
        lax.all_gather(out_bias, "dp", axis=0, tiled=True),
    )
    mlp_params = (
        lax.all_gather(ln2_gain, "dp", axis=0, tiled=True),
        lax.all_gather(ln2_bias, "dp", axis=0, tiled=True),
        lax.all_gather(w_fc1, "dp", axis=0, tiled=True),
        lax.all_gather(w_fc2, "dp", axis=1, tiled=True),
        lax.all_gather(fc2_bias, "dp", axis=0, tiled=True),
    )
    input_rows = layer_input.astype(jnp.float32)
    normed = norm_rows(
        input_rows, attn_params[0].astype(jnp.float32), attn_params[1].astype(jnp.float32)
    )
    first_in = lax.all_gather(normed.astype(jnp.bfloat16), "tensor", axis=0, tiled=True)
    projected = jnp.einsum(
        "sd,cde->cse", first_in, attn_params[2], preferred_element_type=jnp.float32
    )
    bias_rows = qv_bias.astype(jnp.float32)
    query_heads = split_heads((projected[0] + bias_rows[0]).astype(jnp.bfloat16), head_count)
    key_heads = split_heads(projected[1].astype(jnp.bfloat16), head_count)
    value_heads = split_heads((projected[2] + bias_rows[1]).astype(jnp.bfloat16), head_count)
    mixed, logsum = heads_forward(query_heads, key_heads, value_heads, token_image, score_scale)
    attn_out = join_heads(mixed)
    resid = (
        input_rows
        + lax.psum_scatter(
            jnp.dot(attn_out, attn_params[3], preferred_element_type=jnp.float32),
            "tensor",
            scatter_dimension=0,
            tiled=True,
        )
        + attn_params[4].astype(jnp.float32)
    )
    normed_two = norm_rows(
        resid, mlp_params[0].astype(jnp.float32), mlp_params[1].astype(jnp.float32)
    )
    second_in = lax.all_gather(normed_two.astype(jnp.bfloat16), "tensor", axis=0, tiled=True)
    hidden = jnp.dot(
        second_in, mlp_params[2], preferred_element_type=jnp.float32
    ) + fc1_bias.astype(jnp.float32)
    active = gelu_tanh(hidden).astype(jnp.bfloat16)
    layer_output = None
    if full_output:
        summed = lax.psum_scatter(
            jnp.dot(active, mlp_params[3], preferred_element_type=jnp.float32).astype(jnp.bfloat16),
            "tensor",
            scatter_dimension=0,
            tiled=True,
        ).astype(jnp.float32)
        layer_output = (resid + summed + mlp_params[4].astype(jnp.float32)).astype(jnp.bfloat16)
    return (
        attn_params,
        mlp_params,
        input_rows,
        first_in,
        query_heads,
        key_heads,
        value_heads,
        logsum,
        attn_out,
        resid,
        second_in,
        hidden,
        active,
        layer_output,
    )


def shards(
    layer_input,
    token_image,
    cotangent,
    ln1_gain,
    ln1_bias,
    w_qkv,
    qv_bias,
    w_out,
    out_bias,
    ln2_gain,
    ln2_bias,
    w_fc1,
    fc1_bias,
    w_fc2,
    fc2_bias,
):
    inputs = (
        layer_input,
        token_image,
        ln1_gain,
        ln1_bias,
        w_qkv,
        qv_bias,
        w_out,
        out_bias,
        ln2_gain,
        ln2_bias,
        w_fc1,
        fc1_bias,
        w_fc2,
        fc2_bias,
    )
    first_pass = forward_pass(inputs, True)
    layer_output = first_pass[13]
    fenced = lax.optimization_barrier((layer_output, inputs))[1]
    saved = forward_pass(fenced, False)
    (
        attn_params,
        mlp_params,
        input_rows,
        first_in,
        query_heads,
        key_heads,
        value_heads,
        logsum,
        attn_out,
        resid,
        second_in,
        hidden,
        active,
        unused_output,
    ) = saved
    score_scale = HEAD_DIM ** (-0.5)
    row_count = layer_input.shape[0]
    tensor_at = lax.axis_index("tensor")
    image_rows = lax.dynamic_slice_in_dim(token_image, tensor_at * row_count, row_count)
    valid_mask = (image_rows < IMAGES).astype(jnp.float32)
    grad_rows = cotangent.astype(jnp.float32) * valid_mask[:, None]
    grad_low = grad_rows.astype(jnp.bfloat16)
    grad_all = lax.all_gather(grad_low, "tensor", axis=0, tiled=True)
    grad_active = contract_cols(grad_all, mlp_params[3])
    grad_hidden = jax.vjp(gelu_tanh, hidden)[1](grad_active)[0].astype(jnp.bfloat16)
    fc2_grad = contract_rows(active, grad_all)
    fc1_grad = contract_rows(second_in, grad_hidden)
    grad_normed_two = lax.psum_scatter(
        contract_cols(grad_hidden, mlp_params[2]), "tensor", scatter_dimension=0, tiled=True
    )
    norm_two_back = jax.vjp(
        norm_rows, resid, mlp_params[0].astype(jnp.float32), mlp_params[1].astype(jnp.float32)
    )[1]
    resid_part, ln2_gain_sum, ln2_bias_sum = norm_two_back(grad_normed_two)
    grad_resid = grad_rows + resid_part
    resid_low = grad_resid.astype(jnp.bfloat16)
    resid_all = lax.all_gather(resid_low, "tensor", axis=0, tiled=True)
    out_grad = contract_rows(attn_out, resid_all)
    grad_attn = contract_cols(resid_all, attn_params[3]).astype(jnp.bfloat16)
    head_count = query_heads.shape[0]
    grad_query, grad_keys, grad_values = heads_backward(
        query_heads,
        key_heads,
        value_heads,
        split_heads(grad_attn, head_count),
        logsum,
        token_image,
        score_scale,
    )
    grad_qkv = jnp.stack([join_heads(grad_query), join_heads(grad_keys), join_heads(grad_values)])
    qkv_grad = jnp.einsum("sd,cse->cde", first_in, grad_qkv, preferred_element_type=jnp.float32)
    grad_normed = lax.psum_scatter(
        jnp.einsum("cse,cde->sd", grad_qkv, attn_params[2], preferred_element_type=jnp.float32),
        "tensor",
        scatter_dimension=0,
        tiled=True,
    )
    norm_one_back = jax.vjp(
        norm_rows,
        input_rows,
        attn_params[0].astype(jnp.float32),
        attn_params[1].astype(jnp.float32),
    )[1]
    input_part, ln1_gain_sum, ln1_bias_sum = norm_one_back(grad_normed)
    input_grad = grad_resid + input_part
    qkv_piece, out_piece, fc1_piece, fc2_piece = (
        lax.psum_scatter(qkv_grad, "dp", scatter_dimension=1, tiled=True),
        lax.psum_scatter(out_grad, "dp", scatter_dimension=1, tiled=True),
        lax.psum_scatter(fc1_grad, "dp", scatter_dimension=0, tiled=True),
        lax.psum_scatter(fc2_grad, "dp", scatter_dimension=1, tiled=True),
    )
    full_width = layer_input.shape[1]
    head_width = qv_bias.shape[1]
    ff_width = fc1_bias.shape[0]
    row_sums = jnp.stack(
        [
            ln1_gain_sum,
            ln1_bias_sum,
            jnp.sum(resid_low.astype(jnp.float32), axis=0),
            ln2_gain_sum,
            ln2_bias_sum,
            jnp.sum(grad_rows, axis=0),
        ]
    )
    qv_sums = jnp.stack(
        [
            jnp.sum(grad_qkv[0].astype(jnp.float32), axis=0),
            jnp.sum(grad_qkv[2].astype(jnp.float32), axis=0),
        ]
    )
    qv_wide = lax.dynamic_update_slice_in_dim(
        jnp.zeros((2, full_width), jnp.float32), qv_sums, tensor_at * head_width, 1
    )
    fc1_sums = jnp.sum(grad_hidden.astype(jnp.float32), axis=0)
    fc1_wide = lax.dynamic_update_slice_in_dim(
        jnp.zeros((ff_width * lax.axis_size("tensor"),), jnp.float32),
        fc1_sums,
        tensor_at * ff_width,
        0,
    )
    row_total, qv_total, fc1_total = lax.psum((row_sums, qv_wide, fc1_wide), ("dp", "tensor"))
    dp_width = ln1_gain.shape[0]
    row_piece = lax.dynamic_slice_in_dim(row_total, lax.axis_index("dp") * dp_width, dp_width, 1)
    qv_piece = lax.dynamic_slice_in_dim(qv_total, tensor_at * head_width, head_width, 1)
    fc1_bias_piece = lax.dynamic_slice_in_dim(fc1_total, tensor_at * ff_width, ff_width, 0)
    return (
        layer_output,
        input_grad,
        row_piece[0],
        row_piece[1],
        qkv_piece,
        qv_piece,
        out_piece,
        row_piece[2],
        row_piece[3],
        row_piece[4],
        fc1_piece,
        fc1_bias_piece,
        fc2_piece,
        row_piece[5],
    )


def head_window(head, width):
    start = head * HEAD_DIM
    first = start // 128 * 128
    last = min(first + 256, width)
    return start - first, first, last


def spare_lanes(offset):
    if offset >= 2:
        return 0, 1
    return 126, 127


def with_lanes(values, lane, offset, first_column, second_column):
    one, two = spare_lanes(offset)
    inside = (lane >= offset) & (lane < offset + HEAD_DIM)
    kept = jnp.where(inside, values, 0)
    kept = jnp.where(lane == one, first_column, kept)
    return jnp.where(lane == two, second_column, kept)


def only_head(values, lane, offset):
    inside = (lane >= offset) & (lane < offset + HEAD_DIM)
    return jnp.where(inside, values, 0)


def row_columns(kind):
    image = kind == 0
    padding = (kind == 1) | (kind == 2)
    low = jnp.bfloat16
    image_query = jnp.where(image, 1.0, 0.0).astype(low)
    other_query = jnp.where(image, 0.0, 1.0).astype(low)
    image_key = jnp.where(image, 0.0, -1e30).astype(low)
    padding_key = jnp.where(padding, 0.0, -1e30).astype(low)
    return image_query, other_query, image_key, padding_key


def dot_last(left, right):
    return lax.dot_general(left, right, (((1,), (1,)), ((), ())), preferred_element_type=jnp.float32)


def dot_first(left, right):
    return lax.dot_general(left, right, (((0,), (0,)), ((), ())), preferred_element_type=jnp.float32)


def forward_kernel(heads, width, block, kind_ref, block_kind_ref, qkv_ref, query_ref, out_ref, logsum_ref, keys_ref, values_ref, total_ref, log_ref):
    step = pl.program_id(0)
    scale = HEAD_DIM ** (-0.5) * LOG2E

    @pl.when(step == 0)
    def prepare():
        keys_ref[:, :width] = qkv_ref[:, width : 2 * width]
        values_ref[:, :width] = qkv_ref[:, 2 * width :]
        if keys_ref.shape[1] > width:
            blank = jnp.zeros((keys_ref.shape[0], keys_ref.shape[1] - width), keys_ref.dtype)
            keys_ref[:, width:] = blank
            values_ref[:, width:] = blank

    rows = keys_ref.shape[0]
    _, _, image_key, padding_key = row_columns(kind_ref[...])
    image_query, other_query, _, _ = row_columns(block_kind_ref[...])
    total_ref[...] = jnp.zeros_like(total_ref)
    log_ref[...] = jnp.zeros_like(log_ref)
    for head in range(heads):
        offset, first, last = head_window(head, width)
        lane = lax.broadcasted_iota(jnp.int32, (rows, last - first), 1)
        lane_q = lax.broadcasted_iota(jnp.int32, (block, last - first), 1)
        query = with_lanes(query_ref[:, first:last], lane_q, offset, image_query, other_query)
        keys = with_lanes(keys_ref[:, first:last], lane, offset, image_key, padding_key)
        values = only_head(values_ref[:, first:last], lane, offset)
        scores = dot_last(query, keys)
        peak = jnp.max(scores, axis=1, keepdims=True)
        expo = jnp.exp2((scores - peak) * scale)
        total = jnp.sum(expo, axis=1, keepdims=True)
        mixed = jnp.dot(expo.astype(jnp.bfloat16), values, preferred_element_type=jnp.float32)
        total_ref[:, first:last] += mixed * (1.0 / total)
        logsum = peak * scale + jnp.log2(total)
        lane_h = lax.broadcasted_iota(jnp.int32, log_ref.shape, 1)
        log_ref[...] = jnp.where(lane_h == head, logsum, log_ref[...])
    out_ref[...] = total_ref[...].astype(out_ref.dtype)
    logsum_ref[...] = jnp.transpose(log_ref[...])[: logsum_ref.shape[0], :]


def attention_forward(qkv, kind):
    rows, three = qkv.shape
    width = three // 3
    heads = width // HEAD_DIM
    block = 256
    padded = -(-width // 128) * 128
    return pl.pallas_call(
        functools.partial(forward_kernel, heads, width, block),
        grid=(rows // block,),
        in_specs=[
            pl.BlockSpec((rows, 1), lambda i: (0, 0)),
            pl.BlockSpec((block, 1), lambda i: (i, 0)),
            pl.BlockSpec((rows, three), lambda i: (0, 0)),
            pl.BlockSpec((block, three), lambda i: (i, 0)),
        ],
        out_specs=[
            pl.BlockSpec((block, width), lambda i: (i, 0)),
            pl.BlockSpec((8, block), lambda i: (0, i)),
        ],
        out_shape=[
            jax.ShapeDtypeStruct((rows, width), jnp.bfloat16),
            jax.ShapeDtypeStruct((8, rows), jnp.float32),
        ],
        scratch_shapes=[
            pltpu.VMEM((rows, padded), jnp.bfloat16),
            pltpu.VMEM((rows, padded), jnp.bfloat16),
            pltpu.VMEM((block, width), jnp.float32),
            pltpu.VMEM((block, 128), jnp.float32),
        ],
        compiler_params=pltpu.CompilerParams(vmem_limit_bytes=VMEM_BYTES),
        cost_estimate=pl.CostEstimate(flops=heads * 4 * rows * rows * 256, bytes_accessed=rows * three * 4, transcendentals=heads * rows * rows),
        name="attn_fwd",
    )(kind, kind, qkv, qkv)


def backward_kernel(heads, width, block, kind_ref, block_kind_ref, qkv_ref, query_ref, grad_ref, logsum_ref, out_ref, keys_ref, values_ref, key_sum, value_sum, query_sum):
    step = pl.program_id(0)
    last_step = pl.num_programs(0) - 1
    scale = HEAD_DIM ** (-0.5) * LOG2E
    score_scale = HEAD_DIM ** (-0.5)

    @pl.when(step == 0)
    def prepare():
        keys_ref[:, :width] = qkv_ref[:, width : 2 * width]
        values_ref[:, :width] = qkv_ref[:, 2 * width :]
        if keys_ref.shape[1] > width:
            blank = jnp.zeros((keys_ref.shape[0], keys_ref.shape[1] - width), keys_ref.dtype)
            keys_ref[:, width:] = blank
            values_ref[:, width:] = blank
        key_sum[...] = jnp.zeros_like(key_sum)
        value_sum[...] = jnp.zeros_like(value_sum)

    rows = keys_ref.shape[0]
    _, _, image_key, padding_key = row_columns(kind_ref[...])
    image_query, other_query, _, _ = row_columns(block_kind_ref[...])
    query_sum[...] = jnp.zeros_like(query_sum)
    for head in range(heads):
        offset, first, last = head_window(head, width)
        lane = lax.broadcasted_iota(jnp.int32, (rows, last - first), 1)
        lane_q = lax.broadcasted_iota(jnp.int32, (block, last - first), 1)
        query = only_head(query_ref[:, first:last], lane_q, offset)
        query_biased = with_lanes(query, lane_q, offset, image_query, other_query)
        keys = only_head(keys_ref[:, first:last], lane, offset)
        keys_biased = with_lanes(keys, lane, offset, image_key, padding_key)
        values = values_ref[:, first:last]
        grad = only_head(grad_ref[:, first:last], lane_q, offset)
        scores = dot_last(keys_biased, query_biased)
        probs = jnp.exp2(scores * scale - logsum_ref[head : head + 1, :])
        grad_probs = dot_last(values, grad)
        weighted = probs * grad_probs
        centre = jnp.sum(weighted, axis=0, keepdims=True)
        grad_scores = (weighted - probs * centre).astype(jnp.bfloat16)
        value_sum[:, first:last] += jnp.dot(probs.astype(jnp.bfloat16), grad, preferred_element_type=jnp.float32)
        key_sum[:, first:last] += jnp.dot(grad_scores, query, preferred_element_type=jnp.float32)
        query_sum[:, first:last] += dot_first(grad_scores, keys)
    low = out_ref.dtype
    out_ref[pl.ds(step * block, block), :width] = (query_sum[...] * score_scale).astype(low)

    @pl.when(step == last_step)
    def finish():
        out_ref[:, width : 2 * width] = (key_sum[...] * score_scale).astype(low)
        out_ref[:, 2 * width :] = value_sum[...].astype(low)


def attention_backward(qkv, kind, grad, logsum):
    rows, three = qkv.shape
    width = three // 3
    heads = width // HEAD_DIM
    block = 256
    padded = -(-width // 128) * 128
    return pl.pallas_call(
        functools.partial(backward_kernel, heads, width, block),
        grid=(rows // block,),
        in_specs=[
            pl.BlockSpec((rows, 1), lambda i: (0, 0)),
            pl.BlockSpec((block, 1), lambda i: (i, 0)),
            pl.BlockSpec((rows, three), lambda i: (0, 0)),
            pl.BlockSpec((block, three), lambda i: (i, 0)),
            pl.BlockSpec((block, width), lambda i: (i, 0)),
            pl.BlockSpec((8, block), lambda i: (0, i)),
        ],
        out_specs=pl.BlockSpec((rows, three), lambda i: (0, 0)),
        out_shape=jax.ShapeDtypeStruct((rows, three), jnp.bfloat16),
        scratch_shapes=[
            pltpu.VMEM((rows, padded), jnp.bfloat16),
            pltpu.VMEM((rows, padded), jnp.bfloat16),
            pltpu.VMEM((rows, width), jnp.float32),
            pltpu.VMEM((rows, width), jnp.float32),
            pltpu.VMEM((block, width), jnp.float32),
        ],
        compiler_params=pltpu.CompilerParams(vmem_limit_bytes=VMEM_BYTES),
        cost_estimate=pl.CostEstimate(flops=heads * 10 * rows * rows * 256, bytes_accessed=rows * three * 6, transcendentals=heads * rows * rows),
        name="attn_bwd",
    )(kind, kind, qkv, qkv, grad, logsum)


PATCHES = 729
AXES = ("dp", "tensor")


def dual_kernel(spot_ref, left_one, left_two, right_one, right_two, near, *far):
    step = pl.program_id(0)
    side = spot_ref[0] ^ step
    depth, _, high, rows = left_one.shape
    total = None
    for left, right in ((left_one, right_one), (left_two, right_two)):
        strip = left[:, pl.ds(side, 1)].reshape(depth * high, rows)
        product = jnp.dot(strip, right[...], preferred_element_type=jnp.float32)
        total = product if total is None else total + product
    total = total.astype(near.dtype).reshape(depth, high, -1)

    @pl.when(step == 0)
    def write_near():
        near[...] = total

    @pl.when(step == 1)
    def write_far():
        start = 0
        for out in far:
            out[...] = total[start : start + out.shape[0]]
            start += out.shape[0]


def dual_product(x_at, left_one, left_two, right_one, right_two, sizes):
    depth, _, high, rows = left_one.shape
    columns = right_one.shape[1]
    left = pl.BlockSpec(left_one.shape, lambda i: (0, 0, 0, 0))
    right = pl.BlockSpec((rows, columns), lambda i: (0, 0))
    return pl.pallas_call(
        dual_kernel,
        grid=(2,),
        in_specs=[pl.BlockSpec(memory_space=pltpu.SMEM), left, left, right, right],
        out_specs=[pl.BlockSpec((size, high, columns), lambda i: (0, 0, 0)) for size in sizes],
        out_shape=[jax.ShapeDtypeStruct((size, high, columns), jnp.bfloat16) for size in sizes],
        compiler_params=pltpu.CompilerParams(vmem_limit_bytes=VMEM_BYTES),
        cost_estimate=pl.CostEstimate(
            flops=8 * depth * high * rows * columns,
            bytes_accessed=4 * rows * (2 * depth * high + columns) + 4 * depth * high * columns,
            transcendentals=0,
        ),
        name="weight_grad",
    )(x_at, left_one, left_two, right_one, right_two)


class Grid:
    def __init__(self, depth):
        self.depth = depth
        dp_at = lax.axis_index("dp")
        self.y = lax.axis_index("tensor")
        self.c = dp_at % 2
        self.x = dp_at // 2 % 2
        self.z = dp_at // 4

    def move(self, values, where):
        pairs = []
        for z in range(self.depth):
            for x in range(2):
                for c in range(2):
                    for y in range(2):
                        to_z, to_x, to_c, to_y = where(z, x, c, y)
                        pairs.append(
                            (
                                ((z * 2 + x) * 2 + c) * 2 + y,
                                ((to_z * 2 + to_x) * 2 + to_c) * 2 + to_y,
                            )
                        )
        return lax.ppermute(values, AXES, pairs)

    def over_x(self, values):
        return self.move(values, lambda z, x, c, y: (z, 1 - x, c, y))

    def over_y(self, values):
        return self.move(values, lambda z, x, c, y: (z, x, c, 1 - y))

    def over_core(self, values):
        return self.move(values, lambda z, x, c, y: (z, x, 1 - c, y))

    def along_z(self, values, hops):
        return self.move(values, lambda z, x, c, y: ((z + hops) % self.depth, x, c, y))

    def across_z(self, values, bit):
        return self.move(values, lambda z, x, c, y: (z ^ bit, x, c, y))

    def spread(self, block):
        width = block.shape[1] // 2
        mine = lax.dynamic_slice_in_dim(block, self.c * width, width, 1)
        theirs = self.over_core(
            lax.dynamic_slice_in_dim(block, (1 - self.c) * width, width, 1)
        )
        first = jnp.where(self.c == 0, mine, theirs)
        second = jnp.where(self.c == 0, theirs, mine)
        return jnp.concatenate([first, second])

    def gather(self, block):
        depth = self.depth
        half = depth // 2
        block = self.spread(block)[None]
        came = [block] + [self.along_z(block, hops) for hops in range(1, depth)]
        came = came[::-1]
        own = lax.dynamic_slice_in_dim(
            jnp.concatenate(came + came[:-1]), depth - 1 - self.z, depth
        )
        beside = self.over_x(own)
        across = self.over_y(own)
        corner = [self.over_y(beside[:half]), self.over_x(across[half:])]
        groups = [(own, beside), (across, jnp.concatenate(corner))]
        other = [
            (self.over_core(own), self.over_core(beside)),
            (
                self.over_core(across),
                jnp.concatenate([self.over_core(corner[0]), self.over_core(corner[1])]),
            ),
        ]
        return [groups[0], other[0], groups[1], other[1]]

    def assemble(self, group):
        near, far = group
        first = jnp.where(self.x == 0, near, far)
        second = jnp.where(self.x == 0, far, near)
        return jnp.stack([first, second], axis=1).reshape(-1, near.shape[-1])

    def scatter(self, own, beside, across, corner):
        depth = self.depth
        half = depth // 2
        low = jnp.bfloat16
        wide = jnp.float32

        def add(one, two):
            return (one.astype(wide) + two.astype(wide)).astype(low)

        corner_one = self.over_x(corner[0])
        corner_two = self.over_y(corner[1])
        beside = jnp.concatenate([beside[:half], add(beside[half:], corner_two)])
        across = jnp.concatenate([add(across[:half], corner_one), across[half:]])
        total = (
            own.astype(wide)
            + self.over_x(beside).astype(wide)
            + self.over_y(across).astype(wide)
        ).astype(low)
        result = lax.dynamic_index_in_dim(total, self.z, 0, keepdims=False).astype(wide)
        for hops in range(1, depth):
            part = lax.dynamic_index_in_dim(total, (self.z + hops) % depth, 0, keepdims=False)
            result = result + self.along_z(part, hops).astype(wide)
        shard = result.shape[0] // 2
        mine = lax.dynamic_slice_in_dim(result, self.c * shard, shard)
        theirs = self.over_core(
            lax.dynamic_slice_in_dim(result, (1 - self.c) * shard, shard)
        )
        first = jnp.where(self.c == 0, mine, theirs)
        second = jnp.where(self.c == 0, theirs, mine)
        return jnp.stack([first, second])

    def reduce_all(self, values):
        values = values + self.over_core(values)
        values = values + self.over_x(values)
        values = values + self.over_y(values)
        bit = 1
        while bit < self.depth:
            values = values + self.across_z(values, bit)
            bit *= 2
        return values


def norm_parts(values):
    centre = values - jnp.mean(values, axis=1, keepdims=True)
    spread = jnp.mean(centre * centre, axis=1, keepdims=True)
    root = lax.rsqrt(spread + layer_eps)
    return centre * root, root


def norm_back(unit, root, gain, grad):
    scaled = grad * gain
    mean_one = jnp.mean(scaled, axis=1, keepdims=True)
    mean_two = jnp.mean(scaled * unit, axis=1, keepdims=True)
    return (
        root * (scaled - mean_one - unit * mean_two),
        jnp.sum(grad * unit, axis=0),
        jnp.sum(grad, axis=0),
    )


def gelu_slope(values):
    inner = jnp.tanh(gelu_scale * (values + 0.044715 * values * values * values))
    slope = gelu_scale * (1.0 + 3.0 * 0.044715 * values * values)
    return 0.5 * (1.0 + inner) + 0.5 * values * (1.0 - inner * inner) * slope


def image_shards(
    depth,
    layer_input,
    token_image,
    cotangent,
    ln1_gain,
    ln1_bias,
    w_qkv,
    qv_bias,
    w_out,
    out_bias,
    ln2_gain,
    ln2_bias,
    w_fc1,
    fc1_bias,
    w_fc2,
    fc2_bias,
):
    low = jnp.bfloat16
    wide = jnp.float32
    grid = Grid(depth)
    rows, full_width = layer_input.shape
    shard = ln1_gain.shape[0]
    head_width = qv_bias.shape[1]
    ff_width = fc1_bias.shape[0]
    padded = -(-(rows + 1) // 256) * 256

    here = grid.y
    mine = lax.dynamic_slice_in_dim(token_image, here * rows, rows)
    theirs = lax.dynamic_slice_in_dim(token_image, (1 - here) * rows, rows)
    places = lax.iota(jnp.int32, rows)
    stray = mine == 1 - here
    stray_here = jnp.any(stray)
    stray_there = jnp.any(theirs == here)
    blank = mine == IMAGES
    first_blank = jnp.min(jnp.where(blank, places, rows - 1))
    last_blank = jnp.max(jnp.where(blank, places, 0))
    swap_at = jnp.where(stray_here, jnp.max(jnp.where(stray, places, 0)), first_blank)
    swapped = stray_here | stray_there
    blank_at = jnp.where(stray_here, swap_at, last_blank)

    def one_row(values, at):
        return lax.dynamic_slice_in_dim(values, at, 1)

    sent = jnp.concatenate(
        [one_row(layer_input, swap_at), one_row(cotangent, swap_at), one_row(layer_input, last_blank)]
    )
    came = grid.over_y(sent)
    other_blank = jnp.where(stray_there, sent[0:1], came[2:3])
    spread_rows = lax.broadcasted_iota(jnp.int32, (padded, 1), 0)
    at_swap = (spread_rows == swap_at) & swapped

    def stretch(values):
        return jnp.pad(values, ((0, padded - rows), (0, 0)))

    input_rows = jnp.where(at_swap, came[0:1], stretch(layer_input))
    input_rows = jnp.where(spread_rows == rows, other_blank, input_rows)
    grad_low = jnp.where(at_swap, came[1:2], stretch(cotangent))
    grad_low = jnp.where(spread_rows == blank_at, 0, grad_low).astype(low)
    kind = jnp.where(spread_rows > rows, 3, jnp.where(spread_rows == rows, 2, 0))
    kind = jnp.where(spread_rows == blank_at, 1, kind)
    input_rows, grad_low = lax.optimization_barrier((input_rows, grad_low))

    quarter = head_width // 2
    group_width = 4 * quarter
    ff_padding = 2 * group_width - ff_width
    vectors = jnp.stack([ln1_gain, ln1_bias, out_bias, ln2_gain, ln2_bias, fc2_bias])
    vectors = lax.all_gather(vectors, "dp", axis=1, tiled=True).astype(wide)
    gain_one, shift_one, out_shift, gain_two, shift_two, fc2_shift = [
        vectors[i : i + 1] for i in range(6)
    ]
    biases = jnp.concatenate([qv_bias.reshape(-1), fc1_bias])
    biases = jnp.pad(biases, (0, -biases.shape[0] % 128)).reshape(-1, 128)
    other_biases = grid.over_y(biases).reshape(-1)

    def ordered(first, second):
        return jnp.where(grid.c == 0, first, second), jnp.where(grid.c == 0, second, first)

    qv_groups, fc1_groups = [], []
    for flat in (biases.reshape(-1), other_biases):
        flat = flat.astype(wide)
        pair = flat[: 2 * head_width].reshape(2, 2, quarter)
        none = jnp.zeros((quarter,), wide)
        qv_groups += ordered(
            *[jnp.concatenate([pair[0, i], none, pair[1, i]]) for i in range(2)]
        )
        hidden_bias = flat[2 * head_width : 2 * head_width + ff_width]
        hidden_bias = jnp.pad(hidden_bias, (0, ff_padding))
        fc1_groups += ordered(hidden_bias[:group_width], hidden_bias[group_width:])

    sources = [w_qkv[0], w_qkv[1], w_qkv[2], w_out.T]
    first_block = jnp.concatenate(
        [values[:, i * quarter : (i + 1) * quarter] for i in range(2) for values in sources],
        axis=1,
    )
    second_block = jnp.pad(w_fc1, ((0, 0), (0, ff_padding)))
    third_block = jnp.pad(w_fc2.T, ((0, 0), (0, ff_padding)))
    attn_weights = [grid.assemble(group) for group in grid.gather(first_block)]
    up_weights = [grid.assemble(group) for group in grid.gather(second_block)]
    down_weights = [grid.assemble(group) for group in grid.gather(third_block)]

    row_values = input_rows.astype(wide)
    unit_one, root_one = norm_parts(row_values)
    normed = (unit_one * gain_one + shift_one).astype(low)
    resid = row_values + out_shift
    qkv, mixed, logsums = [], [], []
    groups = range(4)
    inner = 3 * quarter
    for side in groups:
        projected = jnp.dot(normed, attn_weights[side][:, :inner], preferred_element_type=wide)
        qkv.append((projected + qv_groups[side]).astype(low))
        side_mixed, logsum = attention_forward(qkv[side], kind)
        mixed.append(side_mixed)
        logsums.append(logsum)
    out_weights = [weights[:, inner:] for weights in attn_weights]
    for side in groups:
        resid = resid + contract_cols(mixed[side], out_weights[side])

    unit_two, root_two = norm_parts(resid)
    normed_two = (unit_two * gain_two + shift_two).astype(low)
    hidden = [
        jnp.dot(normed_two, up_weights[side], preferred_element_type=wide) + fc1_groups[side]
        for side in groups
    ]
    active = [gelu_tanh(values).astype(low) for values in hidden]

    def turned(values):
        own = values.T.reshape(depth, 2, 2 * shard, padded)
        return own, grid.over_core(own)

    half = depth // 2
    x_spot = grid.x.reshape(1)

    def summed(left, sides):
        given = grid.over_core(jnp.stack([sides[1], sides[3]]))
        own, beside = dual_product(x_spot, *left, sides[0], given[0], (depth, depth))
        across, corner_one, corner_two = dual_product(
            x_spot, *left, sides[2], given[1], (depth, half, half)
        )
        return own, beside, across, (corner_one, corner_two)

    fc2_piece = grid.scatter(*summed(turned(grad_low), active))

    grad_hidden = []
    for side in groups:
        grad_active = jnp.dot(grad_low, down_weights[side], preferred_element_type=wide)
        grad_hidden.append((grad_active * gelu_slope(hidden[side])).astype(low))
    fc1_piece = grid.scatter(*summed(turned(normed_two), grad_hidden))
    layer_rows = resid + fc2_shift
    grad_normed_two = 0.0
    for side in groups:
        grad_normed_two = grad_normed_two + contract_cols(grad_hidden[side], up_weights[side])
        layer_rows = layer_rows + contract_cols(active[side], down_weights[side])
    layer_rows = layer_rows.astype(low)

    resid_part, ln2_gain_sum, ln2_bias_sum = norm_back(
        unit_two, root_two, gain_two, grad_normed_two
    )
    grad_resid = grad_low.astype(wide) + resid_part
    resid_low = grad_resid.astype(low)
    grad_qkv = []
    for side in groups:
        grad_attn = jnp.dot(resid_low, out_weights[side], preferred_element_type=wide).astype(low)
        grad_qkv.append(attention_backward(qkv[side], kind, grad_attn, logsums[side]))
    qkv_sums = summed(turned(normed), grad_qkv)
    out_sums = summed(turned(resid_low), mixed)
    joined = [
        jnp.concatenate([one, two], axis=2)
        for one, two in zip(qkv_sums[:3] + qkv_sums[3], out_sums[:3] + out_sums[3])
    ]
    attn_piece = grid.scatter(*joined[:3], joined[3:])
    grad_normed = 0.0
    for side in groups:
        grad_normed = grad_normed + contract_cols(grad_qkv[side], attn_weights[side][:, :inner])
    input_part, ln1_gain_sum, ln1_bias_sum = norm_back(unit_one, root_one, gain_one, grad_normed)
    input_grad = grad_resid + input_part

    returned = (
        grid.over_y(one_row(layer_rows, swap_at)),
        grid.over_y(one_row(input_grad, swap_at)),
    )
    layer_output = jnp.where(at_swap, returned[0], layer_rows)[:rows]
    input_grad = jnp.where(at_swap, returned[1], input_grad)[:rows]

    def column_sum(values):
        return jnp.sum(values.astype(wide), axis=0)

    def absolute(sums):
        grouped = jnp.stack(sums).reshape(2, 2, -1)
        grouped = jnp.where(here == 0, grouped, grouped[::-1])
        return jnp.where(grid.c == 0, grouped, grouped[:, ::-1])

    qkv_totals = absolute([column_sum(values) for values in grad_qkv])
    qkv_totals = qkv_totals.reshape(2, 2, 3, quarter)[:, :, 0::2].transpose(0, 2, 1, 3)
    fc1_totals = absolute([column_sum(values) for values in grad_hidden]).reshape(2, -1)
    flat = jnp.concatenate(
        [
            ln1_gain_sum,
            ln1_bias_sum,
            column_sum(resid_low),
            ln2_gain_sum,
            ln2_bias_sum,
            column_sum(grad_low),
            qkv_totals.reshape(-1),
            fc1_totals[:, :ff_width].reshape(-1),
        ]
    )
    length = flat.shape[0]
    lines = -(-length // 1024) * 8
    flat = jnp.pad(flat, (0, lines * 128 - length)).reshape(lines, 128)
    flat = grid.reduce_all(flat).reshape(-1)
    row_total = flat[: 6 * full_width].reshape(6, full_width)
    row_piece = lax.dynamic_slice_in_dim(row_total, lax.axis_index("dp") * shard, shard, 1)
    start = 6 * full_width
    qv_piece = lax.dynamic_slice_in_dim(flat, start + here * 2 * head_width, 2 * head_width)
    start = start + 4 * head_width
    fc1_bias_piece = lax.dynamic_slice_in_dim(flat, start + here * ff_width, ff_width)
    heads_piece = attn_piece.reshape(2, shard, 4, quarter).transpose(2, 1, 0, 3)
    heads_piece = heads_piece.reshape(4, shard, head_width)

    def whole_columns(pair):
        return jnp.concatenate([pair[0], pair[1][:, : group_width - ff_padding]], axis=1)

    return (
        layer_output,
        input_grad,
        row_piece[0],
        row_piece[1],
        heads_piece[:3],
        qv_piece.reshape(2, head_width),
        heads_piece[3].T,
        row_piece[2],
        row_piece[3],
        row_piece[4],
        whole_columns(fc1_piece),
        fc1_bias_piece,
        whole_columns(fc2_piece).T,
        row_piece[5],
    )


def fits_images(mesh):
    groups = mesh.shape["dp"] // 4
    return (
        mesh.shape["tensor"] == IMAGES
        and mesh.shape["dp"] % 4 == 0
        and groups >= 2
        and groups & (groups - 1) == 0
    )


def solution(mesh):
    in_specs = (
        P(("dp", "tensor"), None),
        P("dp"),
        P(("dp", "tensor"), None),
        P("dp"),
        P("dp"),
        P(None, "dp", "tensor"),
        P(None, "tensor"),
        P("tensor", "dp"),
        P("dp"),
        P("dp"),
        P("dp"),
        P("dp", "tensor"),
        P("tensor"),
        P("tensor", "dp"),
        P("dp"),
    )
    out_specs = (
        P(("dp", "tensor"), None),
        P(("dp", "tensor"), None),
        P("dp"),
        P("dp"),
        P(None, "dp", "tensor"),
        P(None, "tensor"),
        P("tensor", "dp"),
        P("dp"),
        P("dp"),
        P("dp"),
        P("dp", "tensor"),
        P("tensor"),
        P("tensor", "dp"),
        P("dp"),
    )

    def body(*arrays):
        slots = arrays[1].shape[0]
        if fits_images(mesh) and slots == IMAGES * (PATCHES + 1):
            return image_shards(mesh.shape["dp"] // 4, *arrays)
        return shards(*arrays)

    return jax.shard_map(body, mesh=mesh, in_specs=in_specs, out_specs=out_specs, check_vma=False)
```

```python
import functools

import jax
import jax.numpy as jnp
from jax import lax
from jax.experimental import pallas as pl
from jax.experimental.pallas import tpu as pltpu
from jax.sharding import PartitionSpec as P

HEAD_DIM = 72
LOG2E = 1.4426950408889634
VMEM_BYTES = 60 * 1024 * 1024
IMAGES = 2


layer_eps = 1e-06
gelu_scale = 0.7978845608028654


def gelu_tanh(values):
    return (
        0.5 * values * (1.0 + jnp.tanh(gelu_scale * (values + 0.044715 * values * values * values)))
    )


def norm_rows(values, gain, shift):
    centre = values - jnp.mean(values, axis=1, keepdims=True)
    spread = jnp.mean(centre * centre, axis=1, keepdims=True)
    return centre * lax.rsqrt(spread + layer_eps) * gain + shift


def contract_rows(left, right):
    return lax.dot_general(
        left, right, (((0,), (0,)), ((), ())), preferred_element_type=jnp.float32
    )


def contract_cols(left, right):
    return lax.dot_general(
        left, right, (((1,), (1,)), ((), ())), preferred_element_type=jnp.float32
    )


def split_heads(values, head_count):
    slot_count = values.shape[0]
    return values.reshape(slot_count, head_count, -1).transpose(1, 0, 2)


def join_heads(values):
    head_count, slot_count, head_size = values.shape
    return values.transpose(1, 0, 2).reshape(slot_count, head_count * head_size)


def block_rows(slot_count):
    half_rows = slot_count // 2
    return half_rows


def masked_scores(rows_query, head_keys, rows_ids, image_ids, score_scale):
    scores = contract_cols(rows_query, head_keys) * score_scale
    return jnp.where(rows_ids[:, None] == image_ids[None, :], scores, -1e30)


def heads_forward(query_heads, key_heads, value_heads, image_ids, score_scale):
    slot_count, head_size = (query_heads.shape[1], query_heads.shape[2])
    block_size = block_rows(slot_count)
    block_count = slot_count // block_size
    id_blocks = image_ids.reshape(block_count, block_size)

    def one_head(head_inputs):
        head_query, head_keys, head_values = head_inputs

        def one_block(block_inputs):
            rows_query, rows_ids = block_inputs
            scores = masked_scores(rows_query, head_keys, rows_ids, image_ids, score_scale)
            peak = jnp.max(scores, axis=1, keepdims=True)
            expo_rows = jnp.exp(scores - peak)
            row_total = jnp.sum(expo_rows, axis=1, keepdims=True)
            prob_rows = (expo_rows / row_total).astype(jnp.bfloat16)
            mixed = jnp.dot(prob_rows, head_values, preferred_element_type=jnp.float32)
            return (mixed.astype(jnp.bfloat16), peak[:, 0] + jnp.log(row_total[:, 0]))

        mixed, logsum = lax.map(
            one_block, (head_query.reshape(block_count, block_size, head_size), id_blocks)
        )
        return (mixed.reshape(slot_count, head_size), logsum.reshape(slot_count))

    return lax.map(one_head, (query_heads, key_heads, value_heads))


def heads_backward(query_heads, key_heads, value_heads, grad_heads, logsum, image_ids, score_scale):
    slot_count, head_size = (query_heads.shape[1], query_heads.shape[2])
    block_size = block_rows(slot_count)
    block_count = slot_count // block_size
    id_blocks = image_ids.reshape(block_count, block_size)

    def one_head(head_inputs):
        head_query, head_keys, head_values, head_grad, head_logsum = head_inputs

        def one_block(carried, block_inputs):
            key_sum, value_sum = carried
            rows_query, rows_grad, rows_logsum, rows_ids = block_inputs
            scores = masked_scores(rows_query, head_keys, rows_ids, image_ids, score_scale)
            prob_rows = jnp.exp(scores - rows_logsum[:, None])
            value_sum = value_sum + contract_rows(prob_rows.astype(jnp.bfloat16), rows_grad)
            grad_probs = contract_cols(rows_grad, head_values)
            centre = jnp.sum(grad_probs * prob_rows, axis=1, keepdims=True)
            grad_scores = (prob_rows * (grad_probs - centre)).astype(jnp.bfloat16)
            rows_dq = (
                jnp.dot(grad_scores, head_keys, preferred_element_type=jnp.float32) * score_scale
            ).astype(jnp.bfloat16)
            key_sum = key_sum + contract_rows(grad_scores, rows_query) * score_scale
            return ((key_sum, value_sum), rows_dq)

        zeros_init = jnp.zeros((slot_count, head_size), jnp.float32)
        block_inputs = (
            head_query.reshape(block_count, block_size, head_size),
            head_grad.reshape(block_count, block_size, head_size),
            head_logsum.reshape(block_count, block_size),
            id_blocks,
        )
        (key_sum, value_sum), query_grad = lax.scan(
            one_block, (zeros_init, zeros_init), block_inputs
        )
        return (
            query_grad.reshape(slot_count, head_size),
            key_sum.astype(jnp.bfloat16),
            value_sum.astype(jnp.bfloat16),
        )

    return lax.map(one_head, (query_heads, key_heads, value_heads, grad_heads, logsum))


def forward_pass(inputs, full_output):
    (
        layer_input,
        token_image,
        ln1_gain,
        ln1_bias,
        w_qkv,
        qv_bias,
        w_out,
        out_bias,
        ln2_gain,
        ln2_bias,
        w_fc1,
        fc1_bias,
        w_fc2,
        fc2_bias,
    ) = inputs
    head_count = w_qkv.shape[2] // HEAD_DIM
    score_scale = HEAD_DIM ** (-0.5)
    attn_params = (
        lax.all_gather(ln1_gain, "dp", axis=0, tiled=True),
        lax.all_gather(ln1_bias, "dp", axis=0, tiled=True),
        lax.all_gather(w_qkv, "dp", axis=1, tiled=True),
        lax.all_gather(w_out, "dp", axis=1, tiled=True),
        lax.all_gather(out_bias, "dp", axis=0, tiled=True),
    )
    mlp_params = (
        lax.all_gather(ln2_gain, "dp", axis=0, tiled=True),
        lax.all_gather(ln2_bias, "dp", axis=0, tiled=True),
        lax.all_gather(w_fc1, "dp", axis=0, tiled=True),
        lax.all_gather(w_fc2, "dp", axis=1, tiled=True),
        lax.all_gather(fc2_bias, "dp", axis=0, tiled=True),
    )
    input_rows = layer_input.astype(jnp.float32)
    normed = norm_rows(
        input_rows, attn_params[0].astype(jnp.float32), attn_params[1].astype(jnp.float32)
    )
    first_in = lax.all_gather(normed.astype(jnp.bfloat16), "tensor", axis=0, tiled=True)
    projected = jnp.einsum(
        "sd,cde->cse", first_in, attn_params[2], preferred_element_type=jnp.float32
    )
    bias_rows = qv_bias.astype(jnp.float32)
    query_heads = split_heads((projected[0] + bias_rows[0]).astype(jnp.bfloat16), head_count)
    key_heads = split_heads(projected[1].astype(jnp.bfloat16), head_count)
    value_heads = split_heads((projected[2] + bias_rows[1]).astype(jnp.bfloat16), head_count)
    mixed, logsum = heads_forward(query_heads, key_heads, value_heads, token_image, score_scale)
    attn_out = join_heads(mixed)
    resid = (
        input_rows
        + lax.psum_scatter(
            jnp.dot(attn_out, attn_params[3], preferred_element_type=jnp.float32),
            "tensor",
            scatter_dimension=0,
            tiled=True,
        )
        + attn_params[4].astype(jnp.float32)
    )
    normed_two = norm_rows(
        resid, mlp_params[0].astype(jnp.float32), mlp_params[1].astype(jnp.float32)
    )
    second_in = lax.all_gather(normed_two.astype(jnp.bfloat16), "tensor", axis=0, tiled=True)
    hidden = jnp.dot(
        second_in, mlp_params[2], preferred_element_type=jnp.float32
    ) + fc1_bias.astype(jnp.float32)
    active = gelu_tanh(hidden).astype(jnp.bfloat16)
    layer_output = None
    if full_output:
        summed = lax.psum_scatter(
            jnp.dot(active, mlp_params[3], preferred_element_type=jnp.float32).astype(jnp.bfloat16),
            "tensor",
            scatter_dimension=0,
            tiled=True,
        ).astype(jnp.float32)
        layer_output = (resid + summed + mlp_params[4].astype(jnp.float32)).astype(jnp.bfloat16)
    return (
        attn_params,
        mlp_params,
        input_rows,
        first_in,
        query_heads,
        key_heads,
        value_heads,
        logsum,
        attn_out,
        resid,
        second_in,
        hidden,
        active,
        layer_output,
    )


def shards(
    layer_input,
    token_image,
    cotangent,
    ln1_gain,
    ln1_bias,
    w_qkv,
    qv_bias,
    w_out,
    out_bias,
    ln2_gain,
    ln2_bias,
    w_fc1,
    fc1_bias,
    w_fc2,
    fc2_bias,
):
    inputs = (
        layer_input,
        token_image,
        ln1_gain,
        ln1_bias,
        w_qkv,
        qv_bias,
        w_out,
        out_bias,
        ln2_gain,
        ln2_bias,
        w_fc1,
        fc1_bias,
        w_fc2,
        fc2_bias,
    )
    first_pass = forward_pass(inputs, True)
    layer_output = first_pass[13]
    fenced = lax.optimization_barrier((layer_output, inputs))[1]
    saved = forward_pass(fenced, False)
    (
        attn_params,
        mlp_params,
        input_rows,
        first_in,
        query_heads,
        key_heads,
        value_heads,
        logsum,
        attn_out,
        resid,
        second_in,
        hidden,
        active,
        unused_output,
    ) = saved
    score_scale = HEAD_DIM ** (-0.5)
    row_count = layer_input.shape[0]
    tensor_at = lax.axis_index("tensor")
    image_rows = lax.dynamic_slice_in_dim(token_image, tensor_at * row_count, row_count)
    valid_mask = (image_rows < IMAGES).astype(jnp.float32)
    grad_rows = cotangent.astype(jnp.float32) * valid_mask[:, None]
    grad_low = grad_rows.astype(jnp.bfloat16)
    grad_all = lax.all_gather(grad_low, "tensor", axis=0, tiled=True)
    grad_active = contract_cols(grad_all, mlp_params[3])
    grad_hidden = jax.vjp(gelu_tanh, hidden)[1](grad_active)[0].astype(jnp.bfloat16)
    fc2_grad = contract_rows(active, grad_all)
    fc1_grad = contract_rows(second_in, grad_hidden)
    grad_normed_two = lax.psum_scatter(
        contract_cols(grad_hidden, mlp_params[2]), "tensor", scatter_dimension=0, tiled=True
    )
    norm_two_back = jax.vjp(
        norm_rows, resid, mlp_params[0].astype(jnp.float32), mlp_params[1].astype(jnp.float32)
    )[1]
    resid_part, ln2_gain_sum, ln2_bias_sum = norm_two_back(grad_normed_two)
    grad_resid = grad_rows + resid_part
    resid_low = grad_resid.astype(jnp.bfloat16)
    resid_all = lax.all_gather(resid_low, "tensor", axis=0, tiled=True)
    out_grad = contract_rows(attn_out, resid_all)
    grad_attn = contract_cols(resid_all, attn_params[3]).astype(jnp.bfloat16)
    head_count = query_heads.shape[0]
    grad_query, grad_keys, grad_values = heads_backward(
        query_heads,
        key_heads,
        value_heads,
        split_heads(grad_attn, head_count),
        logsum,
        token_image,
        score_scale,
    )
    grad_qkv = jnp.stack([join_heads(grad_query), join_heads(grad_keys), join_heads(grad_values)])
    qkv_grad = jnp.einsum("sd,cse->cde", first_in, grad_qkv, preferred_element_type=jnp.float32)
    grad_normed = lax.psum_scatter(
        jnp.einsum("cse,cde->sd", grad_qkv, attn_params[2], preferred_element_type=jnp.float32),
        "tensor",
        scatter_dimension=0,
        tiled=True,
    )
    norm_one_back = jax.vjp(
        norm_rows,
        input_rows,
        attn_params[0].astype(jnp.float32),
        attn_params[1].astype(jnp.float32),
    )[1]
    input_part, ln1_gain_sum, ln1_bias_sum = norm_one_back(grad_normed)
    input_grad = grad_resid + input_part
    qkv_piece, out_piece, fc1_piece, fc2_piece = (
        lax.psum_scatter(qkv_grad, "dp", scatter_dimension=1, tiled=True),
        lax.psum_scatter(out_grad, "dp", scatter_dimension=1, tiled=True),
        lax.psum_scatter(fc1_grad, "dp", scatter_dimension=0, tiled=True),
        lax.psum_scatter(fc2_grad, "dp", scatter_dimension=1, tiled=True),
    )
    full_width = layer_input.shape[1]
    head_width = qv_bias.shape[1]
    ff_width = fc1_bias.shape[0]
    row_sums = jnp.stack(
        [
            ln1_gain_sum,
            ln1_bias_sum,
            jnp.sum(resid_low.astype(jnp.float32), axis=0),
            ln2_gain_sum,
            ln2_bias_sum,
            jnp.sum(grad_rows, axis=0),
        ]
    )
    qv_sums = jnp.stack(
        [
            jnp.sum(grad_qkv[0].astype(jnp.float32), axis=0),
            jnp.sum(grad_qkv[2].astype(jnp.float32), axis=0),
        ]
    )
    qv_wide = lax.dynamic_update_slice_in_dim(
        jnp.zeros((2, full_width), jnp.float32), qv_sums, tensor_at * head_width, 1
    )
    fc1_sums = jnp.sum(grad_hidden.astype(jnp.float32), axis=0)
    fc1_wide = lax.dynamic_update_slice_in_dim(
        jnp.zeros((ff_width * lax.axis_size("tensor"),), jnp.float32),
        fc1_sums,
        tensor_at * ff_width,
        0,
    )
    row_total, qv_total, fc1_total = lax.psum((row_sums, qv_wide, fc1_wide), ("dp", "tensor"))
    dp_width = ln1_gain.shape[0]
    row_piece = lax.dynamic_slice_in_dim(row_total, lax.axis_index("dp") * dp_width, dp_width, 1)
    qv_piece = lax.dynamic_slice_in_dim(qv_total, tensor_at * head_width, head_width, 1)
    fc1_bias_piece = lax.dynamic_slice_in_dim(fc1_total, tensor_at * ff_width, ff_width, 0)
    return (
        layer_output,
        input_grad,
        row_piece[0],
        row_piece[1],
        qkv_piece,
        qv_piece,
        out_piece,
        row_piece[2],
        row_piece[3],
        row_piece[4],
        fc1_piece,
        fc1_bias_piece,
        fc2_piece,
        row_piece[5],
    )


def head_window(head, base, width):
    start = base + head * HEAD_DIM
    first = start // 128 * 128
    last = min(-(-(start + HEAD_DIM) // 128) * 128, width)
    return start - first, first, last


def only_head(values, lane, offset):
    inside = (lane >= offset) & (lane < offset + HEAD_DIM)
    return jnp.where(inside, values, 0)


def with_lanes(values, lane, offset, first_column, second_column):
    one, two = (0, 1) if offset >= 2 else (126, 127)
    values = jnp.where(lane == one, first_column, values)
    return jnp.where(lane == two, second_column, values)


def lane_index(rows, first, last):
    return lax.broadcasted_iota(jnp.int32, (rows, last - first), 1)


def row_columns(kind):
    image = kind == 0
    padding = (kind == 1) | (kind == 2)
    low = jnp.bfloat16
    image_query = jnp.where(image, 1.0, 0.0).astype(low)
    other_query = jnp.where(image, 0.0, 1.0).astype(low)
    image_key = jnp.where(image, 0.0, -1e30).astype(low)
    padding_key = jnp.where(padding, 0.0, -1e30).astype(low)
    return image_query, other_query, image_key, padding_key


def dot_last(left, right):
    return lax.dot_general(
        left, right, (((1,), (1,)), ((), ())), preferred_element_type=jnp.float32
    )


def dot_first(left, right):
    return lax.dot_general(
        left, right, (((0,), (0,)), ((), ())), preferred_element_type=jnp.float32
    )


def split_rows(rows):
    return [(start, min(start + 256, rows)) for start in range(0, rows, 256)]


def heads_forward_kernel(places, heads, spot, kind_ref, x_ref, bias_ref, *refs):
    count = sum(len(parts) for parts in places)
    pieces = refs[:count]
    qkv_ref, log_ref, own_ref, other_ref = refs[-10:-6]
    weights, sems, keys_ref, values_ref, total_ref, logs_ref = refs[-6:]
    step = pl.program_id(0)
    start_then_wait(weight_copies(places, pieces, weights, sems, spot[0]), step)
    scale = HEAD_DIM ** (-0.5) * LOG2E
    rows = x_ref.shape[0]
    part = heads * HEAD_DIM
    inner = qkv_ref.shape[2]
    width = keys_ref.shape[1]
    base = width - part
    projected = jnp.dot(
        x_ref[...], strips(weights, step)[:, :inner], preferred_element_type=jnp.float32
    )
    qkv_ref[0] = (projected + bias_ref[0]).astype(jnp.bfloat16)
    blank = jnp.zeros((rows, base), jnp.bfloat16)
    keys_ref[:, :part] = qkv_ref[0, :, part : 2 * part]
    keys_ref[:, part:] = blank
    values_ref[:, :base] = blank
    values_ref[:, base:] = qkv_ref[0, :, 2 * part : 3 * part]
    image_query, other_query, image_key, padding_key = row_columns(kind_ref[...])
    total_ref[...] = jnp.zeros_like(total_ref)
    logs_ref[...] = jnp.zeros_like(logs_ref)
    for head in range(heads):
        offset, first, last = head_window(head, 0, width)
        lane = lane_index(rows, first, last)
        keys = with_lanes(
            only_head(keys_ref[:, first:last], lane, offset), lane, offset, image_key, padding_key
        )
        query = with_lanes(
            only_head(qkv_ref[0, :, first:last], lane, offset),
            lane,
            offset,
            image_query,
            other_query,
        )
        v_offset, v_first, v_last = head_window(head, base, width)
        values = only_head(
            values_ref[:, v_first:v_last], lane_index(rows, v_first, v_last), v_offset
        )
        for start, stop in split_rows(rows):
            scores = dot_last(query[start:stop], keys)
            peak = jnp.max(scores, axis=1, keepdims=True)
            expo = jnp.exp2((scores - peak) * scale)
            total = jnp.sum(expo, axis=1, keepdims=True)
            mixed = jnp.dot(expo.astype(jnp.bfloat16), values, preferred_element_type=jnp.float32)
            total_ref[start:stop, v_first:v_last] += mixed * (1.0 / total)
            logsum = peak * scale + jnp.log2(total)
            lane_h = lax.broadcasted_iota(jnp.int32, (stop - start, logs_ref.shape[1]), 1)
            logs_ref[start:stop] = jnp.where(lane_h == head, logsum, logs_ref[start:stop])
    log_ref[0] = jnp.transpose(logs_ref[...])[: log_ref.shape[1], :]

    @pl.when(step == 0)
    def write_own():
        own_ref[...] = total_ref[...].astype(jnp.bfloat16)

    @pl.when(step == 1)
    def write_other():
        other_ref[...] = total_ref[...].astype(jnp.bfloat16)


def heads_forward_call(spot, kind, rows_in, biases, groups, waits=()):
    rows, full = rows_in.shape
    arrays, places = flatten(groups)
    _, high, group_width = arrays[0].shape
    depth = full // (2 * high)
    count = len(groups)
    part = group_width // 4
    heads = part // HEAD_DIM
    inner = -(-3 * part // 128) * 128
    outer = -(-part // 128) * 128
    side = pl.BlockSpec((rows, outer), lambda i: (0, 0))
    return pl.pallas_call(
        functools.partial(heads_forward_kernel, places, heads),
        grid=(count,),
        in_specs=[
            smem_spec(),
            pl.BlockSpec((rows, 1), lambda i: (0, 0)),
            pl.BlockSpec((rows, full), lambda i: (0, 0)),
            pl.BlockSpec((1, 1, inner), lambda i: (i, 0, 0)),
        ]
        + [any_spec()] * (len(arrays) + len(waits)),
        out_specs=[
            pl.BlockSpec((1, rows, inner), lambda i: (i, 0, 0)),
            pl.BlockSpec((1, 8, rows), lambda i: (i, 0, 0)),
            side,
            side,
        ],
        out_shape=[
            jax.ShapeDtypeStruct((count, rows, inner), jnp.bfloat16),
            jax.ShapeDtypeStruct((count, 8, rows), jnp.float32),
            jax.ShapeDtypeStruct((rows, outer), jnp.bfloat16),
            jax.ShapeDtypeStruct((rows, outer), jnp.bfloat16),
        ],
        scratch_shapes=weight_scratch(places, depth, high, group_width)
        + [
            pltpu.VMEM((rows, outer), jnp.bfloat16),
            pltpu.VMEM((rows, outer), jnp.bfloat16),
            pltpu.VMEM((rows, outer), jnp.float32),
            pltpu.VMEM((rows, 128), jnp.float32),
        ],
        compiler_params=limits(),
        cost_estimate=cost(18),
        name="heads_forward",
    )(spot, kind, rows_in, biases, *arrays, *waits)


def heads_backward_kernel(places, heads, spot, kind_ref, grad_ref, one_qkv, two_qkv, one_log, two_log, *refs):
    count = sum(len(parts) for parts in places)
    pieces = refs[:count]
    out_ref, sum_ref = refs[-11:-9]
    weights, sems, query_ref, keys_ref, values_ref, grads_ref, query_sum, key_sum, value_sum = refs[-9:]
    step = pl.program_id(0)
    width = keys_ref.shape[1]
    first_lane = pieces[0].shape[2] - width
    start_then_wait(weight_copies(places, pieces, weights, sems, spot[0], first_lane, width), step)
    score_scale = HEAD_DIM ** (-0.5)
    scale = score_scale * LOG2E
    rows = grad_ref.shape[0]
    part = heads * HEAD_DIM
    base = width - part
    blank = jnp.zeros((rows, base), jnp.bfloat16)

    def load(qkv_ref):
        query_ref[...] = qkv_ref[0, :, :width]
        keys_ref[:, :part] = qkv_ref[0, :, part : 2 * part]
        values_ref[:, base:] = qkv_ref[0, :, 2 * part : 3 * part]

    @pl.when(step == 0)
    def load_one():
        load(one_qkv)

    @pl.when(step == 1)
    def load_two():
        load(two_qkv)

    keys_ref[:, part:] = blank
    values_ref[:, :base] = blank
    logs = jnp.where(step == 0, one_log[0], two_log[0])
    grads_ref[...] = jnp.dot(
        grad_ref[...], strips(weights, step), preferred_element_type=jnp.float32
    ).astype(jnp.bfloat16)
    image_query, other_query, image_key, padding_key = row_columns(kind_ref[...])
    query_sum[...] = jnp.zeros_like(query_sum)
    key_sum[...] = jnp.zeros_like(key_sum)
    value_sum[...] = jnp.zeros_like(value_sum)
    for head in range(heads):
        offset, first, last = head_window(head, 0, width)
        lane = lane_index(rows, first, last)
        query = only_head(query_ref[:, first:last], lane, offset)
        query_biased = with_lanes(query, lane, offset, image_query, other_query)
        keys = only_head(keys_ref[:, first:last], lane, offset)
        keys_biased = with_lanes(keys, lane, offset, image_key, padding_key)
        v_offset, v_first, v_last = head_window(head, base, width)
        values = values_ref[:, v_first:v_last]
        grad = only_head(
            grads_ref[:, v_first:v_last], lane_index(rows, v_first, v_last), v_offset
        )
        for start, stop in split_rows(rows):
            scores = dot_last(keys_biased, query_biased[start:stop])
            probs = jnp.exp2(scores * scale - logs[head : head + 1, start:stop])
            grad_probs = dot_last(values, grad[start:stop])
            weighted = probs * grad_probs
            centre = jnp.sum(weighted, axis=0, keepdims=True)
            grad_scores = (weighted - probs * centre).astype(jnp.bfloat16)
            value_sum[:, v_first:v_last] += jnp.dot(
                probs.astype(jnp.bfloat16), grad[start:stop], preferred_element_type=jnp.float32
            )
            key_sum[:, first:last] += jnp.dot(
                grad_scores, query[start:stop], preferred_element_type=jnp.float32
            )
            query_sum[start:stop, first:last] += dot_first(grad_scores, keys)
    low = jnp.bfloat16
    out_ref[0, :, :part] = (query_sum[...] * score_scale).astype(low)[:, :part]
    out_ref[0, :, part : 2 * part] = (key_sum[...] * score_scale).astype(low)[:, :part]
    out_ref[0, :, 2 * part : 3 * part] = value_sum[...].astype(low)[:, base:]
    tail = out_ref.shape[2] - 3 * part
    if tail:
        out_ref[0, :, 3 * part :] = jnp.zeros((rows, tail), low)
    sum_ref[0] = jnp.sum(out_ref[0].astype(jnp.float32), axis=0, keepdims=True)


def heads_backward_call(spot, kind, grad_rows, qkvs, logs, at, groups, waits=()):
    rows, full = grad_rows.shape
    arrays, places = flatten(groups)
    _, high, group_width = arrays[0].shape
    depth = full // (2 * high)
    count = len(groups)
    part = group_width // 4
    heads = part // HEAD_DIM
    inner = qkvs[0].shape[2]
    outer = -(-part // 128) * 128
    qkv_spec = pl.BlockSpec((1, rows, inner), lambda i: (at, 0, 0))
    log_spec = pl.BlockSpec((1, 8, rows), lambda i: (at, 0, 0))
    low = pltpu.VMEM((rows, outer), jnp.bfloat16)
    wide = pltpu.VMEM((rows, outer), jnp.float32)
    return pl.pallas_call(
        functools.partial(heads_backward_kernel, places, heads),
        grid=(count,),
        in_specs=[
            smem_spec(),
            pl.BlockSpec((rows, 1), lambda i: (0, 0)),
            pl.BlockSpec((rows, full), lambda i: (0, 0)),
            qkv_spec,
            qkv_spec,
            log_spec,
            log_spec,
        ]
        + [any_spec()] * (len(arrays) + len(waits)),
        out_specs=[
            pl.BlockSpec((1, rows, inner), lambda i: (i, 0, 0)),
            pl.BlockSpec((1, 1, inner), lambda i: (i, 0, 0)),
        ],
        out_shape=[
            jax.ShapeDtypeStruct((count, rows, inner), jnp.bfloat16),
            jax.ShapeDtypeStruct((count, 1, inner), jnp.float32),
        ],
        scratch_shapes=weight_scratch(places, depth, high, outer)
        + [low, low, low, low, wide, wide, wide],
        compiler_params=limits(),
        cost_estimate=cost(25),
        name="heads_backward",
    )(spot, kind, grad_rows, *qkvs, *logs, *arrays, *waits)


def any_spec():
    return pl.BlockSpec(memory_space=pl.ANY)


def smem_spec():
    return pl.BlockSpec(memory_space=pltpu.SMEM)


def vmem_spec():
    return pl.BlockSpec(memory_space=pltpu.VMEM)


def limits():
    return pltpu.CompilerParams(vmem_limit_bytes=VMEM_BYTES)


def cost(micros):
    return pl.CostEstimate(flops=0 * micros, bytes_accessed=0, transcendentals=0)


def flatten(groups):
    arrays = [piece for group in groups for piece, _, _ in group]
    places = [[(at, x_off) for _, at, x_off in group] for group in groups]
    return arrays, places


def weight_copies(places, refs, weights, sems, x_at, first=0, width=None):
    copies, at = [], 0
    for group, parts in enumerate(places):
        mine = []
        for part, (start, x_off) in enumerate(parts):
            source = refs[at]
            at += 1
            if width is not None:
                source = source.at[:, :, pl.ds(first, width)]
            target = weights.at[group, pl.ds(start, source.shape[0]), x_at ^ x_off]
            mine.append(pltpu.make_async_copy(source, target, sems.at[group, part]))
        copies.append(mine)
    return copies


def weight_scratch(places, depth, high, width):
    count = len(places)
    return [
        pltpu.VMEM((count, depth, 2, high, width), jnp.bfloat16),
        pltpu.SemaphoreType.DMA((count, max(len(parts) for parts in places))),
    ]


def start_then_wait(copies, step):
    @pl.when(step == 0)
    def begin():
        for mine in copies:
            for copy in mine:
                copy.start()

    for group, mine in enumerate(copies):

        @pl.when(step == group)
        def arrive(mine=mine):
            for copy in mine:
                copy.wait()


def up_kernel(places, spot, x_ref, bias_ref, *refs):
    count = sum(len(parts) for parts in places)
    pieces = refs[:count]
    active_ref, slope_ref, weights, sems = refs[-4:]
    step = pl.program_id(0)
    start_then_wait(weight_copies(places, pieces, weights, sems, spot[0]), step)
    rows, full = x_ref.shape
    width = weights.shape[-1]
    tile = width // 3
    for start in range(0, width, tile):
        strip = weights[step, :, :, :, start : start + tile].reshape(full, tile)
        hidden = jnp.dot(x_ref[...], strip, preferred_element_type=jnp.float32)
        hidden = hidden + bias_ref[0, :, start : start + tile]
        square = hidden * hidden
        inner = jnp.tanh(hidden * (gelu_scale + gelu_scale * 0.044715 * square))
        gate = 0.5 + 0.5 * inner
        active_ref[0, :, start : start + tile] = (hidden * gate).astype(jnp.bfloat16)
        grow = hidden * (gelu_scale + 3.0 * 0.044715 * gelu_scale * square)
        slope = gate + grow * (0.5 - 0.5 * inner * inner)
        slope_ref[0, :, start : start + tile] = slope.astype(jnp.bfloat16)


def up_project(spot, rows_in, biases, groups, waits=()):
    rows, full = rows_in.shape
    arrays, places = flatten(groups)
    _, high, width = arrays[0].shape
    depth = full // (2 * high)
    count = len(groups)
    shape = jax.ShapeDtypeStruct((count, rows, width), jnp.bfloat16)
    block = pl.BlockSpec((1, rows, width), lambda i: (i, 0, 0))
    return pl.pallas_call(
        functools.partial(up_kernel, places),
        grid=(count,),
        in_specs=[
            smem_spec(),
            pl.BlockSpec((rows, full), lambda i: (0, 0)),
            pl.BlockSpec((1, 1, width), lambda i: (i, 0, 0)),
        ]
        + [any_spec()] * (len(arrays) + len(waits)),
        out_specs=[block, block],
        out_shape=[shape, shape],
        scratch_shapes=weight_scratch(places, depth, high, width),
        compiler_params=limits(),
        cost_estimate=cost(14),
        name="mlp_up",
    )(spot, rows_in, biases, *arrays, *waits)


def slope_kernel(places, spot, x_ref, slope_ref, *refs):
    count = sum(len(parts) for parts in places)
    pieces = refs[:count]
    out_ref, sum_ref, weights, sems = refs[-4:]
    step = pl.program_id(0)
    start_then_wait(weight_copies(places, pieces, weights, sems, spot[0]), step)
    rows, full = x_ref.shape
    width = weights.shape[-1]
    tile = width // 3
    for start in range(0, width, tile):
        strip = weights[step, :, :, :, start : start + tile].reshape(full, tile)
        grad = jnp.dot(x_ref[...], strip, preferred_element_type=jnp.float32)
        grad = grad * slope_ref[0, :, start : start + tile].astype(jnp.float32)
        low = grad.astype(jnp.bfloat16)
        out_ref[0, :, start : start + tile] = low
        total = jnp.sum(low.astype(jnp.float32), axis=0, keepdims=True)
        sum_ref[0, :, start : start + tile] = total


def hidden_grad(spot, rows_in, slope, groups, waits=()):
    rows, full = rows_in.shape
    arrays, places = flatten(groups)
    _, high, width = arrays[0].shape
    depth = full // (2 * high)
    count = len(groups)
    block = pl.BlockSpec((1, rows, width), lambda i: (i, 0, 0))
    return pl.pallas_call(
        functools.partial(slope_kernel, places),
        grid=(count,),
        in_specs=[smem_spec(), pl.BlockSpec((rows, full), lambda i: (0, 0)), block]
        + [any_spec()] * (len(arrays) + len(waits)),
        out_specs=[block, pl.BlockSpec((1, 1, width), lambda i: (i, 0, 0))],
        out_shape=[
            jax.ShapeDtypeStruct((count, rows, width), jnp.bfloat16),
            jax.ShapeDtypeStruct((count, 1, width), jnp.float32),
        ],
        scratch_shapes=weight_scratch(places, depth, high, width),
        compiler_params=limits(),
        cost_estimate=cost(12),
        name="mlp_grad",
    )(spot, rows_in, slope, *arrays, *waits)


def accumulate(step, total, product):
    @pl.when(step == 0)
    def first():
        total[...] = product

    @pl.when(step > 0)
    def later():
        total[...] += product


def by_rows(rows, block, body):
    def one(i, carry):
        body(pl.ds(pl.multiple_of(i * block, block), block))
        return carry

    lax.fori_loop(0, rows // block, one, 0)


def unit_rows(values):
    centre = values - jnp.mean(values, axis=1, keepdims=True)
    spread = jnp.mean(centre * centre, axis=1, keepdims=True)
    root = lax.rsqrt(spread + layer_eps)
    return centre * root, root


def norm_rows_back(values, gain, grad):
    unit, root = unit_rows(values)
    scaled = grad * gain
    mean_one = jnp.mean(scaled, axis=1, keepdims=True)
    mean_two = jnp.mean(scaled * unit, axis=1, keepdims=True)
    part = root * (scaled - mean_one - unit * mean_two)
    return part, jnp.sum(grad * unit, axis=0, keepdims=True), jnp.sum(grad, axis=0, keepdims=True)


def strips(weights, step, parts=3):
    _, depth, _, high, width = weights.shape
    full = depth * 2 * high
    return weights[step].reshape(full, width)


def pick(step, refs):
    half = refs[0].shape[0]
    return lambda i: refs[i // half][i % half]


def back_two_kernel(places, spot, later_ref, early_ref, resid_ref, grad_ref, gain_ref, *refs):
    count = sum(len(parts) for parts in places)
    pieces = refs[:count]
    out_ref, low_ref, sum_ref, weights, sems, total = refs[-6:]
    step = pl.program_id(0)
    last = pl.num_programs(0) - 1
    start_then_wait(weight_copies(places, pieces, weights, sems, spot[0]), step)
    half = pl.num_programs(0) // 2

    @pl.when(step < half)
    def from_first():
        accumulate(step, total, dot_last(later_ref[0], strips(weights, step)))

    @pl.when(step >= half)
    def from_second():
        total[...] += dot_last(early_ref[0], strips(weights, step))

    @pl.when(step == last)
    def finish():
        sum_ref[...] = jnp.zeros_like(sum_ref)

        def block(span):
            part, gain_sum, shift_sum = norm_rows_back(
                resid_ref[span, :], gain_ref[...], total[span, :]
            )
            grad = grad_ref[span, :].astype(jnp.float32) + part
            low = grad.astype(jnp.bfloat16)
            out_ref[span, :] = grad
            low_ref[span, :] = low
            sum_ref[0:1, :] += gain_sum
            sum_ref[1:2, :] += shift_sum
            sum_ref[2:3, :] += jnp.sum(low.astype(jnp.float32), axis=0, keepdims=True)

        by_rows(total.shape[0], 64, block)


def two_stage_specs(count, rows, width):
    half = count // 2
    return [
        pl.BlockSpec((1, rows, width), lambda i: (jnp.minimum(i, half - 1), 0, 0)),
        pl.BlockSpec((1, rows, width), lambda i: (jnp.maximum(i - half, 0), 0, 0)),
    ]


def back_two(spot, first, second, resid, grad_low, gain, groups, waits=()):
    rows, full = resid.shape
    arrays, places = flatten(groups)
    _, high, width = arrays[0].shape
    depth = full // (2 * high)
    count = len(groups)
    whole = pl.BlockSpec((rows, full), lambda i: (0, 0))
    return pl.pallas_call(
        functools.partial(back_two_kernel, places),
        grid=(count,),
        in_specs=[smem_spec()]
        + two_stage_specs(count, rows, width)
        + [whole, whole, pl.BlockSpec((1, full), lambda i: (0, 0))]
        + [any_spec()] * (len(arrays) + len(waits)),
        out_specs=[whole, whole, pl.BlockSpec((8, full), lambda i: (0, 0))],
        out_shape=[
            jax.ShapeDtypeStruct((rows, full), jnp.float32),
            jax.ShapeDtypeStruct((rows, full), jnp.bfloat16),
            jax.ShapeDtypeStruct((8, full), jnp.float32),
        ],
        scratch_shapes=weight_scratch(places, depth, high, width)
        + [pltpu.VMEM((rows, full), jnp.float32)],
        compiler_params=limits(),
        cost_estimate=cost(24),
        name="norm_two_back",
    )(spot, first, second, resid, grad_low, gain, *arrays, *waits)


def back_one_kernel(places, spot, later_ref, early_ref, x_ref, grad_ref, gain_ref, *refs):
    count = sum(len(parts) for parts in places)
    pieces = refs[:count]
    out_ref, sum_ref, weights, sems, total = refs[-5:]
    step = pl.program_id(0)
    last = pl.num_programs(0) - 1
    inner = later_ref.shape[2]
    start_then_wait(weight_copies(places, pieces, weights, sems, spot[0], 0, inner), step)
    half = pl.num_programs(0) // 2

    @pl.when(step < half)
    def from_first():
        accumulate(step, total, dot_last(later_ref[0], strips(weights, step)))

    @pl.when(step >= half)
    def from_second():
        total[...] += dot_last(early_ref[0], strips(weights, step))

    @pl.when(step == last)
    def finish():
        sum_ref[...] = jnp.zeros_like(sum_ref)

        def block(span):
            values = x_ref[span, :].astype(jnp.float32)
            part, gain_sum, shift_sum = norm_rows_back(values, gain_ref[...], total[span, :])
            out_ref[span, :] = grad_ref[span, :] + part
            sum_ref[0:1, :] += gain_sum
            sum_ref[1:2, :] += shift_sum

        by_rows(total.shape[0], 64, block)


def back_one(spot, first, second, rows_in, grad_resid, gain, groups, waits=()):
    rows, full = rows_in.shape
    arrays, places = flatten(groups)
    _, high, _ = arrays[0].shape
    width = first.shape[2]
    depth = full // (2 * high)
    count = len(groups)
    whole = pl.BlockSpec((rows, full), lambda i: (0, 0))
    return pl.pallas_call(
        functools.partial(back_one_kernel, places),
        grid=(count,),
        in_specs=[smem_spec()]
        + two_stage_specs(count, rows, width)
        + [whole, whole, pl.BlockSpec((1, full), lambda i: (0, 0))]
        + [any_spec()] * (len(arrays) + len(waits)),
        out_specs=[whole, pl.BlockSpec((8, full), lambda i: (0, 0))],
        out_shape=[
            jax.ShapeDtypeStruct((rows, full), jnp.float32),
            jax.ShapeDtypeStruct((8, full), jnp.float32),
        ],
        scratch_shapes=weight_scratch(places, depth, high, width)
        + [pltpu.VMEM((rows, full), jnp.float32)],
        compiler_params=limits(),
        cost_estimate=cost(21),
        name="norm_one_back",
    )(spot, first, second, rows_in, grad_resid, gain, *arrays, *waits)


def down_kernel(places, spot, later_ref, early_ref, resid_ref, shift_ref, *refs):
    count = sum(len(parts) for parts in places)
    pieces = refs[:count]
    out_ref, weights, sems, total = refs[-4:]
    step = pl.program_id(0)
    last = pl.num_programs(0) - 1
    start_then_wait(weight_copies(places, pieces, weights, sems, spot[0]), step)
    half = pl.num_programs(0) // 2

    @pl.when(step < half)
    def from_first():
        accumulate(step, total, dot_last(later_ref[0], strips(weights, step)))

    @pl.when(step >= half)
    def from_second():
        total[...] += dot_last(early_ref[0], strips(weights, step))

    @pl.when(step == last)
    def finish():
        def block(span):
            values = resid_ref[span, :] + total[span, :] + shift_ref[...]
            out_ref[span, :] = values.astype(out_ref.dtype)

        by_rows(total.shape[0], 64, block)


def down_project(spot, first, second, resid, shift, groups, waits=()):
    rows, full = resid.shape
    arrays, places = flatten(groups)
    _, high, width = arrays[0].shape
    depth = full // (2 * high)
    count = len(groups)
    whole = pl.BlockSpec((rows, full), lambda i: (0, 0))
    return pl.pallas_call(
        functools.partial(down_kernel, places),
        grid=(count,),
        in_specs=[smem_spec()]
        + two_stage_specs(count, rows, width)
        + [whole, pl.BlockSpec((1, full), lambda i: (0, 0))]
        + [any_spec()] * (len(arrays) + len(waits)),
        out_specs=whole,
        out_shape=jax.ShapeDtypeStruct((rows, full), jnp.bfloat16),
        scratch_shapes=weight_scratch(places, depth, high, width)
        + [pltpu.VMEM((rows, full), jnp.float32)],
        compiler_params=limits(),
        cost_estimate=cost(18),
        name="mlp_down",
    )(spot, first, second, resid, shift, *arrays, *waits)


def out_kernel(places, spot, one, two, three, four, x_ref, shift_ref, gain_ref, bias_ref, *refs):
    count = sum(len(parts) for parts in places)
    pieces = refs[:count]
    resid_ref, normed_ref, weights, sems = refs[-4:]
    outer = weights.shape[-1]
    first = pieces[0].shape[-1] - outer
    copies = weight_copies(places, pieces, weights, sems, spot[0], first, outer)
    for mine in copies:
        for copy in mine:
            copy.start()
    for group, mixed in enumerate((one, two, three, four)):
        for copy in copies[group]:
            copy.wait()
        product = dot_last(mixed[...], strips(weights, group))
        if group == 0:
            resid_ref[...] = product
        else:
            resid_ref[...] += product

    def block(span):
        values = resid_ref[span, :] + x_ref[span, :].astype(jnp.float32) + shift_ref[...]
        resid_ref[span, :] = values
        unit, _ = unit_rows(values)
        normed_ref[span, :] = (unit * gain_ref[...] + bias_ref[...]).astype(jnp.bfloat16)

    by_rows(resid_ref.shape[0], 64, block)


def out_project(spot, mixed, rows_in, shift, gain, bias, groups, waits=()):
    rows, full = rows_in.shape
    arrays, places = flatten(groups)
    _, high, _ = arrays[0].shape
    outer = mixed[0].shape[1]
    depth = full // (2 * high)
    return pl.pallas_call(
        functools.partial(out_kernel, places),
        in_specs=[smem_spec()] + [vmem_spec()] * 8 + [any_spec()] * (len(arrays) + len(waits)),
        out_specs=[vmem_spec(), vmem_spec()],
        out_shape=[
            jax.ShapeDtypeStruct((rows, full), jnp.float32),
            jax.ShapeDtypeStruct((rows, full), jnp.bfloat16),
        ],
        scratch_shapes=weight_scratch(places, depth, high, outer),
        compiler_params=limits(),
        cost_estimate=cost(13),
        name="attn_out",
    )(spot, *mixed, rows_in, shift, gain, bias, *arrays, *waits)


def grad_kernel(pairs, waits, spot, *refs):
    width_in = [4] * pairs
    sources = refs[: sum(width_in)]
    rest = refs[sum(width_in) + waits :]
    own, beside, across, corner_one, corner_two = rest[:5]
    holds = rest[5 : 5 + sum(width_in)]
    stage, in_sems, out_sems = rest[-3:]
    x_at = spot[0]
    copies = [
        pltpu.make_async_copy(source, hold, in_sems.at[i])
        for i, (source, hold) in enumerate(zip(sources, holds))
    ]
    for copy in copies:
        copy.start()
    for copy in copies:
        copy.wait()
    _, depth, _, high, width = stage.shape
    half = depth // 2
    full = depth * 2 * high
    out_copies = []
    for side in range(2):
        start = 0
        total = None
        for count in width_in:
            held = holds[start : start + count]
            start += count
            product = dot_first(held[0][...], held[1][side])
            product += dot_first(held[2][...], held[3][side])
            if total is None:
                total = product
            else:
                whole_tile = total.shape[1] + product.shape[1] - width
                left = total.shape[1] - whole_tile
                total = jnp.concatenate(
                    [
                        total[:, :left],
                        total[:, left:] + product[:, :whole_tile],
                        product[:, whole_tile:],
                    ],
                    axis=1,
                )
        stage[side] = total.astype(jnp.bfloat16).reshape(depth, 2, high, width)
        near = stage.at[side, :, x_at]
        far = stage.at[side, :, 1 - x_at]
        if side == 0:
            moves = [(near, own), (far, beside)]
        else:
            moves = [
                (near, across),
                (stage.at[side, pl.ds(0, half), 1 - x_at], corner_one),
                (stage.at[side, pl.ds(half, half), 1 - x_at], corner_two),
            ]
        for source, target in moves:
            copy = pltpu.make_async_copy(source, target, out_sems.at[len(out_copies)])
            copy.start()
            out_copies.append(copy)
    for copy in out_copies:
        copy.wait()


def weight_grad(spot, pairs, depth, waits=()):
    flat = [values for pair in pairs for both in pair for values in both]
    full = flat[0].shape[1]
    high = full // (2 * depth)
    half = depth // 2
    width = sum(pair[0][1].shape[2] for pair in pairs)
    if len(pairs) > 1:
        width = full
    rows = flat[0].shape[0]
    sizes = (depth, depth, depth, half, half)
    return pl.pallas_call(
        functools.partial(grad_kernel, len(pairs), len(waits)),
        in_specs=[smem_spec()] + [any_spec()] * (len(flat) + len(waits)),
        out_specs=[any_spec()] * 5,
        out_shape=[jax.ShapeDtypeStruct((size, high, width), jnp.bfloat16) for size in sizes],
        scratch_shapes=[pltpu.VMEM(values.shape, values.dtype) for values in flat]
        + [
            pltpu.VMEM((2, depth, 2, high, width), jnp.bfloat16),
            pltpu.SemaphoreType.DMA((len(flat),)),
            pltpu.SemaphoreType.DMA((5,)),
        ],
        compiler_params=limits(),
        cost_estimate=cost(15),
        name="weight_grad",
    )(spot, *flat, *waits)


def corner_kernel(beside_ref, across_ref, one_ref, two_ref, beside_out, across_out):
    wide = jnp.float32
    low = beside_out.dtype
    beside_out[...] = (beside_ref[...].astype(wide) + two_ref[...].astype(wide)).astype(low)
    across_out[...] = (across_ref[...].astype(wide) + one_ref[...].astype(wide)).astype(low)


def add_corners(beside, across, corner_one, corner_two):
    block = corner_one.shape
    first = pl.BlockSpec(block, lambda i: (0, 0, 0))
    second = pl.BlockSpec(block, lambda i: (1, 0, 0))
    shape = jax.ShapeDtypeStruct(beside.shape, beside.dtype)
    return pl.pallas_call(
        corner_kernel,
        grid=(1,),
        in_specs=[second, first, first, first],
        out_specs=[second, first],
        out_shape=[shape, shape],
        input_output_aliases={0: 0, 1: 1},
        compiler_params=limits(),
        name="add_corners",
    )(beside, across, corner_one, corner_two)


def square_kernel(own, one, two, out):
    wide = jnp.float32
    total = own[...].astype(wide) + one[...].astype(wide) + two[...].astype(wide)
    out[...] = total.astype(out.dtype)


def add_square(own, one, two):
    depth, high, width = own.shape
    block = pl.BlockSpec((1, high, width), lambda i: (i, 0, 0))
    return pl.pallas_call(
        square_kernel,
        grid=(depth,),
        in_specs=[block, block, block],
        out_specs=block,
        out_shape=jax.ShapeDtypeStruct(own.shape, own.dtype),
        name="add_square",
    )(own, one, two)


PATCHES = 729
AXES = ("dp", "tensor")


def nothing(*refs):
    del refs


def fence(released, waited=()):
    anywhere = pl.BlockSpec(memory_space=pl.ANY)
    released, waited = list(released), list(waited)
    return pl.pallas_call(
        nothing,
        in_specs=[anywhere] * (len(released) + len(waited)),
        out_specs=[anywhere] * len(released),
        out_shape=[jax.ShapeDtypeStruct(values.shape, values.dtype) for values in released],
        input_output_aliases={i: i for i in range(len(released))},
        name="fence",
    )(*released, *waited)


class Grid:
    def __init__(self, depth):
        self.depth = depth
        dp_at = lax.axis_index("dp")
        self.y = lax.axis_index("tensor")
        self.c = dp_at % 2
        self.x = dp_at // 2 % 2
        self.z = dp_at // 4

    def move(self, values, where):
        pairs = []
        for z in range(self.depth):
            for x in range(2):
                for c in range(2):
                    for y in range(2):
                        to_z, to_x, to_c, to_y = where(z, x, c, y)
                        pairs.append(
                            (
                                ((z * 2 + x) * 2 + c) * 2 + y,
                                ((to_z * 2 + to_x) * 2 + to_c) * 2 + to_y,
                            )
                        )
        return lax.ppermute(values, AXES, pairs)

    def over_x(self, values):
        return self.move(values, lambda z, x, c, y: (z, 1 - x, c, y))

    def over_y(self, values):
        return self.move(values, lambda z, x, c, y: (z, x, c, 1 - y))

    def over_core(self, values):
        return self.move(values, lambda z, x, c, y: (z, x, 1 - c, y))

    def along_z(self, values, hops):
        return self.move(values, lambda z, x, c, y: ((z + hops) % self.depth, x, c, y))

    def across_z(self, values, bit):
        return self.move(values, lambda z, x, c, y: (z ^ bit, x, c, y))

    def spread(self, block):
        width = block.shape[1] // 2
        mine = lax.dynamic_slice_in_dim(block, self.c * width, width, 1)
        theirs = self.over_core(
            lax.dynamic_slice_in_dim(block, (1 - self.c) * width, width, 1)
        )
        first = jnp.where(self.c == 0, mine, theirs)
        second = jnp.where(self.c == 0, theirs, mine)
        return jnp.concatenate([first, second])

    def depth_groups(self):
        return [
            [(z * 2 + x) * 2 + c for z in range(self.depth)] for x in range(2) for c in range(2)
        ]

    def gather_depth(self, block):
        return lax.all_gather(block, "dp", axis_index_groups=self.depth_groups())

    def scatter_depth(self, total):
        return lax.psum_scatter(total, "dp", axis_index_groups=self.depth_groups())

    def scatter_core(self, result):
        result = result.astype(jnp.float32)
        shard = result.shape[0] // 2
        mine = lax.dynamic_slice_in_dim(result, self.c * shard, shard)
        theirs = self.over_core(
            lax.dynamic_slice_in_dim(result, (1 - self.c) * shard, shard)
        )
        first = jnp.where(self.c == 0, mine, theirs)
        second = jnp.where(self.c == 0, theirs, mine)
        return jnp.stack([first, second])

    def gather_small(self, values):
        count, shard = values.shape
        parts = jnp.zeros((self.depth, 2, 2, count, shard), values.dtype)
        parts = lax.dynamic_update_slice(
            parts, values[None, None, None], (self.z, self.x, self.c, 0, 0)
        )
        parts = parts + self.over_core(parts)
        parts = parts + self.over_x(parts)
        bit = 1
        while bit < self.depth:
            parts = parts + self.across_z(parts, bit)
            bit *= 2
        return parts.transpose(3, 0, 1, 2, 4).reshape(count, -1)


def image_shards(
    depth,
    layer_input,
    token_image,
    cotangent,
    ln1_gain,
    ln1_bias,
    w_qkv,
    qv_bias,
    w_out,
    out_bias,
    ln2_gain,
    ln2_bias,
    w_fc1,
    fc1_bias,
    w_fc2,
    fc2_bias,
):
    low = jnp.bfloat16
    wide = jnp.float32
    grid = Grid(depth)
    rows, full_width = layer_input.shape
    shard = ln1_gain.shape[0]
    head_width = qv_bias.shape[1]
    ff_width = fc1_bias.shape[0]
    padded = -(-(rows + 1) // 256) * 256

    quarter = head_width // 2
    group_width = 4 * quarter
    ff_padding = 2 * group_width - ff_width
    sources = [w_qkv[0], w_qkv[1], w_qkv[2], w_out.T]
    first_block = jnp.concatenate(
        [values[:, i * quarter : (i + 1) * quarter] for i in range(2) for values in sources],
        axis=1,
    )
    second_block = jnp.pad(w_fc1, ((0, 0), (0, ff_padding)))
    third_block = jnp.pad(w_fc2.T, ((0, 0), (0, ff_padding)))
    half = depth // 2
    blocks = [grid.spread(first_block), grid.spread(second_block), grid.spread(third_block)]
    vectors = jnp.stack([ln1_gain, ln1_bias, out_bias, ln2_gain, ln2_bias, fc2_bias])
    vectors = grid.gather_small(vectors).astype(wide)
    (token_image, qv_bias) = fence([token_image, qv_bias], [blocks[0]])
    own_one = grid.gather_depth(blocks[0])

    here = grid.y
    mine = lax.dynamic_slice_in_dim(token_image, here * rows, rows)
    theirs = lax.dynamic_slice_in_dim(token_image, (1 - here) * rows, rows)
    places = lax.iota(jnp.int32, rows)
    stray = mine == 1 - here
    stray_here = jnp.any(stray)
    stray_there = jnp.any(theirs == here)
    blank = mine == IMAGES
    first_blank = jnp.min(jnp.where(blank, places, rows - 1))
    last_blank = jnp.max(jnp.where(blank, places, 0))
    swap_at = jnp.where(stray_here, jnp.max(jnp.where(stray, places, 0)), first_blank)
    swapped = stray_here | stray_there
    blank_at = jnp.where(stray_here, swap_at, last_blank)

    def one_row(values, at):
        return lax.dynamic_slice_in_dim(values, at, 1)

    sent = jnp.concatenate(
        [one_row(layer_input, swap_at), one_row(cotangent, swap_at), one_row(layer_input, last_blank)]
    )
    came = grid.over_y(sent)
    other_blank = jnp.where(stray_there, sent[0:1], came[2:3])
    spread_rows = lax.broadcasted_iota(jnp.int32, (padded, 1), 0)
    at_swap = (spread_rows == swap_at) & swapped

    def stretch(values):
        return jnp.pad(values, ((0, padded - rows), (0, 0)))

    input_rows = jnp.where(at_swap, came[0:1], stretch(layer_input))
    input_rows = jnp.where(spread_rows == rows, other_blank, input_rows)
    grad_low = jnp.where(at_swap, came[1:2], stretch(cotangent))
    grad_low = jnp.where(spread_rows == blank_at, 0, grad_low).astype(low)
    kind = jnp.where(spread_rows > rows, 3, jnp.where(spread_rows == rows, 2, 0))
    kind = jnp.where(spread_rows == blank_at, 1, kind)
    input_rows, grad_low = lax.optimization_barrier((input_rows, grad_low))

    biases = jnp.concatenate([qv_bias.reshape(-1), fc1_bias])
    biases = jnp.pad(biases, (0, -biases.shape[0] % 128)).reshape(-1, 128)
    other_biases = grid.over_y(biases).reshape(-1)

    def ordered(first, second):
        return jnp.where(grid.c == 0, first, second), jnp.where(grid.c == 0, second, first)

    spot = grid.x.reshape(1)
    inner = -(-3 * quarter // 128) * 128
    qv_groups, fc1_groups = [], []
    for flat in (biases.reshape(-1), other_biases):
        flat = flat.astype(wide)
        pair = flat[: 2 * head_width].reshape(2, 2, quarter)
        none = jnp.zeros((quarter,), wide)
        rest = jnp.zeros((inner - 3 * quarter,), wide)
        qv_groups += ordered(
            *[jnp.concatenate([pair[0, i], none, pair[1, i], rest]) for i in range(2)]
        )
        hidden_bias = flat[2 * head_width : 2 * head_width + ff_width]
        hidden_bias = jnp.pad(hidden_bias, (0, ff_padding))
        fc1_groups += ordered(hidden_bias[:group_width], hidden_bias[group_width:])

    def stacked(rows_of, picked):
        return jnp.stack([rows_of[i] for i in picked])[:, None]

    qv_stacks = [stacked(qv_groups, picked) for picked in ((0, 1), (2, 3))]
    fc1_stacks = [stacked(fc1_groups, picked) for picked in ((1, 3), (0, 2))]

    def sides_of(own):
        return [grid.over_x(own), grid.over_y(own)]

    def corners_of(beside, across):
        return [grid.over_y(beside[:half]), grid.over_x(across[half:])]

    def cores_of(*values):
        return [grid.over_core(value) for value in values]

    def near_groups(own, beside, there):
        return [
            [(own, 0, 0), (beside, 0, 1)],
            [(there[0], 0, 0), (there[1], 0, 1)],
        ]

    def far_groups(across, corner, there):
        return [
            [(across, 0, 0), (corner[0], 0, 1), (corner[1], half, 1)],
            [(there[0], 0, 0), (there[1], 0, 1), (there[2], half, 1)],
        ]

    own_one, vectors, input_rows, grad_low, kind, block_two, block_three, *stacks = fence(
        [own_one, vectors, input_rows, grad_low, kind, blocks[1], blocks[2]]
        + qv_stacks
        + fc1_stacks
    )
    qv_stacks, fc1_stacks = stacks[:2], stacks[2:]
    gain_one, shift_one, out_shift, gain_two, shift_two, fc2_shift = [
        vectors[i : i + 1] for i in range(6)
    ]
    own_two = grid.gather_depth(block_two)
    beside_one, across_one = sides_of(own_one)
    unit_one, _ = unit_rows(input_rows.astype(wide))
    normed = (unit_one * gain_one + shift_one).astype(low)
    own_two, beside_one, across_one, normed, block_three, grad_there = fence(
        [own_two, beside_one, across_one, normed, block_three, grid.over_core(grad_low)]
    )
    corner_one = corners_of(beside_one, across_one)
    there = cores_of(own_one, beside_one)
    across_there = grid.over_core(across_one)
    sides_two = sides_of(own_two)
    own_three = grid.gather_depth(block_three)
    qkv, logs, mixed = [], [], []

    def heads(stack, groups, waits):
        results = heads_forward_call(spot, kind, normed, stack, groups, waits)
        logs.append(results[1])
        mixed.extend(results[2:])
        return results[0]

    attn_weights = near_groups(own_one, beside_one, there)
    first_qkv = heads(qv_stacks[0], attn_weights, [])
    *corner_one, across_there, first_qkv = fence(corner_one + [across_there, first_qkv])
    there = [across_there] + cores_of(*corner_one)
    attn_weights = attn_weights + far_groups(across_one, corner_one, there)
    second_qkv = heads(qv_stacks[1], attn_weights[2:], [])
    own_two_there = grid.over_core(own_two)
    own_three, beside_two, across_two, own_two_there, second_qkv = fence(
        [own_three] + sides_two + [own_two_there, second_qkv]
    )
    qkv = [first_qkv, second_qkv]
    corner_two = corners_of(beside_two, across_two)
    beside_there = grid.over_core(beside_two)
    sides_three = sides_of(own_three)
    resid, normed_two = out_project(
        spot, mixed, input_rows, out_shift, gain_two, shift_two, attn_weights
    )
    *corner_two, normed_two, beside_there = fence(corner_two + [normed_two, beside_there])
    up_weights = near_groups(own_two, beside_two, [own_two_there, beside_there])
    there = cores_of(across_two, *corner_two)
    up_weights = up_weights + far_groups(across_two, corner_two, there)
    classes = ((1, 3), (0, 2))

    def up(at, waits):
        picked = [up_weights[i] for i in classes[at]]
        return up_project(spot, normed_two, fc1_stacks[at], picked, waits)

    other_active, other_slope = up(0, [])
    beside_three, across_three, other_active = fence(sides_three + [other_active])
    corner_three = corners_of(beside_three, across_three)
    there = cores_of(own_three, beside_three)
    across_there = grid.over_core(across_three)
    active_there = grid.over_core(other_active)
    own_active, own_slope = up(1, [other_active])
    *corner_three, own_active = fence(corner_three + [own_active])
    down_weights = near_groups(own_three, beside_three, there)
    there = [across_there] + cores_of(*corner_three)
    down_weights = down_weights + far_groups(across_three, corner_three, there)
    fc2_sums = weight_grad(
        spot, [((grad_low, own_active), (grad_there, active_there))], depth
    )

    def move_corners(sums):
        return [grid.over_x(sums[3]), grid.over_y(sums[4])]

    def back(at, slope, waits):
        picked = [down_weights[i] for i in classes[at]]
        return hidden_grad(spot, grad_low, slope, picked, waits)

    moved = move_corners(fc2_sums)
    other_hidden, other_fc1_sums = back(0, other_slope, [fc2_sums[0]])
    *moved, other_hidden = fence(moved + [other_hidden])
    beside, across = add_corners(fc2_sums[1], fc2_sums[2], *moved)
    moved = [grid.over_x(beside), grid.over_y(across)]
    hidden_there = grid.over_core(other_hidden)
    own_hidden, own_fc1_sums = back(1, own_slope, [beside])
    fc1_sums = weight_grad(
        spot, [((normed_two, own_hidden), (grid.over_core(normed_two), hidden_there))], depth
    )
    *moved, near_sums, corner_a, corner_b = fence(moved + [fc1_sums[0], *fc1_sums[3:]])
    fc2_piece = grid.scatter_depth(add_square(fc2_sums[0], *moved))
    moved = [grid.over_x(corner_a), grid.over_y(corner_b)]
    by_class = [up_weights[i] for i in classes[0] + classes[1]]
    grad_resid, resid_low, sums_two = back_two(
        spot,
        other_hidden,
        own_hidden,
        resid,
        grad_low,
        gain_two,
        by_class,
        [near_sums],
    )
    *moved, resid_low = fence(moved + [resid_low])
    beside, across = add_corners(fc1_sums[1], fc1_sums[2], *moved)
    moved = [grid.over_x(beside), grid.over_y(across)]

    def heads_back(at, waits):
        return heads_backward_call(
            spot, kind, resid_low, qkv, logs, at, [attn_weights[i] for i in classes[1 - at]], waits
        )

    other_qkv, other_qkv_sums = heads_back(1, [beside])
    *moved, other_qkv, fc2_piece = fence(moved + [other_qkv, fc2_piece])
    fc2_piece = grid.scatter_core(fc2_piece)
    fc1_piece = grid.scatter_depth(add_square(near_sums, *moved))
    qkv_there = grid.over_core(other_qkv)
    own_qkv, own_qkv_sums = heads_back(0, [])
    own_mixed = jnp.stack([mixed[0], mixed[2]])
    other_mixed = jnp.stack([mixed[1], mixed[3]])
    attn_sums = weight_grad(
        spot,
        [
            ((normed, own_qkv), (grid.over_core(normed), qkv_there)),
            ((resid_low, own_mixed), (grid.over_core(resid_low), grid.over_core(other_mixed))),
        ],
        depth,
    )
    near_sums, corner_a, corner_b = fence([attn_sums[0], *attn_sums[3:]])
    moved = [grid.over_x(corner_a), grid.over_y(corner_b)]
    by_class = [attn_weights[i] for i in classes[0] + classes[1]]
    input_grad, sums_one = back_one(
        spot, other_qkv, own_qkv, input_rows, grad_resid, gain_one, by_class, [near_sums]
    )
    *moved, sums_one, fc1_piece = fence(moved + [sums_one, fc1_piece])
    beside, across = add_corners(attn_sums[1], attn_sums[2], *moved)
    moved = [grid.over_x(beside), grid.over_y(across)]
    fc1_piece = grid.scatter_core(fc1_piece)
    by_class = [down_weights[i] for i in classes[0] + classes[1]]
    layer_rows = down_project(
        spot, other_active, own_active, resid, fc2_shift, by_class, [beside]
    )

    def column_sum(values):
        return jnp.sum(values.astype(wide), axis=0)

    def absolute(own_sums, other_sums):
        grouped = jnp.concatenate([own_sums, other_sums], axis=1)
        grouped = jnp.where(here == 0, grouped, grouped[::-1])
        return jnp.where(grid.c == 0, grouped, grouped[:, ::-1])

    qkv_totals = absolute(own_qkv_sums, other_qkv_sums)[:, :, : 3 * quarter]
    qkv_totals = qkv_totals.reshape(2, 2, 3, quarter)[:, :, 0::2].transpose(0, 2, 1, 3)
    fc1_totals = absolute(own_fc1_sums, other_fc1_sums).reshape(2, -1)
    flat = jnp.concatenate(
        [
            sums_one[0],
            sums_one[1],
            sums_two[2],
            sums_two[0],
            sums_two[1],
            column_sum(grad_low),
            qkv_totals.reshape(-1),
            fc1_totals[:, :ff_width].reshape(-1),
        ]
    )
    length = flat.shape[0]
    lines = -(-length // 1024) * 8
    flat = jnp.pad(flat, (0, lines * 128 - length)).reshape(lines, 128)
    flat = flat + grid.over_core(flat)
    bit = 1
    while bit < depth:
        flat = flat + grid.across_z(flat, bit)
        bit *= 2
    *moved, flat = fence(moved + [flat], [layer_rows])
    total = add_square(near_sums, *moved)
    attn_piece = grid.scatter_depth(total)
    flat = flat + grid.over_x(flat)
    flat = flat + grid.over_y(flat)
    flat = flat.reshape(-1)
    swap_from = fence([one_row(layer_rows, swap_at), one_row(input_grad, swap_at)], [total])
    returned = [grid.over_y(values) for values in swap_from]
    layer_output = jnp.where(at_swap, returned[0], layer_rows)[:rows]
    input_grad = jnp.where(at_swap, returned[1], input_grad)[:rows]
    attn_piece = grid.scatter_core(attn_piece)
    row_total = flat[: 6 * full_width].reshape(6, full_width)
    row_piece = lax.dynamic_slice_in_dim(row_total, lax.axis_index("dp") * shard, shard, 1)
    start = 6 * full_width
    qv_piece = lax.dynamic_slice_in_dim(flat, start + here * 2 * head_width, 2 * head_width)
    start = start + 4 * head_width
    fc1_bias_piece = lax.dynamic_slice_in_dim(flat, start + here * ff_width, ff_width)
    heads_piece = attn_piece.reshape(2, shard, 4, quarter).transpose(2, 1, 0, 3)
    heads_piece = heads_piece.reshape(4, shard, head_width)

    def whole_columns(pair):
        return jnp.concatenate([pair[0], pair[1][:, : group_width - ff_padding]], axis=1)

    return (
        layer_output,
        input_grad,
        row_piece[0],
        row_piece[1],
        heads_piece[:3],
        qv_piece.reshape(2, head_width),
        heads_piece[3].T,
        row_piece[2],
        row_piece[3],
        row_piece[4],
        whole_columns(fc1_piece),
        fc1_bias_piece,
        whole_columns(fc2_piece).T,
        row_piece[5],
    )


def fits_images(mesh):
    groups = mesh.shape["dp"] // 4
    return (
        mesh.shape["tensor"] == IMAGES
        and mesh.shape["dp"] % 4 == 0
        and groups >= 2
        and groups & (groups - 1) == 0
    )


def solution(mesh):
    in_specs = (
        P(("dp", "tensor"), None),
        P("dp"),
        P(("dp", "tensor"), None),
        P("dp"),
        P("dp"),
        P(None, "dp", "tensor"),
        P(None, "tensor"),
        P("tensor", "dp"),
        P("dp"),
        P("dp"),
        P("dp"),
        P("dp", "tensor"),
        P("tensor"),
        P("tensor", "dp"),
        P("dp"),
    )
    out_specs = (
        P(("dp", "tensor"), None),
        P(("dp", "tensor"), None),
        P("dp"),
        P("dp"),
        P(None, "dp", "tensor"),
        P(None, "tensor"),
        P("tensor", "dp"),
        P("dp"),
        P("dp"),
        P("dp"),
        P("dp", "tensor"),
        P("tensor"),
        P("tensor", "dp"),
        P("dp"),
    )

    def body(*arrays):
        slots = arrays[1].shape[0]
        if fits_images(mesh) and slots == IMAGES * (PATCHES + 1):
            return image_shards(mesh.shape["dp"] // 4, *arrays)
        return shards(*arrays)

    return jax.shard_map(body, mesh=mesh, in_specs=in_specs, out_specs=out_specs, check_vma=False)
```

```python
import functools

import jax
import jax.numpy as jnp
from jax import lax
from jax.experimental import pallas as pl
from jax.experimental.pallas import tpu as pltpu
from jax.sharding import PartitionSpec as P

HEAD_DIM = 72
IMAGES = 2


layer_eps = 1e-06
gelu_scale = 0.7978845608028654


def gelu_tanh(values):
    return (
        0.5 * values * (1.0 + jnp.tanh(gelu_scale * (values + 0.044715 * values * values * values)))
    )


def norm_rows(values, gain, shift):
    centre = values - jnp.mean(values, axis=1, keepdims=True)
    spread = jnp.mean(centre * centre, axis=1, keepdims=True)
    return centre * lax.rsqrt(spread + layer_eps) * gain + shift


def contract_rows(left, right):
    return lax.dot_general(
        left, right, (((0,), (0,)), ((), ())), preferred_element_type=jnp.float32
    )


def contract_cols(left, right):
    return lax.dot_general(
        left, right, (((1,), (1,)), ((), ())), preferred_element_type=jnp.float32
    )


def split_heads(values, head_count):
    slot_count = values.shape[0]
    return values.reshape(slot_count, head_count, -1).transpose(1, 0, 2)


def join_heads(values):
    head_count, slot_count, head_size = values.shape
    return values.transpose(1, 0, 2).reshape(slot_count, head_count * head_size)


def block_rows(slot_count):
    half_rows = slot_count // 2
    return half_rows


def masked_scores(rows_query, head_keys, rows_ids, image_ids, score_scale):
    scores = contract_cols(rows_query, head_keys) * score_scale
    return jnp.where(rows_ids[:, None] == image_ids[None, :], scores, -1e30)


def heads_forward(query_heads, key_heads, value_heads, image_ids, score_scale):
    slot_count, head_size = (query_heads.shape[1], query_heads.shape[2])
    block_size = block_rows(slot_count)
    block_count = slot_count // block_size
    id_blocks = image_ids.reshape(block_count, block_size)

    def one_head(head_inputs):
        head_query, head_keys, head_values = head_inputs

        def one_block(block_inputs):
            rows_query, rows_ids = block_inputs
            scores = masked_scores(rows_query, head_keys, rows_ids, image_ids, score_scale)
            peak = jnp.max(scores, axis=1, keepdims=True)
            expo_rows = jnp.exp(scores - peak)
            row_total = jnp.sum(expo_rows, axis=1, keepdims=True)
            prob_rows = (expo_rows / row_total).astype(jnp.bfloat16)
            mixed = jnp.dot(prob_rows, head_values, preferred_element_type=jnp.float32)
            return (mixed.astype(jnp.bfloat16), peak[:, 0] + jnp.log(row_total[:, 0]))

        mixed, logsum = lax.map(
            one_block, (head_query.reshape(block_count, block_size, head_size), id_blocks)
        )
        return (mixed.reshape(slot_count, head_size), logsum.reshape(slot_count))

    return lax.map(one_head, (query_heads, key_heads, value_heads))


def heads_backward(query_heads, key_heads, value_heads, grad_heads, logsum, image_ids, score_scale):
    slot_count, head_size = (query_heads.shape[1], query_heads.shape[2])
    block_size = block_rows(slot_count)
    block_count = slot_count // block_size
    id_blocks = image_ids.reshape(block_count, block_size)

    def one_head(head_inputs):
        head_query, head_keys, head_values, head_grad, head_logsum = head_inputs

        def one_block(carried, block_inputs):
            key_sum, value_sum = carried
            rows_query, rows_grad, rows_logsum, rows_ids = block_inputs
            scores = masked_scores(rows_query, head_keys, rows_ids, image_ids, score_scale)
            prob_rows = jnp.exp(scores - rows_logsum[:, None])
            value_sum = value_sum + contract_rows(prob_rows.astype(jnp.bfloat16), rows_grad)
            grad_probs = contract_cols(rows_grad, head_values)
            centre = jnp.sum(grad_probs * prob_rows, axis=1, keepdims=True)
            grad_scores = (prob_rows * (grad_probs - centre)).astype(jnp.bfloat16)
            rows_dq = (
                jnp.dot(grad_scores, head_keys, preferred_element_type=jnp.float32) * score_scale
            ).astype(jnp.bfloat16)
            key_sum = key_sum + contract_rows(grad_scores, rows_query) * score_scale
            return ((key_sum, value_sum), rows_dq)

        zeros_init = jnp.zeros((slot_count, head_size), jnp.float32)
        block_inputs = (
            head_query.reshape(block_count, block_size, head_size),
            head_grad.reshape(block_count, block_size, head_size),
            head_logsum.reshape(block_count, block_size),
            id_blocks,
        )
        (key_sum, value_sum), query_grad = lax.scan(
            one_block, (zeros_init, zeros_init), block_inputs
        )
        return (
            query_grad.reshape(slot_count, head_size),
            key_sum.astype(jnp.bfloat16),
            value_sum.astype(jnp.bfloat16),
        )

    return lax.map(one_head, (query_heads, key_heads, value_heads, grad_heads, logsum))


def forward_pass(inputs, full_output):
    (
        layer_input,
        token_image,
        ln1_gain,
        ln1_bias,
        w_qkv,
        qv_bias,
        w_out,
        out_bias,
        ln2_gain,
        ln2_bias,
        w_fc1,
        fc1_bias,
        w_fc2,
        fc2_bias,
    ) = inputs
    head_count = w_qkv.shape[2] // HEAD_DIM
    score_scale = HEAD_DIM ** (-0.5)
    attn_params = (
        lax.all_gather(ln1_gain, "dp", axis=0, tiled=True),
        lax.all_gather(ln1_bias, "dp", axis=0, tiled=True),
        lax.all_gather(w_qkv, "dp", axis=1, tiled=True),
        lax.all_gather(w_out, "dp", axis=1, tiled=True),
        lax.all_gather(out_bias, "dp", axis=0, tiled=True),
    )
    mlp_params = (
        lax.all_gather(ln2_gain, "dp", axis=0, tiled=True),
        lax.all_gather(ln2_bias, "dp", axis=0, tiled=True),
        lax.all_gather(w_fc1, "dp", axis=0, tiled=True),
        lax.all_gather(w_fc2, "dp", axis=1, tiled=True),
        lax.all_gather(fc2_bias, "dp", axis=0, tiled=True),
    )
    input_rows = layer_input.astype(jnp.float32)
    normed = norm_rows(
        input_rows, attn_params[0].astype(jnp.float32), attn_params[1].astype(jnp.float32)
    )
    first_in = lax.all_gather(normed.astype(jnp.bfloat16), "tensor", axis=0, tiled=True)
    projected = jnp.einsum(
        "sd,cde->cse", first_in, attn_params[2], preferred_element_type=jnp.float32
    )
    bias_rows = qv_bias.astype(jnp.float32)
    query_heads = split_heads((projected[0] + bias_rows[0]).astype(jnp.bfloat16), head_count)
    key_heads = split_heads(projected[1].astype(jnp.bfloat16), head_count)
    value_heads = split_heads((projected[2] + bias_rows[1]).astype(jnp.bfloat16), head_count)
    mixed, logsum = heads_forward(query_heads, key_heads, value_heads, token_image, score_scale)
    attn_out = join_heads(mixed)
    resid = (
        input_rows
        + lax.psum_scatter(
            jnp.dot(attn_out, attn_params[3], preferred_element_type=jnp.float32),
            "tensor",
            scatter_dimension=0,
            tiled=True,
        )
        + attn_params[4].astype(jnp.float32)
    )
    normed_two = norm_rows(
        resid, mlp_params[0].astype(jnp.float32), mlp_params[1].astype(jnp.float32)
    )
    second_in = lax.all_gather(normed_two.astype(jnp.bfloat16), "tensor", axis=0, tiled=True)
    hidden = jnp.dot(
        second_in, mlp_params[2], preferred_element_type=jnp.float32
    ) + fc1_bias.astype(jnp.float32)
    active = gelu_tanh(hidden).astype(jnp.bfloat16)
    layer_output = None
    if full_output:
        summed = lax.psum_scatter(
            jnp.dot(active, mlp_params[3], preferred_element_type=jnp.float32).astype(jnp.bfloat16),
            "tensor",
            scatter_dimension=0,
            tiled=True,
        ).astype(jnp.float32)
        layer_output = (resid + summed + mlp_params[4].astype(jnp.float32)).astype(jnp.bfloat16)
    return (
        attn_params,
        mlp_params,
        input_rows,
        first_in,
        query_heads,
        key_heads,
        value_heads,
        logsum,
        attn_out,
        resid,
        second_in,
        hidden,
        active,
        layer_output,
    )


def shards(
    layer_input,
    token_image,
    cotangent,
    ln1_gain,
    ln1_bias,
    w_qkv,
    qv_bias,
    w_out,
    out_bias,
    ln2_gain,
    ln2_bias,
    w_fc1,
    fc1_bias,
    w_fc2,
    fc2_bias,
):
    inputs = (
        layer_input,
        token_image,
        ln1_gain,
        ln1_bias,
        w_qkv,
        qv_bias,
        w_out,
        out_bias,
        ln2_gain,
        ln2_bias,
        w_fc1,
        fc1_bias,
        w_fc2,
        fc2_bias,
    )
    first_pass = forward_pass(inputs, True)
    layer_output = first_pass[13]
    fenced = lax.optimization_barrier((layer_output, inputs))[1]
    saved = forward_pass(fenced, False)
    (
        attn_params,
        mlp_params,
        input_rows,
        first_in,
        query_heads,
        key_heads,
        value_heads,
        logsum,
        attn_out,
        resid,
        second_in,
        hidden,
        active,
        unused_output,
    ) = saved
    score_scale = HEAD_DIM ** (-0.5)
    row_count = layer_input.shape[0]
    tensor_at = lax.axis_index("tensor")
    image_rows = lax.dynamic_slice_in_dim(token_image, tensor_at * row_count, row_count)
    valid_mask = (image_rows < IMAGES).astype(jnp.float32)
    grad_rows = cotangent.astype(jnp.float32) * valid_mask[:, None]
    grad_low = grad_rows.astype(jnp.bfloat16)
    grad_all = lax.all_gather(grad_low, "tensor", axis=0, tiled=True)
    grad_active = contract_cols(grad_all, mlp_params[3])
    grad_hidden = jax.vjp(gelu_tanh, hidden)[1](grad_active)[0].astype(jnp.bfloat16)
    fc2_grad = contract_rows(active, grad_all)
    fc1_grad = contract_rows(second_in, grad_hidden)
    grad_normed_two = lax.psum_scatter(
        contract_cols(grad_hidden, mlp_params[2]), "tensor", scatter_dimension=0, tiled=True
    )
    norm_two_back = jax.vjp(
        norm_rows, resid, mlp_params[0].astype(jnp.float32), mlp_params[1].astype(jnp.float32)
    )[1]
    resid_part, ln2_gain_sum, ln2_bias_sum = norm_two_back(grad_normed_two)
    grad_resid = grad_rows + resid_part
    resid_low = grad_resid.astype(jnp.bfloat16)
    resid_all = lax.all_gather(resid_low, "tensor", axis=0, tiled=True)
    out_grad = contract_rows(attn_out, resid_all)
    grad_attn = contract_cols(resid_all, attn_params[3]).astype(jnp.bfloat16)
    head_count = query_heads.shape[0]
    grad_query, grad_keys, grad_values = heads_backward(
        query_heads,
        key_heads,
        value_heads,
        split_heads(grad_attn, head_count),
        logsum,
        token_image,
        score_scale,
    )
    grad_qkv = jnp.stack([join_heads(grad_query), join_heads(grad_keys), join_heads(grad_values)])
    qkv_grad = jnp.einsum("sd,cse->cde", first_in, grad_qkv, preferred_element_type=jnp.float32)
    grad_normed = lax.psum_scatter(
        jnp.einsum("cse,cde->sd", grad_qkv, attn_params[2], preferred_element_type=jnp.float32),
        "tensor",
        scatter_dimension=0,
        tiled=True,
    )
    norm_one_back = jax.vjp(
        norm_rows,
        input_rows,
        attn_params[0].astype(jnp.float32),
        attn_params[1].astype(jnp.float32),
    )[1]
    input_part, ln1_gain_sum, ln1_bias_sum = norm_one_back(grad_normed)
    input_grad = grad_resid + input_part
    qkv_piece, out_piece, fc1_piece, fc2_piece = (
        lax.psum_scatter(qkv_grad, "dp", scatter_dimension=1, tiled=True),
        lax.psum_scatter(out_grad, "dp", scatter_dimension=1, tiled=True),
        lax.psum_scatter(fc1_grad, "dp", scatter_dimension=0, tiled=True),
        lax.psum_scatter(fc2_grad, "dp", scatter_dimension=1, tiled=True),
    )
    full_width = layer_input.shape[1]
    head_width = qv_bias.shape[1]
    ff_width = fc1_bias.shape[0]
    row_sums = jnp.stack(
        [
            ln1_gain_sum,
            ln1_bias_sum,
            jnp.sum(resid_low.astype(jnp.float32), axis=0),
            ln2_gain_sum,
            ln2_bias_sum,
            jnp.sum(grad_rows, axis=0),
        ]
    )
    qv_sums = jnp.stack(
        [
            jnp.sum(grad_qkv[0].astype(jnp.float32), axis=0),
            jnp.sum(grad_qkv[2].astype(jnp.float32), axis=0),
        ]
    )
    qv_wide = lax.dynamic_update_slice_in_dim(
        jnp.zeros((2, full_width), jnp.float32), qv_sums, tensor_at * head_width, 1
    )
    fc1_sums = jnp.sum(grad_hidden.astype(jnp.float32), axis=0)
    fc1_wide = lax.dynamic_update_slice_in_dim(
        jnp.zeros((ff_width * lax.axis_size("tensor"),), jnp.float32),
        fc1_sums,
        tensor_at * ff_width,
        0,
    )
    row_total, qv_total, fc1_total = lax.psum((row_sums, qv_wide, fc1_wide), ("dp", "tensor"))
    dp_width = ln1_gain.shape[0]
    row_piece = lax.dynamic_slice_in_dim(row_total, lax.axis_index("dp") * dp_width, dp_width, 1)
    qv_piece = lax.dynamic_slice_in_dim(qv_total, tensor_at * head_width, head_width, 1)
    fc1_bias_piece = lax.dynamic_slice_in_dim(fc1_total, tensor_at * ff_width, ff_width, 0)
    return (
        layer_output,
        input_grad,
        row_piece[0],
        row_piece[1],
        qkv_piece,
        qv_piece,
        out_piece,
        row_piece[2],
        row_piece[3],
        row_piece[4],
        fc1_piece,
        fc1_bias_piece,
        fc2_piece,
        row_piece[5],
    )


LOG2E = 1.4426950408889634
VMEM_BYTES = 60 * 1024 * 1024


def head_window(head, base, width):
    start = base + head * HEAD_DIM
    first = start // 128 * 128
    last = min(-(-(start + HEAD_DIM) // 128) * 128, width)
    return start - first, first, last


def only_head(values, lane, offset):
    inside = (lane >= offset) & (lane < offset + HEAD_DIM)
    return jnp.where(inside, values, 0)


def with_lanes(values, lane, offset, first_column, second_column):
    one, two = (0, 1) if offset >= 2 else (126, 127)
    values = jnp.where(lane == one, first_column, values)
    return jnp.where(lane == two, second_column, values)


def lane_index(rows, first, last):
    return lax.broadcasted_iota(jnp.int32, (rows, last - first), 1)


def row_columns(kind):
    image = kind == 0
    padding = (kind == 1) | (kind == 2)
    low = jnp.bfloat16
    image_query = jnp.where(image, 1.0, 0.0).astype(low)
    other_query = jnp.where(image, 0.0, 1.0).astype(low)
    image_key = jnp.where(image, 0.0, -1e30).astype(low)
    padding_key = jnp.where(padding, 0.0, -1e30).astype(low)
    return image_query, other_query, image_key, padding_key


def dot_last(left, right):
    return lax.dot_general(
        left, right, (((1,), (1,)), ((), ())), preferred_element_type=jnp.float32
    )


def dot_first(left, right):
    return lax.dot_general(
        left, right, (((0,), (0,)), ((), ())), preferred_element_type=jnp.float32
    )


def heads_forward_kernel(places, heads, waits, spot, kind_ref, x_any, bias_ref, *refs):
    count = sum(len(parts) for parts in places)
    pieces = refs[:count]
    qkv_any, probs_any, *mixed_any = refs[count + waits : count + waits + 4]
    x_ref, qkv_ref, probs_ref, keys_ref, values_ref, total_ref, mixed_ref = refs[-12:-5]
    in_sems, out_sems, probs_sems, weights, sems = refs[-5:]
    scale = HEAD_DIM ** (-0.5) * LOG2E
    rows = x_ref.shape[0]
    part = heads * HEAD_DIM
    inner = qkv_ref.shape[2]
    width = keys_ref.shape[1]
    base = width - part
    groups = len(places)
    slots = probs_ref.shape[0]
    copies = weight_copies(places, pieces, weights, sems, spot[0])
    x_copy = pltpu.make_async_copy(x_any, x_ref, in_sems.at[0])
    begin([x_copy] + copies[0])
    arrive([x_copy] + copies[0])
    image_query, other_query, image_key, padding_key = row_columns(kind_ref[...])
    blank = jnp.zeros((rows, base), jnp.bfloat16)
    sent, writes = [], []
    for group in range(groups):
        if group + 1 < groups:
            begin(copies[group + 1])
        if group:
            arrive(copies[group])
        projected = jnp.dot(
            x_ref[...], strips(weights, group)[:, :inner], preferred_element_type=jnp.float32
        )
        qkv_ref[group] = (projected + bias_ref[group]).astype(jnp.bfloat16)
        copy = pltpu.make_async_copy(qkv_ref.at[group], qkv_any.at[group], out_sems.at[group])
        copy.start()
        sent.append(copy)
        keys_ref[:, :part] = qkv_ref[group, :, part : 2 * part]
        keys_ref[:, part:] = blank
        values_ref[:, :base] = blank
        values_ref[:, base:] = qkv_ref[group, :, 2 * part : 3 * part]
        total_ref[...] = jnp.zeros_like(total_ref)
        for head in range(heads):
            offset, first, last = head_window(head, 0, width)
            lane = lane_index(rows, first, last)
            keys = with_lanes(
                only_head(keys_ref[:, first:last], lane, offset),
                lane,
                offset,
                image_key,
                padding_key,
            )
            query = with_lanes(
                only_head(qkv_ref[group, :, first:last], lane, offset),
                lane,
                offset,
                image_query,
                other_query,
            )
            v_offset, v_first, v_last = head_window(head, base, width)
            values = only_head(
                values_ref[:, v_first:v_last], lane_index(rows, v_first, v_last), v_offset
            )
            at = group * heads + head
            slot = at % slots
            if at >= slots:
                writes[at - slots].wait()
            for tile in row_tiles(rows, 384):
                scores = dot_last(query[tile], keys)
                peak = jnp.max(scores, axis=1, keepdims=True)
                expo = jnp.exp2((scores - peak) * scale)
                total = jnp.sum(expo, axis=1, keepdims=True)
                probs = (expo * (1.0 / total)).astype(jnp.bfloat16)
                probs_ref[slot, tile, :] = probs
                total_ref[tile, v_first:v_last] += jnp.dot(
                    probs, values, preferred_element_type=jnp.float32
                )
            copy = pltpu.make_async_copy(
                probs_ref.at[slot], probs_any.at[group, head], probs_sems.at[slot]
            )
            copy.start()
            writes.append(copy)
        mixed_ref[group] = total_ref[...].astype(jnp.bfloat16)
        copy = pltpu.make_async_copy(
            mixed_ref.at[group], mixed_any[group], out_sems.at[groups + group]
        )
        copy.start()
        sent.append(copy)
    arrive(sent + writes[-slots:])


def heads_forward_call(spot, kind, rows_in, biases, groups, waits=()):
    rows, full = rows_in.shape
    arrays, places = flatten(groups)
    _, high, group_width = arrays[0].shape
    depth = full // (2 * high)
    count = len(groups)
    part = group_width // 4
    heads = part // HEAD_DIM
    inner = -(-3 * part // 128) * 128
    outer = -(-part // 128) * 128
    slots = min(8, count * heads)
    return call(
        functools.partial(heads_forward_kernel, places, heads, len(waits)),
        "heads_forward",
        [spot, kind, rows_in, biases, *arrays],
        [smem_spec(), vmem_spec(), any_spec(), vmem_spec()] + [any_spec()] * len(arrays),
        [
            (any_spec(), (count, rows, inner), jnp.bfloat16),
            (any_spec(), (count, heads, rows, rows), jnp.bfloat16),
            (any_spec(), (rows, outer), jnp.bfloat16),
            (any_spec(), (rows, outer), jnp.bfloat16),
        ],
        [
            low_scratch(rows, full),
            low_scratch(count, rows, inner),
            low_scratch(slots, rows, rows),
            low_scratch(rows, outer),
            low_scratch(rows, outer),
            wide_scratch(rows, outer),
            low_scratch(count, rows, outer),
            copy_sems(1),
            copy_sems(2 * count),
            copy_sems(slots),
        ]
        + weight_scratch(places, depth, high, group_width),
        waits,
    )


def heads_backward_kernel(places, heads, picks, waits, spot, grad_any, qkv_any, probs_any, *refs):
    count = sum(len(parts) for parts in places)
    groups = len(places)
    mixed_any = refs[:groups]
    pieces = refs[groups : groups + count]
    first_out = groups + count + waits
    outs_any = refs[first_out : first_out + groups]
    sum_ref = refs[first_out + groups]
    grad_ref, qkv_ref, probs_ref, mixed_ref, out_ref, keys_ref, values_ref, grads_ref = refs[-16:-8]
    query_sum, key_sum, value_sum, in_sems, probs_sems, out_sems, weights, sems = refs[-8:]
    width = keys_ref.shape[1]
    first_lane = pieces[0].shape[2] - width
    loads = weight_copies(places, pieces, weights, sems, spot[0], first_lane, width)
    grad_copy = pltpu.make_async_copy(grad_any, grad_ref, in_sems.at[2 * groups])
    slots = probs_ref.shape[0]
    seconds, reads = [], []
    for group in range(groups):
        seconds.append(
            [
                pltpu.make_async_copy(
                    qkv_any.at[picks[group]], qkv_ref.at[group], in_sems.at[2 * group]
                ),
                pltpu.make_async_copy(
                    mixed_any[group], mixed_ref.at[group], in_sems.at[2 * group + 1]
                ),
            ]
        )
        for head in range(heads):
            slot = len(reads) % slots
            reads.append(
                pltpu.make_async_copy(
                    probs_any.at[picks[group], head], probs_ref.at[slot], probs_sems.at[slot]
                )
            )
    begin([grad_copy] + loads[0])
    begin(seconds[0])
    begin(reads[:2])
    score_scale = HEAD_DIM ** (-0.5)
    rows = grad_ref.shape[0]
    part = heads * HEAD_DIM
    base = width - part
    low = jnp.bfloat16
    blank = jnp.zeros((rows, base), low)
    sent = []
    started = 2
    for group in range(groups):
        arrive(([grad_copy] if group == 0 else []) + loads[group])
        grads_ref[...] = jnp.dot(
            grad_ref[...], strips(weights, group), preferred_element_type=jnp.float32
        ).astype(low)
        arrive(seconds[group])
        if group + 1 < groups:
            begin(loads[group + 1] + seconds[group + 1])
        keys_ref[:, :part] = qkv_ref[group, :, part : 2 * part]
        keys_ref[:, part:] = blank
        values_ref[:, :base] = blank
        values_ref[:, base:] = qkv_ref[group, :, 2 * part : 3 * part]
        query_sum[...] = jnp.zeros_like(query_sum)
        key_sum[...] = jnp.zeros_like(key_sum)
        value_sum[...] = jnp.zeros_like(value_sum)
        weighted = grads_ref[...].astype(jnp.float32) * mixed_ref[group].astype(jnp.float32)
        for head in range(heads):
            at = group * heads + head
            offset, first, last = head_window(head, 0, width)
            lane = lane_index(rows, first, last)
            query = only_head(qkv_ref[group, :, first:last], lane, offset)
            keys = only_head(keys_ref[:, first:last], lane, offset)
            v_offset, v_first, v_last = head_window(head, base, width)
            v_lane = lane_index(rows, v_first, v_last)
            values = values_ref[:, v_first:v_last]
            grad = only_head(grads_ref[:, v_first:v_last], v_lane, v_offset)
            centre = jnp.sum(
                only_head(weighted[:, v_first:v_last], v_lane, v_offset), axis=1, keepdims=True
            )
            while started < len(reads) and started - at < slots:
                reads[started].start()
                started += 1
            reads[at].wait()
            probs = probs_ref[at % slots]
            grad_probs = dot_last(grad, values)
            grad_scores = (probs.astype(jnp.float32) * (grad_probs - centre)).astype(low)
            value_sum[:, v_first:v_last] += dot_first(probs, grad)
            key_sum[:, first:last] += dot_first(grad_scores, query)
            query_sum[:, first:last] += jnp.dot(
                grad_scores, keys, preferred_element_type=jnp.float32
            )
        out_ref[group, :, :part] = (query_sum[...] * score_scale).astype(low)[:, :part]
        out_ref[group, :, part : 2 * part] = (key_sum[...] * score_scale).astype(low)[:, :part]
        out_ref[group, :, 2 * part : 3 * part] = value_sum[...].astype(low)[:, base:]
        tail = out_ref.shape[2] - 3 * part
        if tail:
            out_ref[group, :, 3 * part :] = jnp.zeros((rows, tail), low)
        copy = pltpu.make_async_copy(out_ref.at[group], outs_any[group], out_sems.at[group])
        copy.start()
        sent.append(copy)
        sum_ref[group] = jnp.sum(out_ref[group].astype(jnp.float32), axis=0, keepdims=True)
    arrive(sent)


def heads_backward_call(spot, grad_rows, qkv, probs, mixed, groups, picks, waits=()):
    rows, full = grad_rows.shape
    arrays, places = flatten(groups)
    _, high, group_width = arrays[0].shape
    depth = full // (2 * high)
    part = group_width // 4
    heads = part // HEAD_DIM
    inner = qkv.shape[2]
    outer = mixed[0].shape[1]
    count = len(groups)
    slots = min(count * heads, 6)
    return call(
        functools.partial(heads_backward_kernel, places, heads, picks, len(waits)),
        "heads_backward",
        [spot, grad_rows, qkv, probs, *mixed, *arrays],
        [smem_spec()] + [any_spec()] * (3 + count + len(arrays)),
        [(any_spec(), (rows, inner), jnp.bfloat16)] * count
        + [(vmem_spec(), (count, 1, inner), jnp.float32)],
        [
            low_scratch(rows, full),
            low_scratch(count, rows, inner),
            low_scratch(slots, rows, rows),
            low_scratch(count, rows, outer),
            low_scratch(count, rows, inner),
            low_scratch(rows, outer),
            low_scratch(rows, outer),
            low_scratch(rows, outer),
            wide_scratch(rows, outer),
            wide_scratch(rows, outer),
            wide_scratch(rows, outer),
            copy_sems(2 * count + 1),
            copy_sems(slots),
            copy_sems(count),
        ]
        + weight_scratch(places, depth, high, outer),
        waits,
    )


def any_spec():
    return pl.BlockSpec(memory_space=pl.ANY)


def smem_spec():
    return pl.BlockSpec(memory_space=pltpu.SMEM)


def vmem_spec():
    return pl.BlockSpec(memory_space=pltpu.VMEM)


def limits():
    return pltpu.CompilerParams(vmem_limit_bytes=VMEM_BYTES)


def low_scratch(*shape):
    return pltpu.VMEM(shape, jnp.bfloat16)


def wide_scratch(*shape):
    return pltpu.VMEM(shape, jnp.float32)


def copy_sems(*shape):
    return pltpu.SemaphoreType.DMA(shape)


def begin(copies):
    for copy in copies:
        copy.start()


def arrive(copies):
    for copy in copies:
        copy.wait()


def call(kernel, name, operands, specs, outs, scratch, waits=()):
    no_cost = pl.CostEstimate(flops=0, bytes_accessed=0, transcendentals=0)
    out_specs = [spec for spec, _, _ in outs]
    return pl.pallas_call(
        kernel,
        in_specs=list(specs) + [any_spec()] * len(waits),
        out_specs=out_specs,
        out_shape=[jax.ShapeDtypeStruct(shape, kind) for _, shape, kind in outs],
        scratch_shapes=scratch,
        compiler_params=limits(),
        cost_estimate=no_cost,
        name=name,
    )(*operands, *waits)


def flatten(groups):
    arrays = [piece for group in groups for piece, _, _ in group]
    places = [[(at, x_off) for _, at, x_off in group] for group in groups]
    return arrays, places


def weight_copies(places, refs, weights, sems, x_at, first=0, width=None):
    copies, at = [], 0
    for group, parts in enumerate(places):
        mine = []
        for part, (start, x_off) in enumerate(parts):
            source = refs[at]
            at += 1
            if width is not None:
                source = source.at[:, :, pl.ds(first, width)]
            target = weights.at[group, pl.ds(start, source.shape[0]), x_at ^ x_off]
            mine.append(pltpu.make_async_copy(source, target, sems.at[group, part]))
        copies.append(mine)
    return copies


def weight_scratch(places, depth, high, width):
    count = len(places)
    return [
        pltpu.VMEM((count, depth, 2, high, width), jnp.bfloat16),
        copy_sems(count, max(len(parts) for parts in places)),
    ]


def strips(weights, at):
    _, depth, _, high, width = weights.shape
    return weights[at].reshape(depth * 2 * high, width)


def row_tiles(rows, size):
    return [slice(start, min(start + size, rows)) for start in range(0, rows, size)]


def out_copies(pairs, sems):
    return [
        pltpu.make_async_copy(source, target, sems.at[i])
        for i, (source, target) in enumerate(pairs)
    ]


def up_kernel(places, waits, spot, x_any, bias_ref, *refs):
    count = sum(len(parts) for parts in places)
    pieces = refs[:count]
    active_any, slope_any = refs[count + waits : count + waits + 2]
    x_ref, active_ref, slope_ref, x_sem, out_sems, weights, sems = refs[-7:]
    rows = x_ref.shape[0]
    groups = len(places)
    copies = weight_copies(places, pieces, weights, sems, spot[0])
    x_copy = pltpu.make_async_copy(x_any, x_ref, x_sem.at[0])
    begin([x_copy] + copies[0])
    arrive([x_copy] + copies[0])
    sent = []
    for group in range(groups):
        if group + 1 < groups:
            begin(copies[group + 1])
        if group:
            arrive(copies[group])
        whole = strips(weights, group)
        for tile in row_tiles(rows, 128):
            hidden = jnp.dot(x_ref[tile, :], whole, preferred_element_type=jnp.float32)
            hidden = hidden + bias_ref[group]
            square = hidden * hidden
            inner = jnp.tanh(hidden * (gelu_scale + gelu_scale * 0.044715 * square))
            gate = 0.5 + 0.5 * inner
            active_ref[group, tile, :] = (hidden * gate).astype(jnp.bfloat16)
            grow = hidden * (gelu_scale + 3.0 * 0.044715 * gelu_scale * square)
            slope = gate + grow * (0.5 - 0.5 * inner * inner)
            slope_ref[group, tile, :] = slope.astype(jnp.bfloat16)
        for half, tile in enumerate(row_tiles(rows, rows // 2)):
            span = pl.ds(tile.start, rows // 2)
            for at, (source, target) in enumerate(
                ((active_ref, active_any), (slope_ref, slope_any))
            ):
                copy = pltpu.make_async_copy(
                    source.at[group, span], target.at[group, span], out_sems.at[group, half, at]
                )
                copy.start()
                sent.append(copy)
    arrive(sent)


def up_project(spot, rows_in, biases, groups, waits=()):
    rows, full = rows_in.shape
    arrays, places = flatten(groups)
    _, high, width = arrays[0].shape
    depth = full // (2 * high)
    count = len(groups)
    shape = (count, rows, width)
    return call(
        functools.partial(up_kernel, places, len(waits)),
        "mlp_up",
        [spot, rows_in, biases, *arrays],
        [smem_spec(), any_spec(), vmem_spec()] + [any_spec()] * len(arrays),
        [(any_spec(), shape, jnp.bfloat16)] * 2,
        [
            low_scratch(rows, full),
            low_scratch(*shape),
            low_scratch(*shape),
            copy_sems(1),
            copy_sems(count, 2, 2),
        ]
        + weight_scratch(places, depth, high, width),
        waits,
    )


def slope_kernel(places, waits, spot, x_any, slope_any, *refs):
    count = sum(len(parts) for parts in places)
    pieces = refs[:count]
    out_any, sum_ref = refs[count + waits : count + waits + 2]
    x_ref, slope_ref, out_ref, in_sems, out_sems, weights, sems = refs[-7:]
    rows = x_ref.shape[0]
    groups = len(places)
    copies = weight_copies(places, pieces, weights, sems, spot[0])
    x_copy = pltpu.make_async_copy(x_any, x_ref, in_sems.at[groups])
    for group, mine in enumerate(copies):
        mine.append(
            pltpu.make_async_copy(slope_any.at[group], slope_ref.at[group], in_sems.at[group])
        )
    begin([x_copy] + copies[0])
    arrive([x_copy] + copies[0])
    sent = []
    for group in range(groups):
        if group + 1 < groups:
            begin(copies[group + 1])
        if group:
            arrive(copies[group])
        whole = strips(weights, group)
        total = jnp.zeros((1, weights.shape[-1]), jnp.float32)
        for tile in row_tiles(rows, 256):
            grad = jnp.dot(x_ref[tile, :], whole, preferred_element_type=jnp.float32)
            low = (grad * slope_ref[group, tile, :].astype(jnp.float32)).astype(jnp.bfloat16)
            out_ref[group, tile, :] = low
            total += jnp.sum(low.astype(jnp.float32), axis=0, keepdims=True)
        sum_ref[group] = total
        for half, tile in enumerate(row_tiles(rows, rows // 2)):
            span = pl.ds(tile.start, rows // 2)
            copy = pltpu.make_async_copy(
                out_ref.at[group, span], out_any.at[group, span], out_sems.at[group, half]
            )
            copy.start()
            sent.append(copy)
    arrive(sent)


def hidden_grad(spot, rows_in, slope, groups, waits=()):
    rows, full = rows_in.shape
    arrays, places = flatten(groups)
    _, high, width = arrays[0].shape
    depth = full // (2 * high)
    count = len(groups)
    shape = (count, rows, width)
    return call(
        functools.partial(slope_kernel, places, len(waits)),
        "mlp_grad",
        [spot, rows_in, slope, *arrays],
        [smem_spec(), any_spec(), any_spec()] + [any_spec()] * len(arrays),
        [
            (any_spec(), shape, jnp.bfloat16),
            (vmem_spec(), (count, 1, width), jnp.float32),
        ],
        [
            low_scratch(rows, full),
            low_scratch(*shape),
            low_scratch(*shape),
            copy_sems(count + 1),
            copy_sems(count, 2),
        ]
        + weight_scratch(places, depth, high, width),
        waits,
    )


def unit_rows(values):
    centre = values - jnp.mean(values, axis=1, keepdims=True)
    spread = jnp.mean(centre * centre, axis=1, keepdims=True)
    root = lax.rsqrt(spread + layer_eps)
    return centre * root, root


def norm_rows_back(values, gain, grad):
    unit, root = unit_rows(values)
    scaled = grad * gain
    mean_one = jnp.mean(scaled, axis=1, keepdims=True)
    mean_two = jnp.mean(scaled * unit, axis=1, keepdims=True)
    part = root * (scaled - mean_one - unit * mean_two)
    return part, jnp.sum(grad * unit, axis=0, keepdims=True), jnp.sum(grad, axis=0, keepdims=True)


def back_kernel(places, sources, waits, keep_low, spot, *refs):
    count = sum(len(parts) for parts in places)
    grads_any = refs[:sources]
    base_any, grad_any, gain_ref = refs[sources : sources + 3]
    pieces = refs[sources + 3 : sources + 3 + count]
    outs = 3 if keep_low else 2
    first_out = sources + 3 + count + waits
    out_any, *low_any, sum_ref = refs[first_out : first_out + outs]
    grads_ref, base_ref, grad_ref, total, in_sems, out_sems, weights, sems = refs[
        first_out + outs : first_out + outs + 8
    ]
    rows = total.shape[0]
    groups = len(places)
    width = weights.shape[-1]
    copies = weight_copies(places, pieces, weights, sems, spot[0], 0, width)
    at = 0
    for source in grads_any:
        parts = [source] if len(source.shape) == 2 else [source.at[i] for i in range(source.shape[0])]
        for part in parts:
            copies[at].append(pltpu.make_async_copy(part, grads_ref.at[at], in_sems.at[at]))
            at += 1
    late = [
        pltpu.make_async_copy(base_any, base_ref, in_sems.at[groups]),
        pltpu.make_async_copy(grad_any, grad_ref, in_sems.at[groups + 1]),
    ]
    begin(copies[0])
    for group in range(groups):
        if group + 1 < groups:
            begin(copies[group + 1])
        else:
            begin(late)
        arrive(copies[group])
        whole = strips(weights, group)
        if group == 0:
            total[...] = dot_last(grads_ref[group], whole)
        elif group + 1 < groups:
            total[...] += dot_last(grads_ref[group], whole)
        else:
            products = [
                (tile, dot_last(grads_ref[group, tile, :], whole)) for tile in row_tiles(rows, 256)
            ]
    arrive(late)
    sums = [jnp.zeros((1, total.shape[1]), jnp.float32) for _ in range(3)]
    sent = []
    for tile, product in products:
        for small in range(tile.start, tile.stop, 128):
            span = slice(small, small + 128)
            inside = slice(small - tile.start, small - tile.start + 128)
            part, gain_sum, shift_sum = norm_rows_back(
                base_ref[span, :].astype(jnp.float32),
                gain_ref[...],
                total[span, :] + product[inside],
            )
            grad = grad_ref[span, :].astype(jnp.float32) + part
            total[span, :] = grad
            sums[0] += gain_sum
            sums[1] += shift_sum
            if keep_low:
                low = grad.astype(jnp.bfloat16)
                grads_ref[0, span, :] = low
                sums[2] += jnp.sum(low.astype(jnp.float32), axis=0, keepdims=True)
        long = pl.ds(tile.start, tile.stop - tile.start)
        pairs = [(total.at[long], out_any.at[long])]
        if keep_low:
            pairs.append((grads_ref.at[0, long], low_any[0].at[long]))
        for source, target in pairs:
            copy = pltpu.make_async_copy(source, target, out_sems.at[len(sent)])
            copy.start()
            sent.append(copy)
    sum_ref[...] = jnp.concatenate(sums + [jnp.zeros((5, total.shape[1]), jnp.float32)])
    arrive(sent)


def norm_back(name, spot, grads, base, grad, gain, groups, keep_low, waits=()):
    rows, full = base.shape
    arrays, places = flatten(groups)
    _, high, _ = arrays[0].shape
    width = grads[0].shape[-1]
    depth = full // (2 * high)
    outs = [(any_spec(), (rows, full), jnp.float32)]
    if keep_low:
        outs.append((any_spec(), (rows, full), jnp.bfloat16))
    outs.append((vmem_spec(), (8, full), jnp.float32))
    return call(
        functools.partial(back_kernel, places, len(grads), len(waits), keep_low),
        name,
        [spot, *grads, base, grad, gain, *arrays],
        [smem_spec()] + [any_spec()] * (len(grads) + 2) + [vmem_spec()] + [any_spec()] * len(arrays),
        outs,
        [
            low_scratch(len(groups), rows, width),
            pltpu.VMEM(base.shape, base.dtype),
            pltpu.VMEM(grad.shape, grad.dtype),
            wide_scratch(rows, full),
            copy_sems(len(groups) + 2),
            copy_sems(2 * -(-rows // 256)),
        ]
        + weight_scratch(places, depth, high, width),
        waits,
    )


def down_kernel(places, waits, spot, later_any, early_any, resid_any, shift_ref, *refs):
    count = sum(len(parts) for parts in places)
    pieces = refs[:count]
    out_any = refs[count + waits]
    active_ref, resid_ref, total, out_ref, in_sems, out_sems, weights, sems = refs[-8:]
    rows = total.shape[0]
    groups = len(places)
    copies = weight_copies(places, pieces, weights, sems, spot[0])
    half = groups // 2
    for group in range(groups):
        source = later_any.at[group] if group < half else early_any.at[group - half]
        copies[group].append(
            pltpu.make_async_copy(source, active_ref.at[group], in_sems.at[group])
        )
    late = [pltpu.make_async_copy(resid_any, resid_ref, in_sems.at[groups])]
    begin(copies[0])
    for group in range(groups):
        begin(copies[group + 1] if group + 1 < groups else late)
        arrive(copies[group])
        product = dot_last(active_ref[group], strips(weights, group))
        if group == 0:
            total[...] = product
        else:
            total[...] += product
    arrive(late)
    out_ref[...] = (total[...] + resid_ref[...] + shift_ref[...]).astype(out_ref.dtype)
    copy = pltpu.make_async_copy(out_ref, out_any, out_sems.at[0])
    copy.start()
    copy.wait()


def down_project(spot, first, second, resid, shift, groups, waits=()):
    rows, full = resid.shape
    arrays, places = flatten(groups)
    _, high, width = arrays[0].shape
    depth = full // (2 * high)
    return call(
        functools.partial(down_kernel, places, len(waits)),
        "mlp_down",
        [spot, first, second, resid, shift, *arrays],
        [smem_spec()] + [any_spec()] * 3 + [vmem_spec()] + [any_spec()] * len(arrays),
        [(any_spec(), (rows, full), jnp.bfloat16)],
        [
            low_scratch(len(groups), rows, width),
            wide_scratch(rows, full),
            wide_scratch(rows, full),
            low_scratch(rows, full),
            copy_sems(len(groups) + 1),
            copy_sems(1),
        ]
        + weight_scratch(places, depth, high, width),
        waits,
    )[0]


def out_kernel(places, waits, spot, one, two, three, four, x_any, shift_ref, gain_ref, bias_ref, *refs):
    count = sum(len(parts) for parts in places)
    pieces = refs[:count]
    resid_any, normed_any = refs[count + waits : count + waits + 2]
    mixed_ref, x_ref, resid_ref, normed_ref, in_sems, out_sems, weights, sems = refs[-8:]
    rows = x_ref.shape[0]
    outer = weights.shape[-1]
    first = pieces[0].shape[-1] - outer
    copies = weight_copies(places, pieces, weights, sems, spot[0], first, outer)
    for group, mixed in enumerate((one, two, three, four)):
        copies[group].append(
            pltpu.make_async_copy(mixed, mixed_ref.at[group], in_sems.at[group])
        )
    late = [pltpu.make_async_copy(x_any, x_ref, in_sems.at[4])]
    for mine in copies:
        begin(mine)
    begin(late)
    for group in range(4):
        arrive(copies[group])
        if group < 3:
            product = dot_last(mixed_ref[group], strips(weights, group))
            if group == 0:
                resid_ref[...] = product
            else:
                resid_ref[...] += product
    arrive(late)
    whole = strips(weights, 3)
    products = [(tile, dot_last(mixed_ref[3, tile, :], whole)) for tile in row_tiles(rows, 256)]
    sent = []
    for tile, product in products:
        for small in range(tile.start, tile.stop, 128):
            span = slice(small, small + 128)
            inside = slice(small - tile.start, small - tile.start + 128)
            values = resid_ref[span, :] + product[inside] + x_ref[span, :].astype(jnp.float32)
            values = values + shift_ref[...]
            resid_ref[span, :] = values
            unit, _ = unit_rows(values)
            normed_ref[span, :] = (unit * gain_ref[...] + bias_ref[...]).astype(jnp.bfloat16)
        long = pl.ds(tile.start, tile.stop - tile.start)
        for source, target in ((resid_ref, resid_any), (normed_ref, normed_any)):
            copy = pltpu.make_async_copy(source.at[long], target.at[long], out_sems.at[len(sent)])
            copy.start()
            sent.append(copy)
    arrive(sent)


def out_project(spot, mixed, rows_in, shift, gain, bias, groups, waits=()):
    rows, full = rows_in.shape
    arrays, places = flatten(groups)
    _, high, _ = arrays[0].shape
    outer = mixed[0].shape[1]
    depth = full // (2 * high)
    return call(
        functools.partial(out_kernel, places, len(waits)),
        "attn_out",
        [spot, *mixed, rows_in, shift, gain, bias, *arrays],
        [smem_spec()] + [any_spec()] * 5 + [vmem_spec()] * 3 + [any_spec()] * len(arrays),
        [
            (any_spec(), (rows, full), jnp.float32),
            (any_spec(), (rows, full), jnp.bfloat16),
        ],
        [
            low_scratch(4, rows, outer),
            low_scratch(rows, full),
            wide_scratch(rows, full),
            low_scratch(rows, full),
            copy_sems(5),
            copy_sems(2 * -(-rows // 256)),
        ]
        + weight_scratch(places, depth, high, outer),
        waits,
    )


def grad_kernel(sides, extra, waits, spot, *refs):
    inputs = 4 + (4 if extra else 0)
    sources = refs[:inputs]
    outs_at = inputs + waits
    count = sum(2 + side for side in sides)
    outs = list(refs[outs_at : outs_at + count])
    holds = refs[outs_at + count : outs_at + count + inputs]
    stage, in_sems, out_sems = refs[-3:]
    x_at = spot[0]
    def load(source, hold, at):
        return pltpu.make_async_copy(source, hold, in_sems.at[at])

    count = len(sides)
    first_x = load(sources[0], holds[0], 0)
    second_x = load(sources[2], holds[2], 1)
    firsts = [load(sources[1].at[i], holds[1].at[i], 2 + 2 * i) for i in range(count)]
    seconds = [load(sources[3].at[i], holds[3].at[i], 3 + 2 * i) for i in range(count)]
    extras = [load(sources[j], holds[j], 2 * count + j - 2) for j in range(4, inputs)]
    _, depth, _, high, width = stage.shape
    half = depth // 2
    begin([first_x, firsts[0]])
    arrive([first_x, firsts[0]])
    begin([second_x, seconds[0]])
    begin(extras)
    sent = []
    starts = []
    for side in sides:
        starts.append(sum(2 + before for before in sides[: len(starts)]))
    for i, side in enumerate(sides):
        if i:
            arrive([firsts[i], seconds[i]])
        for part in range(2):
            cut = slice(part * half * 2 * high, (part + 1) * half * 2 * high)
            span = pl.ds(part * half, half)
            product = dot_first(holds[0][:, cut], holds[1][i])
            if i == 0 and part == 0:
                arrive([second_x, seconds[0]])
                for later in range(1, count):
                    begin([firsts[later], seconds[later]])
            product += dot_first(holds[2][:, cut], holds[3][i])
            if extra:
                if i == 0 and part == 0:
                    arrive(extras)
                other = dot_first(holds[4][:, cut], holds[5][...])
                other += dot_first(holds[6][:, cut], holds[7][...])
                both = product.shape[1] + other.shape[1] - width
                left = product.shape[1] - both
                product = jnp.concatenate(
                    [product[:, :left], product[:, left:] + other[:, :both], other[:, both:]],
                    axis=1,
                )
            stage[i, part * half : (part + 1) * half] = product.astype(jnp.bfloat16).reshape(
                half, 2, high, width
            )
            near_out = outs[starts[i]].at[span]
            if side == 0:
                far_out = outs[starts[i] + 1].at[span]
            else:
                far_out = outs[starts[i] + 1 + part]
            for source, target in (
                (stage.at[i, span, x_at], near_out),
                (stage.at[i, span, 1 - x_at], far_out),
            ):
                copy = pltpu.make_async_copy(source, target, out_sems.at[len(sent)])
                copy.start()
                sent.append(copy)
    arrive(sent)


def weight_grad(spot, left, right, depth, sides=(0, 1), extra=(), waits=()):
    rows, full = left[0].shape
    high = full // (2 * depth)
    half = depth // 2
    count = len(sides)
    rights = [values.reshape(count, rows, -1) for values in right]
    width = full if extra else rights[0].shape[2]
    operands = [left[0], rights[0], left[1], rights[1], *extra]
    shapes = []
    for side in sides:
        shapes += [depth, depth] if side == 0 else [depth, half, half]
    outs = [(any_spec(), (size, high, width), jnp.bfloat16) for size in shapes]
    return call(
        functools.partial(grad_kernel, sides, bool(extra), len(waits)),
        "weight_grad",
        [spot, *operands],
        [smem_spec()] + [any_spec()] * len(operands),
        outs,
        [pltpu.VMEM(values.shape, values.dtype) for values in operands]
        + [
            low_scratch(count, depth, 2, high, width),
            copy_sems(2 + 2 * count + 4),
            copy_sems(4 * count),
        ],
        waits,
    )


def corner_kernel(beside_ref, across_ref, one_ref, two_ref, beside_out, across_out):
    wide = jnp.float32
    low = beside_out.dtype
    beside_out[...] = (beside_ref[...].astype(wide) + two_ref[...].astype(wide)).astype(low)
    across_out[...] = (across_ref[...].astype(wide) + one_ref[...].astype(wide)).astype(low)


def add_corners(beside, across, corner_one, corner_two):
    block = corner_one.shape
    first = pl.BlockSpec(block, lambda i: (0, 0, 0))
    second = pl.BlockSpec(block, lambda i: (1, 0, 0))
    shape = jax.ShapeDtypeStruct(beside.shape, beside.dtype)
    return pl.pallas_call(
        corner_kernel,
        grid=(1,),
        in_specs=[second, first, first, first],
        out_specs=[second, first],
        out_shape=[shape, shape],
        input_output_aliases={0: 0, 1: 1},
        compiler_params=limits(),
        name="add_corners",
    )(beside, across, corner_one, corner_two)


def one_corner_kernel(base_ref, part_ref, out_ref):
    total = base_ref[...].astype(jnp.float32) + part_ref[...].astype(jnp.float32)
    out_ref[...] = total.astype(out_ref.dtype)


def add_corner(base, part, half):
    block = part.shape
    spec = pl.BlockSpec(block, lambda i: (half, 0, 0))
    return pl.pallas_call(
        one_corner_kernel,
        grid=(1,),
        in_specs=[spec, pl.BlockSpec(block, lambda i: (0, 0, 0))],
        out_specs=spec,
        out_shape=jax.ShapeDtypeStruct(base.shape, base.dtype),
        input_output_aliases={0: 0},
        compiler_params=limits(),
        name="add_corner",
    )(base, part)


def square_kernel(own, one, two, out):
    wide = jnp.float32
    total = own[...].astype(wide) + one[...].astype(wide) + two[...].astype(wide)
    out[...] = total.astype(out.dtype)


def add_square(own, one, two):
    depth, high, width = own.shape
    block = pl.BlockSpec((depth // 2, high, width), lambda i: (i, 0, 0))
    return pl.pallas_call(
        square_kernel,
        grid=(2,),
        in_specs=[block, block, block],
        out_specs=block,
        out_shape=jax.ShapeDtypeStruct(own.shape, own.dtype),
        compiler_params=limits(),
        name="add_square",
    )(own, one, two)


def halves_kernel(first_ref, second_ref, first_out, second_out):
    first_out[...] = first_ref[...]
    second_out[...] = second_ref[...]


def take_halves(first, second):
    half = (first.shape[0] // 2,) + first.shape[1:]
    front = pl.BlockSpec(half, lambda i: (0, 0, 0))
    back = pl.BlockSpec(half, lambda i: (1, 0, 0))
    shape = jax.ShapeDtypeStruct(half, first.dtype)
    return pl.pallas_call(
        halves_kernel,
        grid=(1,),
        in_specs=[front, back],
        out_specs=[front, front],
        out_shape=[shape, shape],
        compiler_params=limits(),
        name="take_halves",
    )(first, second)


PATCHES = 729
AXES = ("dp", "tensor")


def nothing(*refs):
    del refs


def fence(released, waited=()):
    anywhere = pl.BlockSpec(memory_space=pl.ANY)
    released, waited = list(released), list(waited)
    return pl.pallas_call(
        nothing,
        in_specs=[anywhere] * (len(released) + len(waited)),
        out_specs=[anywhere] * len(released),
        out_shape=[jax.ShapeDtypeStruct(values.shape, values.dtype) for values in released],
        input_output_aliases={i: i for i in range(len(released))},
        name="fence",
    )(*released, *waited)


class Grid:
    def __init__(self, depth):
        self.depth = depth
        dp_at = lax.axis_index("dp")
        self.y = lax.axis_index("tensor")
        self.c = dp_at % 2
        self.x = dp_at // 2 % 2
        self.z = dp_at // 4

    def move(self, values, where):
        pairs = []
        for z in range(self.depth):
            for x in range(2):
                for c in range(2):
                    for y in range(2):
                        to_z, to_x, to_c, to_y = where(z, x, c, y)
                        pairs.append(
                            (
                                ((z * 2 + x) * 2 + c) * 2 + y,
                                ((to_z * 2 + to_x) * 2 + to_c) * 2 + to_y,
                            )
                        )
        return lax.ppermute(values, AXES, pairs)

    def over_x(self, values):
        return self.move(values, lambda z, x, c, y: (z, 1 - x, c, y))

    def over_y(self, values):
        return self.move(values, lambda z, x, c, y: (z, x, c, 1 - y))

    def over_core(self, values):
        return self.move(values, lambda z, x, c, y: (z, x, 1 - c, y))

    def along_z(self, values, hops):
        return self.move(values, lambda z, x, c, y: ((z + hops) % self.depth, x, c, y))

    def across_z(self, values, bit):
        return self.move(values, lambda z, x, c, y: (z ^ bit, x, c, y))

    def spread(self, block):
        width = block.shape[1] // 2
        mine = lax.dynamic_slice_in_dim(block, self.c * width, width, 1)
        theirs = self.over_core(
            lax.dynamic_slice_in_dim(block, (1 - self.c) * width, width, 1)
        )
        first = jnp.where(self.c == 0, mine, theirs)
        second = jnp.where(self.c == 0, theirs, mine)
        return jnp.concatenate([first, second])

    def depth_groups(self):
        return [
            [(z * 2 + x) * 2 + c for z in range(self.depth)] for x in range(2) for c in range(2)
        ]

    def gather_depth(self, block):
        return lax.all_gather(block, "dp", axis_index_groups=self.depth_groups())

    def scatter_depth(self, total):
        return lax.psum_scatter(total, "dp", axis_index_groups=self.depth_groups())

    def scatter_core(self, result):
        result = result.astype(jnp.float32)
        shard = result.shape[0] // 2
        mine = lax.dynamic_slice_in_dim(result, self.c * shard, shard)
        theirs = self.over_core(
            lax.dynamic_slice_in_dim(result, (1 - self.c) * shard, shard)
        )
        first = jnp.where(self.c == 0, mine, theirs)
        second = jnp.where(self.c == 0, theirs, mine)
        return jnp.stack([first, second])

    def gather_small(self, values):
        count, shard = values.shape
        parts = jnp.zeros((self.depth, 2, 2, count, shard), values.dtype)
        parts = lax.dynamic_update_slice(
            parts, values[None, None, None], (self.z, self.x, self.c, 0, 0)
        )
        parts = parts + self.over_core(parts)
        parts = parts + self.over_x(parts)
        bit = 1
        while bit < self.depth:
            parts = parts + self.across_z(parts, bit)
            bit *= 2
        return parts.transpose(3, 0, 1, 2, 4).reshape(count, -1)


def image_shards(
    depth,
    layer_input,
    token_image,
    cotangent,
    ln1_gain,
    ln1_bias,
    w_qkv,
    qv_bias,
    w_out,
    out_bias,
    ln2_gain,
    ln2_bias,
    w_fc1,
    fc1_bias,
    w_fc2,
    fc2_bias,
):
    low = jnp.bfloat16
    wide = jnp.float32
    grid = Grid(depth)
    rows, full_width = layer_input.shape
    shard = ln1_gain.shape[0]
    head_width = qv_bias.shape[1]
    ff_width = fc1_bias.shape[0]
    padded = -(-(rows + 1) // 256) * 256

    quarter = head_width // 2
    group_width = 4 * quarter
    ff_padding = 2 * group_width - ff_width
    sources = [w_qkv[0], w_qkv[1], w_qkv[2], w_out.T]
    first_block = jnp.concatenate(
        [values[:, i * quarter : (i + 1) * quarter] for i in range(2) for values in sources],
        axis=1,
    )
    second_block = jnp.pad(w_fc1, ((0, 0), (0, ff_padding)))
    third_block = jnp.pad(w_fc2.T, ((0, 0), (0, ff_padding)))
    half = depth // 2
    blocks = [grid.spread(first_block), grid.spread(second_block), grid.spread(third_block)]
    vectors = jnp.stack([ln1_gain, ln1_bias, out_bias, ln2_gain, ln2_bias, fc2_bias])
    (vectors,) = fence([vectors], [blocks[0]])
    vectors = grid.gather_small(vectors).astype(wide)
    own_one = grid.gather_depth(blocks[0])

    here = grid.y
    mine = lax.dynamic_slice_in_dim(token_image, here * rows, rows)
    theirs = lax.dynamic_slice_in_dim(token_image, (1 - here) * rows, rows)
    mine, theirs = fence([mine, theirs], [blocks[0]])
    places = lax.iota(jnp.int32, rows)
    stray = mine == 1 - here
    stray_here = jnp.any(stray)
    stray_there = jnp.any(theirs == here)
    blank = mine == IMAGES
    first_blank = jnp.min(jnp.where(blank, places, rows - 1))
    last_blank = jnp.max(jnp.where(blank, places, 0))
    swap_at = jnp.where(stray_here, jnp.max(jnp.where(stray, places, 0)), first_blank)
    swapped = stray_here | stray_there
    blank_at = jnp.where(stray_here, swap_at, last_blank)

    def one_row(values, at):
        return lax.dynamic_slice_in_dim(values, at, 1)

    sent = jnp.concatenate(
        [one_row(layer_input, swap_at), one_row(cotangent, swap_at), one_row(layer_input, last_blank)]
    )
    came = grid.over_y(sent)
    other_blank = jnp.where(stray_there, sent[0:1], came[2:3])
    spread_rows = lax.broadcasted_iota(jnp.int32, (padded, 1), 0)
    at_swap = (spread_rows == swap_at) & swapped

    def stretch(values):
        return jnp.pad(values, ((0, padded - rows), (0, 0)))

    input_rows = jnp.where(at_swap, came[0:1], stretch(layer_input))
    input_rows = jnp.where(spread_rows == rows, other_blank, input_rows)
    grad_low = jnp.where(at_swap, came[1:2], stretch(cotangent))
    grad_low = jnp.where(spread_rows == blank_at, 0, grad_low).astype(low)
    kind = jnp.where(spread_rows > rows, 3, jnp.where(spread_rows == rows, 2, 0))
    kind = jnp.where(spread_rows == blank_at, 1, kind)
    input_rows, grad_low = lax.optimization_barrier((input_rows, grad_low))

    biases = jnp.concatenate([qv_bias.reshape(-1), fc1_bias])
    biases = jnp.pad(biases, (0, -biases.shape[0] % 128)).reshape(-1, 128)
    (biases,) = fence([biases], [blocks[0]])
    other_biases = grid.over_y(biases).reshape(-1)

    def ordered(first, second):
        return jnp.where(grid.c == 0, first, second), jnp.where(grid.c == 0, second, first)

    spot = grid.x.reshape(1)
    inner = -(-3 * quarter // 128) * 128
    qv_groups, fc1_groups = [], []
    for flat in (biases.reshape(-1), other_biases):
        flat = flat.astype(wide)
        pair = flat[: 2 * head_width].reshape(2, 2, quarter)
        none = jnp.zeros((quarter,), wide)
        rest = jnp.zeros((inner - 3 * quarter,), wide)
        qv_groups += ordered(
            *[jnp.concatenate([pair[0, i], none, pair[1, i], rest]) for i in range(2)]
        )
        hidden_bias = flat[2 * head_width : 2 * head_width + ff_width]
        hidden_bias = jnp.pad(hidden_bias, (0, ff_padding))
        fc1_groups += ordered(hidden_bias[:group_width], hidden_bias[group_width:])

    def stacked(rows_of, picked):
        return jnp.stack([rows_of[i] for i in picked])[:, None]

    qv_stacks = [stacked(qv_groups, picked) for picked in ((0, 1), (2, 3))]
    fc1_stacks = [stacked(fc1_groups, picked) for picked in ((1, 3), (0, 2))]

    def sides_of(own):
        return [grid.over_x(own), grid.over_y(own)]

    def corners_of(beside, across):
        first, second = take_halves(beside, across)
        return [grid.over_y(first), grid.over_x(second)]

    def cores_of(*values):
        return [grid.over_core(value) for value in values]

    def near_groups(own, beside, there):
        return [
            [(own, 0, 0), (beside, 0, 1)],
            [(there[0], 0, 0), (there[1], 0, 1)],
        ]

    def far_groups(across, corner, there):
        return [
            [(across, 0, 0), (corner[0], 0, 1), (corner[1], half, 1)],
            [(there[0], 0, 0), (there[1], 0, 1), (there[2], half, 1)],
        ]

    own_one, vectors, input_rows, grad_low, kind, block_two, block_three, *stacks = fence(
        [own_one, vectors, input_rows, grad_low, kind, blocks[1], blocks[2]]
        + qv_stacks
        + fc1_stacks
    )
    qv_stacks, fc1_stacks = stacks[:2], stacks[2:]
    gain_one, shift_one, out_shift, gain_two, shift_two, fc2_shift = [
        vectors[i : i + 1] for i in range(6)
    ]
    own_two = grid.gather_depth(block_two)
    beside_one, across_one = sides_of(own_one)
    unit_one, _ = unit_rows(input_rows.astype(wide))
    normed = (unit_one * gain_one + shift_one).astype(low)
    own_two, beside_one, across_one, normed, block_three, grad_there = fence(
        [own_two, beside_one, across_one, normed, block_three, grid.over_core(grad_low)]
    )
    corner_one = corners_of(beside_one, across_one)
    there = cores_of(own_one, beside_one)
    own_two_there = grid.over_core(own_two)
    across_there = grid.over_core(across_one)
    sides_two = sides_of(own_two)
    own_three = grid.gather_depth(block_three)

    def heads(stack, groups, waits=()):
        return heads_forward_call(spot, kind, normed, stack, groups, waits)

    attn_weights = near_groups(own_one, beside_one, there)
    first_qkv, first_probs, *mixed = heads(qv_stacks[0], attn_weights, [own_two_there])
    *corner_one, across_there, first_qkv = fence(corner_one + [across_there, first_qkv])
    there = [across_there] + cores_of(*corner_one)
    attn_weights = attn_weights + far_groups(across_one, corner_one, there)
    second_qkv, second_probs, *more = heads(qv_stacks[1], attn_weights[2:])
    mixed = mixed + more
    own_three, beside_two, across_two, second_qkv = fence(
        [own_three] + sides_two + [second_qkv]
    )
    corner_two = corners_of(beside_two, across_two)
    sides_three = sides_of(own_three)
    beside_there, across_there = cores_of(beside_two, across_two)
    own_three_there = grid.over_core(own_three)
    resid, normed_two = out_project(
        spot,
        mixed,
        input_rows,
        out_shift,
        gain_two,
        shift_two,
        attn_weights,
        [beside_there, across_there, own_three_there],
    )
    *corner_two, normed_two = fence(corner_two + [normed_two])
    up_weights = near_groups(own_two, beside_two, [own_two_there, beside_there])
    there = [across_there] + cores_of(*corner_two)
    up_weights = up_weights + far_groups(across_two, corner_two, there)
    classes = ((1, 3), (0, 2))

    def up(at, waits):
        picked = [up_weights[i] for i in classes[at]]
        return up_project(spot, normed_two, fc1_stacks[at], picked, waits)

    other_active, other_slope = up(0, [])
    beside_three, across_three, other_active = fence(sides_three + [other_active])
    corner_three = corners_of(beside_three, across_three)
    beside_there = grid.over_core(beside_three)
    across_there = grid.over_core(across_three)
    active_there = grid.over_core(other_active)
    own_active, own_slope = up(1, [other_active])
    *corner_three, own_active, active_there = fence(corner_three + [own_active, active_there])
    down_weights = near_groups(own_three, beside_three, [own_three_there, beside_there])
    there = [across_there] + cores_of(*corner_three)
    down_weights = down_weights + far_groups(across_three, corner_three, there)
    fc2_sums = weight_grad(spot, (grad_low, grad_there), (own_active, active_there), depth)

    def move_corners(sums):
        return [grid.over_x(sums[3]), grid.over_y(sums[4])]

    def back(at, slope, waits):
        picked = [down_weights[i] for i in classes[at]]
        return hidden_grad(spot, grad_low, slope, picked, waits)

    moved = move_corners(fc2_sums)
    other_hidden, other_fc1_sums = back(0, other_slope, [fc2_sums[0]])
    hidden_there = grid.over_core(other_hidden)
    normed_two_there = grid.over_core(normed_two)
    own_hidden, own_fc1_sums = back(1, own_slope, [other_hidden])
    *moved, own_hidden, hidden_there, normed_two_there = fence(
        moved + [own_hidden, hidden_there, normed_two_there]
    )
    beside, across = add_corners(fc2_sums[1], fc2_sums[2], *moved)
    moved = [grid.over_x(beside), grid.over_y(across)]
    fc1_sums = weight_grad(
        spot, (normed_two, normed_two_there), (own_hidden, hidden_there), depth, waits=[beside]
    )
    normed_there = grid.over_core(normed)
    by_class = [up_weights[i] for i in classes[0] + classes[1]]
    grad_resid, resid_low, sums_two = norm_back(
        "norm_two_back",
        spot,
        [other_hidden, own_hidden],
        resid,
        grad_low,
        gain_two,
        by_class,
        True,
        [fc1_sums[0], normed_there],
    )
    *moved, resid_low, corner_a, corner_b = fence(moved + [resid_low, *fc1_sums[3:]])
    fc2_piece = grid.scatter_depth(add_square(fc2_sums[0], *moved))
    moved = [grid.over_x(corner_a), grid.over_y(corner_b)]
    resid_there = grid.over_core(resid_low)

    def heads_back(qkv, probs, side, waits):
        order = [1 + 2 * side, 2 * side]
        return heads_backward_call(
            spot,
            resid_low,
            qkv,
            probs,
            [mixed[i] for i in order],
            [attn_weights[i] for i in order],
            (1, 0),
            waits,
        )

    far_other, far_own, far_sums = heads_back(second_qkv, second_probs, 1, [])
    *moved, far_other = fence(moved + [far_other])
    far_there = grid.over_core(far_other)
    beside, across = add_corners(fc1_sums[1], fc1_sums[2], *moved)
    moved = [grid.over_x(beside), grid.over_y(across)]
    far_mixed = grid.over_core(mixed[3])
    near_other, near_own, near_sums_qkv = heads_back(first_qkv, first_probs, 0, [beside])
    near_other, far_there, far_mixed, resid_there, fc2_piece = fence(
        [near_other, far_there, far_mixed, resid_there, fc2_piece]
    )
    near_there = grid.over_core(near_other)
    near_mixed = grid.over_core(mixed[1])

    def attn_grad(side, own_part, there_part, own_mixed, there_mixed, waits):
        return weight_grad(
            spot,
            (normed, normed_there),
            (own_part, there_part),
            depth,
            (side,),
            (resid_low, own_mixed, resid_there, there_mixed),
            waits,
        )

    far_across, corner_a, corner_b = attn_grad(1, far_own, far_there, mixed[2], far_mixed, [])
    *moved, corner_a, corner_b = fence(moved + [corner_a, corner_b])
    fc1_piece = grid.scatter_depth(add_square(fc1_sums[0], *moved))
    moved = [grid.over_x(corner_a), grid.over_y(corner_b)]
    near_sums, beside = attn_grad(0, near_own, near_there, mixed[0], near_mixed, [far_across])
    *moved, beside = fence(moved + [beside])
    beside, across = add_corners(beside, far_across, *moved)
    moved = [grid.over_x(beside), grid.over_y(across)]
    by_class = [down_weights[i] for i in classes[0] + classes[1]]
    layer_rows = down_project(
        spot, other_active, own_active, resid, fc2_shift, by_class, [beside]
    )
    by_class = [attn_weights[i] for i in (1, 3, 0, 2)]
    input_grad, sums_one = norm_back(
        "norm_one_back",
        spot,
        [near_other, far_other, near_own, far_own],
        input_rows,
        grad_resid,
        gain_one,
        by_class,
        False,
        [layer_rows],
    )

    def column_sum(values):
        return jnp.sum(values.astype(wide), axis=0)

    def absolute(near_other, near_own, far_other, far_own):
        near = ordered(near_own, near_other)
        far = ordered(far_own, far_other)
        return [
            (jnp.where(here == 0, one, two), jnp.where(here == 0, two, one))
            for one, two in zip(near, far)
        ]

    qkv_totals = absolute(near_sums_qkv[0], near_sums_qkv[1], far_sums[0], far_sums[1])
    query_and_value = [
        qkv_totals[half_at][side][0, at : at + quarter]
        for side in range(2)
        for at in (0, 2 * quarter)
        for half_at in range(2)
    ]
    fc1_totals = absolute(
        other_fc1_sums[0], own_fc1_sums[0], other_fc1_sums[1], own_fc1_sums[1]
    )
    fc1_rows = []
    for side in range(2):
        fc1_rows += [fc1_totals[0][side][0], fc1_totals[1][side][0, : ff_width - group_width]]
    flat = jnp.concatenate(
        [
            sums_one[0],
            sums_one[1],
            sums_two[2],
            sums_two[0],
            sums_two[1],
            column_sum(grad_low),
            *query_and_value,
            *fc1_rows,
        ]
    )
    length = flat.shape[0]
    lines = -(-length // 1024) * 8
    flat = jnp.pad(flat, (0, lines * 128 - length)).reshape(lines, 128)
    *moved, flat, fc1_piece = fence(moved + [flat, fc1_piece])
    total = add_square(near_sums, *moved)
    attn_piece = grid.scatter_depth(total)
    (flat, fc1_piece, fc2_piece) = fence([flat, fc1_piece, fc2_piece], [total])
    flat = flat + grid.over_core(flat)
    flat = flat + grid.over_x(flat)
    flat = flat + grid.over_y(flat)
    bit = 1
    while bit < depth:
        flat = flat + grid.across_z(flat, bit)
        bit *= 2
    flat = flat.reshape(-1)
    fc1_piece = grid.scatter_core(fc1_piece)
    fc2_piece = grid.scatter_core(fc2_piece)
    swap_from = fence([one_row(layer_rows, swap_at), one_row(input_grad, swap_at)], [total])
    returned = [grid.over_y(values) for values in swap_from]
    layer_output = jnp.where(at_swap, returned[0], layer_rows)[:rows]
    input_grad = jnp.where(at_swap, returned[1], input_grad)[:rows]
    attn_piece = grid.scatter_core(attn_piece)
    row_total = flat[: 6 * full_width].reshape(6, full_width)
    row_piece = lax.dynamic_slice_in_dim(row_total, lax.axis_index("dp") * shard, shard, 1)
    start = 6 * full_width
    qv_piece = lax.dynamic_slice_in_dim(flat, start + here * 2 * head_width, 2 * head_width)
    start = start + 4 * head_width
    fc1_bias_piece = lax.dynamic_slice_in_dim(flat, start + here * ff_width, ff_width)
    heads_piece = attn_piece.reshape(2, shard, 4, quarter).transpose(2, 1, 0, 3)
    heads_piece = heads_piece.reshape(4, shard, head_width)

    def whole_columns(pair):
        return jnp.concatenate([pair[0], pair[1][:, : group_width - ff_padding]], axis=1)

    return (
        layer_output,
        input_grad,
        row_piece[0],
        row_piece[1],
        heads_piece[:3],
        qv_piece.reshape(2, head_width),
        heads_piece[3].T,
        row_piece[2],
        row_piece[3],
        row_piece[4],
        whole_columns(fc1_piece),
        fc1_bias_piece,
        whole_columns(fc2_piece).T,
        row_piece[5],
    )


def fits_images(mesh):
    groups = mesh.shape["dp"] // 4
    return (
        mesh.shape["tensor"] == IMAGES
        and mesh.shape["dp"] % 4 == 0
        and groups >= 2
        and groups & (groups - 1) == 0
    )


def solution(mesh):
    in_specs = (
        P(("dp", "tensor"), None),
        P("dp"),
        P(("dp", "tensor"), None),
        P("dp"),
        P("dp"),
        P(None, "dp", "tensor"),
        P(None, "tensor"),
        P("tensor", "dp"),
        P("dp"),
        P("dp"),
        P("dp"),
        P("dp", "tensor"),
        P("tensor"),
        P("tensor", "dp"),
        P("dp"),
    )
    out_specs = (
        P(("dp", "tensor"), None),
        P(("dp", "tensor"), None),
        P("dp"),
        P("dp"),
        P(None, "dp", "tensor"),
        P(None, "tensor"),
        P("tensor", "dp"),
        P("dp"),
        P("dp"),
        P("dp"),
        P("dp", "tensor"),
        P("tensor"),
        P("tensor", "dp"),
        P("dp"),
    )

    def body(*arrays):
        slots = arrays[1].shape[0]
        if fits_images(mesh) and slots == IMAGES * (PATCHES + 1):
            return image_shards(mesh.shape["dp"] // 4, *arrays)
        return shards(*arrays)

    return jax.shard_map(body, mesh=mesh, in_specs=in_specs, out_specs=out_specs, check_vma=False)
```

```python
import functools

import jax
import jax.numpy as jnp
from jax import lax
from jax.experimental import pallas as pl
from jax.experimental.pallas import tpu as pltpu
from jax.sharding import PartitionSpec as P

HEAD_DIM = 72
IMAGES = 2


layer_eps = 1e-06
gelu_scale = 0.7978845608028654


def gelu_tanh(values):
    return (
        0.5 * values * (1.0 + jnp.tanh(gelu_scale * (values + 0.044715 * values * values * values)))
    )


def norm_rows(values, gain, shift):
    centre = values - jnp.mean(values, axis=1, keepdims=True)
    spread = jnp.mean(centre * centre, axis=1, keepdims=True)
    return centre * lax.rsqrt(spread + layer_eps) * gain + shift


def contract_rows(left, right):
    return lax.dot_general(
        left, right, (((0,), (0,)), ((), ())), preferred_element_type=jnp.float32
    )


def contract_cols(left, right):
    return lax.dot_general(
        left, right, (((1,), (1,)), ((), ())), preferred_element_type=jnp.float32
    )


def split_heads(values, head_count):
    slot_count = values.shape[0]
    return values.reshape(slot_count, head_count, -1).transpose(1, 0, 2)


def join_heads(values):
    head_count, slot_count, head_size = values.shape
    return values.transpose(1, 0, 2).reshape(slot_count, head_count * head_size)


def block_rows(slot_count):
    half_rows = slot_count // 2
    return half_rows


def masked_scores(rows_query, head_keys, rows_ids, image_ids, score_scale):
    scores = contract_cols(rows_query, head_keys) * score_scale
    return jnp.where(rows_ids[:, None] == image_ids[None, :], scores, -1e30)


def heads_forward(query_heads, key_heads, value_heads, image_ids, score_scale):
    slot_count, head_size = (query_heads.shape[1], query_heads.shape[2])
    block_size = block_rows(slot_count)
    block_count = slot_count // block_size
    id_blocks = image_ids.reshape(block_count, block_size)

    def one_head(head_inputs):
        head_query, head_keys, head_values = head_inputs

        def one_block(block_inputs):
            rows_query, rows_ids = block_inputs
            scores = masked_scores(rows_query, head_keys, rows_ids, image_ids, score_scale)
            peak = jnp.max(scores, axis=1, keepdims=True)
            expo_rows = jnp.exp(scores - peak)
            row_total = jnp.sum(expo_rows, axis=1, keepdims=True)
            prob_rows = (expo_rows / row_total).astype(jnp.bfloat16)
            mixed = jnp.dot(prob_rows, head_values, preferred_element_type=jnp.float32)
            return (mixed.astype(jnp.bfloat16), peak[:, 0] + jnp.log(row_total[:, 0]))

        mixed, logsum = lax.map(
            one_block, (head_query.reshape(block_count, block_size, head_size), id_blocks)
        )
        return (mixed.reshape(slot_count, head_size), logsum.reshape(slot_count))

    return lax.map(one_head, (query_heads, key_heads, value_heads))


def heads_backward(query_heads, key_heads, value_heads, grad_heads, logsum, image_ids, score_scale):
    slot_count, head_size = (query_heads.shape[1], query_heads.shape[2])
    block_size = block_rows(slot_count)
    block_count = slot_count // block_size
    id_blocks = image_ids.reshape(block_count, block_size)

    def one_head(head_inputs):
        head_query, head_keys, head_values, head_grad, head_logsum = head_inputs

        def one_block(carried, block_inputs):
            key_sum, value_sum = carried
            rows_query, rows_grad, rows_logsum, rows_ids = block_inputs
            scores = masked_scores(rows_query, head_keys, rows_ids, image_ids, score_scale)
            prob_rows = jnp.exp(scores - rows_logsum[:, None])
            value_sum = value_sum + contract_rows(prob_rows.astype(jnp.bfloat16), rows_grad)
            grad_probs = contract_cols(rows_grad, head_values)
            centre = jnp.sum(grad_probs * prob_rows, axis=1, keepdims=True)
            grad_scores = (prob_rows * (grad_probs - centre)).astype(jnp.bfloat16)
            rows_dq = (
                jnp.dot(grad_scores, head_keys, preferred_element_type=jnp.float32) * score_scale
            ).astype(jnp.bfloat16)
            key_sum = key_sum + contract_rows(grad_scores, rows_query) * score_scale
            return ((key_sum, value_sum), rows_dq)

        zeros_init = jnp.zeros((slot_count, head_size), jnp.float32)
        block_inputs = (
            head_query.reshape(block_count, block_size, head_size),
            head_grad.reshape(block_count, block_size, head_size),
            head_logsum.reshape(block_count, block_size),
            id_blocks,
        )
        (key_sum, value_sum), query_grad = lax.scan(
            one_block, (zeros_init, zeros_init), block_inputs
        )
        return (
            query_grad.reshape(slot_count, head_size),
            key_sum.astype(jnp.bfloat16),
            value_sum.astype(jnp.bfloat16),
        )

    return lax.map(one_head, (query_heads, key_heads, value_heads, grad_heads, logsum))


def forward_pass(inputs, full_output):
    (
        layer_input,
        token_image,
        ln1_gain,
        ln1_bias,
        w_qkv,
        qv_bias,
        w_out,
        out_bias,
        ln2_gain,
        ln2_bias,
        w_fc1,
        fc1_bias,
        w_fc2,
        fc2_bias,
    ) = inputs
    head_count = w_qkv.shape[2] // HEAD_DIM
    score_scale = HEAD_DIM ** (-0.5)
    attn_params = (
        lax.all_gather(ln1_gain, "dp", axis=0, tiled=True),
        lax.all_gather(ln1_bias, "dp", axis=0, tiled=True),
        lax.all_gather(w_qkv, "dp", axis=1, tiled=True),
        lax.all_gather(w_out, "dp", axis=1, tiled=True),
        lax.all_gather(out_bias, "dp", axis=0, tiled=True),
    )
    mlp_params = (
        lax.all_gather(ln2_gain, "dp", axis=0, tiled=True),
        lax.all_gather(ln2_bias, "dp", axis=0, tiled=True),
        lax.all_gather(w_fc1, "dp", axis=0, tiled=True),
        lax.all_gather(w_fc2, "dp", axis=1, tiled=True),
        lax.all_gather(fc2_bias, "dp", axis=0, tiled=True),
    )
    input_rows = layer_input.astype(jnp.float32)
    normed = norm_rows(
        input_rows, attn_params[0].astype(jnp.float32), attn_params[1].astype(jnp.float32)
    )
    first_in = lax.all_gather(normed.astype(jnp.bfloat16), "tensor", axis=0, tiled=True)
    projected = jnp.einsum(
        "sd,cde->cse", first_in, attn_params[2], preferred_element_type=jnp.float32
    )
    bias_rows = qv_bias.astype(jnp.float32)
    query_heads = split_heads((projected[0] + bias_rows[0]).astype(jnp.bfloat16), head_count)
    key_heads = split_heads(projected[1].astype(jnp.bfloat16), head_count)
    value_heads = split_heads((projected[2] + bias_rows[1]).astype(jnp.bfloat16), head_count)
    mixed, logsum = heads_forward(query_heads, key_heads, value_heads, token_image, score_scale)
    attn_out = join_heads(mixed)
    resid = (
        input_rows
        + lax.psum_scatter(
            jnp.dot(attn_out, attn_params[3], preferred_element_type=jnp.float32),
            "tensor",
            scatter_dimension=0,
            tiled=True,
        )
        + attn_params[4].astype(jnp.float32)
    )
    normed_two = norm_rows(
        resid, mlp_params[0].astype(jnp.float32), mlp_params[1].astype(jnp.float32)
    )
    second_in = lax.all_gather(normed_two.astype(jnp.bfloat16), "tensor", axis=0, tiled=True)
    hidden = jnp.dot(
        second_in, mlp_params[2], preferred_element_type=jnp.float32
    ) + fc1_bias.astype(jnp.float32)
    active = gelu_tanh(hidden).astype(jnp.bfloat16)
    layer_output = None
    if full_output:
        summed = lax.psum_scatter(
            jnp.dot(active, mlp_params[3], preferred_element_type=jnp.float32).astype(jnp.bfloat16),
            "tensor",
            scatter_dimension=0,
            tiled=True,
        ).astype(jnp.float32)
        layer_output = (resid + summed + mlp_params[4].astype(jnp.float32)).astype(jnp.bfloat16)
    return (
        attn_params,
        mlp_params,
        input_rows,
        first_in,
        query_heads,
        key_heads,
        value_heads,
        logsum,
        attn_out,
        resid,
        second_in,
        hidden,
        active,
        layer_output,
    )


def shards(
    layer_input,
    token_image,
    cotangent,
    ln1_gain,
    ln1_bias,
    w_qkv,
    qv_bias,
    w_out,
    out_bias,
    ln2_gain,
    ln2_bias,
    w_fc1,
    fc1_bias,
    w_fc2,
    fc2_bias,
):
    inputs = (
        layer_input,
        token_image,
        ln1_gain,
        ln1_bias,
        w_qkv,
        qv_bias,
        w_out,
        out_bias,
        ln2_gain,
        ln2_bias,
        w_fc1,
        fc1_bias,
        w_fc2,
        fc2_bias,
    )
    first_pass = forward_pass(inputs, True)
    layer_output = first_pass[13]
    fenced = lax.optimization_barrier((layer_output, inputs))[1]
    saved = forward_pass(fenced, False)
    (
        attn_params,
        mlp_params,
        input_rows,
        first_in,
        query_heads,
        key_heads,
        value_heads,
        logsum,
        attn_out,
        resid,
        second_in,
        hidden,
        active,
        unused_output,
    ) = saved
    score_scale = HEAD_DIM ** (-0.5)
    row_count = layer_input.shape[0]
    tensor_at = lax.axis_index("tensor")
    image_rows = lax.dynamic_slice_in_dim(token_image, tensor_at * row_count, row_count)
    valid_mask = (image_rows < IMAGES).astype(jnp.float32)
    grad_rows = cotangent.astype(jnp.float32) * valid_mask[:, None]
    grad_low = grad_rows.astype(jnp.bfloat16)
    grad_all = lax.all_gather(grad_low, "tensor", axis=0, tiled=True)
    grad_active = contract_cols(grad_all, mlp_params[3])
    grad_hidden = jax.vjp(gelu_tanh, hidden)[1](grad_active)[0].astype(jnp.bfloat16)
    fc2_grad = contract_rows(active, grad_all)
    fc1_grad = contract_rows(second_in, grad_hidden)
    grad_normed_two = lax.psum_scatter(
        contract_cols(grad_hidden, mlp_params[2]), "tensor", scatter_dimension=0, tiled=True
    )
    norm_two_back = jax.vjp(
        norm_rows, resid, mlp_params[0].astype(jnp.float32), mlp_params[1].astype(jnp.float32)
    )[1]
    resid_part, ln2_gain_sum, ln2_bias_sum = norm_two_back(grad_normed_two)
    grad_resid = grad_rows + resid_part
    resid_low = grad_resid.astype(jnp.bfloat16)
    resid_all = lax.all_gather(resid_low, "tensor", axis=0, tiled=True)
    out_grad = contract_rows(attn_out, resid_all)
    grad_attn = contract_cols(resid_all, attn_params[3]).astype(jnp.bfloat16)
    head_count = query_heads.shape[0]
    grad_query, grad_keys, grad_values = heads_backward(
        query_heads,
        key_heads,
        value_heads,
        split_heads(grad_attn, head_count),
        logsum,
        token_image,
        score_scale,
    )
    grad_qkv = jnp.stack([join_heads(grad_query), join_heads(grad_keys), join_heads(grad_values)])
    qkv_grad = jnp.einsum("sd,cse->cde", first_in, grad_qkv, preferred_element_type=jnp.float32)
    grad_normed = lax.psum_scatter(
        jnp.einsum("cse,cde->sd", grad_qkv, attn_params[2], preferred_element_type=jnp.float32),
        "tensor",
        scatter_dimension=0,
        tiled=True,
    )
    norm_one_back = jax.vjp(
        norm_rows,
        input_rows,
        attn_params[0].astype(jnp.float32),
        attn_params[1].astype(jnp.float32),
    )[1]
    input_part, ln1_gain_sum, ln1_bias_sum = norm_one_back(grad_normed)
    input_grad = grad_resid + input_part
    qkv_piece, out_piece, fc1_piece, fc2_piece = (
        lax.psum_scatter(qkv_grad, "dp", scatter_dimension=1, tiled=True),
        lax.psum_scatter(out_grad, "dp", scatter_dimension=1, tiled=True),
        lax.psum_scatter(fc1_grad, "dp", scatter_dimension=0, tiled=True),
        lax.psum_scatter(fc2_grad, "dp", scatter_dimension=1, tiled=True),
    )
    full_width = layer_input.shape[1]
    head_width = qv_bias.shape[1]
    ff_width = fc1_bias.shape[0]
    row_sums = jnp.stack(
        [
            ln1_gain_sum,
            ln1_bias_sum,
            jnp.sum(resid_low.astype(jnp.float32), axis=0),
            ln2_gain_sum,
            ln2_bias_sum,
            jnp.sum(grad_rows, axis=0),
        ]
    )
    qv_sums = jnp.stack(
        [
            jnp.sum(grad_qkv[0].astype(jnp.float32), axis=0),
            jnp.sum(grad_qkv[2].astype(jnp.float32), axis=0),
        ]
    )
    qv_wide = lax.dynamic_update_slice_in_dim(
        jnp.zeros((2, full_width), jnp.float32), qv_sums, tensor_at * head_width, 1
    )
    fc1_sums = jnp.sum(grad_hidden.astype(jnp.float32), axis=0)
    fc1_wide = lax.dynamic_update_slice_in_dim(
        jnp.zeros((ff_width * lax.axis_size("tensor"),), jnp.float32),
        fc1_sums,
        tensor_at * ff_width,
        0,
    )
    row_total, qv_total, fc1_total = lax.psum((row_sums, qv_wide, fc1_wide), ("dp", "tensor"))
    dp_width = ln1_gain.shape[0]
    row_piece = lax.dynamic_slice_in_dim(row_total, lax.axis_index("dp") * dp_width, dp_width, 1)
    qv_piece = lax.dynamic_slice_in_dim(qv_total, tensor_at * head_width, head_width, 1)
    fc1_bias_piece = lax.dynamic_slice_in_dim(fc1_total, tensor_at * ff_width, ff_width, 0)
    return (
        layer_output,
        input_grad,
        row_piece[0],
        row_piece[1],
        qkv_piece,
        qv_piece,
        out_piece,
        row_piece[2],
        row_piece[3],
        row_piece[4],
        fc1_piece,
        fc1_bias_piece,
        fc2_piece,
        row_piece[5],
    )


LOG2E = 1.4426950408889634
VMEM_BYTES = 60 * 1024 * 1024


def head_window(head, base, width):
    start = base + head * HEAD_DIM
    first = start // 128 * 128
    last = min(-(-(start + HEAD_DIM) // 128) * 128, width)
    return start - first, first, last


def only_head(values, lane, offset):
    inside = (lane >= offset) & (lane < offset + HEAD_DIM)
    return jnp.where(inside, values, 0)


def with_lanes(values, lane, offset, first_column, second_column):
    one, two = (0, 1) if offset >= 2 else (126, 127)
    values = jnp.where(lane == one, first_column, values)
    return jnp.where(lane == two, second_column, values)


def lane_index(rows, first, last):
    return lax.broadcasted_iota(jnp.int32, (rows, last - first), 1)


def row_columns(kind):
    image = kind == 0
    padding = (kind == 1) | (kind == 2)
    low = jnp.bfloat16
    image_query = jnp.where(image, 1.0, 0.0).astype(low)
    other_query = jnp.where(image, 0.0, 1.0).astype(low)
    image_key = jnp.where(image, 0.0, -1e30).astype(low)
    padding_key = jnp.where(padding, 0.0, -1e30).astype(low)
    return image_query, other_query, image_key, padding_key


def dot_last(left, right):
    return lax.dot_general(
        left, right, (((1,), (1,)), ((), ())), preferred_element_type=jnp.float32
    )


def dot_first(left, right):
    return lax.dot_general(
        left, right, (((0,), (0,)), ((), ())), preferred_element_type=jnp.float32
    )


def heads_forward_kernel(places, heads, waits, spot, kind_ref, x_any, bias_ref, *refs):
    count = sum(len(parts) for parts in places)
    pieces = refs[:count]
    qkv_any, probs_any, *mixed_any = refs[count + waits : count + waits + 4]
    x_ref, qkv_ref, probs_ref, keys_ref, values_ref, total_ref, mixed_ref = refs[-12:-5]
    in_sems, out_sems, probs_sems, weights, sems = refs[-5:]
    scale = HEAD_DIM ** (-0.5) * LOG2E
    rows = x_ref.shape[0]
    part = heads * HEAD_DIM
    inner = qkv_ref.shape[2]
    width = keys_ref.shape[1]
    base = width - part
    groups = len(places)
    slots = probs_ref.shape[0]
    copies = weight_copies(places, pieces, weights, sems, spot[0])
    x_copy = pltpu.make_async_copy(x_any, x_ref, in_sems.at[0])
    begin([x_copy] + copies[0])
    arrive([x_copy] + copies[0])
    image_query, other_query, image_key, padding_key = row_columns(kind_ref[...])
    blank = jnp.zeros((rows, base), jnp.bfloat16)
    sent, writes = [], []
    for group in range(groups):
        if group + 1 < groups:
            begin(copies[group + 1])
        if group:
            arrive(copies[group])
        projected = jnp.dot(
            x_ref[...], strips(weights, group)[:, :inner], preferred_element_type=jnp.float32
        )
        qkv_ref[group] = (projected + bias_ref[group]).astype(jnp.bfloat16)
        copy = pltpu.make_async_copy(qkv_ref.at[group], qkv_any.at[group], out_sems.at[group])
        copy.start()
        sent.append(copy)
        keys_ref[:, :part] = qkv_ref[group, :, part : 2 * part]
        keys_ref[:, part:] = blank
        values_ref[:, :base] = blank
        values_ref[:, base:] = qkv_ref[group, :, 2 * part : 3 * part]
        total_ref[...] = jnp.zeros_like(total_ref)
        for head in range(heads):
            offset, first, last = head_window(head, 0, width)
            lane = lane_index(rows, first, last)
            keys = with_lanes(
                only_head(keys_ref[:, first:last], lane, offset),
                lane,
                offset,
                image_key,
                padding_key,
            )
            query = with_lanes(
                only_head(qkv_ref[group, :, first:last], lane, offset),
                lane,
                offset,
                image_query,
                other_query,
            )
            v_offset, v_first, v_last = head_window(head, base, width)
            values = only_head(
                values_ref[:, v_first:v_last], lane_index(rows, v_first, v_last), v_offset
            )
            at = group * heads + head
            slot = at % slots
            if at >= slots:
                writes[at - slots].wait()
            for tile in row_tiles(rows, 384):
                scores = dot_last(query[tile], keys)
                peak = jnp.max(scores, axis=1, keepdims=True)
                expo = jnp.exp2((scores - peak) * scale)
                total = jnp.sum(expo, axis=1, keepdims=True)
                probs = (expo * (1.0 / total)).astype(jnp.bfloat16)
                probs_ref[slot, tile, :] = probs
                total_ref[tile, v_first:v_last] += jnp.dot(
                    probs, values, preferred_element_type=jnp.float32
                )
            copy = pltpu.make_async_copy(
                probs_ref.at[slot], probs_any.at[group, head], probs_sems.at[slot]
            )
            copy.start()
            writes.append(copy)
        mixed_ref[group] = total_ref[...].astype(jnp.bfloat16)
        copy = pltpu.make_async_copy(
            mixed_ref.at[group], mixed_any[group], out_sems.at[groups + group]
        )
        copy.start()
        sent.append(copy)
    arrive(sent + writes[-slots:])


def heads_forward_call(spot, kind, rows_in, biases, groups, waits=()):
    rows, full = rows_in.shape
    arrays, places = flatten(groups)
    high, group_width = arrays[0].shape[-2:]
    depth = full // (2 * high)
    count = len(groups)
    part = group_width // 4
    heads = part // HEAD_DIM
    inner = -(-3 * part // 128) * 128
    outer = -(-part // 128) * 128
    slots = min(8, count * heads)
    return call(
        functools.partial(heads_forward_kernel, places, heads, len(waits)),
        "heads_forward",
        [spot, kind, rows_in, biases, *arrays],
        [smem_spec(), vmem_spec(), any_spec(), vmem_spec()] + [any_spec()] * len(arrays),
        [
            (any_spec(), (count, rows, inner), jnp.bfloat16),
            (any_spec(), (count, heads, rows, rows), jnp.bfloat16),
            (any_spec(), (rows, outer), jnp.bfloat16),
            (any_spec(), (rows, outer), jnp.bfloat16),
        ],
        [
            low_scratch(rows, full),
            low_scratch(count, rows, inner),
            low_scratch(slots, rows, rows),
            low_scratch(rows, outer),
            low_scratch(rows, outer),
            wide_scratch(rows, outer),
            low_scratch(count, rows, outer),
            copy_sems(1),
            copy_sems(2 * count),
            copy_sems(slots),
        ]
        + weight_scratch(places, depth, high, group_width),
        waits,
    )


def heads_backward_kernel(places, heads, picks, waits, spot, grad_any, qkv_any, probs_any, *refs):
    count = sum(len(parts) for parts in places)
    groups = len(places)
    mixed_any = refs[:groups]
    pieces = refs[groups : groups + count]
    first_out = groups + count + waits
    outs_any = refs[first_out : first_out + groups]
    sum_ref = refs[first_out + groups]
    grad_ref, qkv_ref, probs_ref, mixed_ref, out_ref, keys_ref, values_ref, grads_ref = refs[-16:-8]
    query_sum, key_sum, value_sum, in_sems, probs_sems, out_sems, weights, sems = refs[-8:]
    width = keys_ref.shape[1]
    first_lane = pieces[0].shape[-1] - width
    loads = weight_copies(places, pieces, weights, sems, spot[0], first_lane, width)
    grad_copy = pltpu.make_async_copy(grad_any, grad_ref, in_sems.at[2 * groups])
    slots = probs_ref.shape[0]
    seconds, reads = [], []
    for group in range(groups):
        seconds.append(
            [
                pltpu.make_async_copy(
                    qkv_any.at[picks[group]], qkv_ref.at[group], in_sems.at[2 * group]
                ),
                pltpu.make_async_copy(
                    mixed_any[group], mixed_ref.at[group], in_sems.at[2 * group + 1]
                ),
            ]
        )
        for head in range(heads):
            slot = len(reads) % slots
            reads.append(
                pltpu.make_async_copy(
                    probs_any.at[picks[group], head], probs_ref.at[slot], probs_sems.at[slot]
                )
            )
    begin([grad_copy] + loads[0])
    begin(seconds[0])
    begin(reads[:2])
    score_scale = HEAD_DIM ** (-0.5)
    rows = grad_ref.shape[0]
    part = heads * HEAD_DIM
    base = width - part
    low = jnp.bfloat16
    blank = jnp.zeros((rows, base), low)
    sent = []
    started = 2
    for group in range(groups):
        arrive(([grad_copy] if group == 0 else []) + loads[group])
        grads_ref[...] = jnp.dot(
            grad_ref[...], strips(weights, group), preferred_element_type=jnp.float32
        ).astype(low)
        arrive(seconds[group])
        if group + 1 < groups:
            begin(loads[group + 1] + seconds[group + 1])
        keys_ref[:, :part] = qkv_ref[group, :, part : 2 * part]
        keys_ref[:, part:] = blank
        values_ref[:, :base] = blank
        values_ref[:, base:] = qkv_ref[group, :, 2 * part : 3 * part]
        query_sum[...] = jnp.zeros_like(query_sum)
        key_sum[...] = jnp.zeros_like(key_sum)
        value_sum[...] = jnp.zeros_like(value_sum)
        weighted = grads_ref[...].astype(jnp.float32) * mixed_ref[group].astype(jnp.float32)
        for head in range(heads):
            at = group * heads + head
            offset, first, last = head_window(head, 0, width)
            lane = lane_index(rows, first, last)
            query = only_head(qkv_ref[group, :, first:last], lane, offset)
            keys = only_head(keys_ref[:, first:last], lane, offset)
            v_offset, v_first, v_last = head_window(head, base, width)
            v_lane = lane_index(rows, v_first, v_last)
            values = values_ref[:, v_first:v_last]
            grad = only_head(grads_ref[:, v_first:v_last], v_lane, v_offset)
            centre = jnp.sum(
                only_head(weighted[:, v_first:v_last], v_lane, v_offset), axis=1, keepdims=True
            )
            while started < len(reads) and started - at < slots:
                reads[started].start()
                started += 1
            reads[at].wait()
            probs = probs_ref[at % slots]
            grad_probs = dot_last(grad, values)
            grad_scores = (probs.astype(jnp.float32) * (grad_probs - centre)).astype(low)
            value_sum[:, v_first:v_last] += dot_first(probs, grad)
            key_sum[:, first:last] += dot_first(grad_scores, query)
            query_sum[:, first:last] += jnp.dot(
                grad_scores, keys, preferred_element_type=jnp.float32
            )
        out_ref[group, :, :part] = (query_sum[...] * score_scale).astype(low)[:, :part]
        out_ref[group, :, part : 2 * part] = (key_sum[...] * score_scale).astype(low)[:, :part]
        out_ref[group, :, 2 * part : 3 * part] = value_sum[...].astype(low)[:, base:]
        tail = out_ref.shape[2] - 3 * part
        if tail:
            out_ref[group, :, 3 * part :] = jnp.zeros((rows, tail), low)
        copy = pltpu.make_async_copy(out_ref.at[group], outs_any[group], out_sems.at[group])
        copy.start()
        sent.append(copy)
        sum_ref[group] = jnp.sum(out_ref[group].astype(jnp.float32), axis=0, keepdims=True)
    arrive(sent)


def heads_backward_call(spot, grad_rows, qkv, probs, mixed, groups, picks, waits=()):
    rows, full = grad_rows.shape
    arrays, places = flatten(groups)
    high, group_width = arrays[0].shape[-2:]
    depth = full // (2 * high)
    part = group_width // 4
    heads = part // HEAD_DIM
    inner = qkv.shape[2]
    outer = mixed[0].shape[1]
    count = len(groups)
    slots = min(count * heads, 6)
    return call(
        functools.partial(heads_backward_kernel, places, heads, picks, len(waits)),
        "heads_backward",
        [spot, grad_rows, qkv, probs, *mixed, *arrays],
        [smem_spec()] + [any_spec()] * (3 + count + len(arrays)),
        [(any_spec(), (rows, inner), jnp.bfloat16)] * count
        + [(vmem_spec(), (count, 1, inner), jnp.float32)],
        [
            low_scratch(rows, full),
            low_scratch(count, rows, inner),
            low_scratch(slots, rows, rows),
            low_scratch(count, rows, outer),
            low_scratch(count, rows, inner),
            low_scratch(rows, outer),
            low_scratch(rows, outer),
            low_scratch(rows, outer),
            wide_scratch(rows, outer),
            wide_scratch(rows, outer),
            wide_scratch(rows, outer),
            copy_sems(2 * count + 1),
            copy_sems(slots),
            copy_sems(count),
        ]
        + weight_scratch(places, depth, high, outer),
        waits,
    )


def any_spec():
    return pl.BlockSpec(memory_space=pl.ANY)


def smem_spec():
    return pl.BlockSpec(memory_space=pltpu.SMEM)


def vmem_spec():
    return pl.BlockSpec(memory_space=pltpu.VMEM)


def limits():
    return pltpu.CompilerParams(vmem_limit_bytes=VMEM_BYTES)


def low_scratch(*shape):
    return pltpu.VMEM(shape, jnp.bfloat16)


def wide_scratch(*shape):
    return pltpu.VMEM(shape, jnp.float32)


def copy_sems(*shape):
    return pltpu.SemaphoreType.DMA(shape)


def begin(copies):
    for copy in copies:
        copy.start()


def arrive(copies):
    for copy in copies:
        copy.wait()


def call(kernel, name, operands, specs, outs, scratch, waits=()):
    no_cost = pl.CostEstimate(flops=1024, bytes_accessed=1024, transcendentals=0)
    out_specs = [spec for spec, _, _ in outs]
    return pl.pallas_call(
        kernel,
        in_specs=list(specs) + [any_spec()] * len(waits),
        out_specs=out_specs,
        out_shape=[jax.ShapeDtypeStruct(shape, kind) for _, shape, kind in outs],
        scratch_shapes=scratch,
        compiler_params=limits(),
        cost_estimate=no_cost,
        name=name,
    )(*operands, *waits)


def flatten(groups):
    arrays = [part[0] for group in groups for part in group]
    places = [[part[1:] for part in group] for group in groups]
    return arrays, places


def weight_copies(places, refs, weights, sems, x_at, first=0, width=None):
    copies, at = [], 0
    for group, parts in enumerate(places):
        mine = []
        for part, (start, x_off, *pick) in enumerate(parts):
            source = refs[at].at[:, pick[0]] if pick else refs[at]
            at += 1
            if width is not None:
                source = source.at[:, :, pl.ds(first, width)]
            target = weights.at[group, pl.ds(start, source.shape[0]), x_at ^ x_off]
            mine.append(pltpu.make_async_copy(source, target, sems.at[group, part]))
        copies.append(mine)
    return copies


def weight_scratch(places, depth, high, width):
    count = len(places)
    return [
        pltpu.VMEM((count, depth, 2, high, width), jnp.bfloat16),
        copy_sems(count, max(len(parts) for parts in places)),
    ]


def strips(weights, at):
    _, depth, _, high, width = weights.shape
    return weights[at].reshape(depth * 2 * high, width)


def row_tiles(rows, size):
    return [slice(start, min(start + size, rows)) for start in range(0, rows, size)]


def out_copies(pairs, sems):
    return [
        pltpu.make_async_copy(source, target, sems.at[i])
        for i, (source, target) in enumerate(pairs)
    ]


def up_kernel(places, waits, spot, x_any, bias_ref, *refs):
    count = sum(len(parts) for parts in places)
    pieces = refs[:count]
    active_any, slope_any = refs[count + waits : count + waits + 2]
    x_ref, active_ref, slope_ref, x_sem, out_sems, weights, sems = refs[-7:]
    rows = x_ref.shape[0]
    groups = len(places)
    copies = weight_copies(places, pieces, weights, sems, spot[0])
    x_copy = pltpu.make_async_copy(x_any, x_ref, x_sem.at[0])
    begin([x_copy] + copies[0])
    arrive([x_copy] + copies[0])
    sent = []
    for group in range(groups):
        if group + 1 < groups:
            begin(copies[group + 1])
        if group:
            arrive(copies[group])
        whole = strips(weights, group)
        for tile in row_tiles(rows, 128):
            hidden = jnp.dot(x_ref[tile, :], whole, preferred_element_type=jnp.float32)
            hidden = hidden + bias_ref[group]
            square = hidden * hidden
            inner = jnp.tanh(hidden * (gelu_scale + gelu_scale * 0.044715 * square))
            gate = 0.5 + 0.5 * inner
            active_ref[group, tile, :] = (hidden * gate).astype(jnp.bfloat16)
            grow = hidden * (gelu_scale + 3.0 * 0.044715 * gelu_scale * square)
            slope = gate + grow * (0.5 - 0.5 * inner * inner)
            slope_ref[group, tile, :] = slope.astype(jnp.bfloat16)
        for half, tile in enumerate(row_tiles(rows, rows // 2)):
            span = pl.ds(tile.start, rows // 2)
            for at, (source, target) in enumerate(
                ((active_ref, active_any), (slope_ref, slope_any))
            ):
                copy = pltpu.make_async_copy(
                    source.at[group, span], target.at[group, span], out_sems.at[group, half, at]
                )
                copy.start()
                sent.append(copy)
    arrive(sent)


def up_project(spot, rows_in, biases, groups, waits=()):
    rows, full = rows_in.shape
    arrays, places = flatten(groups)
    high, width = arrays[0].shape[-2:]
    depth = full // (2 * high)
    count = len(groups)
    shape = (count, rows, width)
    return call(
        functools.partial(up_kernel, places, len(waits)),
        "mlp_up",
        [spot, rows_in, biases, *arrays],
        [smem_spec(), any_spec(), vmem_spec()] + [any_spec()] * len(arrays),
        [(any_spec(), shape, jnp.bfloat16)] * 2,
        [
            low_scratch(rows, full),
            low_scratch(*shape),
            low_scratch(*shape),
            copy_sems(1),
            copy_sems(count, 2, 2),
        ]
        + weight_scratch(places, depth, high, width),
        waits,
    )


def unit_rows(values):
    centre = values - jnp.mean(values, axis=1, keepdims=True)
    spread = jnp.mean(centre * centre, axis=1, keepdims=True)
    root = lax.rsqrt(spread + layer_eps)
    return centre * root, root


def norm_rows_back(values, gain, grad):
    unit, root = unit_rows(values)
    scaled = grad * gain
    mean_one = jnp.mean(scaled, axis=1, keepdims=True)
    mean_two = jnp.mean(scaled * unit, axis=1, keepdims=True)
    part = root * (scaled - mean_one - unit * mean_two)
    return part, jnp.sum(grad * unit, axis=0, keepdims=True), jnp.sum(grad, axis=0, keepdims=True)


def mlp_back_kernel(down_places, up_places, waits, spot, x_any, one_any, two_any, resid_any, gain_ref, *refs):
    count = [sum(len(parts) for parts in places) for places in (down_places, up_places)]
    down_pieces = refs[: count[0]]
    up_pieces = refs[count[0] : count[0] + count[1]]
    at = count[0] + count[1] + waits
    one_out, two_out, low_any, sum_ref, hidden_sums = refs[at : at + 5]
    x_ref, slope_ref, hidden_ref, resid_ref, total, low_ref, in_sems, hidden_sems, out_sems = refs[
        at + 5 : at + 14
    ]
    down_weights, down_sems, up_weights, up_sems = refs[at + 14 :]
    rows = x_ref.shape[0]
    groups = len(down_places)
    half = groups // 2
    slots = down_weights.shape[0]

    def slotted(places, pieces, weights, sems):
        copies, first = [], 0
        for group, parts in enumerate(places):
            mine = pieces[first : first + len(parts)]
            first += len(parts)
            slot = group % slots
            copies += weight_copies(
                [parts],
                mine,
                weights.at[pl.ds(slot, 1)],
                sems.at[pl.ds(slot, 1)],
                spot[0],
            )
        return copies

    downs = slotted(down_places, down_pieces, down_weights, down_sems)
    ups = slotted(up_places, up_pieces, up_weights, up_sems)
    for group in range(groups):
        source = one_any.at[group] if group < half else two_any.at[group - half]
        slot = group % slots
        downs[group].append(
            pltpu.make_async_copy(source, slope_ref.at[slot], in_sems.at[2 + slot])
        )
    x_copy = pltpu.make_async_copy(x_any, x_ref, in_sems.at[0])
    late = pltpu.make_async_copy(resid_any, resid_ref, in_sems.at[1])
    begin([x_copy] + downs[0])
    arrive([x_copy] + downs[0])
    sent = []
    for group in range(groups):
        slot = group % slots
        begin(ups[group])
        whole = strips(down_weights, slot)
        column_total = jnp.zeros((1, total.shape[1]), jnp.float32)
        if group >= slots:
            sent[group - slots].wait()
        for tile in row_tiles(rows, 256):
            grad = jnp.dot(x_ref[tile, :], whole, preferred_element_type=jnp.float32)
            low = (grad * slope_ref[slot, tile, :].astype(jnp.float32)).astype(jnp.bfloat16)
            hidden_ref[slot, tile, :] = low
            column_total += jnp.sum(low.astype(jnp.float32), axis=0, keepdims=True)
        hidden_sums[group] = column_total
        target = one_out.at[group] if group < half else two_out.at[group - half]
        copy = pltpu.make_async_copy(hidden_ref.at[slot], target, hidden_sems.at[slot])
        copy.start()
        sent.append(copy)
        arrive(ups[group])
        if group + 1 < groups:
            begin(downs[group + 1])
        else:
            begin([late])
        whole = strips(up_weights, slot)
        if group == 0:
            total[...] = dot_last(hidden_ref[slot], whole)
        elif group + 1 < groups:
            total[...] += dot_last(hidden_ref[slot], whole)
        else:
            products = [
                (tile, dot_last(hidden_ref[slot, tile, :], whole)) for tile in row_tiles(rows, 256)
            ]
        if group + 1 < groups:
            arrive(downs[group + 1])
    arrive([late])
    sums = [jnp.zeros((1, total.shape[1]), jnp.float32) for _ in range(3)]
    low_sent = []
    for tile, product in products:
        for small in range(tile.start, tile.stop, 128):
            span = slice(small, small + 128)
            inside = slice(small - tile.start, small - tile.start + 128)
            part, gain_sum, shift_sum = norm_rows_back(
                resid_ref[span, :].astype(jnp.float32),
                gain_ref[...],
                total[span, :] + product[inside],
            )
            low = (x_ref[span, :].astype(jnp.float32) + part).astype(jnp.bfloat16)
            low_ref[span, :] = low
            sums[0] += gain_sum
            sums[1] += shift_sum
            sums[2] += jnp.sum(low.astype(jnp.float32), axis=0, keepdims=True)
        long = pl.ds(tile.start, tile.stop - tile.start)
        copy = pltpu.make_async_copy(
            low_ref.at[long], low_any.at[long], out_sems.at[len(low_sent)]
        )
        copy.start()
        low_sent.append(copy)
    sum_ref[...] = jnp.concatenate(sums + [jnp.zeros((5, total.shape[1]), jnp.float32)])
    arrive(sent[-slots:] + low_sent)


def mlp_back(spot, grad_low, first_slope, second_slope, resid, gain, downs, ups, waits=()):
    rows, full = grad_low.shape
    down_arrays, down_places = flatten(downs)
    up_arrays, up_places = flatten(ups)
    high, width = up_arrays[0].shape[-2:]
    depth = full // (2 * high)
    count = len(downs)
    slots = 2
    shape = (count // 2, rows, width)

    def slot_scratch(places):
        return [
            pltpu.VMEM((slots, depth, 2, high, width), jnp.bfloat16),
            copy_sems(slots, max(len(parts) for parts in places)),
        ]

    return call(
        functools.partial(mlp_back_kernel, down_places, up_places, len(waits)),
        "mlp_back",
        [spot, grad_low, first_slope, second_slope, resid, gain, *down_arrays, *up_arrays],
        [smem_spec()]
        + [any_spec()] * 4
        + [vmem_spec()]
        + [any_spec()] * (len(down_arrays) + len(up_arrays)),
        [
            (any_spec(), shape, jnp.bfloat16),
            (any_spec(), shape, jnp.bfloat16),
            (any_spec(), (rows, full), jnp.bfloat16),
            (vmem_spec(), (8, full), jnp.float32),
            (vmem_spec(), (count, 1, width), jnp.float32),
        ],
        [
            low_scratch(rows, full),
            low_scratch(slots, rows, width),
            low_scratch(slots, rows, width),
            pltpu.VMEM(resid.shape, resid.dtype),
            wide_scratch(rows, full),
            low_scratch(rows, full),
            copy_sems(2 + slots),
            copy_sems(slots),
            copy_sems(-(-rows // 256)),
        ]
        + slot_scratch(down_places)
        + slot_scratch(up_places),
        waits,
    )


def back_kernel(places, sources, waits, spot, *refs):
    count = sum(len(parts) for parts in places)
    grads_any = refs[:sources]
    base_any, grad_any, gain_ref = refs[sources : sources + 3]
    pieces = refs[sources + 3 : sources + 3 + count]
    first_out = sources + 3 + count + waits
    out_any, sum_ref = refs[first_out : first_out + 2]
    grads_ref, base_ref, grad_ref, total, in_sems, out_sems, weights, sems = refs[first_out + 2 :]
    rows = total.shape[0]
    groups = len(places)
    width = weights.shape[-1]
    copies = weight_copies(places, pieces, weights, sems, spot[0], 0, width)
    at = 0
    for source in grads_any:
        parts = [source] if len(source.shape) == 2 else [source.at[i] for i in range(source.shape[0])]
        for part in parts:
            copies[at].append(pltpu.make_async_copy(part, grads_ref.at[at], in_sems.at[at]))
            at += 1
    late = [
        pltpu.make_async_copy(base_any, base_ref, in_sems.at[groups]),
        pltpu.make_async_copy(grad_any, grad_ref, in_sems.at[groups + 1]),
    ]
    begin(copies[0])
    for group in range(groups):
        arrive(copies[group])
        begin(copies[group + 1] if group + 1 < groups else late)
        whole = strips(weights, group)
        if group == 0:
            total[...] = dot_last(grads_ref[group], whole)
        elif group + 1 < groups:
            total[...] += dot_last(grads_ref[group], whole)
        else:
            products = [
                (tile, dot_last(grads_ref[group, tile, :], whole)) for tile in row_tiles(rows, 256)
            ]
    arrive(late)
    sums = [jnp.zeros((1, total.shape[1]), jnp.float32) for _ in range(2)]
    sent = []
    for tile, product in products:
        for small in range(tile.start, tile.stop, 128):
            span = slice(small, small + 128)
            inside = slice(small - tile.start, small - tile.start + 128)
            part, gain_sum, shift_sum = norm_rows_back(
                base_ref[span, :].astype(jnp.float32),
                gain_ref[...],
                total[span, :] + product[inside],
            )
            grad = grad_ref[span, :].astype(jnp.float32) + part
            total[span, :] = grad
            sums[0] += gain_sum
            sums[1] += shift_sum
        long = pl.ds(tile.start, tile.stop - tile.start)
        copy = pltpu.make_async_copy(total.at[long], out_any.at[long], out_sems.at[len(sent)])
        copy.start()
        sent.append(copy)
    sum_ref[...] = jnp.concatenate(sums + [jnp.zeros((6, total.shape[1]), jnp.float32)])
    arrive(sent)


def norm_back(spot, grads, base, grad, gain, groups, waits=()):
    rows, full = base.shape
    arrays, places = flatten(groups)
    high, _ = arrays[0].shape[-2:]
    width = grads[0].shape[-1]
    depth = full // (2 * high)
    outs = [
        (any_spec(), (rows, full), jnp.float32),
        (vmem_spec(), (8, full), jnp.float32),
    ]
    return call(
        functools.partial(back_kernel, places, len(grads), len(waits)),
        "norm_one_back",
        [spot, *grads, base, grad, gain, *arrays],
        [smem_spec()] + [any_spec()] * (len(grads) + 2) + [vmem_spec()] + [any_spec()] * len(arrays),
        outs,
        [
            low_scratch(len(groups), rows, width),
            pltpu.VMEM(base.shape, base.dtype),
            pltpu.VMEM(grad.shape, grad.dtype),
            wide_scratch(rows, full),
            copy_sems(len(groups) + 2),
            copy_sems(-(-rows // 256)),
        ]
        + weight_scratch(places, depth, high, width),
        waits,
    )


def down_kernel(places, waits, spot, later_any, early_any, resid_any, shift_ref, *refs):
    count = sum(len(parts) for parts in places)
    pieces = refs[:count]
    out_any = refs[count + waits]
    active_ref, resid_ref, total, out_ref, in_sems, out_sems, weights, sems = refs[-8:]
    rows = total.shape[0]
    groups = len(places)
    copies = weight_copies(places, pieces, weights, sems, spot[0])
    half = groups // 2
    for group in range(groups):
        source = later_any.at[group] if group < half else early_any.at[group - half]
        copies[group].append(
            pltpu.make_async_copy(source, active_ref.at[group], in_sems.at[group])
        )
    late = [pltpu.make_async_copy(resid_any, resid_ref, in_sems.at[groups])]
    begin(copies[0])
    for group in range(groups - 1):
        arrive(copies[group])
        begin(copies[group + 1])
        if group + 2 == groups:
            begin(late)
        product = dot_last(active_ref[group], strips(weights, group))
        if group == 0:
            total[...] = product
        else:
            total[...] += product
    arrive(copies[-1] + late)
    whole = strips(weights, groups - 1)
    sent = []
    for tile in row_tiles(rows, 256):
        product = dot_last(active_ref[groups - 1, tile, :], whole)
        product = product + total[tile, :] + shift_ref[...]
        product = product + resid_ref[tile, :].astype(jnp.float32)
        out_ref[tile, :] = product.astype(out_ref.dtype)
        long = pl.ds(tile.start, tile.stop - tile.start)
        copy = pltpu.make_async_copy(out_ref.at[long], out_any.at[long], out_sems.at[len(sent)])
        copy.start()
        sent.append(copy)
    arrive(sent)


def down_project(spot, first, second, resid, shift, groups, waits=()):
    rows, full = resid.shape
    arrays, places = flatten(groups)
    high, width = arrays[0].shape[-2:]
    depth = full // (2 * high)
    return call(
        functools.partial(down_kernel, places, len(waits)),
        "mlp_down",
        [spot, first, second, resid, shift, *arrays],
        [smem_spec()] + [any_spec()] * 3 + [vmem_spec()] + [any_spec()] * len(arrays),
        [(any_spec(), (rows, full), jnp.bfloat16)],
        [
            low_scratch(len(groups), rows, width),
            pltpu.VMEM(resid.shape, resid.dtype),
            wide_scratch(rows, full),
            low_scratch(rows, full),
            copy_sems(len(groups) + 1),
            copy_sems(-(-rows // 256)),
        ]
        + weight_scratch(places, depth, high, width),
        waits,
    )[0]


def out_kernel(places, waits, spot, one, two, three, four, x_any, shift_ref, gain_ref, bias_ref, *refs):
    count = sum(len(parts) for parts in places)
    pieces = refs[:count]
    resid_any, normed_any = refs[count + waits : count + waits + 2]
    mixed_ref, x_ref, resid_ref, low_ref, normed_ref, in_sems, out_sems, weights, sems = refs[-9:]
    rows = x_ref.shape[0]
    outer = weights.shape[-1]
    first = pieces[0].shape[-1] - outer
    copies = weight_copies(places, pieces, weights, sems, spot[0], first, outer)
    for group, mixed in enumerate((one, two, three, four)):
        copies[group].append(
            pltpu.make_async_copy(mixed, mixed_ref.at[group], in_sems.at[group])
        )
    late = [pltpu.make_async_copy(x_any, x_ref, in_sems.at[4])]
    for mine in copies:
        begin(mine)
    begin(late)
    for group in range(4):
        arrive(copies[group])
        if group < 3:
            product = dot_last(mixed_ref[group], strips(weights, group))
            if group == 0:
                resid_ref[...] = product
            else:
                resid_ref[...] += product
    arrive(late)
    whole = strips(weights, 3)
    products = [(tile, dot_last(mixed_ref[3, tile, :], whole)) for tile in row_tiles(rows, 256)]
    sent = []
    for tile, product in products:
        for small in range(tile.start, tile.stop, 128):
            span = slice(small, small + 128)
            inside = slice(small - tile.start, small - tile.start + 128)
            values = resid_ref[span, :] + product[inside] + x_ref[span, :].astype(jnp.float32)
            values = values + shift_ref[...]
            low_ref[span, :] = values.astype(jnp.bfloat16)
            unit, _ = unit_rows(values)
            normed_ref[span, :] = (unit * gain_ref[...] + bias_ref[...]).astype(jnp.bfloat16)
        long = pl.ds(tile.start, tile.stop - tile.start)
        for source, target in ((low_ref, resid_any), (normed_ref, normed_any)):
            copy = pltpu.make_async_copy(source.at[long], target.at[long], out_sems.at[len(sent)])
            copy.start()
            sent.append(copy)
    arrive(sent)


def out_project(spot, mixed, rows_in, shift, gain, bias, groups, waits=()):
    rows, full = rows_in.shape
    arrays, places = flatten(groups)
    high, _ = arrays[0].shape[-2:]
    outer = mixed[0].shape[1]
    depth = full // (2 * high)
    return call(
        functools.partial(out_kernel, places, len(waits)),
        "attn_out",
        [spot, *mixed, rows_in, shift, gain, bias, *arrays],
        [smem_spec()] + [any_spec()] * 5 + [vmem_spec()] * 3 + [any_spec()] * len(arrays),
        [
            (any_spec(), (rows, full), jnp.bfloat16),
            (any_spec(), (rows, full), jnp.bfloat16),
        ],
        [
            low_scratch(4, rows, outer),
            low_scratch(rows, full),
            wide_scratch(rows, full),
            low_scratch(rows, full),
            low_scratch(rows, full),
            copy_sems(5),
            copy_sems(2 * -(-rows // 256)),
        ]
        + weight_scratch(places, depth, high, outer),
        waits,
    )


def grad_kernel(sides, extra, waits, spot, *refs):
    inputs = 4 + (4 if extra else 0)
    sources = refs[:inputs]
    outs_at = inputs + waits
    count = sum(3 + side // 2 for side in sides)
    outs = list(refs[outs_at : outs_at + count])
    holds = refs[outs_at + count : outs_at + count + inputs]
    stage, in_sems, out_sems = refs[-3:]
    x_at = spot[0]
    def load(source, hold, at):
        return pltpu.make_async_copy(source, hold, in_sems.at[at])

    count = len(sides)
    first_x = load(sources[0], holds[0], 0)
    second_x = load(sources[2], holds[2], 1)
    firsts = [load(sources[1].at[i], holds[1].at[i], 2 + 2 * i) for i in range(count)]
    seconds = [load(sources[3].at[i], holds[3].at[i], 3 + 2 * i) for i in range(count)]
    extras = [load(sources[j], holds[j], 2 * count + j - 2) for j in range(4, inputs)]
    _, depth, _, high, width = stage.shape
    half = depth // 2
    begin([first_x, firsts[0]])
    arrive([first_x, firsts[0]])
    begin([second_x, seconds[0]])
    begin(extras)
    sent = []
    starts = []
    for side in sides:
        starts.append(sum(3 + before // 2 for before in sides[: len(starts)]))
    for i, side in enumerate(sides):
        if i:
            arrive([firsts[i], seconds[i]])
        for part in range(2):
            cut = slice(part * half * 2 * high, (part + 1) * half * 2 * high)
            span = pl.ds(part * half, half)
            product = dot_first(holds[0][:, cut], holds[1][i])
            if i == 0 and part == 0:
                arrive([second_x, seconds[0]])
                for later in range(1, count):
                    begin([firsts[later], seconds[later]])
            product += dot_first(holds[2][:, cut], holds[3][i])
            if extra:
                if i == 0 and part == 0:
                    arrive(extras)
                other = dot_first(holds[4][:, cut], holds[5][...])
                other += dot_first(holds[6][:, cut], holds[7][...])
                both = product.shape[1] + other.shape[1] - width
                left = product.shape[1] - both
                product = jnp.concatenate(
                    [product[:, :left], product[:, left:] + other[:, :both], other[:, both:]],
                    axis=1,
                )
            stage[i, part * half : (part + 1) * half] = product.astype(jnp.bfloat16).reshape(
                half, 2, high, width
            )
            if side == 0:
                near_out = outs[starts[i]].at[span]
                far_out = outs[starts[i] + 1 + part]
            else:
                near_out = outs[starts[i] + part]
                far_out = outs[starts[i] + 2 + part]
            for source, target in (
                (stage.at[i, span, x_at], near_out),
                (stage.at[i, span, 1 - x_at], far_out),
            ):
                copy = pltpu.make_async_copy(source, target, out_sems.at[len(sent)])
                copy.start()
                sent.append(copy)
    arrive(sent)


def weight_grad(spot, left, right, depth, sides=(0, 2), extra=(), waits=()):
    rows, full = left[0].shape
    high = full // (2 * depth)
    half = depth // 2
    count = len(sides)
    rights = [values.reshape(count, rows, -1) for values in right]
    width = full if extra else rights[0].shape[2]
    operands = [left[0], rights[0], left[1], rights[1], *extra]
    shapes = []
    for side in sides:
        shapes += [depth, half, half] if side == 0 else [half] * 4
    outs = [(any_spec(), (size, high, width), jnp.bfloat16) for size in shapes]
    return call(
        functools.partial(grad_kernel, sides, bool(extra), len(waits)),
        "weight_grad",
        [spot, *operands],
        [smem_spec()] + [any_spec()] * len(operands),
        outs,
        [pltpu.VMEM(values.shape, values.dtype) for values in operands]
        + [
            low_scratch(count, depth, 2, high, width),
            copy_sems(2 + 2 * count + 4),
            copy_sems(4 * count),
        ],
        waits,
    )


def pair_kernel(one_ref, two_ref, three_ref, four_ref, first_out, second_out):
    wide = jnp.float32
    low = first_out.dtype
    first_out[...] = (one_ref[...].astype(wide) + two_ref[...].astype(wide)).astype(low)
    second_out[...] = (three_ref[...].astype(wide) + four_ref[...].astype(wide)).astype(low)


def add_pairs(one, two, three, four):
    shape = jax.ShapeDtypeStruct(one.shape, one.dtype)
    return pl.pallas_call(
        pair_kernel,
        in_specs=[vmem_spec()] * 4,
        out_specs=[vmem_spec()] * 2,
        out_shape=[shape, shape],
        compiler_params=limits(),
        name="add_pairs",
    )(one, two, three, four)


def square_kernel(own, one_lo, one_hi, two_lo, two_hi, out):
    wide = jnp.float32
    half = one_lo.shape[0]
    for part, (one, two) in enumerate(((one_lo, two_lo), (one_hi, two_hi))):
        span = slice(part * half, (part + 1) * half)
        total = own[span].astype(wide) + one[...].astype(wide) + two[...].astype(wide)
        out[span] = total.astype(out.dtype)


def add_square(own, *parts):
    return pl.pallas_call(
        square_kernel,
        in_specs=[vmem_spec()] * 5,
        out_specs=vmem_spec(),
        out_shape=jax.ShapeDtypeStruct(own.shape, own.dtype),
        compiler_params=limits(),
        name="add_square",
    )(own, *parts)


def halves_kernel(first_ref, second_ref, first_out, second_out):
    first_out[...] = first_ref[...]
    second_out[...] = second_ref[...]


def take_halves(first, second):
    half = (first.shape[0] // 2,) + first.shape[1:]
    front = pl.BlockSpec(half, lambda i: (0, 0, 0))
    back = pl.BlockSpec(half, lambda i: (1, 0, 0))
    shape = jax.ShapeDtypeStruct(half, first.dtype)
    return pl.pallas_call(
        halves_kernel,
        grid=(1,),
        in_specs=[front, back],
        out_specs=[front, front],
        out_shape=[shape, shape],
        compiler_params=limits(),
        name="take_halves",
    )(first, second)


PATCHES = 729
AXES = ("dp", "tensor")


def nothing(*refs):
    del refs


def fence(released, waited=()):
    anywhere = pl.BlockSpec(memory_space=pl.ANY)
    released, waited = list(released), list(waited)
    return pl.pallas_call(
        nothing,
        in_specs=[anywhere] * (len(released) + len(waited)),
        out_specs=[anywhere] * len(released),
        out_shape=[jax.ShapeDtypeStruct(values.shape, values.dtype) for values in released],
        input_output_aliases={i: i for i in range(len(released))},
        name="fence",
    )(*released, *waited)


class Grid:
    def __init__(self, depth):
        self.depth = depth
        dp_at = lax.axis_index("dp")
        self.y = lax.axis_index("tensor")
        self.c = dp_at % 2
        self.x = dp_at // 2 % 2
        self.z = dp_at // 4

    def move(self, values, where):
        pairs = []
        for z in range(self.depth):
            for x in range(2):
                for c in range(2):
                    for y in range(2):
                        to_z, to_x, to_c, to_y = where(z, x, c, y)
                        pairs.append(
                            (
                                ((z * 2 + x) * 2 + c) * 2 + y,
                                ((to_z * 2 + to_x) * 2 + to_c) * 2 + to_y,
                            )
                        )
        return lax.ppermute(values, AXES, pairs)

    def over_x(self, values):
        return self.move(values, lambda z, x, c, y: (z, 1 - x, c, y))

    def over_y(self, values):
        return self.move(values, lambda z, x, c, y: (z, x, c, 1 - y))

    def over_both(self, values):
        return self.move(values, lambda z, x, c, y: (z, 1 - x, c, 1 - y))

    def over_core(self, values):
        return self.move(values, lambda z, x, c, y: (z, x, 1 - c, y))

    def along_z(self, values, hops):
        return self.move(values, lambda z, x, c, y: ((z + hops) % self.depth, x, c, y))

    def across_z(self, values, bit):
        return self.move(values, lambda z, x, c, y: (z ^ bit, x, c, y))

    def spread(self, block):
        width = block.shape[1] // 2
        mine = lax.dynamic_slice_in_dim(block, self.c * width, width, 1)
        theirs = self.over_core(
            lax.dynamic_slice_in_dim(block, (1 - self.c) * width, width, 1)
        )
        first = jnp.where(self.c == 0, mine, theirs)
        second = jnp.where(self.c == 0, theirs, mine)
        return jnp.concatenate([first, second])

    def depth_groups(self):
        return [
            [(z * 2 + x) * 2 + c for z in range(self.depth)] for x in range(2) for c in range(2)
        ]

    def gather_depth(self, block):
        return lax.all_gather(block, "dp", axis_index_groups=self.depth_groups())

    def scatter_depth(self, total):
        return lax.psum_scatter(total, "dp", axis_index_groups=self.depth_groups())

    def scatter_core(self, result):
        result = result.astype(jnp.float32)
        shard = result.shape[0] // 2
        mine = lax.dynamic_slice_in_dim(result, self.c * shard, shard)
        theirs = self.over_core(
            lax.dynamic_slice_in_dim(result, (1 - self.c) * shard, shard)
        )
        first = jnp.where(self.c == 0, mine, theirs)
        second = jnp.where(self.c == 0, theirs, mine)
        return jnp.stack([first, second])

    def gather_small(self, values):
        count, shard = values.shape
        parts = jnp.zeros((self.depth, 2, 2, count, shard), values.dtype)
        parts = lax.dynamic_update_slice(
            parts, values[None, None, None], (self.z, self.x, self.c, 0, 0)
        )
        parts = parts + self.over_core(parts)
        parts = parts + self.over_x(parts)
        bit = 1
        while bit < self.depth:
            parts = parts + self.across_z(parts, bit)
            bit *= 2
        return parts.transpose(3, 0, 1, 2, 4).reshape(count, -1)


def image_shards(
    depth,
    layer_input,
    token_image,
    cotangent,
    ln1_gain,
    ln1_bias,
    w_qkv,
    qv_bias,
    w_out,
    out_bias,
    ln2_gain,
    ln2_bias,
    w_fc1,
    fc1_bias,
    w_fc2,
    fc2_bias,
):
    low = jnp.bfloat16
    wide = jnp.float32
    grid = Grid(depth)
    rows, full_width = layer_input.shape
    shard = ln1_gain.shape[0]
    head_width = qv_bias.shape[1]
    ff_width = fc1_bias.shape[0]
    padded = -(-(rows + 1) // 256) * 256

    quarter = head_width // 2
    group_width = 4 * quarter
    ff_padding = 2 * group_width - ff_width
    sources = [w_qkv[0], w_qkv[1], w_qkv[2], w_out.T]
    first_block = jnp.concatenate(
        [values[:, i * quarter : (i + 1) * quarter] for i in range(2) for values in sources],
        axis=1,
    )
    second_block = jnp.pad(w_fc1, ((0, 0), (0, ff_padding)))
    third_block = jnp.pad(w_fc2.T, ((0, 0), (0, ff_padding)))
    half = depth // 2
    blocks = [grid.spread(first_block), grid.spread(second_block), grid.spread(third_block)]
    vectors = jnp.stack([ln1_gain, ln1_bias, out_bias, ln2_gain, ln2_bias, fc2_bias])
    (vectors,) = fence([vectors], [blocks[0]])
    vectors = grid.gather_small(vectors)
    own_one = grid.gather_depth(blocks[0])

    here = grid.y
    mine = lax.dynamic_slice_in_dim(token_image, here * rows, rows)
    theirs = lax.dynamic_slice_in_dim(token_image, (1 - here) * rows, rows)
    mine, theirs = fence([mine, theirs], [blocks[0]])
    places = lax.iota(jnp.int32, rows)
    stray = mine == 1 - here
    stray_here = jnp.any(stray)
    stray_there = jnp.any(theirs == here)
    blank = mine == IMAGES
    first_blank = jnp.min(jnp.where(blank, places, rows - 1))
    last_blank = jnp.max(jnp.where(blank, places, 0))
    swap_at = jnp.where(stray_here, jnp.max(jnp.where(stray, places, 0)), first_blank)
    swapped = stray_here | stray_there
    blank_at = jnp.where(stray_here, swap_at, last_blank)

    def one_row(values, at):
        return lax.dynamic_slice_in_dim(values, at, 1)

    sent = jnp.concatenate(
        [one_row(layer_input, swap_at), one_row(cotangent, swap_at), one_row(layer_input, last_blank)]
    )
    came = grid.over_y(sent)
    biases = jnp.concatenate([qv_bias.reshape(-1), fc1_bias])
    biases = jnp.pad(biases, (0, -biases.shape[0] % 128)).reshape(-1, 128)
    (biases,) = fence([biases], [blocks[0]])
    other_biases = grid.over_y(biases)

    def sides_of(own):
        return [grid.over_x(own), grid.over_y(own)]

    beside_three, across_three = sides_of(blocks[2])
    quad = [blocks[2], beside_three, across_three, grid.over_both(blocks[2])]
    (block_two,) = fence([blocks[1]], [vectors, came])
    own_two = grid.gather_depth(block_two)
    own_one, vectors, came, other_biases, *quad = fence(
        [own_one, vectors, came, other_biases] + quad
    )
    vectors = vectors.astype(wide)
    other_biases = other_biases.reshape(-1)
    other_blank = jnp.where(stray_there, sent[0:1], came[2:3])
    spread_rows = lax.broadcasted_iota(jnp.int32, (padded, 1), 0)
    at_swap = (spread_rows == swap_at) & swapped

    def stretch(values):
        return jnp.pad(values, ((0, padded - rows), (0, 0)))

    input_rows = jnp.where(at_swap, came[0:1], stretch(layer_input))
    input_rows = jnp.where(spread_rows == rows, other_blank, input_rows)
    grad_low = jnp.where(at_swap, came[1:2], stretch(cotangent))
    grad_low = jnp.where(spread_rows == blank_at, 0, grad_low).astype(low)
    kind = jnp.where(spread_rows > rows, 3, jnp.where(spread_rows == rows, 2, 0))
    kind = jnp.where(spread_rows == blank_at, 1, kind)
    input_rows, grad_low = lax.optimization_barrier((input_rows, grad_low))

    def ordered(first, second):
        return jnp.where(grid.c == 0, first, second), jnp.where(grid.c == 0, second, first)

    spot = grid.x.reshape(1)
    inner = -(-3 * quarter // 128) * 128
    qv_groups, fc1_groups = [], []
    for flat in (biases.reshape(-1), other_biases):
        flat = flat.astype(wide)
        pair = flat[: 2 * head_width].reshape(2, 2, quarter)
        none = jnp.zeros((quarter,), wide)
        rest = jnp.zeros((inner - 3 * quarter,), wide)
        qv_groups += ordered(
            *[jnp.concatenate([pair[0, i], none, pair[1, i], rest]) for i in range(2)]
        )
        hidden_bias = flat[2 * head_width : 2 * head_width + ff_width]
        hidden_bias = jnp.pad(hidden_bias, (0, ff_padding))
        fc1_groups += ordered(hidden_bias[:group_width], hidden_bias[group_width:])

    def stacked(rows_of, picked):
        return jnp.stack([rows_of[i] for i in picked])[:, None]

    qv_stacks = [stacked(qv_groups, picked) for picked in ((0, 1), (2, 3))]
    fc1_stacks = [stacked(fc1_groups, picked) for picked in ((1, 3), (0, 2))]

    def corners_of(beside, across):
        first, second = take_halves(beside, across)
        return [grid.over_y(first), grid.over_x(second)]

    def cores_of(*values):
        return [grid.over_core(value) for value in values]

    def near_groups(own, beside, there):
        return [
            [(own, 0, 0), (beside, 0, 1)],
            [(there[0], 0, 0), (there[1], 0, 1)],
        ]

    def far_groups(across, corner, there):
        return [
            [(across, 0, 0), (corner[0], 0, 1), (corner[1], half, 1)],
            [(there[0], 0, 0), (there[1], 0, 1), (there[2], half, 1)],
        ]

    quad = jnp.stack(quad)
    gain_one, shift_one, out_shift, gain_two, shift_two, fc2_shift = [
        vectors[i : i + 1] for i in range(6)
    ]
    beside_one, across_one = sides_of(own_one)
    unit_one, _ = unit_rows(input_rows.astype(wide))
    normed = (unit_one * gain_one + shift_one).astype(low)
    own_two, beside_one, across_one, normed, quad, grad_there, kind, *stacks = fence(
        [own_two, beside_one, across_one, normed, quad, grid.over_core(grad_low), kind]
        + qv_stacks
        + fc1_stacks
    )
    qv_stacks, fc1_stacks = stacks[:2], stacks[2:]
    corner_one = corners_of(beside_one, across_one)
    there = cores_of(own_one, beside_one)
    own_two_there = grid.over_core(own_two)
    across_there = grid.over_core(across_one)
    sides_two = sides_of(own_two)
    quads = grid.gather_depth(quad)

    def heads(stack, groups, waits=()):
        return heads_forward_call(spot, kind, normed, stack, groups, waits)

    attn_weights = near_groups(own_one, beside_one, there)
    first_qkv, first_probs, *mixed = heads(qv_stacks[0], attn_weights, [own_two_there])
    *corner_one, across_there, first_qkv = fence(corner_one + [across_there, first_qkv])
    there = [across_there] + cores_of(*corner_one)
    attn_weights = attn_weights + far_groups(across_one, corner_one, there)
    second_qkv, second_probs, *more = heads(qv_stacks[1], attn_weights[2:])
    mixed = mixed + more
    beside_two, across_two, second_qkv = fence(sides_two + [second_qkv])
    corner_two = corners_of(beside_two, across_two)
    beside_there, across_there = cores_of(beside_two, across_two)
    resid, normed_two = out_project(
        spot,
        mixed,
        input_rows,
        out_shift,
        gain_two,
        shift_two,
        attn_weights,
        [beside_there, across_there],
    )
    normed_there = grid.over_core(normed)
    *corner_two, normed_two, normed_there = fence(corner_two + [normed_two, normed_there])
    up_weights = near_groups(own_two, beside_two, [own_two_there, beside_there])
    there = [across_there] + cores_of(*corner_two)
    up_weights = up_weights + far_groups(across_two, corner_two, there)
    classes = ((1, 3), (0, 2))

    def up(at, waits):
        picked = [up_weights[i] for i in classes[at]]
        return up_project(spot, normed_two, fc1_stacks[at], picked, waits)

    other_active, other_slope = up(0, [])
    (other_active,) = fence([other_active])
    active_there = grid.over_core(other_active)
    own_active, own_slope = up(1, [other_active])
    normed_two_there = grid.over_core(normed_two)
    near_mixed, far_mixed = grid.over_core(mixed[1]), grid.over_core(mixed[3])
    own_active, active_there, normed_two_there, near_mixed, far_mixed = fence(
        [own_active, active_there, normed_two_there, near_mixed, far_mixed]
    )
    fc2_sums = weight_grad(spot, (grad_low, grad_there), (own_active, active_there), depth)
    fc2_near, quads = fence([fc2_sums[0], quads])
    quads_there = grid.over_core(quads)
    down_weights = [
        [(source, 0, 0, at), (source, 0, 1, at + 1)]
        for at in (0, 2)
        for source in (quads, quads_there)
    ]

    def move_first(sums):
        _, beside_lo, _, _, across_hi, corner_lo, corner_hi = sums
        return [
            grid.over_x(corner_lo),
            grid.over_y(corner_hi),
            grid.over_x(beside_lo),
            grid.over_y(across_hi),
        ]

    def move_second(sums, corner_lo, corner_hi):
        beside_hi, across_lo = add_pairs(sums[2], corner_hi, sums[3], corner_lo)
        return [grid.over_x(beside_hi), grid.over_y(across_lo)]

    def join(own, first, second):
        return add_square(own, first[0], second[0], second[1], first[1])

    fc2_moved = move_first(fc2_sums)
    order = (0, 2, 1, 3)
    own_hidden, other_hidden, resid_low, sums_two, fc1_bias_sums = mlp_back(
        spot,
        grad_low,
        own_slope,
        other_slope,
        resid,
        gain_two,
        [down_weights[i] for i in order],
        [up_weights[i] for i in order],
        [fc2_near],
    )
    resid_low, other_hidden, *fc2_moved = fence([resid_low, other_hidden] + fc2_moved)
    fc2_second = move_second(fc2_sums, *fc2_moved[:2])
    hidden_there = grid.over_core(other_hidden)
    resid_there = grid.over_core(resid_low)

    def heads_back(qkv, probs, side, waits):
        order = [1 + 2 * side, 2 * side]
        return heads_backward_call(
            spot,
            resid_low,
            qkv,
            probs,
            [mixed[i] for i in order],
            [attn_weights[i] for i in order],
            (1, 0),
            waits,
        )

    far_other, far_own, far_sums = heads_back(second_qkv, second_probs, 1, [])
    *fc2_second, far_other, hidden_there, resid_there = fence(
        fc2_second + [far_other, hidden_there, resid_there]
    )
    far_there = grid.over_core(far_other)
    fc2_total = join(fc2_near, fc2_moved[2:], fc2_second)
    fc1_sums = weight_grad(
        spot, (normed_two, normed_two_there), (own_hidden, hidden_there), depth, waits=[fc2_total]
    )
    far_there, fc2_total, fc1_near = fence([far_there, fc2_total, fc1_sums[0]])
    fc2_piece = grid.scatter_depth(fc2_total)
    fc1_moved = move_first(fc1_sums)
    near_other, near_own, near_sums_qkv = heads_back(first_qkv, first_probs, 0, [fc1_near])
    near_other, *fc1_moved = fence([near_other] + fc1_moved)
    fc1_second = move_second(fc1_sums, *fc1_moved[:2])
    near_there = grid.over_core(near_other)

    def attn_grad(side, own_part, there_part, own_mixed, there_mixed, waits):
        return weight_grad(
            spot,
            (normed, normed_there),
            (own_part, there_part),
            depth,
            (side,),
            (resid_low, own_mixed, resid_there, there_mixed),
            waits,
        )

    across_lo, across_hi, corner_lo, corner_hi = attn_grad(
        2, far_own, far_there, mixed[2], far_mixed, [near_other]
    )
    across_lo, across_hi, corner_lo, corner_hi, near_there = fence(
        [across_lo, across_hi, corner_lo, corner_hi, near_there]
    )
    corners = [grid.over_x(corner_lo), grid.over_y(corner_hi)]
    attn_first = grid.over_y(across_hi)
    near_sums, beside_lo, beside_hi = attn_grad(
        0, near_own, near_there, mixed[0], near_mixed, [across_lo]
    )
    *fc1_second, beside_lo, beside_hi, fc2_piece = fence(
        fc1_second + [beside_lo, beside_hi, fc2_piece]
    )
    beside_first = grid.over_x(beside_lo)
    fc1_total = join(fc1_near, fc1_moved[2:], fc1_second)
    by_class = [down_weights[i] for i in classes[0] + classes[1]]
    layer_rows = down_project(
        spot, other_active, own_active, resid, fc2_shift, by_class, [fc1_total]
    )
    *corners, attn_first, beside_first, fc1_total = fence(
        corners + [attn_first, beside_first, fc1_total], [layer_rows]
    )
    fc1_piece = grid.scatter_depth(fc1_total)
    beside_hi, across_lo = add_pairs(beside_hi, corners[1], across_lo, corners[0])
    moved = [grid.over_x(beside_hi), grid.over_y(across_lo)]
    by_class = [attn_weights[i] for i in (1, 3, 0, 2)]
    input_grad, sums_one = norm_back(
        spot,
        [near_other, far_other, near_own, far_own],
        input_rows,
        resid_low,
        gain_one,
        by_class,
        [beside_hi],
    )

    def column_sum(values):
        return jnp.sum(values.astype(wide), axis=0)

    def absolute(near_other, near_own, far_other, far_own):
        near = ordered(near_own, near_other)
        far = ordered(far_own, far_other)
        return [
            (jnp.where(here == 0, one, two), jnp.where(here == 0, two, one))
            for one, two in zip(near, far)
        ]

    qkv_totals = absolute(near_sums_qkv[0], near_sums_qkv[1], far_sums[0], far_sums[1])
    query_and_value = [
        qkv_totals[half_at][side][0, at : at + quarter]
        for side in range(2)
        for at in (0, 2 * quarter)
        for half_at in range(2)
    ]
    fc1_totals = absolute(*[fc1_bias_sums[i] for i in (2, 0, 3, 1)])
    fc1_rows = []
    for side in range(2):
        fc1_rows += [fc1_totals[0][side][0], fc1_totals[1][side][0, : ff_width - group_width]]
    flat = jnp.concatenate(
        [
            sums_one[0],
            sums_one[1],
            sums_two[2],
            sums_two[0],
            sums_two[1],
            column_sum(grad_low),
            *query_and_value,
            *fc1_rows,
        ]
    )
    length = flat.shape[0]
    lines = -(-length // 1024) * 8
    flat = jnp.pad(flat, (0, lines * 128 - length)).reshape(lines, 128)
    *moved, flat, fc1_piece = fence(moved + [flat, fc1_piece])
    total = join(near_sums, [beside_first, attn_first], moved)
    attn_piece = grid.scatter_depth(total)
    (flat, fc1_piece, fc2_piece) = fence([flat, fc1_piece, fc2_piece], [total])
    flat = flat + grid.over_core(flat)
    flat = flat + grid.over_x(flat)
    flat = flat + grid.over_y(flat)
    bit = 1
    while bit < depth:
        flat = flat + grid.across_z(flat, bit)
        bit *= 2
    flat = flat.reshape(-1)
    fc1_piece = grid.scatter_core(fc1_piece)
    fc2_piece = grid.scatter_core(fc2_piece)
    swap_from = fence([one_row(layer_rows, swap_at), one_row(input_grad, swap_at)], [total])
    returned = [grid.over_y(values) for values in swap_from]
    layer_output = jnp.where(at_swap, returned[0], layer_rows)[:rows]
    input_grad = jnp.where(at_swap, returned[1], input_grad)[:rows]
    attn_piece = grid.scatter_core(attn_piece)
    row_total = flat[: 6 * full_width].reshape(6, full_width)
    row_piece = lax.dynamic_slice_in_dim(row_total, lax.axis_index("dp") * shard, shard, 1)
    start = 6 * full_width
    qv_piece = lax.dynamic_slice_in_dim(flat, start + here * 2 * head_width, 2 * head_width)
    start = start + 4 * head_width
    fc1_bias_piece = lax.dynamic_slice_in_dim(flat, start + here * ff_width, ff_width)
    heads_piece = attn_piece.reshape(2, shard, 4, quarter).transpose(2, 1, 0, 3)
    heads_piece = heads_piece.reshape(4, shard, head_width)

    def whole_columns(pair):
        return jnp.concatenate([pair[0], pair[1][:, : group_width - ff_padding]], axis=1)

    return (
        layer_output,
        input_grad,
        row_piece[0],
        row_piece[1],
        heads_piece[:3],
        qv_piece.reshape(2, head_width),
        heads_piece[3].T,
        row_piece[2],
        row_piece[3],
        row_piece[4],
        whole_columns(fc1_piece),
        fc1_bias_piece,
        whole_columns(fc2_piece).T,
        row_piece[5],
    )


def fits_images(mesh):
    groups = mesh.shape["dp"] // 4
    return (
        mesh.shape["tensor"] == IMAGES
        and mesh.shape["dp"] % 4 == 0
        and groups >= 2
        and groups & (groups - 1) == 0
    )


def solution(mesh):
    in_specs = (
        P(("dp", "tensor"), None),
        P("dp"),
        P(("dp", "tensor"), None),
        P("dp"),
        P("dp"),
        P(None, "dp", "tensor"),
        P(None, "tensor"),
        P("tensor", "dp"),
        P("dp"),
        P("dp"),
        P("dp"),
        P("dp", "tensor"),
        P("tensor"),
        P("tensor", "dp"),
        P("dp"),
    )
    out_specs = (
        P(("dp", "tensor"), None),
        P(("dp", "tensor"), None),
        P("dp"),
        P("dp"),
        P(None, "dp", "tensor"),
        P(None, "tensor"),
        P("tensor", "dp"),
        P("dp"),
        P("dp"),
        P("dp"),
        P("dp", "tensor"),
        P("tensor"),
        P("tensor", "dp"),
        P("dp"),
    )

    def body(*arrays):
        slots = arrays[1].shape[0]
        if fits_images(mesh) and slots == IMAGES * (PATCHES + 1):
            return image_shards(mesh.shape["dp"] // 4, *arrays)
        return shards(*arrays)

    return jax.shard_map(body, mesh=mesh, in_specs=in_specs, out_specs=out_specs, check_vma=False)
```

```python
import functools

import jax
import jax.numpy as jnp
from jax import lax
from jax.experimental import pallas as pl
from jax.experimental.pallas import tpu as pltpu
from jax.sharding import PartitionSpec as P

HEAD_DIM = 72
IMAGES = 2


layer_eps = 1e-06
gelu_scale = 0.7978845608028654


def gelu_tanh(values):
    return (
        0.5 * values * (1.0 + jnp.tanh(gelu_scale * (values + 0.044715 * values * values * values)))
    )


def norm_rows(values, gain, shift):
    centre = values - jnp.mean(values, axis=1, keepdims=True)
    spread = jnp.mean(centre * centre, axis=1, keepdims=True)
    return centre * lax.rsqrt(spread + layer_eps) * gain + shift


def contract_rows(left, right):
    return lax.dot_general(
        left, right, (((0,), (0,)), ((), ())), preferred_element_type=jnp.float32
    )


def contract_cols(left, right):
    return lax.dot_general(
        left, right, (((1,), (1,)), ((), ())), preferred_element_type=jnp.float32
    )


def split_heads(values, head_count):
    slot_count = values.shape[0]
    return values.reshape(slot_count, head_count, -1).transpose(1, 0, 2)


def join_heads(values):
    head_count, slot_count, head_size = values.shape
    return values.transpose(1, 0, 2).reshape(slot_count, head_count * head_size)


def block_rows(slot_count):
    half_rows = slot_count // 2
    return half_rows


def masked_scores(rows_query, head_keys, rows_ids, image_ids, score_scale):
    scores = contract_cols(rows_query, head_keys) * score_scale
    return jnp.where(rows_ids[:, None] == image_ids[None, :], scores, -1e30)


def heads_forward(query_heads, key_heads, value_heads, image_ids, score_scale):
    slot_count, head_size = (query_heads.shape[1], query_heads.shape[2])
    block_size = block_rows(slot_count)
    block_count = slot_count // block_size
    id_blocks = image_ids.reshape(block_count, block_size)

    def one_head(head_inputs):
        head_query, head_keys, head_values = head_inputs

        def one_block(block_inputs):
            rows_query, rows_ids = block_inputs
            scores = masked_scores(rows_query, head_keys, rows_ids, image_ids, score_scale)
            peak = jnp.max(scores, axis=1, keepdims=True)
            expo_rows = jnp.exp(scores - peak)
            row_total = jnp.sum(expo_rows, axis=1, keepdims=True)
            prob_rows = (expo_rows / row_total).astype(jnp.bfloat16)
            mixed = jnp.dot(prob_rows, head_values, preferred_element_type=jnp.float32)
            return (mixed.astype(jnp.bfloat16), peak[:, 0] + jnp.log(row_total[:, 0]))

        mixed, logsum = lax.map(
            one_block, (head_query.reshape(block_count, block_size, head_size), id_blocks)
        )
        return (mixed.reshape(slot_count, head_size), logsum.reshape(slot_count))

    return lax.map(one_head, (query_heads, key_heads, value_heads))


def heads_backward(query_heads, key_heads, value_heads, grad_heads, logsum, image_ids, score_scale):
    slot_count, head_size = (query_heads.shape[1], query_heads.shape[2])
    block_size = block_rows(slot_count)
    block_count = slot_count // block_size
    id_blocks = image_ids.reshape(block_count, block_size)

    def one_head(head_inputs):
        head_query, head_keys, head_values, head_grad, head_logsum = head_inputs

        def one_block(carried, block_inputs):
            key_sum, value_sum = carried
            rows_query, rows_grad, rows_logsum, rows_ids = block_inputs
            scores = masked_scores(rows_query, head_keys, rows_ids, image_ids, score_scale)
            prob_rows = jnp.exp(scores - rows_logsum[:, None])
            value_sum = value_sum + contract_rows(prob_rows.astype(jnp.bfloat16), rows_grad)
            grad_probs = contract_cols(rows_grad, head_values)
            centre = jnp.sum(grad_probs * prob_rows, axis=1, keepdims=True)
            grad_scores = (prob_rows * (grad_probs - centre)).astype(jnp.bfloat16)
            rows_dq = (
                jnp.dot(grad_scores, head_keys, preferred_element_type=jnp.float32) * score_scale
            ).astype(jnp.bfloat16)
            key_sum = key_sum + contract_rows(grad_scores, rows_query) * score_scale
            return ((key_sum, value_sum), rows_dq)

        zeros_init = jnp.zeros((slot_count, head_size), jnp.float32)
        block_inputs = (
            head_query.reshape(block_count, block_size, head_size),
            head_grad.reshape(block_count, block_size, head_size),
            head_logsum.reshape(block_count, block_size),
            id_blocks,
        )
        (key_sum, value_sum), query_grad = lax.scan(
            one_block, (zeros_init, zeros_init), block_inputs
        )
        return (
            query_grad.reshape(slot_count, head_size),
            key_sum.astype(jnp.bfloat16),
            value_sum.astype(jnp.bfloat16),
        )

    return lax.map(one_head, (query_heads, key_heads, value_heads, grad_heads, logsum))


def forward_pass(inputs, full_output):
    (
        layer_input,
        token_image,
        ln1_gain,
        ln1_bias,
        w_qkv,
        qv_bias,
        w_out,
        out_bias,
        ln2_gain,
        ln2_bias,
        w_fc1,
        fc1_bias,
        w_fc2,
        fc2_bias,
    ) = inputs
    head_count = w_qkv.shape[2] // HEAD_DIM
    score_scale = HEAD_DIM ** (-0.5)
    attn_params = (
        lax.all_gather(ln1_gain, "dp", axis=0, tiled=True),
        lax.all_gather(ln1_bias, "dp", axis=0, tiled=True),
        lax.all_gather(w_qkv, "dp", axis=1, tiled=True),
        lax.all_gather(w_out, "dp", axis=1, tiled=True),
        lax.all_gather(out_bias, "dp", axis=0, tiled=True),
    )
    mlp_params = (
        lax.all_gather(ln2_gain, "dp", axis=0, tiled=True),
        lax.all_gather(ln2_bias, "dp", axis=0, tiled=True),
        lax.all_gather(w_fc1, "dp", axis=0, tiled=True),
        lax.all_gather(w_fc2, "dp", axis=1, tiled=True),
        lax.all_gather(fc2_bias, "dp", axis=0, tiled=True),
    )
    input_rows = layer_input.astype(jnp.float32)
    normed = norm_rows(
        input_rows, attn_params[0].astype(jnp.float32), attn_params[1].astype(jnp.float32)
    )
    first_in = lax.all_gather(normed.astype(jnp.bfloat16), "tensor", axis=0, tiled=True)
    projected = jnp.einsum(
        "sd,cde->cse", first_in, attn_params[2], preferred_element_type=jnp.float32
    )
    bias_rows = qv_bias.astype(jnp.float32)
    query_heads = split_heads((projected[0] + bias_rows[0]).astype(jnp.bfloat16), head_count)
    key_heads = split_heads(projected[1].astype(jnp.bfloat16), head_count)
    value_heads = split_heads((projected[2] + bias_rows[1]).astype(jnp.bfloat16), head_count)
    mixed, logsum = heads_forward(query_heads, key_heads, value_heads, token_image, score_scale)
    attn_out = join_heads(mixed)
    resid = (
        input_rows
        + lax.psum_scatter(
            jnp.dot(attn_out, attn_params[3], preferred_element_type=jnp.float32),
            "tensor",
            scatter_dimension=0,
            tiled=True,
        )
        + attn_params[4].astype(jnp.float32)
    )
    normed_two = norm_rows(
        resid, mlp_params[0].astype(jnp.float32), mlp_params[1].astype(jnp.float32)
    )
    second_in = lax.all_gather(normed_two.astype(jnp.bfloat16), "tensor", axis=0, tiled=True)
    hidden = jnp.dot(
        second_in, mlp_params[2], preferred_element_type=jnp.float32
    ) + fc1_bias.astype(jnp.float32)
    active = gelu_tanh(hidden).astype(jnp.bfloat16)
    layer_output = None
    if full_output:
        summed = lax.psum_scatter(
            jnp.dot(active, mlp_params[3], preferred_element_type=jnp.float32).astype(jnp.bfloat16),
            "tensor",
            scatter_dimension=0,
            tiled=True,
        ).astype(jnp.float32)
        layer_output = (resid + summed + mlp_params[4].astype(jnp.float32)).astype(jnp.bfloat16)
    return (
        attn_params,
        mlp_params,
        input_rows,
        first_in,
        query_heads,
        key_heads,
        value_heads,
        logsum,
        attn_out,
        resid,
        second_in,
        hidden,
        active,
        layer_output,
    )


def shards(
    layer_input,
    token_image,
    cotangent,
    ln1_gain,
    ln1_bias,
    w_qkv,
    qv_bias,
    w_out,
    out_bias,
    ln2_gain,
    ln2_bias,
    w_fc1,
    fc1_bias,
    w_fc2,
    fc2_bias,
):
    inputs = (
        layer_input,
        token_image,
        ln1_gain,
        ln1_bias,
        w_qkv,
        qv_bias,
        w_out,
        out_bias,
        ln2_gain,
        ln2_bias,
        w_fc1,
        fc1_bias,
        w_fc2,
        fc2_bias,
    )
    first_pass = forward_pass(inputs, True)
    layer_output = first_pass[13]
    fenced = lax.optimization_barrier((layer_output, inputs))[1]
    saved = forward_pass(fenced, False)
    (
        attn_params,
        mlp_params,
        input_rows,
        first_in,
        query_heads,
        key_heads,
        value_heads,
        logsum,
        attn_out,
        resid,
        second_in,
        hidden,
        active,
        unused_output,
    ) = saved
    score_scale = HEAD_DIM ** (-0.5)
    row_count = layer_input.shape[0]
    tensor_at = lax.axis_index("tensor")
    image_rows = lax.dynamic_slice_in_dim(token_image, tensor_at * row_count, row_count)
    valid_mask = (image_rows < IMAGES).astype(jnp.float32)
    grad_rows = cotangent.astype(jnp.float32) * valid_mask[:, None]
    grad_low = grad_rows.astype(jnp.bfloat16)
    grad_all = lax.all_gather(grad_low, "tensor", axis=0, tiled=True)
    grad_active = contract_cols(grad_all, mlp_params[3])
    grad_hidden = jax.vjp(gelu_tanh, hidden)[1](grad_active)[0].astype(jnp.bfloat16)
    fc2_grad = contract_rows(active, grad_all)
    fc1_grad = contract_rows(second_in, grad_hidden)
    grad_normed_two = lax.psum_scatter(
        contract_cols(grad_hidden, mlp_params[2]), "tensor", scatter_dimension=0, tiled=True
    )
    norm_two_back = jax.vjp(
        norm_rows, resid, mlp_params[0].astype(jnp.float32), mlp_params[1].astype(jnp.float32)
    )[1]
    resid_part, ln2_gain_sum, ln2_bias_sum = norm_two_back(grad_normed_two)
    grad_resid = grad_rows + resid_part
    resid_low = grad_resid.astype(jnp.bfloat16)
    resid_all = lax.all_gather(resid_low, "tensor", axis=0, tiled=True)
    out_grad = contract_rows(attn_out, resid_all)
    grad_attn = contract_cols(resid_all, attn_params[3]).astype(jnp.bfloat16)
    head_count = query_heads.shape[0]
    grad_query, grad_keys, grad_values = heads_backward(
        query_heads,
        key_heads,
        value_heads,
        split_heads(grad_attn, head_count),
        logsum,
        token_image,
        score_scale,
    )
    grad_qkv = jnp.stack([join_heads(grad_query), join_heads(grad_keys), join_heads(grad_values)])
    qkv_grad = jnp.einsum("sd,cse->cde", first_in, grad_qkv, preferred_element_type=jnp.float32)
    grad_normed = lax.psum_scatter(
        jnp.einsum("cse,cde->sd", grad_qkv, attn_params[2], preferred_element_type=jnp.float32),
        "tensor",
        scatter_dimension=0,
        tiled=True,
    )
    norm_one_back = jax.vjp(
        norm_rows,
        input_rows,
        attn_params[0].astype(jnp.float32),
        attn_params[1].astype(jnp.float32),
    )[1]
    input_part, ln1_gain_sum, ln1_bias_sum = norm_one_back(grad_normed)
    input_grad = grad_resid + input_part
    qkv_piece, out_piece, fc1_piece, fc2_piece = (
        lax.psum_scatter(qkv_grad, "dp", scatter_dimension=1, tiled=True),
        lax.psum_scatter(out_grad, "dp", scatter_dimension=1, tiled=True),
        lax.psum_scatter(fc1_grad, "dp", scatter_dimension=0, tiled=True),
        lax.psum_scatter(fc2_grad, "dp", scatter_dimension=1, tiled=True),
    )
    full_width = layer_input.shape[1]
    head_width = qv_bias.shape[1]
    ff_width = fc1_bias.shape[0]
    row_sums = jnp.stack(
        [
            ln1_gain_sum,
            ln1_bias_sum,
            jnp.sum(resid_low.astype(jnp.float32), axis=0),
            ln2_gain_sum,
            ln2_bias_sum,
            jnp.sum(grad_rows, axis=0),
        ]
    )
    qv_sums = jnp.stack(
        [
            jnp.sum(grad_qkv[0].astype(jnp.float32), axis=0),
            jnp.sum(grad_qkv[2].astype(jnp.float32), axis=0),
        ]
    )
    qv_wide = lax.dynamic_update_slice_in_dim(
        jnp.zeros((2, full_width), jnp.float32), qv_sums, tensor_at * head_width, 1
    )
    fc1_sums = jnp.sum(grad_hidden.astype(jnp.float32), axis=0)
    fc1_wide = lax.dynamic_update_slice_in_dim(
        jnp.zeros((ff_width * lax.axis_size("tensor"),), jnp.float32),
        fc1_sums,
        tensor_at * ff_width,
        0,
    )
    row_total, qv_total, fc1_total = lax.psum((row_sums, qv_wide, fc1_wide), ("dp", "tensor"))
    dp_width = ln1_gain.shape[0]
    row_piece = lax.dynamic_slice_in_dim(row_total, lax.axis_index("dp") * dp_width, dp_width, 1)
    qv_piece = lax.dynamic_slice_in_dim(qv_total, tensor_at * head_width, head_width, 1)
    fc1_bias_piece = lax.dynamic_slice_in_dim(fc1_total, tensor_at * ff_width, ff_width, 0)
    return (
        layer_output,
        input_grad,
        row_piece[0],
        row_piece[1],
        qkv_piece,
        qv_piece,
        out_piece,
        row_piece[2],
        row_piece[3],
        row_piece[4],
        fc1_piece,
        fc1_bias_piece,
        fc2_piece,
        row_piece[5],
    )


LOG2E = 1.4426950408889634
VMEM_BYTES = 60 * 1024 * 1024


def head_window(head, base, width):
    start = base + head * HEAD_DIM
    first = start // 128 * 128
    last = min(-(-(start + HEAD_DIM) // 128) * 128, width)
    return start - first, first, last


def only_head(values, lane, offset):
    inside = (lane >= offset) & (lane < offset + HEAD_DIM)
    return jnp.where(inside, values, 0)


def with_lanes(values, lane, offset, first_column, second_column):
    one, two = (0, 1) if offset >= 2 else (126, 127)
    values = jnp.where(lane == one, first_column, values)
    return jnp.where(lane == two, second_column, values)


def lane_index(rows, first, last):
    return lax.broadcasted_iota(jnp.int32, (rows, last - first), 1)


def row_columns(kind):
    image = kind == 0
    padding = (kind == 1) | (kind == 2)
    low = jnp.bfloat16
    image_query = jnp.where(image, 1.0, 0.0).astype(low)
    other_query = jnp.where(image, 0.0, 1.0).astype(low)
    image_key = jnp.where(image, 0.0, -1e30).astype(low)
    padding_key = jnp.where(padding, 0.0, -1e30).astype(low)
    return image_query, other_query, image_key, padding_key


def dot_last(left, right):
    return lax.dot_general(
        left, right, (((1,), (1,)), ((), ())), preferred_element_type=jnp.float32
    )


def dot_first(left, right):
    return lax.dot_general(
        left, right, (((0,), (0,)), ((), ())), preferred_element_type=jnp.float32
    )


def heads_forward_kernel(places, heads, waits, spot, kind_ref, x_any, bias_ref, *refs):
    count = sum(len(parts) for parts in places)
    pieces = refs[:count]
    qkv_any, probs_any, *mixed_any = refs[count + waits : count + waits + 4]
    x_ref, qkv_ref, probs_ref, keys_ref, values_ref, total_ref, mixed_ref = refs[-12:-5]
    in_sems, out_sems, probs_sems, weights, sems = refs[-5:]
    scale = HEAD_DIM ** (-0.5) * LOG2E
    rows = x_ref.shape[0]
    part = heads * HEAD_DIM
    inner = qkv_ref.shape[2]
    width = keys_ref.shape[1]
    base = width - part
    groups = len(places)
    slots = probs_ref.shape[0]
    copies = weight_copies(places, pieces, weights, sems, spot[0])
    x_copy = pltpu.make_async_copy(x_any, x_ref, in_sems.at[0])
    begin([x_copy] + copies[0])
    arrive([x_copy] + copies[0])
    image_query, other_query, image_key, padding_key = row_columns(kind_ref[...])
    blank = jnp.zeros((rows, base), jnp.bfloat16)
    sent, writes = [], []
    for group in range(groups):
        if group + 1 < groups:
            begin(copies[group + 1])
        if group:
            arrive(copies[group])
        projected = jnp.dot(
            x_ref[...], strips(weights, group)[:, :inner], preferred_element_type=jnp.float32
        )
        qkv_ref[group] = (projected + bias_ref[group]).astype(jnp.bfloat16)
        copy = pltpu.make_async_copy(qkv_ref.at[group], qkv_any.at[group], out_sems.at[group])
        copy.start()
        sent.append(copy)
        keys_ref[:, :part] = qkv_ref[group, :, part : 2 * part]
        keys_ref[:, part:] = blank
        values_ref[:, :base] = blank
        values_ref[:, base:] = qkv_ref[group, :, 2 * part : 3 * part]
        total_ref[...] = jnp.zeros_like(total_ref)
        for head in range(heads):
            offset, first, last = head_window(head, 0, width)
            lane = lane_index(rows, first, last)
            keys = with_lanes(
                only_head(keys_ref[:, first:last], lane, offset),
                lane,
                offset,
                image_key,
                padding_key,
            )
            query = with_lanes(
                only_head(qkv_ref[group, :, first:last], lane, offset),
                lane,
                offset,
                image_query,
                other_query,
            )
            v_offset, v_first, v_last = head_window(head, base, width)
            values = only_head(
                values_ref[:, v_first:v_last], lane_index(rows, v_first, v_last), v_offset
            )
            at = group * heads + head
            slot = at % slots
            if at >= slots:
                writes[at - slots].wait()
            for tile in row_tiles(rows, 384):
                scores = dot_last(query[tile], keys)
                peak = jnp.max(scores, axis=1, keepdims=True)
                expo = jnp.exp2((scores - peak) * scale)
                total = jnp.sum(expo, axis=1, keepdims=True)
                probs = (expo * (1.0 / total)).astype(jnp.bfloat16)
                probs_ref[slot, tile, :] = probs
                total_ref[tile, v_first:v_last] += jnp.dot(
                    probs, values, preferred_element_type=jnp.float32
                )
            copy = pltpu.make_async_copy(
                probs_ref.at[slot], probs_any.at[group, head], probs_sems.at[slot]
            )
            copy.start()
            writes.append(copy)
        mixed_ref[group] = total_ref[...].astype(jnp.bfloat16)
        copy = pltpu.make_async_copy(
            mixed_ref.at[group], mixed_any[group], out_sems.at[groups + group]
        )
        copy.start()
        sent.append(copy)
    arrive(sent + writes[-slots:])


def heads_forward_call(spot, kind, rows_in, biases, groups, waits=()):
    rows, full = rows_in.shape
    arrays, places = flatten(groups)
    high, group_width = arrays[0].shape[-2:]
    depth = full // (2 * high)
    count = len(groups)
    part = group_width // 4
    heads = part // HEAD_DIM
    inner = -(-3 * part // 128) * 128
    outer = -(-part // 128) * 128
    slots = min(8, count * heads)
    return call(
        functools.partial(heads_forward_kernel, places, heads, len(waits)),
        "heads_forward",
        [spot, kind, rows_in, biases, *arrays],
        [smem_spec(), vmem_spec(), any_spec(), vmem_spec()] + [any_spec()] * len(arrays),
        [
            (any_spec(), (count, rows, inner), jnp.bfloat16),
            (any_spec(), (count, heads, rows, rows), jnp.bfloat16),
            (any_spec(), (rows, outer), jnp.bfloat16),
            (any_spec(), (rows, outer), jnp.bfloat16),
        ],
        [
            low_scratch(rows, full),
            low_scratch(count, rows, inner),
            low_scratch(slots, rows, rows),
            low_scratch(rows, outer),
            low_scratch(rows, outer),
            wide_scratch(rows, outer),
            low_scratch(count, rows, outer),
            copy_sems(1),
            copy_sems(2 * count),
            copy_sems(slots),
        ]
        + weight_scratch(places, depth, high, group_width),
        waits,
    )


def heads_backward_kernel(places, heads, picks, waits, spot, grad_any, qkv_any, probs_any, *refs):
    count = sum(len(parts) for parts in places)
    groups = len(places)
    mixed_any = refs[:groups]
    pieces = refs[groups : groups + count]
    first_out = groups + count + waits
    outs_any = refs[first_out : first_out + groups]
    sum_ref = refs[first_out + groups]
    grad_ref, qkv_ref, probs_ref, mixed_ref, out_ref, keys_ref, values_ref, grads_ref = refs[-16:-8]
    query_sum, key_sum, value_sum, in_sems, probs_sems, out_sems, weights, sems = refs[-8:]
    width = keys_ref.shape[1]
    first_lane = pieces[0].shape[-1] - width
    loads = weight_copies(places, pieces, weights, sems, spot[0], first_lane, width)
    grad_copy = pltpu.make_async_copy(grad_any, grad_ref, in_sems.at[2 * groups])
    slots = probs_ref.shape[0]
    seconds, reads = [], []
    for group in range(groups):
        seconds.append(
            [
                pltpu.make_async_copy(
                    qkv_any.at[picks[group]], qkv_ref.at[group], in_sems.at[2 * group]
                ),
                pltpu.make_async_copy(
                    mixed_any[group], mixed_ref.at[group], in_sems.at[2 * group + 1]
                ),
            ]
        )
        for head in range(heads):
            slot = len(reads) % slots
            reads.append(
                pltpu.make_async_copy(
                    probs_any.at[picks[group], head], probs_ref.at[slot], probs_sems.at[slot]
                )
            )
    begin([grad_copy] + loads[0])
    begin(seconds[0])
    begin(reads[:2])
    score_scale = HEAD_DIM ** (-0.5)
    rows = grad_ref.shape[0]
    part = heads * HEAD_DIM
    base = width - part
    low = jnp.bfloat16
    blank = jnp.zeros((rows, base), low)
    sent = []
    started = 2
    for group in range(groups):
        arrive(([grad_copy] if group == 0 else []) + loads[group])
        grads_ref[...] = jnp.dot(
            grad_ref[...], strips(weights, group), preferred_element_type=jnp.float32
        ).astype(low)
        arrive(seconds[group])
        if group + 1 < groups:
            begin(loads[group + 1] + seconds[group + 1])
        keys_ref[:, :part] = qkv_ref[group, :, part : 2 * part]
        keys_ref[:, part:] = blank
        values_ref[:, :base] = blank
        values_ref[:, base:] = qkv_ref[group, :, 2 * part : 3 * part]
        query_sum[...] = jnp.zeros_like(query_sum)
        key_sum[...] = jnp.zeros_like(key_sum)
        value_sum[...] = jnp.zeros_like(value_sum)
        weighted = grads_ref[...].astype(jnp.float32) * mixed_ref[group].astype(jnp.float32)
        for head in range(heads):
            at = group * heads + head
            offset, first, last = head_window(head, 0, width)
            lane = lane_index(rows, first, last)
            query = only_head(qkv_ref[group, :, first:last], lane, offset)
            keys = only_head(keys_ref[:, first:last], lane, offset)
            v_offset, v_first, v_last = head_window(head, base, width)
            v_lane = lane_index(rows, v_first, v_last)
            values = values_ref[:, v_first:v_last]
            grad = only_head(grads_ref[:, v_first:v_last], v_lane, v_offset)
            centre = jnp.sum(
                only_head(weighted[:, v_first:v_last], v_lane, v_offset), axis=1, keepdims=True
            )
            while started < len(reads) and started - at < slots:
                reads[started].start()
                started += 1
            reads[at].wait()
            probs = probs_ref[at % slots]
            grad_probs = dot_last(grad, values)
            grad_scores = (probs.astype(jnp.float32) * (grad_probs - centre)).astype(low)
            value_sum[:, v_first:v_last] += dot_first(probs, grad)
            key_sum[:, first:last] += dot_first(grad_scores, query)
            query_sum[:, first:last] += jnp.dot(
                grad_scores, keys, preferred_element_type=jnp.float32
            )
        out_ref[group, :, :part] = (query_sum[...] * score_scale).astype(low)[:, :part]
        out_ref[group, :, part : 2 * part] = (key_sum[...] * score_scale).astype(low)[:, :part]
        out_ref[group, :, 2 * part : 3 * part] = value_sum[...].astype(low)[:, base:]
        tail = out_ref.shape[2] - 3 * part
        if tail:
            out_ref[group, :, 3 * part :] = jnp.zeros((rows, tail), low)
        copy = pltpu.make_async_copy(out_ref.at[group], outs_any[group], out_sems.at[group])
        copy.start()
        sent.append(copy)
        sum_ref[group] = jnp.sum(out_ref[group].astype(jnp.float32), axis=0, keepdims=True)
    arrive(sent)


def heads_backward_call(spot, grad_rows, qkv, probs, mixed, groups, picks, waits=()):
    rows, full = grad_rows.shape
    arrays, places = flatten(groups)
    high, group_width = arrays[0].shape[-2:]
    depth = full // (2 * high)
    part = group_width // 4
    heads = part // HEAD_DIM
    inner = qkv.shape[2]
    outer = mixed[0].shape[1]
    count = len(groups)
    slots = min(count * heads, 6)
    return call(
        functools.partial(heads_backward_kernel, places, heads, picks, len(waits)),
        "heads_backward",
        [spot, grad_rows, qkv, probs, *mixed, *arrays],
        [smem_spec()] + [any_spec()] * (3 + count + len(arrays)),
        [(any_spec(), (rows, inner), jnp.bfloat16)] * count
        + [(vmem_spec(), (count, 1, inner), jnp.float32)],
        [
            low_scratch(rows, full),
            low_scratch(count, rows, inner),
            low_scratch(slots, rows, rows),
            low_scratch(count, rows, outer),
            low_scratch(count, rows, inner),
            low_scratch(rows, outer),
            low_scratch(rows, outer),
            low_scratch(rows, outer),
            wide_scratch(rows, outer),
            wide_scratch(rows, outer),
            wide_scratch(rows, outer),
            copy_sems(2 * count + 1),
            copy_sems(slots),
            copy_sems(count),
        ]
        + weight_scratch(places, depth, high, outer),
        waits,
    )


def any_spec():
    return pl.BlockSpec(memory_space=pl.ANY)


def smem_spec():
    return pl.BlockSpec(memory_space=pltpu.SMEM)


def vmem_spec():
    return pl.BlockSpec(memory_space=pltpu.VMEM)


def limits():
    return pltpu.CompilerParams(vmem_limit_bytes=VMEM_BYTES)


def low_scratch(*shape):
    return pltpu.VMEM(shape, jnp.bfloat16)


def wide_scratch(*shape):
    return pltpu.VMEM(shape, jnp.float32)


def copy_sems(*shape):
    return pltpu.SemaphoreType.DMA(shape)


def begin(copies):
    for copy in copies:
        copy.start()


def arrive(copies):
    for copy in copies:
        copy.wait()


def call(kernel, name, operands, specs, outs, scratch, waits=()):
    no_cost = pl.CostEstimate(flops=1024, bytes_accessed=1024, transcendentals=0)
    out_specs = [spec for spec, _, _ in outs]
    return pl.pallas_call(
        kernel,
        in_specs=list(specs) + [any_spec()] * len(waits),
        out_specs=out_specs,
        out_shape=[jax.ShapeDtypeStruct(shape, kind) for _, shape, kind in outs],
        scratch_shapes=scratch,
        compiler_params=limits(),
        cost_estimate=no_cost,
        name=name,
    )(*operands, *waits)


def flatten(groups):
    arrays = [part[0] for group in groups for part in group]
    places = [[part[1:] for part in group] for group in groups]
    return arrays, places


def weight_copies(places, refs, weights, sems, x_at, first=0, width=None):
    copies, at = [], 0
    for group, parts in enumerate(places):
        mine = []
        for part, (start, x_off, *pick) in enumerate(parts):
            source = refs[at].at[:, pick[0]] if pick else refs[at]
            at += 1
            if width is not None:
                source = source.at[:, :, pl.ds(first, width)]
            target = weights.at[group, pl.ds(start, source.shape[0]), x_at ^ x_off]
            mine.append(pltpu.make_async_copy(source, target, sems.at[group, part]))
        copies.append(mine)
    return copies


def weight_scratch(places, depth, high, width):
    count = len(places)
    return [
        pltpu.VMEM((count, depth, 2, high, width), jnp.bfloat16),
        copy_sems(count, max(len(parts) for parts in places)),
    ]


def strips(weights, at):
    _, depth, _, high, width = weights.shape
    return weights[at].reshape(depth * 2 * high, width)


def row_tiles(rows, size):
    return [slice(start, min(start + size, rows)) for start in range(0, rows, size)]


def out_copies(pairs, sems):
    return [
        pltpu.make_async_copy(source, target, sems.at[i])
        for i, (source, target) in enumerate(pairs)
    ]


def up_kernel(places, waits, spot, x_any, bias_ref, *refs):
    count = sum(len(parts) for parts in places)
    pieces = refs[:count]
    active_any, slope_any = refs[count + waits : count + waits + 2]
    x_ref, active_ref, slope_ref, x_sem, out_sems, weights, sems = refs[-7:]
    rows = x_ref.shape[0]
    groups = len(places)
    copies = weight_copies(places, pieces, weights, sems, spot[0])
    x_copy = pltpu.make_async_copy(x_any, x_ref, x_sem.at[0])
    begin([x_copy] + copies[0])
    arrive([x_copy] + copies[0])
    sent = []
    for group in range(groups):
        if group + 1 < groups:
            begin(copies[group + 1])
        if group:
            arrive(copies[group])
        whole = strips(weights, group)
        for tile in row_tiles(rows, 128):
            hidden = jnp.dot(x_ref[tile, :], whole, preferred_element_type=jnp.float32)
            hidden = hidden + bias_ref[group]
            square = hidden * hidden
            inner = jnp.tanh(hidden * (gelu_scale + gelu_scale * 0.044715 * square))
            gate = 0.5 + 0.5 * inner
            active_ref[group, tile, :] = (hidden * gate).astype(jnp.bfloat16)
            grow = hidden * (gelu_scale + 3.0 * 0.044715 * gelu_scale * square)
            slope = gate + grow * (0.5 - 0.5 * inner * inner)
            slope_ref[group, tile, :] = slope.astype(jnp.bfloat16)
        for half, tile in enumerate(row_tiles(rows, rows // 2)):
            span = pl.ds(tile.start, rows // 2)
            for at, (source, target) in enumerate(
                ((active_ref, active_any), (slope_ref, slope_any))
            ):
                copy = pltpu.make_async_copy(
                    source.at[group, span], target.at[group, span], out_sems.at[group, half, at]
                )
                copy.start()
                sent.append(copy)
    arrive(sent)


def up_project(spot, rows_in, biases, groups, waits=()):
    rows, full = rows_in.shape
    arrays, places = flatten(groups)
    high, width = arrays[0].shape[-2:]
    depth = full // (2 * high)
    count = len(groups)
    shape = (count, rows, width)
    return call(
        functools.partial(up_kernel, places, len(waits)),
        "mlp_up",
        [spot, rows_in, biases, *arrays],
        [smem_spec(), any_spec(), vmem_spec()] + [any_spec()] * len(arrays),
        [(any_spec(), shape, jnp.bfloat16)] * 2,
        [
            low_scratch(rows, full),
            low_scratch(*shape),
            low_scratch(*shape),
            copy_sems(1),
            copy_sems(count, 2, 2),
        ]
        + weight_scratch(places, depth, high, width),
        waits,
    )


def unit_rows(values):
    centre = values - jnp.mean(values, axis=1, keepdims=True)
    spread = jnp.mean(centre * centre, axis=1, keepdims=True)
    root = lax.rsqrt(spread + layer_eps)
    return centre * root, root


def norm_rows_back(values, gain, grad):
    unit, root = unit_rows(values)
    scaled = grad * gain
    mean_one = jnp.mean(scaled, axis=1, keepdims=True)
    mean_two = jnp.mean(scaled * unit, axis=1, keepdims=True)
    part = root * (scaled - mean_one - unit * mean_two)
    return part, jnp.sum(grad * unit, axis=0, keepdims=True), jnp.sum(grad, axis=0, keepdims=True)


def mlp_back_kernel(down_places, up_places, waits, spot, x_any, one_any, two_any, resid_any, gain_ref, *refs):
    count = [sum(len(parts) for parts in places) for places in (down_places, up_places)]
    down_pieces = refs[: count[0]]
    up_pieces = refs[count[0] : count[0] + count[1]]
    at = count[0] + count[1] + waits
    one_out, two_out, low_any, sum_ref, hidden_sums = refs[at : at + 5]
    x_ref, slope_ref, hidden_ref, resid_ref, total, low_ref, in_sems, hidden_sems, out_sems = refs[
        at + 5 : at + 14
    ]
    down_weights, down_sems, up_weights, up_sems = refs[at + 14 :]
    rows = x_ref.shape[0]
    groups = len(down_places)
    half = groups // 2
    slots = down_weights.shape[0]

    def slotted(places, pieces, weights, sems):
        copies, first = [], 0
        for group, parts in enumerate(places):
            mine = pieces[first : first + len(parts)]
            first += len(parts)
            slot = group % slots
            copies += weight_copies(
                [parts],
                mine,
                weights.at[pl.ds(slot, 1)],
                sems.at[pl.ds(slot, 1)],
                spot[0],
            )
        return copies

    downs = slotted(down_places, down_pieces, down_weights, down_sems)
    ups = slotted(up_places, up_pieces, up_weights, up_sems)
    for group in range(groups):
        source = one_any.at[group] if group < half else two_any.at[group - half]
        slot = group % slots
        downs[group].append(
            pltpu.make_async_copy(source, slope_ref.at[slot], in_sems.at[2 + slot])
        )
    x_copy = pltpu.make_async_copy(x_any, x_ref, in_sems.at[0])
    late = pltpu.make_async_copy(resid_any, resid_ref, in_sems.at[1])
    begin([x_copy] + downs[0])
    arrive([x_copy] + downs[0])
    sent = []
    for group in range(groups):
        slot = group % slots
        begin(ups[group])
        whole = strips(down_weights, slot)
        column_total = jnp.zeros((1, total.shape[1]), jnp.float32)
        if group >= slots:
            sent[group - slots].wait()
        for tile in row_tiles(rows, 256):
            grad = jnp.dot(x_ref[tile, :], whole, preferred_element_type=jnp.float32)
            low = (grad * slope_ref[slot, tile, :].astype(jnp.float32)).astype(jnp.bfloat16)
            hidden_ref[slot, tile, :] = low
            column_total += jnp.sum(low.astype(jnp.float32), axis=0, keepdims=True)
        hidden_sums[group] = column_total
        target = one_out.at[group] if group < half else two_out.at[group - half]
        copy = pltpu.make_async_copy(hidden_ref.at[slot], target, hidden_sems.at[slot])
        copy.start()
        sent.append(copy)
        arrive(ups[group])
        if group + 1 < groups:
            begin(downs[group + 1])
        else:
            begin([late])
        whole = strips(up_weights, slot)
        if group == 0:
            total[...] = dot_last(hidden_ref[slot], whole)
        elif group + 1 < groups:
            total[...] += dot_last(hidden_ref[slot], whole)
        else:
            products = [
                (tile, dot_last(hidden_ref[slot, tile, :], whole)) for tile in row_tiles(rows, 256)
            ]
        if group + 1 < groups:
            arrive(downs[group + 1])
    arrive([late])
    sums = [jnp.zeros((1, total.shape[1]), jnp.float32) for _ in range(3)]
    low_sent = []
    for tile, product in products:
        for small in range(tile.start, tile.stop, 128):
            span = slice(small, small + 128)
            inside = slice(small - tile.start, small - tile.start + 128)
            part, gain_sum, shift_sum = norm_rows_back(
                resid_ref[span, :].astype(jnp.float32),
                gain_ref[...],
                total[span, :] + product[inside],
            )
            low = (x_ref[span, :].astype(jnp.float32) + part).astype(jnp.bfloat16)
            low_ref[span, :] = low
            sums[0] += gain_sum
            sums[1] += shift_sum
            sums[2] += jnp.sum(low.astype(jnp.float32), axis=0, keepdims=True)
        long = pl.ds(tile.start, tile.stop - tile.start)
        copy = pltpu.make_async_copy(
            low_ref.at[long], low_any.at[long], out_sems.at[len(low_sent)]
        )
        copy.start()
        low_sent.append(copy)
    sum_ref[...] = jnp.concatenate(sums + [jnp.zeros((5, total.shape[1]), jnp.float32)])
    arrive(sent[-slots:] + low_sent)


def mlp_back(spot, grad_low, first_slope, second_slope, resid, gain, downs, ups, waits=()):
    rows, full = grad_low.shape
    down_arrays, down_places = flatten(downs)
    up_arrays, up_places = flatten(ups)
    high, width = up_arrays[0].shape[-2:]
    depth = full // (2 * high)
    count = len(downs)
    slots = 2
    shape = (count // 2, rows, width)

    def slot_scratch(places):
        return [
            pltpu.VMEM((slots, depth, 2, high, width), jnp.bfloat16),
            copy_sems(slots, max(len(parts) for parts in places)),
        ]

    return call(
        functools.partial(mlp_back_kernel, down_places, up_places, len(waits)),
        "mlp_back",
        [spot, grad_low, first_slope, second_slope, resid, gain, *down_arrays, *up_arrays],
        [smem_spec()]
        + [any_spec()] * 4
        + [vmem_spec()]
        + [any_spec()] * (len(down_arrays) + len(up_arrays)),
        [
            (any_spec(), shape, jnp.bfloat16),
            (any_spec(), shape, jnp.bfloat16),
            (any_spec(), (rows, full), jnp.bfloat16),
            (vmem_spec(), (8, full), jnp.float32),
            (vmem_spec(), (count, 1, width), jnp.float32),
        ],
        [
            low_scratch(rows, full),
            low_scratch(slots, rows, width),
            low_scratch(slots, rows, width),
            pltpu.VMEM(resid.shape, resid.dtype),
            wide_scratch(rows, full),
            low_scratch(rows, full),
            copy_sems(2 + slots),
            copy_sems(slots),
            copy_sems(-(-rows // 256)),
        ]
        + slot_scratch(down_places)
        + slot_scratch(up_places),
        waits,
    )


def back_kernel(places, sources, waits, spot, *refs):
    count = sum(len(parts) for parts in places)
    grads_any = refs[:sources]
    base_any, grad_any, gain_ref = refs[sources : sources + 3]
    pieces = refs[sources + 3 : sources + 3 + count]
    first_out = sources + 3 + count + waits
    out_any, sum_ref = refs[first_out : first_out + 2]
    grads_ref, base_ref, grad_ref, total, in_sems, out_sems, weights, sems = refs[first_out + 2 :]
    rows = total.shape[0]
    groups = len(places)
    width = weights.shape[-1]
    copies = weight_copies(places, pieces, weights, sems, spot[0], 0, width)
    at = 0
    for source in grads_any:
        parts = [source] if len(source.shape) == 2 else [source.at[i] for i in range(source.shape[0])]
        for part in parts:
            copies[at].append(pltpu.make_async_copy(part, grads_ref.at[at], in_sems.at[at]))
            at += 1
    late = [
        pltpu.make_async_copy(base_any, base_ref, in_sems.at[groups]),
        pltpu.make_async_copy(grad_any, grad_ref, in_sems.at[groups + 1]),
    ]
    begin(copies[0])
    for group in range(groups):
        arrive(copies[group])
        begin(copies[group + 1] if group + 1 < groups else late)
        whole = strips(weights, group)
        if group == 0:
            total[...] = dot_last(grads_ref[group], whole)
        elif group + 1 < groups:
            total[...] += dot_last(grads_ref[group], whole)
        else:
            products = [
                (tile, dot_last(grads_ref[group, tile, :], whole)) for tile in row_tiles(rows, 256)
            ]
    arrive(late)
    sums = [jnp.zeros((1, total.shape[1]), jnp.float32) for _ in range(2)]
    sent = []
    for tile, product in products:
        for small in range(tile.start, tile.stop, 128):
            span = slice(small, small + 128)
            inside = slice(small - tile.start, small - tile.start + 128)
            part, gain_sum, shift_sum = norm_rows_back(
                base_ref[span, :].astype(jnp.float32),
                gain_ref[...],
                total[span, :] + product[inside],
            )
            grad = grad_ref[span, :].astype(jnp.float32) + part
            total[span, :] = grad
            sums[0] += gain_sum
            sums[1] += shift_sum
        long = pl.ds(tile.start, tile.stop - tile.start)
        copy = pltpu.make_async_copy(total.at[long], out_any.at[long], out_sems.at[len(sent)])
        copy.start()
        sent.append(copy)
    sum_ref[...] = jnp.concatenate(sums + [jnp.zeros((6, total.shape[1]), jnp.float32)])
    arrive(sent)


def norm_back(spot, grads, base, grad, gain, groups, waits=()):
    rows, full = base.shape
    arrays, places = flatten(groups)
    high, _ = arrays[0].shape[-2:]
    width = grads[0].shape[-1]
    depth = full // (2 * high)
    outs = [
        (any_spec(), (rows, full), jnp.float32),
        (vmem_spec(), (8, full), jnp.float32),
    ]
    return call(
        functools.partial(back_kernel, places, len(grads), len(waits)),
        "norm_one_back",
        [spot, *grads, base, grad, gain, *arrays],
        [smem_spec()] + [any_spec()] * (len(grads) + 2) + [vmem_spec()] + [any_spec()] * len(arrays),
        outs,
        [
            low_scratch(len(groups), rows, width),
            pltpu.VMEM(base.shape, base.dtype),
            pltpu.VMEM(grad.shape, grad.dtype),
            wide_scratch(rows, full),
            copy_sems(len(groups) + 2),
            copy_sems(-(-rows // 256)),
        ]
        + weight_scratch(places, depth, high, width),
        waits,
    )


def down_kernel(places, waits, spot, later_any, early_any, resid_any, shift_ref, *refs):
    count = sum(len(parts) for parts in places)
    pieces = refs[:count]
    out_any = refs[count + waits]
    active_ref, resid_ref, total, out_ref, in_sems, out_sems, weights, sems = refs[-8:]
    rows = total.shape[0]
    groups = len(places)
    copies = weight_copies(places, pieces, weights, sems, spot[0])
    half = groups // 2
    for group in range(groups):
        source = later_any.at[group] if group < half else early_any.at[group - half]
        copies[group].append(
            pltpu.make_async_copy(source, active_ref.at[group], in_sems.at[group])
        )
    late = [pltpu.make_async_copy(resid_any, resid_ref, in_sems.at[groups])]
    begin(copies[0])
    for group in range(groups - 1):
        arrive(copies[group])
        begin(copies[group + 1])
        if group + 2 == groups:
            begin(late)
        product = dot_last(active_ref[group], strips(weights, group))
        if group == 0:
            total[...] = product
        else:
            total[...] += product
    arrive(copies[-1] + late)
    whole = strips(weights, groups - 1)
    sent = []
    for tile in row_tiles(rows, 256):
        product = dot_last(active_ref[groups - 1, tile, :], whole)
        product = product + total[tile, :] + shift_ref[...]
        product = product + resid_ref[tile, :].astype(jnp.float32)
        out_ref[tile, :] = product.astype(out_ref.dtype)
        long = pl.ds(tile.start, tile.stop - tile.start)
        copy = pltpu.make_async_copy(out_ref.at[long], out_any.at[long], out_sems.at[len(sent)])
        copy.start()
        sent.append(copy)
    arrive(sent)


def down_project(spot, first, second, resid, shift, groups, waits=()):
    rows, full = resid.shape
    arrays, places = flatten(groups)
    high, width = arrays[0].shape[-2:]
    depth = full // (2 * high)
    return call(
        functools.partial(down_kernel, places, len(waits)),
        "mlp_down",
        [spot, first, second, resid, shift, *arrays],
        [smem_spec()] + [any_spec()] * 3 + [vmem_spec()] + [any_spec()] * len(arrays),
        [(any_spec(), (rows, full), jnp.bfloat16)],
        [
            low_scratch(len(groups), rows, width),
            pltpu.VMEM(resid.shape, resid.dtype),
            wide_scratch(rows, full),
            low_scratch(rows, full),
            copy_sems(len(groups) + 1),
            copy_sems(-(-rows // 256)),
        ]
        + weight_scratch(places, depth, high, width),
        waits,
    )[0]


def out_kernel(places, waits, spot, one, two, three, four, x_any, shift_ref, gain_ref, bias_ref, *refs):
    count = sum(len(parts) for parts in places)
    pieces = refs[:count]
    resid_any, normed_any = refs[count + waits : count + waits + 2]
    mixed_ref, x_ref, resid_ref, low_ref, normed_ref, in_sems, out_sems, weights, sems = refs[-9:]
    rows = x_ref.shape[0]
    outer = weights.shape[-1]
    first = pieces[0].shape[-1] - outer
    copies = weight_copies(places, pieces, weights, sems, spot[0], first, outer)
    for group, mixed in enumerate((one, two, three, four)):
        copies[group].append(
            pltpu.make_async_copy(mixed, mixed_ref.at[group], in_sems.at[group])
        )
    late = [pltpu.make_async_copy(x_any, x_ref, in_sems.at[4])]
    for mine in copies:
        begin(mine)
    begin(late)
    for group in range(4):
        arrive(copies[group])
        if group < 3:
            product = dot_last(mixed_ref[group], strips(weights, group))
            if group == 0:
                resid_ref[...] = product
            else:
                resid_ref[...] += product
    arrive(late)
    whole = strips(weights, 3)
    products = [(tile, dot_last(mixed_ref[3, tile, :], whole)) for tile in row_tiles(rows, 256)]
    sent = []
    for tile, product in products:
        for small in range(tile.start, tile.stop, 128):
            span = slice(small, small + 128)
            inside = slice(small - tile.start, small - tile.start + 128)
            values = resid_ref[span, :] + product[inside] + x_ref[span, :].astype(jnp.float32)
            values = values + shift_ref[...]
            low_ref[span, :] = values.astype(jnp.bfloat16)
            unit, _ = unit_rows(values)
            normed_ref[span, :] = (unit * gain_ref[...] + bias_ref[...]).astype(jnp.bfloat16)
        long = pl.ds(tile.start, tile.stop - tile.start)
        for source, target in ((low_ref, resid_any), (normed_ref, normed_any)):
            copy = pltpu.make_async_copy(source.at[long], target.at[long], out_sems.at[len(sent)])
            copy.start()
            sent.append(copy)
    arrive(sent)


def out_project(spot, mixed, rows_in, shift, gain, bias, groups, waits=()):
    rows, full = rows_in.shape
    arrays, places = flatten(groups)
    high, _ = arrays[0].shape[-2:]
    outer = mixed[0].shape[1]
    depth = full // (2 * high)
    return call(
        functools.partial(out_kernel, places, len(waits)),
        "attn_out",
        [spot, *mixed, rows_in, shift, gain, bias, *arrays],
        [smem_spec()] + [any_spec()] * 5 + [vmem_spec()] * 3 + [any_spec()] * len(arrays),
        [
            (any_spec(), (rows, full), jnp.bfloat16),
            (any_spec(), (rows, full), jnp.bfloat16),
        ],
        [
            low_scratch(4, rows, outer),
            low_scratch(rows, full),
            wide_scratch(rows, full),
            low_scratch(rows, full),
            low_scratch(rows, full),
            copy_sems(5),
            copy_sems(2 * -(-rows // 256)),
        ]
        + weight_scratch(places, depth, high, outer),
        waits,
    )


def grad_kernel(sides, extra, waits, spot, *refs):
    inputs = 4 + (4 if extra else 0)
    sources = refs[:inputs]
    outs_at = inputs + waits
    count = sum(3 + side // 2 for side in sides)
    outs = list(refs[outs_at : outs_at + count])
    holds = refs[outs_at + count : outs_at + count + inputs]
    stage, in_sems, out_sems = refs[-3:]
    x_at = spot[0]
    def load(source, hold, at):
        return pltpu.make_async_copy(source, hold, in_sems.at[at])

    count = len(sides)
    first_x = load(sources[0], holds[0], 0)
    second_x = load(sources[2], holds[2], 1)
    firsts = [load(sources[1].at[i], holds[1].at[i], 2 + 2 * i) for i in range(count)]
    seconds = [load(sources[3].at[i], holds[3].at[i], 3 + 2 * i) for i in range(count)]
    extras = [load(sources[j], holds[j], 2 * count + j - 2) for j in range(4, inputs)]
    _, depth, _, high, width = stage.shape
    half = depth // 2
    begin([first_x, firsts[0]])
    arrive([first_x, firsts[0]])
    begin([second_x, seconds[0]])
    begin(extras)
    sent = []
    starts = []
    for side in sides:
        starts.append(sum(3 + before // 2 for before in sides[: len(starts)]))
    for i, side in enumerate(sides):
        if i:
            arrive([firsts[i], seconds[i]])
        for part in range(2):
            cut = slice(part * half * 2 * high, (part + 1) * half * 2 * high)
            span = pl.ds(part * half, half)
            product = dot_first(holds[0][:, cut], holds[1][i])
            if i == 0 and part == 0:
                arrive([second_x, seconds[0]])
                for later in range(1, count):
                    begin([firsts[later], seconds[later]])
            product += dot_first(holds[2][:, cut], holds[3][i])
            if extra:
                if i == 0 and part == 0:
                    arrive(extras)
                other = dot_first(holds[4][:, cut], holds[5][...])
                other += dot_first(holds[6][:, cut], holds[7][...])
                both = product.shape[1] + other.shape[1] - width
                left = product.shape[1] - both
                product = jnp.concatenate(
                    [product[:, :left], product[:, left:] + other[:, :both], other[:, both:]],
                    axis=1,
                )
            stage[i, part * half : (part + 1) * half] = product.astype(jnp.bfloat16).reshape(
                half, 2, high, width
            )
            if side == 0:
                near_out = outs[starts[i]].at[span]
                far_out = outs[starts[i] + 1 + part]
            else:
                near_out = outs[starts[i] + part]
                far_out = outs[starts[i] + 2 + part]
            for source, target in (
                (stage.at[i, span, x_at], near_out),
                (stage.at[i, span, 1 - x_at], far_out),
            ):
                copy = pltpu.make_async_copy(source, target, out_sems.at[len(sent)])
                copy.start()
                sent.append(copy)
    arrive(sent)


def weight_grad(spot, left, right, depth, sides=(0, 2), extra=(), waits=()):
    rows, full = left[0].shape
    high = full // (2 * depth)
    half = depth // 2
    count = len(sides)
    rights = [values.reshape(count, rows, -1) for values in right]
    width = full if extra else rights[0].shape[2]
    operands = [left[0], rights[0], left[1], rights[1], *extra]
    shapes = []
    for side in sides:
        shapes += [depth, half, half] if side == 0 else [half] * 4
    outs = [(any_spec(), (size, high, width), jnp.bfloat16) for size in shapes]
    return call(
        functools.partial(grad_kernel, sides, bool(extra), len(waits)),
        "weight_grad",
        [spot, *operands],
        [smem_spec()] + [any_spec()] * len(operands),
        outs,
        [pltpu.VMEM(values.shape, values.dtype) for values in operands]
        + [
            low_scratch(count, depth, 2, high, width),
            copy_sems(2 + 2 * count + 4),
            copy_sems(4 * count),
        ],
        waits,
    )


def pair_kernel(one_ref, two_ref, three_ref, four_ref, first_out, second_out):
    wide = jnp.float32
    low = first_out.dtype
    first_out[...] = (one_ref[...].astype(wide) + two_ref[...].astype(wide)).astype(low)
    second_out[...] = (three_ref[...].astype(wide) + four_ref[...].astype(wide)).astype(low)


def add_pairs(one, two, three, four):
    shape = jax.ShapeDtypeStruct(one.shape, one.dtype)
    return pl.pallas_call(
        pair_kernel,
        in_specs=[vmem_spec()] * 4,
        out_specs=[vmem_spec()] * 2,
        out_shape=[shape, shape],
        compiler_params=limits(),
        name="add_pairs",
    )(one, two, three, four)


def square_kernel(own, one_lo, one_hi, two_lo, two_hi, out):
    wide = jnp.float32
    half = one_lo.shape[0]
    for part, (one, two) in enumerate(((one_lo, two_lo), (one_hi, two_hi))):
        span = slice(part * half, (part + 1) * half)
        total = own[span].astype(wide) + one[...].astype(wide) + two[...].astype(wide)
        out[span] = total.astype(out.dtype)


def add_square(own, *parts):
    return pl.pallas_call(
        square_kernel,
        in_specs=[vmem_spec()] * 5,
        out_specs=vmem_spec(),
        out_shape=jax.ShapeDtypeStruct(own.shape, own.dtype),
        compiler_params=limits(),
        name="add_square",
    )(own, *parts)


def halves_kernel(first_ref, second_ref, first_out, second_out):
    first_out[...] = first_ref[...]
    second_out[...] = second_ref[...]


def take_halves(first, second):
    half = (first.shape[0] // 2,) + first.shape[1:]
    front = pl.BlockSpec(half, lambda i: (0, 0, 0))
    back = pl.BlockSpec(half, lambda i: (1, 0, 0))
    shape = jax.ShapeDtypeStruct(half, first.dtype)
    return pl.pallas_call(
        halves_kernel,
        grid=(1,),
        in_specs=[front, back],
        out_specs=[front, front],
        out_shape=[shape, shape],
        compiler_params=limits(),
        name="take_halves",
    )(first, second)


PATCHES = 729
AXES = ("dp", "tensor")


def nothing(*refs):
    del refs


def fence(released, waited=()):
    anywhere = pl.BlockSpec(memory_space=pl.ANY)
    released, waited = list(released), list(waited)
    return pl.pallas_call(
        nothing,
        in_specs=[anywhere] * (len(released) + len(waited)),
        out_specs=[anywhere] * len(released),
        out_shape=[jax.ShapeDtypeStruct(values.shape, values.dtype) for values in released],
        input_output_aliases={i: i for i in range(len(released))},
        name="fence",
    )(*released, *waited)


class Grid:
    def __init__(self, depth):
        self.depth = depth
        dp_at = lax.axis_index("dp")
        self.y = lax.axis_index("tensor")
        self.c = dp_at % 2
        self.x = dp_at // 2 % 2
        self.z = dp_at // 4

    def move(self, values, where):
        pairs = []
        for z in range(self.depth):
            for x in range(2):
                for c in range(2):
                    for y in range(2):
                        to_z, to_x, to_c, to_y = where(z, x, c, y)
                        pairs.append(
                            (
                                ((z * 2 + x) * 2 + c) * 2 + y,
                                ((to_z * 2 + to_x) * 2 + to_c) * 2 + to_y,
                            )
                        )
        return lax.ppermute(values, AXES, pairs)

    def over_x(self, values):
        return self.move(values, lambda z, x, c, y: (z, 1 - x, c, y))

    def over_y(self, values):
        return self.move(values, lambda z, x, c, y: (z, x, c, 1 - y))

    def over_both(self, values):
        return self.move(values, lambda z, x, c, y: (z, 1 - x, c, 1 - y))

    def over_core(self, values):
        return self.move(values, lambda z, x, c, y: (z, x, 1 - c, y))

    def along_z(self, values, hops):
        return self.move(values, lambda z, x, c, y: ((z + hops) % self.depth, x, c, y))

    def across_z(self, values, bit):
        return self.move(values, lambda z, x, c, y: (z ^ bit, x, c, y))

    def spread(self, block):
        width = block.shape[1] // 2
        mine = lax.dynamic_slice_in_dim(block, self.c * width, width, 1)
        theirs = self.over_core(
            lax.dynamic_slice_in_dim(block, (1 - self.c) * width, width, 1)
        )
        first = jnp.where(self.c == 0, mine, theirs)
        second = jnp.where(self.c == 0, theirs, mine)
        return jnp.concatenate([first, second])

    def depth_groups(self):
        return [
            [(z * 2 + x) * 2 + c for z in range(self.depth)] for x in range(2) for c in range(2)
        ]

    def gather_depth(self, block):
        return lax.all_gather(block, "dp", axis_index_groups=self.depth_groups())

    def scatter_depth(self, total):
        return lax.psum_scatter(total, "dp", axis_index_groups=self.depth_groups())

    def scatter_core(self, result):
        result = result.astype(jnp.float32)
        shard = result.shape[0] // 2
        mine = lax.dynamic_slice_in_dim(result, self.c * shard, shard)
        theirs = self.over_core(
            lax.dynamic_slice_in_dim(result, (1 - self.c) * shard, shard)
        )
        first = jnp.where(self.c == 0, mine, theirs)
        second = jnp.where(self.c == 0, theirs, mine)
        return jnp.stack([first, second])

    def gather_small(self, values):
        count, shard = values.shape
        parts = jnp.zeros((self.depth, 2, 2, count, shard), values.dtype)
        parts = lax.dynamic_update_slice(
            parts, values[None, None, None], (self.z, self.x, self.c, 0, 0)
        )
        parts = parts + self.over_core(parts)
        parts = parts + self.over_x(parts)
        bit = 1
        while bit < self.depth:
            parts = parts + self.across_z(parts, bit)
            bit *= 2
        return parts.transpose(3, 0, 1, 2, 4).reshape(count, -1)


def image_shards(
    depth,
    layer_input,
    token_image,
    cotangent,
    ln1_gain,
    ln1_bias,
    w_qkv,
    qv_bias,
    w_out,
    out_bias,
    ln2_gain,
    ln2_bias,
    w_fc1,
    fc1_bias,
    w_fc2,
    fc2_bias,
):
    low = jnp.bfloat16
    wide = jnp.float32
    grid = Grid(depth)
    rows, full_width = layer_input.shape
    shard = ln1_gain.shape[0]
    head_width = qv_bias.shape[1]
    ff_width = fc1_bias.shape[0]
    padded = -(-(rows + 1) // 256) * 256

    quarter = head_width // 2
    group_width = 4 * quarter
    ff_padding = 2 * group_width - ff_width
    sources = [w_qkv[0], w_qkv[1], w_qkv[2], w_out.T]
    first_block = jnp.concatenate(
        [values[:, i * quarter : (i + 1) * quarter] for i in range(2) for values in sources],
        axis=1,
    )
    second_block = jnp.pad(w_fc1, ((0, 0), (0, ff_padding)))
    third_block = jnp.pad(w_fc2.T, ((0, 0), (0, ff_padding)))
    half = depth // 2
    blocks = [grid.spread(first_block), grid.spread(second_block), grid.spread(third_block)]
    vectors = jnp.stack([ln1_gain, ln1_bias, out_bias, ln2_gain, ln2_bias, fc2_bias])
    (vectors,) = fence([vectors], [blocks[0]])
    vectors = grid.gather_small(vectors)
    own_one = grid.gather_depth(blocks[0])

    here = grid.y
    mine = lax.dynamic_slice_in_dim(token_image, here * rows, rows)
    theirs = lax.dynamic_slice_in_dim(token_image, (1 - here) * rows, rows)
    mine, theirs = fence([mine, theirs], [blocks[0]])
    places = lax.iota(jnp.int32, rows)
    stray = mine == 1 - here
    stray_here = jnp.any(stray)
    stray_there = jnp.any(theirs == here)
    blank = mine == IMAGES
    first_blank = jnp.min(jnp.where(blank, places, rows - 1))
    last_blank = jnp.max(jnp.where(blank, places, 0))
    swap_at = jnp.where(stray_here, jnp.max(jnp.where(stray, places, 0)), first_blank)
    swapped = stray_here | stray_there
    blank_at = jnp.where(stray_here, swap_at, last_blank)

    def one_row(values, at):
        return lax.dynamic_slice_in_dim(values, at, 1)

    sent = jnp.concatenate(
        [one_row(layer_input, swap_at), one_row(cotangent, swap_at), one_row(layer_input, last_blank)]
    )
    came = grid.over_y(sent)
    biases = jnp.concatenate([qv_bias.reshape(-1), fc1_bias])
    biases = jnp.pad(biases, (0, -biases.shape[0] % 128)).reshape(-1, 128)
    (biases,) = fence([biases], [blocks[0]])
    other_biases = grid.over_y(biases)

    def sides_of(own):
        return [grid.over_x(own), grid.over_y(own)]

    beside_three, across_three = sides_of(blocks[2])
    quad = [blocks[2], beside_three, across_three, grid.over_both(blocks[2])]
    (block_two,) = fence([blocks[1]], [vectors, came])
    own_two = grid.gather_depth(block_two)
    own_one, vectors, came, other_biases, *quad = fence(
        [own_one, vectors, came, other_biases] + quad
    )
    vectors = vectors.astype(wide)
    other_biases = other_biases.reshape(-1)
    other_blank = jnp.where(stray_there, sent[0:1], came[2:3])
    spread_rows = lax.broadcasted_iota(jnp.int32, (padded, 1), 0)
    at_swap = (spread_rows == swap_at) & swapped

    def stretch(values):
        return jnp.pad(values, ((0, padded - rows), (0, 0)))

    input_rows = jnp.where(at_swap, came[0:1], stretch(layer_input))
    input_rows = jnp.where(spread_rows == rows, other_blank, input_rows)
    grad_low = jnp.where(at_swap, came[1:2], stretch(cotangent))
    grad_low = jnp.where(spread_rows == blank_at, 0, grad_low).astype(low)
    kind = jnp.where(spread_rows > rows, 3, jnp.where(spread_rows == rows, 2, 0))
    kind = jnp.where(spread_rows == blank_at, 1, kind)
    input_rows, grad_low = lax.optimization_barrier((input_rows, grad_low))

    def ordered(first, second):
        return jnp.where(grid.c == 0, first, second), jnp.where(grid.c == 0, second, first)

    spot = grid.x.reshape(1)
    inner = -(-3 * quarter // 128) * 128
    qv_groups, fc1_groups = [], []
    for flat in (biases.reshape(-1), other_biases):
        flat = flat.astype(wide)
        pair = flat[: 2 * head_width].reshape(2, 2, quarter)
        none = jnp.zeros((quarter,), wide)
        rest = jnp.zeros((inner - 3 * quarter,), wide)
        qv_groups += ordered(
            *[jnp.concatenate([pair[0, i], none, pair[1, i], rest]) for i in range(2)]
        )
        hidden_bias = flat[2 * head_width : 2 * head_width + ff_width]
        hidden_bias = jnp.pad(hidden_bias, (0, ff_padding))
        fc1_groups += ordered(hidden_bias[:group_width], hidden_bias[group_width:])

    def stacked(rows_of, picked):
        return jnp.stack([rows_of[i] for i in picked])[:, None]

    qv_stacks = [stacked(qv_groups, picked) for picked in ((0, 1), (2, 3))]
    fc1_stacks = [stacked(fc1_groups, picked) for picked in ((1, 3), (0, 2))]

    def corners_of(beside, across):
        first, second = take_halves(beside, across)
        return [grid.over_y(first), grid.over_x(second)]

    def cores_of(*values):
        return [grid.over_core(value) for value in values]

    def near_groups(own, beside, there):
        return [
            [(own, 0, 0), (beside, 0, 1)],
            [(there[0], 0, 0), (there[1], 0, 1)],
        ]

    def far_groups(across, corner, there):
        return [
            [(across, 0, 0), (corner[0], 0, 1), (corner[1], half, 1)],
            [(there[0], 0, 0), (there[1], 0, 1), (there[2], half, 1)],
        ]

    quad = jnp.stack(quad)
    gain_one, shift_one, out_shift, gain_two, shift_two, fc2_shift = [
        vectors[i : i + 1] for i in range(6)
    ]
    beside_one, across_one = sides_of(own_one)
    unit_one, _ = unit_rows(input_rows.astype(wide))
    normed = (unit_one * gain_one + shift_one).astype(low)
    own_two, beside_one, across_one, normed, quad, grad_there, kind, *stacks = fence(
        [own_two, beside_one, across_one, normed, quad, grid.over_core(grad_low), kind]
        + qv_stacks
        + fc1_stacks
    )
    qv_stacks, fc1_stacks = stacks[:2], stacks[2:]
    corner_one = corners_of(beside_one, across_one)
    there = cores_of(own_one, beside_one)
    own_two_there = grid.over_core(own_two)
    across_there = grid.over_core(across_one)
    sides_two = sides_of(own_two)
    quads = grid.gather_depth(quad)

    def heads(stack, groups, waits=()):
        return heads_forward_call(spot, kind, normed, stack, groups, waits)

    attn_weights = near_groups(own_one, beside_one, there)
    first_qkv, first_probs, *mixed = heads(qv_stacks[0], attn_weights, [own_two_there])
    *corner_one, across_there, first_qkv = fence(corner_one + [across_there, first_qkv])
    there = [across_there] + cores_of(*corner_one)
    attn_weights = attn_weights + far_groups(across_one, corner_one, there)
    second_qkv, second_probs, *more = heads(qv_stacks[1], attn_weights[2:])
    mixed = mixed + more
    beside_two, across_two, second_qkv = fence(sides_two + [second_qkv])
    corner_two = corners_of(beside_two, across_two)
    beside_there, across_there = cores_of(beside_two, across_two)
    resid, normed_two = out_project(
        spot,
        mixed,
        input_rows,
        out_shift,
        gain_two,
        shift_two,
        attn_weights,
        [beside_there, across_there],
    )
    normed_there = grid.over_core(normed)
    *corner_two, normed_two, normed_there = fence(corner_two + [normed_two, normed_there])
    up_weights = near_groups(own_two, beside_two, [own_two_there, beside_there])
    there = [across_there] + cores_of(*corner_two)
    up_weights = up_weights + far_groups(across_two, corner_two, there)
    classes = ((1, 3), (0, 2))

    def up(at, waits):
        picked = [up_weights[i] for i in classes[at]]
        return up_project(spot, normed_two, fc1_stacks[at], picked, waits)

    other_active, other_slope = up(0, [])
    (other_active,) = fence([other_active])
    active_there = grid.over_core(other_active)
    own_active, own_slope = up(1, [other_active])
    normed_two_there = grid.over_core(normed_two)
    near_mixed, far_mixed = grid.over_core(mixed[1]), grid.over_core(mixed[3])
    own_active, active_there, normed_two_there, near_mixed, far_mixed, quads = fence(
        [own_active, active_there, normed_two_there, near_mixed, far_mixed, quads]
    )
    quads_there = grid.over_core(quads)
    fc2_sums = weight_grad(spot, (grad_low, grad_there), (own_active, active_there), depth)
    fc2_near, quads_there = fence([fc2_sums[0], quads_there])
    down_weights = [
        [(source, 0, 0, at), (source, 0, 1, at + 1)]
        for at in (0, 2)
        for source in (quads, quads_there)
    ]

    def move_first(sums):
        _, beside_lo, _, _, across_hi, corner_lo, corner_hi = sums
        return [
            grid.over_x(corner_lo),
            grid.over_y(corner_hi),
            grid.over_x(beside_lo),
            grid.over_y(across_hi),
        ]

    def move_second(sums, corner_lo, corner_hi):
        beside_hi, across_lo = add_pairs(sums[2], corner_hi, sums[3], corner_lo)
        return [grid.over_x(beside_hi), grid.over_y(across_lo)]

    def join(own, first, second):
        return add_square(own, first[0], second[0], second[1], first[1])

    fc2_moved = move_first(fc2_sums)
    order = (0, 2, 1, 3)
    own_hidden, other_hidden, resid_low, sums_two, fc1_bias_sums = mlp_back(
        spot,
        grad_low,
        own_slope,
        other_slope,
        resid,
        gain_two,
        [down_weights[i] for i in order],
        [up_weights[i] for i in order],
        [fc2_near],
    )
    resid_low, other_hidden, *fc2_moved = fence([resid_low, other_hidden] + fc2_moved)
    fc2_second = move_second(fc2_sums, *fc2_moved[:2])
    hidden_there = grid.over_core(other_hidden)
    resid_there = grid.over_core(resid_low)

    def heads_back(qkv, probs, side, waits):
        order = [1 + 2 * side, 2 * side]
        return heads_backward_call(
            spot,
            resid_low,
            qkv,
            probs,
            [mixed[i] for i in order],
            [attn_weights[i] for i in order],
            (1, 0),
            waits,
        )

    far_other, far_own, far_sums = heads_back(second_qkv, second_probs, 1, [])
    *fc2_second, far_other, hidden_there, resid_there = fence(
        fc2_second + [far_other, hidden_there, resid_there]
    )
    far_there = grid.over_core(far_other)
    fc2_total = join(fc2_near, fc2_moved[2:], fc2_second)
    fc1_sums = weight_grad(
        spot, (normed_two, normed_two_there), (own_hidden, hidden_there), depth, waits=[fc2_total]
    )
    far_there, fc2_total, fc1_near = fence([far_there, fc2_total, fc1_sums[0]])
    fc2_piece = grid.scatter_depth(fc2_total)
    fc1_moved = move_first(fc1_sums)
    near_other, near_own, near_sums_qkv = heads_back(first_qkv, first_probs, 0, [fc1_near])
    near_other, *fc1_moved = fence([near_other] + fc1_moved)
    fc1_second = move_second(fc1_sums, *fc1_moved[:2])
    near_there = grid.over_core(near_other)

    def attn_grad(side, own_part, there_part, own_mixed, there_mixed, waits):
        return weight_grad(
            spot,
            (normed, normed_there),
            (own_part, there_part),
            depth,
            (side,),
            (resid_low, own_mixed, resid_there, there_mixed),
            waits,
        )

    across_lo, across_hi, corner_lo, corner_hi = attn_grad(
        2, far_own, far_there, mixed[2], far_mixed, [near_other]
    )
    across_lo, across_hi, corner_lo, corner_hi, near_there = fence(
        [across_lo, across_hi, corner_lo, corner_hi, near_there]
    )
    corners = [grid.over_x(corner_lo), grid.over_y(corner_hi)]
    attn_first = grid.over_y(across_hi)
    near_sums, beside_lo, beside_hi = attn_grad(
        0, near_own, near_there, mixed[0], near_mixed, [across_lo]
    )
    *fc1_second, beside_lo, beside_hi, fc2_piece = fence(
        fc1_second + [beside_lo, beside_hi, fc2_piece]
    )
    beside_first = grid.over_x(beside_lo)
    fc1_total = join(fc1_near, fc1_moved[2:], fc1_second)
    *corners, fc1_total = fence(corners + [fc1_total])
    fc1_piece = grid.scatter_depth(fc1_total)
    beside_hi, across_lo = add_pairs(beside_hi, corners[1], across_lo, corners[0])
    moved = [grid.over_x(beside_hi), grid.over_y(across_lo)]
    by_class = [down_weights[i] for i in classes[0] + classes[1]]
    layer_rows = down_project(
        spot, other_active, own_active, resid, fc2_shift, by_class, [beside_hi]
    )
    by_class = [attn_weights[i] for i in (1, 3, 0, 2)]
    input_grad, sums_one = norm_back(
        spot,
        [near_other, far_other, near_own, far_own],
        input_rows,
        resid_low,
        gain_one,
        by_class,
        [layer_rows],
    )

    def column_sum(values):
        return jnp.sum(values.astype(wide), axis=0)

    def absolute(near_other, near_own, far_other, far_own):
        near = ordered(near_own, near_other)
        far = ordered(far_own, far_other)
        return [
            (jnp.where(here == 0, one, two), jnp.where(here == 0, two, one))
            for one, two in zip(near, far)
        ]

    qkv_totals = absolute(near_sums_qkv[0], near_sums_qkv[1], far_sums[0], far_sums[1])
    query_and_value = [
        qkv_totals[half_at][side][0, at : at + quarter]
        for side in range(2)
        for at in (0, 2 * quarter)
        for half_at in range(2)
    ]
    fc1_totals = absolute(*[fc1_bias_sums[i] for i in (2, 0, 3, 1)])
    fc1_rows = []
    for side in range(2):
        fc1_rows += [fc1_totals[0][side][0], fc1_totals[1][side][0, : ff_width - group_width]]
    flat = jnp.concatenate(
        [
            sums_one[0],
            sums_one[1],
            sums_two[2],
            sums_two[0],
            sums_two[1],
            column_sum(grad_low),
            *query_and_value,
            *fc1_rows,
        ]
    )
    length = flat.shape[0]
    lines = -(-length // 1024) * 8
    flat = jnp.pad(flat, (0, lines * 128 - length)).reshape(lines, 128)
    *moved, beside_first, attn_first, flat, fc1_piece = fence(
        moved + [beside_first, attn_first, flat, fc1_piece]
    )
    total = join(near_sums, [beside_first, attn_first], moved)
    attn_piece = grid.scatter_depth(total)
    (flat, fc1_piece, fc2_piece) = fence([flat, fc1_piece, fc2_piece], [total])
    flat = flat + grid.over_core(flat)
    flat = flat + grid.over_x(flat)
    flat = flat + grid.over_y(flat)
    bit = 1
    while bit < depth:
        flat = flat + grid.across_z(flat, bit)
        bit *= 2
    flat = flat.reshape(-1)
    fc1_piece = grid.scatter_core(fc1_piece)
    fc2_piece = grid.scatter_core(fc2_piece)
    swap_from = fence([one_row(layer_rows, swap_at), one_row(input_grad, swap_at)], [total])
    returned = [grid.over_y(values) for values in swap_from]
    layer_output = jnp.where(at_swap, returned[0], layer_rows)[:rows]
    input_grad = jnp.where(at_swap, returned[1], input_grad)[:rows]
    attn_piece = grid.scatter_core(attn_piece)
    row_total = flat[: 6 * full_width].reshape(6, full_width)
    row_piece = lax.dynamic_slice_in_dim(row_total, lax.axis_index("dp") * shard, shard, 1)
    start = 6 * full_width
    qv_piece = lax.dynamic_slice_in_dim(flat, start + here * 2 * head_width, 2 * head_width)
    start = start + 4 * head_width
    fc1_bias_piece = lax.dynamic_slice_in_dim(flat, start + here * ff_width, ff_width)
    heads_piece = attn_piece.reshape(2, shard, 4, quarter).transpose(2, 1, 0, 3)
    heads_piece = heads_piece.reshape(4, shard, head_width)

    def whole_columns(pair):
        return jnp.concatenate([pair[0], pair[1][:, : group_width - ff_padding]], axis=1)

    return (
        layer_output,
        input_grad,
        row_piece[0],
        row_piece[1],
        heads_piece[:3],
        qv_piece.reshape(2, head_width),
        heads_piece[3].T,
        row_piece[2],
        row_piece[3],
        row_piece[4],
        whole_columns(fc1_piece),
        fc1_bias_piece,
        whole_columns(fc2_piece).T,
        row_piece[5],
    )


def fits_images(mesh):
    groups = mesh.shape["dp"] // 4
    return (
        mesh.shape["tensor"] == IMAGES
        and mesh.shape["dp"] % 4 == 0
        and groups >= 2
        and groups & (groups - 1) == 0
    )


def solution(mesh):
    in_specs = (
        P(("dp", "tensor"), None),
        P("dp"),
        P(("dp", "tensor"), None),
        P("dp"),
        P("dp"),
        P(None, "dp", "tensor"),
        P(None, "tensor"),
        P("tensor", "dp"),
        P("dp"),
        P("dp"),
        P("dp"),
        P("dp", "tensor"),
        P("tensor"),
        P("tensor", "dp"),
        P("dp"),
    )
    out_specs = (
        P(("dp", "tensor"), None),
        P(("dp", "tensor"), None),
        P("dp"),
        P("dp"),
        P(None, "dp", "tensor"),
        P(None, "tensor"),
        P("tensor", "dp"),
        P("dp"),
        P("dp"),
        P("dp"),
        P("dp", "tensor"),
        P("tensor"),
        P("tensor", "dp"),
        P("dp"),
    )

    def body(*arrays):
        slots = arrays[1].shape[0]
        if fits_images(mesh) and slots == IMAGES * (PATCHES + 1):
            return image_shards(mesh.shape["dp"] // 4, *arrays)
        return shards(*arrays)

    return jax.shard_map(body, mesh=mesh, in_specs=in_specs, out_specs=out_specs, check_vma=False)
```

```python
import functools

import jax
import jax.numpy as jnp
from jax import lax
from jax.experimental import pallas as pl
from jax.experimental.pallas import tpu as pltpu
from jax.sharding import PartitionSpec as P

HEAD_DIM = 72
IMAGES = 2


layer_eps = 1e-06
gelu_scale = 0.7978845608028654


def gelu_tanh(values):
    return (
        0.5 * values * (1.0 + jnp.tanh(gelu_scale * (values + 0.044715 * values * values * values)))
    )


def norm_rows(values, gain, shift):
    centre = values - jnp.mean(values, axis=1, keepdims=True)
    spread = jnp.mean(centre * centre, axis=1, keepdims=True)
    return centre * lax.rsqrt(spread + layer_eps) * gain + shift


def contract_rows(left, right):
    return lax.dot_general(
        left, right, (((0,), (0,)), ((), ())), preferred_element_type=jnp.float32
    )


def contract_cols(left, right):
    return lax.dot_general(
        left, right, (((1,), (1,)), ((), ())), preferred_element_type=jnp.float32
    )


def split_heads(values, head_count):
    slot_count = values.shape[0]
    return values.reshape(slot_count, head_count, -1).transpose(1, 0, 2)


def join_heads(values):
    head_count, slot_count, head_size = values.shape
    return values.transpose(1, 0, 2).reshape(slot_count, head_count * head_size)


def block_rows(slot_count):
    half_rows = slot_count // 2
    return half_rows


def masked_scores(rows_query, head_keys, rows_ids, image_ids, score_scale):
    scores = contract_cols(rows_query, head_keys) * score_scale
    return jnp.where(rows_ids[:, None] == image_ids[None, :], scores, -1e30)


def heads_forward(query_heads, key_heads, value_heads, image_ids, score_scale):
    slot_count, head_size = (query_heads.shape[1], query_heads.shape[2])
    block_size = block_rows(slot_count)
    block_count = slot_count // block_size
    id_blocks = image_ids.reshape(block_count, block_size)

    def one_head(head_inputs):
        head_query, head_keys, head_values = head_inputs

        def one_block(block_inputs):
            rows_query, rows_ids = block_inputs
            scores = masked_scores(rows_query, head_keys, rows_ids, image_ids, score_scale)
            peak = jnp.max(scores, axis=1, keepdims=True)
            expo_rows = jnp.exp(scores - peak)
            row_total = jnp.sum(expo_rows, axis=1, keepdims=True)
            prob_rows = (expo_rows / row_total).astype(jnp.bfloat16)
            mixed = jnp.dot(prob_rows, head_values, preferred_element_type=jnp.float32)
            return (mixed.astype(jnp.bfloat16), peak[:, 0] + jnp.log(row_total[:, 0]))

        mixed, logsum = lax.map(
            one_block, (head_query.reshape(block_count, block_size, head_size), id_blocks)
        )
        return (mixed.reshape(slot_count, head_size), logsum.reshape(slot_count))

    return lax.map(one_head, (query_heads, key_heads, value_heads))


def heads_backward(query_heads, key_heads, value_heads, grad_heads, logsum, image_ids, score_scale):
    slot_count, head_size = (query_heads.shape[1], query_heads.shape[2])
    block_size = block_rows(slot_count)
    block_count = slot_count // block_size
    id_blocks = image_ids.reshape(block_count, block_size)

    def one_head(head_inputs):
        head_query, head_keys, head_values, head_grad, head_logsum = head_inputs

        def one_block(carried, block_inputs):
            key_sum, value_sum = carried
            rows_query, rows_grad, rows_logsum, rows_ids = block_inputs
            scores = masked_scores(rows_query, head_keys, rows_ids, image_ids, score_scale)
            prob_rows = jnp.exp(scores - rows_logsum[:, None])
            value_sum = value_sum + contract_rows(prob_rows.astype(jnp.bfloat16), rows_grad)
            grad_probs = contract_cols(rows_grad, head_values)
            centre = jnp.sum(grad_probs * prob_rows, axis=1, keepdims=True)
            grad_scores = (prob_rows * (grad_probs - centre)).astype(jnp.bfloat16)
            rows_dq = (
                jnp.dot(grad_scores, head_keys, preferred_element_type=jnp.float32) * score_scale
            ).astype(jnp.bfloat16)
            key_sum = key_sum + contract_rows(grad_scores, rows_query) * score_scale
            return ((key_sum, value_sum), rows_dq)

        zeros_init = jnp.zeros((slot_count, head_size), jnp.float32)
        block_inputs = (
            head_query.reshape(block_count, block_size, head_size),
            head_grad.reshape(block_count, block_size, head_size),
            head_logsum.reshape(block_count, block_size),
            id_blocks,
        )
        (key_sum, value_sum), query_grad = lax.scan(
            one_block, (zeros_init, zeros_init), block_inputs
        )
        return (
            query_grad.reshape(slot_count, head_size),
            key_sum.astype(jnp.bfloat16),
            value_sum.astype(jnp.bfloat16),
        )

    return lax.map(one_head, (query_heads, key_heads, value_heads, grad_heads, logsum))


def forward_pass(inputs, full_output):
    (
        layer_input,
        token_image,
        ln1_gain,
        ln1_bias,
        w_qkv,
        qv_bias,
        w_out,
        out_bias,
        ln2_gain,
        ln2_bias,
        w_fc1,
        fc1_bias,
        w_fc2,
        fc2_bias,
    ) = inputs
    head_count = w_qkv.shape[2] // HEAD_DIM
    score_scale = HEAD_DIM ** (-0.5)
    attn_params = (
        lax.all_gather(ln1_gain, "dp", axis=0, tiled=True),
        lax.all_gather(ln1_bias, "dp", axis=0, tiled=True),
        lax.all_gather(w_qkv, "dp", axis=1, tiled=True),
        lax.all_gather(w_out, "dp", axis=1, tiled=True),
        lax.all_gather(out_bias, "dp", axis=0, tiled=True),
    )
    mlp_params = (
        lax.all_gather(ln2_gain, "dp", axis=0, tiled=True),
        lax.all_gather(ln2_bias, "dp", axis=0, tiled=True),
        lax.all_gather(w_fc1, "dp", axis=0, tiled=True),
        lax.all_gather(w_fc2, "dp", axis=1, tiled=True),
        lax.all_gather(fc2_bias, "dp", axis=0, tiled=True),
    )
    input_rows = layer_input.astype(jnp.float32)
    normed = norm_rows(
        input_rows, attn_params[0].astype(jnp.float32), attn_params[1].astype(jnp.float32)
    )
    first_in = lax.all_gather(normed.astype(jnp.bfloat16), "tensor", axis=0, tiled=True)
    projected = jnp.einsum(
        "sd,cde->cse", first_in, attn_params[2], preferred_element_type=jnp.float32
    )
    bias_rows = qv_bias.astype(jnp.float32)
    query_heads = split_heads((projected[0] + bias_rows[0]).astype(jnp.bfloat16), head_count)
    key_heads = split_heads(projected[1].astype(jnp.bfloat16), head_count)
    value_heads = split_heads((projected[2] + bias_rows[1]).astype(jnp.bfloat16), head_count)
    mixed, logsum = heads_forward(query_heads, key_heads, value_heads, token_image, score_scale)
    attn_out = join_heads(mixed)
    resid = (
        input_rows
        + lax.psum_scatter(
            jnp.dot(attn_out, attn_params[3], preferred_element_type=jnp.float32),
            "tensor",
            scatter_dimension=0,
            tiled=True,
        )
        + attn_params[4].astype(jnp.float32)
    )
    normed_two = norm_rows(
        resid, mlp_params[0].astype(jnp.float32), mlp_params[1].astype(jnp.float32)
    )
    second_in = lax.all_gather(normed_two.astype(jnp.bfloat16), "tensor", axis=0, tiled=True)
    hidden = jnp.dot(
        second_in, mlp_params[2], preferred_element_type=jnp.float32
    ) + fc1_bias.astype(jnp.float32)
    active = gelu_tanh(hidden).astype(jnp.bfloat16)
    layer_output = None
    if full_output:
        summed = lax.psum_scatter(
            jnp.dot(active, mlp_params[3], preferred_element_type=jnp.float32).astype(jnp.bfloat16),
            "tensor",
            scatter_dimension=0,
            tiled=True,
        ).astype(jnp.float32)
        layer_output = (resid + summed + mlp_params[4].astype(jnp.float32)).astype(jnp.bfloat16)
    return (
        attn_params,
        mlp_params,
        input_rows,
        first_in,
        query_heads,
        key_heads,
        value_heads,
        logsum,
        attn_out,
        resid,
        second_in,
        hidden,
        active,
        layer_output,
    )


def shards(
    layer_input,
    token_image,
    cotangent,
    ln1_gain,
    ln1_bias,
    w_qkv,
    qv_bias,
    w_out,
    out_bias,
    ln2_gain,
    ln2_bias,
    w_fc1,
    fc1_bias,
    w_fc2,
    fc2_bias,
):
    inputs = (
        layer_input,
        token_image,
        ln1_gain,
        ln1_bias,
        w_qkv,
        qv_bias,
        w_out,
        out_bias,
        ln2_gain,
        ln2_bias,
        w_fc1,
        fc1_bias,
        w_fc2,
        fc2_bias,
    )
    first_pass = forward_pass(inputs, True)
    layer_output = first_pass[13]
    fenced = lax.optimization_barrier((layer_output, inputs))[1]
    saved = forward_pass(fenced, False)
    (
        attn_params,
        mlp_params,
        input_rows,
        first_in,
        query_heads,
        key_heads,
        value_heads,
        logsum,
        attn_out,
        resid,
        second_in,
        hidden,
        active,
        unused_output,
    ) = saved
    score_scale = HEAD_DIM ** (-0.5)
    row_count = layer_input.shape[0]
    tensor_at = lax.axis_index("tensor")
    image_rows = lax.dynamic_slice_in_dim(token_image, tensor_at * row_count, row_count)
    valid_mask = (image_rows < IMAGES).astype(jnp.float32)
    grad_rows = cotangent.astype(jnp.float32) * valid_mask[:, None]
    grad_low = grad_rows.astype(jnp.bfloat16)
    grad_all = lax.all_gather(grad_low, "tensor", axis=0, tiled=True)
    grad_active = contract_cols(grad_all, mlp_params[3])
    grad_hidden = jax.vjp(gelu_tanh, hidden)[1](grad_active)[0].astype(jnp.bfloat16)
    fc2_grad = contract_rows(active, grad_all)
    fc1_grad = contract_rows(second_in, grad_hidden)
    grad_normed_two = lax.psum_scatter(
        contract_cols(grad_hidden, mlp_params[2]), "tensor", scatter_dimension=0, tiled=True
    )
    norm_two_back = jax.vjp(
        norm_rows, resid, mlp_params[0].astype(jnp.float32), mlp_params[1].astype(jnp.float32)
    )[1]
    resid_part, ln2_gain_sum, ln2_bias_sum = norm_two_back(grad_normed_two)
    grad_resid = grad_rows + resid_part
    resid_low = grad_resid.astype(jnp.bfloat16)
    resid_all = lax.all_gather(resid_low, "tensor", axis=0, tiled=True)
    out_grad = contract_rows(attn_out, resid_all)
    grad_attn = contract_cols(resid_all, attn_params[3]).astype(jnp.bfloat16)
    head_count = query_heads.shape[0]
    grad_query, grad_keys, grad_values = heads_backward(
        query_heads,
        key_heads,
        value_heads,
        split_heads(grad_attn, head_count),
        logsum,
        token_image,
        score_scale,
    )
    grad_qkv = jnp.stack([join_heads(grad_query), join_heads(grad_keys), join_heads(grad_values)])
    qkv_grad = jnp.einsum("sd,cse->cde", first_in, grad_qkv, preferred_element_type=jnp.float32)
    grad_normed = lax.psum_scatter(
        jnp.einsum("cse,cde->sd", grad_qkv, attn_params[2], preferred_element_type=jnp.float32),
        "tensor",
        scatter_dimension=0,
        tiled=True,
    )
    norm_one_back = jax.vjp(
        norm_rows,
        input_rows,
        attn_params[0].astype(jnp.float32),
        attn_params[1].astype(jnp.float32),
    )[1]
    input_part, ln1_gain_sum, ln1_bias_sum = norm_one_back(grad_normed)
    input_grad = grad_resid + input_part
    qkv_piece, out_piece, fc1_piece, fc2_piece = (
        lax.psum_scatter(qkv_grad, "dp", scatter_dimension=1, tiled=True),
        lax.psum_scatter(out_grad, "dp", scatter_dimension=1, tiled=True),
        lax.psum_scatter(fc1_grad, "dp", scatter_dimension=0, tiled=True),
        lax.psum_scatter(fc2_grad, "dp", scatter_dimension=1, tiled=True),
    )
    full_width = layer_input.shape[1]
    head_width = qv_bias.shape[1]
    ff_width = fc1_bias.shape[0]
    row_sums = jnp.stack(
        [
            ln1_gain_sum,
            ln1_bias_sum,
            jnp.sum(resid_low.astype(jnp.float32), axis=0),
            ln2_gain_sum,
            ln2_bias_sum,
            jnp.sum(grad_rows, axis=0),
        ]
    )
    qv_sums = jnp.stack(
        [
            jnp.sum(grad_qkv[0].astype(jnp.float32), axis=0),
            jnp.sum(grad_qkv[2].astype(jnp.float32), axis=0),
        ]
    )
    qv_wide = lax.dynamic_update_slice_in_dim(
        jnp.zeros((2, full_width), jnp.float32), qv_sums, tensor_at * head_width, 1
    )
    fc1_sums = jnp.sum(grad_hidden.astype(jnp.float32), axis=0)
    fc1_wide = lax.dynamic_update_slice_in_dim(
        jnp.zeros((ff_width * lax.axis_size("tensor"),), jnp.float32),
        fc1_sums,
        tensor_at * ff_width,
        0,
    )
    row_total, qv_total, fc1_total = lax.psum((row_sums, qv_wide, fc1_wide), ("dp", "tensor"))
    dp_width = ln1_gain.shape[0]
    row_piece = lax.dynamic_slice_in_dim(row_total, lax.axis_index("dp") * dp_width, dp_width, 1)
    qv_piece = lax.dynamic_slice_in_dim(qv_total, tensor_at * head_width, head_width, 1)
    fc1_bias_piece = lax.dynamic_slice_in_dim(fc1_total, tensor_at * ff_width, ff_width, 0)
    return (
        layer_output,
        input_grad,
        row_piece[0],
        row_piece[1],
        qkv_piece,
        qv_piece,
        out_piece,
        row_piece[2],
        row_piece[3],
        row_piece[4],
        fc1_piece,
        fc1_bias_piece,
        fc2_piece,
        row_piece[5],
    )


LOG2E = 1.4426950408889634
VMEM_BYTES = 60 * 1024 * 1024


def head_window(head, base, width):
    start = base + head * HEAD_DIM
    first = start // 128 * 128
    last = min(-(-(start + HEAD_DIM) // 128) * 128, width)
    return start - first, first, last


def only_head(values, lane, offset):
    inside = (lane >= offset) & (lane < offset + HEAD_DIM)
    return jnp.where(inside, values, 0)


def with_lanes(values, lane, offset, first_column, second_column):
    one, two = (0, 1) if offset >= 2 else (126, 127)
    values = jnp.where(lane == one, first_column, values)
    return jnp.where(lane == two, second_column, values)


def lane_index(rows, first, last):
    return lax.broadcasted_iota(jnp.int32, (rows, last - first), 1)


def row_columns(kind):
    image = kind == 0
    padding = (kind == 1) | (kind == 2)
    low = jnp.bfloat16
    image_query = jnp.where(image, 1.0, 0.0).astype(low)
    other_query = jnp.where(image, 0.0, 1.0).astype(low)
    image_key = jnp.where(image, 0.0, -1e30).astype(low)
    padding_key = jnp.where(padding, 0.0, -1e30).astype(low)
    return image_query, other_query, image_key, padding_key


def dot_last(left, right):
    return lax.dot_general(
        left, right, (((1,), (1,)), ((), ())), preferred_element_type=jnp.float32
    )


def dot_first(left, right):
    return lax.dot_general(
        left, right, (((0,), (0,)), ((), ())), preferred_element_type=jnp.float32
    )


def heads_forward_kernel(places, heads, waits, spot, kind_ref, x_any, bias_ref, *refs):
    count = sum(len(parts) for parts in places)
    pieces = refs[:count]
    qkv_any, probs_any, *mixed_any = refs[count + waits : count + waits + 4]
    x_ref, qkv_ref, probs_ref, keys_ref, values_ref, total_ref, mixed_ref = refs[-12:-5]
    in_sems, out_sems, probs_sems, weights, sems = refs[-5:]
    scale = HEAD_DIM ** (-0.5) * LOG2E
    rows = x_ref.shape[0]
    part = heads * HEAD_DIM
    inner = qkv_ref.shape[2]
    width = keys_ref.shape[1]
    base = width - part
    groups = len(places)
    slots = probs_ref.shape[0]
    copies = weight_copies(places, pieces, weights, sems, spot[0])
    x_copy = pltpu.make_async_copy(x_any, x_ref, in_sems.at[0])
    begin([x_copy] + copies[0])
    arrive([x_copy] + copies[0])
    image_query, other_query, image_key, padding_key = row_columns(kind_ref[...])
    blank = jnp.zeros((rows, base), jnp.bfloat16)
    sent, writes = [], []
    for group in range(groups):
        if group + 1 < groups:
            begin(copies[group + 1])
        if group:
            arrive(copies[group])
        projected = jnp.dot(
            x_ref[...], strips(weights, group)[:, :inner], preferred_element_type=jnp.float32
        )
        qkv_ref[group] = (projected + bias_ref[group]).astype(jnp.bfloat16)
        copy = pltpu.make_async_copy(qkv_ref.at[group], qkv_any.at[group], out_sems.at[group])
        copy.start()
        sent.append(copy)
        keys_ref[:, :part] = qkv_ref[group, :, part : 2 * part]
        keys_ref[:, part:] = blank
        values_ref[:, :base] = blank
        values_ref[:, base:] = qkv_ref[group, :, 2 * part : 3 * part]
        total_ref[...] = jnp.zeros_like(total_ref)
        for head in range(heads):
            offset, first, last = head_window(head, 0, width)
            lane = lane_index(rows, first, last)
            keys = with_lanes(
                only_head(keys_ref[:, first:last], lane, offset),
                lane,
                offset,
                image_key,
                padding_key,
            )
            query = with_lanes(
                only_head(qkv_ref[group, :, first:last], lane, offset),
                lane,
                offset,
                image_query,
                other_query,
            )
            v_offset, v_first, v_last = head_window(head, base, width)
            values = only_head(
                values_ref[:, v_first:v_last], lane_index(rows, v_first, v_last), v_offset
            )
            at = group * heads + head
            slot = at % slots
            if at >= slots:
                writes[at - slots].wait()
            for tile in row_tiles(rows, 384):
                scores = dot_last(query[tile], keys)
                peak = jnp.max(scores, axis=1, keepdims=True)
                expo = jnp.exp2((scores - peak) * scale)
                total = jnp.sum(expo, axis=1, keepdims=True)
                probs = (expo * (1.0 / total)).astype(jnp.bfloat16)
                probs_ref[slot, tile, :] = probs
                total_ref[tile, v_first:v_last] += jnp.dot(
                    probs, values, preferred_element_type=jnp.float32
                )
            copy = pltpu.make_async_copy(
                probs_ref.at[slot], probs_any.at[group, head], probs_sems.at[slot]
            )
            copy.start()
            writes.append(copy)
        mixed_ref[group] = total_ref[...].astype(jnp.bfloat16)
        copy = pltpu.make_async_copy(
            mixed_ref.at[group], mixed_any[group], out_sems.at[groups + group]
        )
        copy.start()
        sent.append(copy)
    arrive(sent + writes[-slots:])


def heads_forward_call(spot, kind, rows_in, biases, groups, waits=()):
    rows, full = rows_in.shape
    arrays, places = flatten(groups)
    high, group_width = arrays[0].shape[-2:]
    depth = full // (2 * high)
    count = len(groups)
    part = group_width // 4
    heads = part // HEAD_DIM
    inner = -(-3 * part // 128) * 128
    outer = -(-part // 128) * 128
    slots = min(8, count * heads)
    return call(
        functools.partial(heads_forward_kernel, places, heads, len(waits)),
        "heads_forward",
        [spot, kind, rows_in, biases, *arrays],
        [smem_spec(), vmem_spec(), any_spec(), vmem_spec()] + [any_spec()] * len(arrays),
        [
            (any_spec(), (count, rows, inner), jnp.bfloat16),
            (any_spec(), (count, heads, rows, rows), jnp.bfloat16),
            (any_spec(), (rows, outer), jnp.bfloat16),
            (any_spec(), (rows, outer), jnp.bfloat16),
        ],
        [
            low_scratch(rows, full),
            low_scratch(count, rows, inner),
            low_scratch(slots, rows, rows),
            low_scratch(rows, outer),
            low_scratch(rows, outer),
            wide_scratch(rows, outer),
            low_scratch(count, rows, outer),
            copy_sems(1),
            copy_sems(2 * count),
            copy_sems(slots),
        ]
        + weight_scratch(places, depth, high, group_width),
        waits,
    )


def heads_backward_kernel(places, heads, picks, waits, spot, grad_any, qkv_any, probs_any, *refs):
    count = sum(len(parts) for parts in places)
    groups = len(places)
    mixed_any = refs[:groups]
    pieces = refs[groups : groups + count]
    first_out = groups + count + waits
    outs_any = refs[first_out : first_out + groups]
    sum_ref = refs[first_out + groups]
    grad_ref, qkv_ref, probs_ref, mixed_ref, out_ref, keys_ref, values_ref, grads_ref = refs[-16:-8]
    query_sum, key_sum, value_sum, in_sems, probs_sems, out_sems, weights, sems = refs[-8:]
    width = keys_ref.shape[1]
    first_lane = pieces[0].shape[-1] - width
    loads = weight_copies(places, pieces, weights, sems, spot[0], first_lane, width)
    grad_copy = pltpu.make_async_copy(grad_any, grad_ref, in_sems.at[2 * groups])
    slots = probs_ref.shape[0]
    seconds, reads = [], []
    for group in range(groups):
        seconds.append(
            [
                pltpu.make_async_copy(
                    qkv_any.at[picks[group]], qkv_ref.at[group], in_sems.at[2 * group]
                ),
                pltpu.make_async_copy(
                    mixed_any[group], mixed_ref.at[group], in_sems.at[2 * group + 1]
                ),
            ]
        )
        for head in range(heads):
            slot = len(reads) % slots
            reads.append(
                pltpu.make_async_copy(
                    probs_any.at[picks[group], head], probs_ref.at[slot], probs_sems.at[slot]
                )
            )
    begin([grad_copy] + loads[0])
    begin(seconds[0])
    begin(reads[:2])
    score_scale = HEAD_DIM ** (-0.5)
    rows = grad_ref.shape[0]
    part = heads * HEAD_DIM
    base = width - part
    low = jnp.bfloat16
    blank = jnp.zeros((rows, base), low)
    sent = []
    started = 2
    for group in range(groups):
        arrive(([grad_copy] if group == 0 else []) + loads[group])
        grads_ref[...] = jnp.dot(
            grad_ref[...], strips(weights, group), preferred_element_type=jnp.float32
        ).astype(low)
        arrive(seconds[group])
        if group + 1 < groups:
            begin(loads[group + 1] + seconds[group + 1])
        keys_ref[:, :part] = qkv_ref[group, :, part : 2 * part]
        keys_ref[:, part:] = blank
        values_ref[:, :base] = blank
        values_ref[:, base:] = qkv_ref[group, :, 2 * part : 3 * part]
        query_sum[...] = jnp.zeros_like(query_sum)
        key_sum[...] = jnp.zeros_like(key_sum)
        value_sum[...] = jnp.zeros_like(value_sum)
        weighted = grads_ref[...].astype(jnp.float32) * mixed_ref[group].astype(jnp.float32)
        for head in range(heads):
            at = group * heads + head
            offset, first, last = head_window(head, 0, width)
            lane = lane_index(rows, first, last)
            query = only_head(qkv_ref[group, :, first:last], lane, offset)
            keys = only_head(keys_ref[:, first:last], lane, offset)
            v_offset, v_first, v_last = head_window(head, base, width)
            v_lane = lane_index(rows, v_first, v_last)
            values = values_ref[:, v_first:v_last]
            grad = only_head(grads_ref[:, v_first:v_last], v_lane, v_offset)
            centre = jnp.sum(
                only_head(weighted[:, v_first:v_last], v_lane, v_offset), axis=1, keepdims=True
            )
            while started < len(reads) and started - at < slots:
                reads[started].start()
                started += 1
            reads[at].wait()
            probs = probs_ref[at % slots]
            grad_probs = dot_last(grad, values)
            grad_scores = (probs.astype(jnp.float32) * (grad_probs - centre)).astype(low)
            value_sum[:, v_first:v_last] += dot_first(probs, grad)
            key_sum[:, first:last] += dot_first(grad_scores, query)
            query_sum[:, first:last] += jnp.dot(
                grad_scores, keys, preferred_element_type=jnp.float32
            )
        out_ref[group, :, :part] = (query_sum[...] * score_scale).astype(low)[:, :part]
        out_ref[group, :, part : 2 * part] = (key_sum[...] * score_scale).astype(low)[:, :part]
        out_ref[group, :, 2 * part : 3 * part] = value_sum[...].astype(low)[:, base:]
        tail = out_ref.shape[2] - 3 * part
        if tail:
            out_ref[group, :, 3 * part :] = jnp.zeros((rows, tail), low)
        copy = pltpu.make_async_copy(out_ref.at[group], outs_any[group], out_sems.at[group])
        copy.start()
        sent.append(copy)
        sum_ref[group] = jnp.sum(out_ref[group].astype(jnp.float32), axis=0, keepdims=True)
    arrive(sent)


def heads_backward_call(spot, grad_rows, qkv, probs, mixed, groups, picks, waits=()):
    rows, full = grad_rows.shape
    arrays, places = flatten(groups)
    high, group_width = arrays[0].shape[-2:]
    depth = full // (2 * high)
    part = group_width // 4
    heads = part // HEAD_DIM
    inner = qkv.shape[2]
    outer = mixed[0].shape[1]
    count = len(groups)
    slots = min(count * heads, 6)
    return call(
        functools.partial(heads_backward_kernel, places, heads, picks, len(waits)),
        "heads_backward",
        [spot, grad_rows, qkv, probs, *mixed, *arrays],
        [smem_spec()] + [any_spec()] * (3 + count + len(arrays)),
        [(any_spec(), (rows, inner), jnp.bfloat16)] * count
        + [(vmem_spec(), (count, 1, inner), jnp.float32)],
        [
            low_scratch(rows, full),
            low_scratch(count, rows, inner),
            low_scratch(slots, rows, rows),
            low_scratch(count, rows, outer),
            low_scratch(count, rows, inner),
            low_scratch(rows, outer),
            low_scratch(rows, outer),
            low_scratch(rows, outer),
            wide_scratch(rows, outer),
            wide_scratch(rows, outer),
            wide_scratch(rows, outer),
            copy_sems(2 * count + 1),
            copy_sems(slots),
            copy_sems(count),
        ]
        + weight_scratch(places, depth, high, outer),
        waits,
    )


def any_spec():
    return pl.BlockSpec(memory_space=pl.ANY)


def smem_spec():
    return pl.BlockSpec(memory_space=pltpu.SMEM)


def vmem_spec():
    return pl.BlockSpec(memory_space=pltpu.VMEM)


def limits():
    return pltpu.CompilerParams(vmem_limit_bytes=VMEM_BYTES)


def low_scratch(*shape):
    return pltpu.VMEM(shape, jnp.bfloat16)


def wide_scratch(*shape):
    return pltpu.VMEM(shape, jnp.float32)


def copy_sems(*shape):
    return pltpu.SemaphoreType.DMA(shape)


def begin(copies):
    for copy in copies:
        copy.start()


def arrive(copies):
    for copy in copies:
        copy.wait()


def call(kernel, name, operands, specs, outs, scratch, waits=()):
    no_cost = pl.CostEstimate(flops=1024, bytes_accessed=1024, transcendentals=0)
    out_specs = [spec for spec, _, _ in outs]
    return pl.pallas_call(
        kernel,
        in_specs=list(specs) + [any_spec()] * len(waits),
        out_specs=out_specs,
        out_shape=[jax.ShapeDtypeStruct(shape, kind) for _, shape, kind in outs],
        scratch_shapes=scratch,
        compiler_params=limits(),
        cost_estimate=no_cost,
        name=name,
    )(*operands, *waits)


def flatten(groups):
    arrays = [part[0] for group in groups for part in group]
    places = [[part[1:] for part in group] for group in groups]
    return arrays, places


def weight_copies(places, refs, weights, sems, x_at, first=0, width=None):
    copies, at = [], 0
    for group, parts in enumerate(places):
        mine = []
        for part, (start, x_off, *pick) in enumerate(parts):
            source = refs[at].at[:, pick[0]] if pick else refs[at]
            at += 1
            if width is not None:
                source = source.at[:, :, pl.ds(first, width)]
            target = weights.at[group, pl.ds(start, source.shape[0]), x_at ^ x_off]
            mine.append(pltpu.make_async_copy(source, target, sems.at[group, part]))
        copies.append(mine)
    return copies


def weight_scratch(places, depth, high, width):
    count = len(places)
    return [
        pltpu.VMEM((count, depth, 2, high, width), jnp.bfloat16),
        copy_sems(count, max(len(parts) for parts in places)),
    ]


def strips(weights, at):
    _, depth, _, high, width = weights.shape
    return weights[at].reshape(depth * 2 * high, width)


def row_tiles(rows, size):
    return [slice(start, min(start + size, rows)) for start in range(0, rows, size)]


def out_copies(pairs, sems):
    return [
        pltpu.make_async_copy(source, target, sems.at[i])
        for i, (source, target) in enumerate(pairs)
    ]


def up_kernel(places, waits, spot, x_any, bias_ref, *refs):
    count = sum(len(parts) for parts in places)
    pieces = refs[:count]
    active_any, slope_any = refs[count + waits : count + waits + 2]
    x_ref, active_ref, slope_ref, x_sem, out_sems, weights, sems = refs[-7:]
    rows = x_ref.shape[0]
    groups = len(places)
    copies = weight_copies(places, pieces, weights, sems, spot[0])
    x_copy = pltpu.make_async_copy(x_any, x_ref, x_sem.at[0])
    begin([x_copy] + copies[0])
    arrive([x_copy] + copies[0])
    sent = []
    for group in range(groups):
        if group + 1 < groups:
            begin(copies[group + 1])
        if group:
            arrive(copies[group])
        whole = strips(weights, group)
        for tile in row_tiles(rows, 128):
            hidden = jnp.dot(x_ref[tile, :], whole, preferred_element_type=jnp.float32)
            hidden = hidden + bias_ref[group]
            square = hidden * hidden
            inner = jnp.tanh(hidden * (gelu_scale + gelu_scale * 0.044715 * square))
            gate = 0.5 + 0.5 * inner
            active_ref[group, tile, :] = (hidden * gate).astype(jnp.bfloat16)
            grow = hidden * (gelu_scale + 3.0 * 0.044715 * gelu_scale * square)
            slope = gate + grow * (0.5 - 0.5 * inner * inner)
            slope_ref[group, tile, :] = slope.astype(jnp.bfloat16)
        for half, tile in enumerate(row_tiles(rows, rows // 2)):
            span = pl.ds(tile.start, rows // 2)
            for at, (source, target) in enumerate(
                ((active_ref, active_any), (slope_ref, slope_any))
            ):
                copy = pltpu.make_async_copy(
                    source.at[group, span], target.at[group, span], out_sems.at[group, half, at]
                )
                copy.start()
                sent.append(copy)
    arrive(sent)


def up_project(spot, rows_in, biases, groups, waits=()):
    rows, full = rows_in.shape
    arrays, places = flatten(groups)
    high, width = arrays[0].shape[-2:]
    depth = full // (2 * high)
    count = len(groups)
    shape = (count, rows, width)
    return call(
        functools.partial(up_kernel, places, len(waits)),
        "mlp_up",
        [spot, rows_in, biases, *arrays],
        [smem_spec(), any_spec(), vmem_spec()] + [any_spec()] * len(arrays),
        [(any_spec(), shape, jnp.bfloat16)] * 2,
        [
            low_scratch(rows, full),
            low_scratch(*shape),
            low_scratch(*shape),
            copy_sems(1),
            copy_sems(count, 2, 2),
        ]
        + weight_scratch(places, depth, high, width),
        waits,
    )


def unit_rows(values):
    centre = values - jnp.mean(values, axis=1, keepdims=True)
    spread = jnp.mean(centre * centre, axis=1, keepdims=True)
    root = lax.rsqrt(spread + layer_eps)
    return centre * root, root


def norm_rows_back(values, gain, grad):
    unit, root = unit_rows(values)
    scaled = grad * gain
    mean_one = jnp.mean(scaled, axis=1, keepdims=True)
    mean_two = jnp.mean(scaled * unit, axis=1, keepdims=True)
    part = root * (scaled - mean_one - unit * mean_two)
    return part, jnp.sum(grad * unit, axis=0, keepdims=True), jnp.sum(grad, axis=0, keepdims=True)


def mlp_back_kernel(down_places, up_places, waits, spot, x_any, one_any, two_any, resid_any, gain_ref, *refs):
    count = [sum(len(parts) for parts in places) for places in (down_places, up_places)]
    down_pieces = refs[: count[0]]
    up_pieces = refs[count[0] : count[0] + count[1]]
    at = count[0] + count[1] + waits
    one_out, two_out, low_any, sum_ref, hidden_sums = refs[at : at + 5]
    x_ref, slope_ref, hidden_ref, resid_ref, total, low_ref, in_sems, hidden_sems, out_sems = refs[
        at + 5 : at + 14
    ]
    down_weights, down_sems, up_weights, up_sems = refs[at + 14 :]
    rows = x_ref.shape[0]
    groups = len(down_places)
    half = groups // 2
    slots = down_weights.shape[0]

    def slotted(places, pieces, weights, sems):
        copies, first = [], 0
        for group, parts in enumerate(places):
            mine = pieces[first : first + len(parts)]
            first += len(parts)
            slot = group % slots
            copies += weight_copies(
                [parts],
                mine,
                weights.at[pl.ds(slot, 1)],
                sems.at[pl.ds(slot, 1)],
                spot[0],
            )
        return copies

    downs = slotted(down_places, down_pieces, down_weights, down_sems)
    ups = slotted(up_places, up_pieces, up_weights, up_sems)
    for group in range(groups):
        source = one_any.at[group] if group < half else two_any.at[group - half]
        slot = group % slots
        downs[group].append(
            pltpu.make_async_copy(source, slope_ref.at[slot], in_sems.at[2 + slot])
        )
    x_copy = pltpu.make_async_copy(x_any, x_ref, in_sems.at[0])
    late = pltpu.make_async_copy(resid_any, resid_ref, in_sems.at[1])
    begin([x_copy] + downs[0])
    arrive([x_copy] + downs[0])
    sent = []
    for group in range(groups):
        slot = group % slots
        begin(ups[group])
        whole = strips(down_weights, slot)
        column_total = jnp.zeros((1, total.shape[1]), jnp.float32)
        if group >= slots:
            sent[group - slots].wait()
        for tile in row_tiles(rows, 256):
            grad = jnp.dot(x_ref[tile, :], whole, preferred_element_type=jnp.float32)
            low = (grad * slope_ref[slot, tile, :].astype(jnp.float32)).astype(jnp.bfloat16)
            hidden_ref[slot, tile, :] = low
            column_total += jnp.sum(low.astype(jnp.float32), axis=0, keepdims=True)
        hidden_sums[group] = column_total
        target = one_out.at[group] if group < half else two_out.at[group - half]
        copy = pltpu.make_async_copy(hidden_ref.at[slot], target, hidden_sems.at[slot])
        copy.start()
        sent.append(copy)
        arrive(ups[group])
        if group + 1 < groups:
            begin(downs[group + 1])
        else:
            begin([late])
        whole = strips(up_weights, slot)
        if group == 0:
            total[...] = dot_last(hidden_ref[slot], whole)
        elif group + 1 < groups:
            total[...] += dot_last(hidden_ref[slot], whole)
        else:
            products = [
                (tile, dot_last(hidden_ref[slot, tile, :], whole)) for tile in row_tiles(rows, 256)
            ]
        if group + 1 < groups:
            arrive(downs[group + 1])
    arrive([late])
    sums = [jnp.zeros((1, total.shape[1]), jnp.float32) for _ in range(3)]
    low_sent = []
    for tile, product in products:
        for small in range(tile.start, tile.stop, 128):
            span = slice(small, small + 128)
            inside = slice(small - tile.start, small - tile.start + 128)
            part, gain_sum, shift_sum = norm_rows_back(
                resid_ref[span, :].astype(jnp.float32),
                gain_ref[...],
                total[span, :] + product[inside],
            )
            low = (x_ref[span, :].astype(jnp.float32) + part).astype(jnp.bfloat16)
            low_ref[span, :] = low
            sums[0] += gain_sum
            sums[1] += shift_sum
            sums[2] += jnp.sum(low.astype(jnp.float32), axis=0, keepdims=True)
        long = pl.ds(tile.start, tile.stop - tile.start)
        copy = pltpu.make_async_copy(
            low_ref.at[long], low_any.at[long], out_sems.at[len(low_sent)]
        )
        copy.start()
        low_sent.append(copy)
    sum_ref[...] = jnp.concatenate(sums + [jnp.zeros((5, total.shape[1]), jnp.float32)])
    arrive(sent[-slots:] + low_sent)


def mlp_back(spot, grad_low, first_slope, second_slope, resid, gain, downs, ups, waits=()):
    rows, full = grad_low.shape
    down_arrays, down_places = flatten(downs)
    up_arrays, up_places = flatten(ups)
    high, width = up_arrays[0].shape[-2:]
    depth = full // (2 * high)
    count = len(downs)
    slots = 2
    shape = (count // 2, rows, width)

    def slot_scratch(places):
        return [
            pltpu.VMEM((slots, depth, 2, high, width), jnp.bfloat16),
            copy_sems(slots, max(len(parts) for parts in places)),
        ]

    return call(
        functools.partial(mlp_back_kernel, down_places, up_places, len(waits)),
        "mlp_back",
        [spot, grad_low, first_slope, second_slope, resid, gain, *down_arrays, *up_arrays],
        [smem_spec()]
        + [any_spec()] * 4
        + [vmem_spec()]
        + [any_spec()] * (len(down_arrays) + len(up_arrays)),
        [
            (any_spec(), shape, jnp.bfloat16),
            (any_spec(), shape, jnp.bfloat16),
            (any_spec(), (rows, full), jnp.bfloat16),
            (vmem_spec(), (8, full), jnp.float32),
            (vmem_spec(), (count, 1, width), jnp.float32),
        ],
        [
            low_scratch(rows, full),
            low_scratch(slots, rows, width),
            low_scratch(slots, rows, width),
            pltpu.VMEM(resid.shape, resid.dtype),
            wide_scratch(rows, full),
            low_scratch(rows, full),
            copy_sems(2 + slots),
            copy_sems(slots),
            copy_sems(-(-rows // 256)),
        ]
        + slot_scratch(down_places)
        + slot_scratch(up_places),
        waits,
    )


def back_kernel(places, sources, waits, spot, *refs):
    count = sum(len(parts) for parts in places)
    grads_any = refs[:sources]
    base_any, grad_any, gain_ref = refs[sources : sources + 3]
    pieces = refs[sources + 3 : sources + 3 + count]
    first_out = sources + 3 + count + waits
    out_any, sum_ref = refs[first_out : first_out + 2]
    grads_ref, base_ref, grad_ref, total, in_sems, out_sems, weights, sems = refs[first_out + 2 :]
    rows = total.shape[0]
    groups = len(places)
    width = weights.shape[-1]
    copies = weight_copies(places, pieces, weights, sems, spot[0], 0, width)
    at = 0
    for source in grads_any:
        parts = [source] if len(source.shape) == 2 else [source.at[i] for i in range(source.shape[0])]
        for part in parts:
            copies[at].append(pltpu.make_async_copy(part, grads_ref.at[at], in_sems.at[at]))
            at += 1
    late = [
        pltpu.make_async_copy(base_any, base_ref, in_sems.at[groups]),
        pltpu.make_async_copy(grad_any, grad_ref, in_sems.at[groups + 1]),
    ]
    begin(copies[0])
    for group in range(groups):
        arrive(copies[group])
        begin(copies[group + 1] if group + 1 < groups else late)
        whole = strips(weights, group)
        if group == 0:
            total[...] = dot_last(grads_ref[group], whole)
        elif group + 1 < groups:
            total[...] += dot_last(grads_ref[group], whole)
        else:
            products = [
                (tile, dot_last(grads_ref[group, tile, :], whole)) for tile in row_tiles(rows, 256)
            ]
    arrive(late)
    sums = [jnp.zeros((1, total.shape[1]), jnp.float32) for _ in range(2)]
    sent = []
    for tile, product in products:
        for small in range(tile.start, tile.stop, 128):
            span = slice(small, small + 128)
            inside = slice(small - tile.start, small - tile.start + 128)
            part, gain_sum, shift_sum = norm_rows_back(
                base_ref[span, :].astype(jnp.float32),
                gain_ref[...],
                total[span, :] + product[inside],
            )
            grad = grad_ref[span, :].astype(jnp.float32) + part
            total[span, :] = grad
            sums[0] += gain_sum
            sums[1] += shift_sum
        long = pl.ds(tile.start, tile.stop - tile.start)
        copy = pltpu.make_async_copy(total.at[long], out_any.at[long], out_sems.at[len(sent)])
        copy.start()
        sent.append(copy)
    sum_ref[...] = jnp.concatenate(sums + [jnp.zeros((6, total.shape[1]), jnp.float32)])
    arrive(sent)


def norm_back(spot, grads, base, grad, gain, groups, waits=()):
    rows, full = base.shape
    arrays, places = flatten(groups)
    high, _ = arrays[0].shape[-2:]
    width = grads[0].shape[-1]
    depth = full // (2 * high)
    outs = [
        (any_spec(), (rows, full), jnp.float32),
        (vmem_spec(), (8, full), jnp.float32),
    ]
    return call(
        functools.partial(back_kernel, places, len(grads), len(waits)),
        "norm_one_back",
        [spot, *grads, base, grad, gain, *arrays],
        [smem_spec()] + [any_spec()] * (len(grads) + 2) + [vmem_spec()] + [any_spec()] * len(arrays),
        outs,
        [
            low_scratch(len(groups), rows, width),
            pltpu.VMEM(base.shape, base.dtype),
            pltpu.VMEM(grad.shape, grad.dtype),
            wide_scratch(rows, full),
            copy_sems(len(groups) + 2),
            copy_sems(-(-rows // 256)),
        ]
        + weight_scratch(places, depth, high, width),
        waits,
    )


def down_kernel(places, waits, spot, later_any, early_any, resid_any, shift_ref, *refs):
    count = sum(len(parts) for parts in places)
    pieces = refs[:count]
    out_any = refs[count + waits]
    active_ref, resid_ref, total, out_ref, in_sems, out_sems, weights, sems = refs[-8:]
    rows = total.shape[0]
    groups = len(places)
    copies = weight_copies(places, pieces, weights, sems, spot[0])
    half = groups // 2
    for group in range(groups):
        source = later_any.at[group] if group < half else early_any.at[group - half]
        copies[group].append(
            pltpu.make_async_copy(source, active_ref.at[group], in_sems.at[group])
        )
    late = [pltpu.make_async_copy(resid_any, resid_ref, in_sems.at[groups])]
    begin(copies[0])
    for group in range(groups - 1):
        arrive(copies[group])
        begin(copies[group + 1])
        if group + 2 == groups:
            begin(late)
        product = dot_last(active_ref[group], strips(weights, group))
        if group == 0:
            total[...] = product
        else:
            total[...] += product
    arrive(copies[-1] + late)
    whole = strips(weights, groups - 1)
    sent = []
    for tile in row_tiles(rows, 256):
        product = dot_last(active_ref[groups - 1, tile, :], whole)
        product = product + total[tile, :] + shift_ref[...]
        product = product + resid_ref[tile, :].astype(jnp.float32)
        out_ref[tile, :] = product.astype(out_ref.dtype)
        long = pl.ds(tile.start, tile.stop - tile.start)
        copy = pltpu.make_async_copy(out_ref.at[long], out_any.at[long], out_sems.at[len(sent)])
        copy.start()
        sent.append(copy)
    arrive(sent)


def down_project(spot, first, second, resid, shift, groups, waits=()):
    rows, full = resid.shape
    arrays, places = flatten(groups)
    high, width = arrays[0].shape[-2:]
    depth = full // (2 * high)
    return call(
        functools.partial(down_kernel, places, len(waits)),
        "mlp_down",
        [spot, first, second, resid, shift, *arrays],
        [smem_spec()] + [any_spec()] * 3 + [vmem_spec()] + [any_spec()] * len(arrays),
        [(any_spec(), (rows, full), jnp.bfloat16)],
        [
            low_scratch(len(groups), rows, width),
            pltpu.VMEM(resid.shape, resid.dtype),
            wide_scratch(rows, full),
            low_scratch(rows, full),
            copy_sems(len(groups) + 1),
            copy_sems(-(-rows // 256)),
        ]
        + weight_scratch(places, depth, high, width),
        waits,
    )[0]


def out_kernel(places, waits, spot, one, two, three, four, x_any, shift_ref, gain_ref, bias_ref, *refs):
    count = sum(len(parts) for parts in places)
    pieces = refs[:count]
    resid_any, normed_any = refs[count + waits : count + waits + 2]
    mixed_ref, x_ref, resid_ref, low_ref, normed_ref, in_sems, out_sems, weights, sems = refs[-9:]
    rows = x_ref.shape[0]
    outer = weights.shape[-1]
    first = pieces[0].shape[-1] - outer
    copies = weight_copies(places, pieces, weights, sems, spot[0], first, outer)
    for group, mixed in enumerate((one, two, three, four)):
        copies[group].append(
            pltpu.make_async_copy(mixed, mixed_ref.at[group], in_sems.at[group])
        )
    late = [pltpu.make_async_copy(x_any, x_ref, in_sems.at[4])]
    for mine in copies:
        begin(mine)
    begin(late)
    for group in range(4):
        arrive(copies[group])
        if group < 3:
            product = dot_last(mixed_ref[group], strips(weights, group))
            if group == 0:
                resid_ref[...] = product
            else:
                resid_ref[...] += product
    arrive(late)
    whole = strips(weights, 3)
    products = [(tile, dot_last(mixed_ref[3, tile, :], whole)) for tile in row_tiles(rows, 256)]
    sent = []
    for tile, product in products:
        for small in range(tile.start, tile.stop, 128):
            span = slice(small, small + 128)
            inside = slice(small - tile.start, small - tile.start + 128)
            values = resid_ref[span, :] + product[inside] + x_ref[span, :].astype(jnp.float32)
            values = values + shift_ref[...]
            low_ref[span, :] = values.astype(jnp.bfloat16)
            unit, _ = unit_rows(values)
            normed_ref[span, :] = (unit * gain_ref[...] + bias_ref[...]).astype(jnp.bfloat16)
        long = pl.ds(tile.start, tile.stop - tile.start)
        for source, target in ((low_ref, resid_any), (normed_ref, normed_any)):
            copy = pltpu.make_async_copy(source.at[long], target.at[long], out_sems.at[len(sent)])
            copy.start()
            sent.append(copy)
    arrive(sent)


def out_project(spot, mixed, rows_in, shift, gain, bias, groups, waits=()):
    rows, full = rows_in.shape
    arrays, places = flatten(groups)
    high, _ = arrays[0].shape[-2:]
    outer = mixed[0].shape[1]
    depth = full // (2 * high)
    return call(
        functools.partial(out_kernel, places, len(waits)),
        "attn_out",
        [spot, *mixed, rows_in, shift, gain, bias, *arrays],
        [smem_spec()] + [any_spec()] * 5 + [vmem_spec()] * 3 + [any_spec()] * len(arrays),
        [
            (any_spec(), (rows, full), jnp.bfloat16),
            (any_spec(), (rows, full), jnp.bfloat16),
        ],
        [
            low_scratch(4, rows, outer),
            low_scratch(rows, full),
            wide_scratch(rows, full),
            low_scratch(rows, full),
            low_scratch(rows, full),
            copy_sems(5),
            copy_sems(2 * -(-rows // 256)),
        ]
        + weight_scratch(places, depth, high, outer),
        waits,
    )


def grad_kernel(sides, extra, waits, spot, *refs):
    inputs = 4 + (4 if extra else 0)
    sources = refs[:inputs]
    outs_at = inputs + waits
    count = sum(3 + side // 2 for side in sides)
    outs = list(refs[outs_at : outs_at + count])
    holds = refs[outs_at + count : outs_at + count + inputs]
    stage, in_sems, out_sems = refs[-3:]
    x_at = spot[0]
    def load(source, hold, at):
        return pltpu.make_async_copy(source, hold, in_sems.at[at])

    count = len(sides)
    first_x = load(sources[0], holds[0], 0)
    second_x = load(sources[2], holds[2], 1)
    firsts = [load(sources[1].at[i], holds[1].at[i], 2 + 2 * i) for i in range(count)]
    seconds = [load(sources[3].at[i], holds[3].at[i], 3 + 2 * i) for i in range(count)]
    extras = [load(sources[j], holds[j], 2 * count + j - 2) for j in range(4, inputs)]
    _, depth, _, high, width = stage.shape
    half = depth // 2
    begin([first_x, firsts[0]])
    arrive([first_x, firsts[0]])
    begin([second_x, seconds[0]])
    begin(extras)
    sent = []
    starts = []
    for side in sides:
        starts.append(sum(3 + before // 2 for before in sides[: len(starts)]))
    for i, side in enumerate(sides):
        if i:
            arrive([firsts[i], seconds[i]])
        for part in range(2):
            cut = slice(part * half * 2 * high, (part + 1) * half * 2 * high)
            span = pl.ds(part * half, half)
            product = dot_first(holds[0][:, cut], holds[1][i])
            if i == 0 and part == 0:
                arrive([second_x, seconds[0]])
                for later in range(1, count):
                    begin([firsts[later], seconds[later]])
            product += dot_first(holds[2][:, cut], holds[3][i])
            if extra:
                if i == 0 and part == 0:
                    arrive(extras)
                other = dot_first(holds[4][:, cut], holds[5][...])
                other += dot_first(holds[6][:, cut], holds[7][...])
                both = product.shape[1] + other.shape[1] - width
                left = product.shape[1] - both
                product = jnp.concatenate(
                    [product[:, :left], product[:, left:] + other[:, :both], other[:, both:]],
                    axis=1,
                )
            stage[i, part * half : (part + 1) * half] = product.astype(jnp.bfloat16).reshape(
                half, 2, high, width
            )
            if side == 0:
                near_out = outs[starts[i]].at[span]
                far_out = outs[starts[i] + 1 + part]
            else:
                near_out = outs[starts[i] + part]
                far_out = outs[starts[i] + 2 + part]
            for source, target in (
                (stage.at[i, span, x_at], near_out),
                (stage.at[i, span, 1 - x_at], far_out),
            ):
                copy = pltpu.make_async_copy(source, target, out_sems.at[len(sent)])
                copy.start()
                sent.append(copy)
    arrive(sent)


def weight_grad(spot, left, right, depth, sides=(0, 2), extra=(), waits=()):
    rows, full = left[0].shape
    high = full // (2 * depth)
    half = depth // 2
    count = len(sides)
    rights = [values.reshape(count, rows, -1) for values in right]
    width = full if extra else rights[0].shape[2]
    operands = [left[0], rights[0], left[1], rights[1], *extra]
    shapes = []
    for side in sides:
        shapes += [depth, half, half] if side == 0 else [half] * 4
    outs = [(any_spec(), (size, high, width), jnp.bfloat16) for size in shapes]
    return call(
        functools.partial(grad_kernel, sides, bool(extra), len(waits)),
        "weight_grad",
        [spot, *operands],
        [smem_spec()] + [any_spec()] * len(operands),
        outs,
        [pltpu.VMEM(values.shape, values.dtype) for values in operands]
        + [
            low_scratch(count, depth, 2, high, width),
            copy_sems(2 + 2 * count + 4),
            copy_sems(4 * count),
        ],
        waits,
    )


def pair_kernel(one_ref, two_ref, three_ref, four_ref, first_out, second_out):
    wide = jnp.float32
    low = first_out.dtype
    first_out[...] = (one_ref[...].astype(wide) + two_ref[...].astype(wide)).astype(low)
    second_out[...] = (three_ref[...].astype(wide) + four_ref[...].astype(wide)).astype(low)


def add_pairs(one, two, three, four):
    shape = jax.ShapeDtypeStruct(one.shape, one.dtype)
    return pl.pallas_call(
        pair_kernel,
        in_specs=[vmem_spec()] * 4,
        out_specs=[vmem_spec()] * 2,
        out_shape=[shape, shape],
        compiler_params=limits(),
        name="add_pairs",
    )(one, two, three, four)


def square_kernel(own, one_lo, one_hi, two_lo, two_hi, out):
    wide = jnp.float32
    half = one_lo.shape[0]
    for part, (one, two) in enumerate(((one_lo, two_lo), (one_hi, two_hi))):
        span = slice(part * half, (part + 1) * half)
        total = own[span].astype(wide) + one[...].astype(wide) + two[...].astype(wide)
        out[span] = total.astype(out.dtype)


def add_square(own, *parts):
    return pl.pallas_call(
        square_kernel,
        in_specs=[vmem_spec()] * 5,
        out_specs=vmem_spec(),
        out_shape=jax.ShapeDtypeStruct(own.shape, own.dtype),
        compiler_params=limits(),
        name="add_square",
    )(own, *parts)


def halves_kernel(first_ref, second_ref, first_out, second_out):
    first_out[...] = first_ref[...]
    second_out[...] = second_ref[...]


def take_halves(first, second):
    half = (first.shape[0] // 2,) + first.shape[1:]
    front = pl.BlockSpec(half, lambda i: (0, 0, 0))
    back = pl.BlockSpec(half, lambda i: (1, 0, 0))
    shape = jax.ShapeDtypeStruct(half, first.dtype)
    return pl.pallas_call(
        halves_kernel,
        grid=(1,),
        in_specs=[front, back],
        out_specs=[front, front],
        out_shape=[shape, shape],
        compiler_params=limits(),
        name="take_halves",
    )(first, second)


PATCHES = 729
AXES = ("dp", "tensor")


def nothing(*refs):
    del refs


def fence(released, waited=()):
    anywhere = pl.BlockSpec(memory_space=pl.ANY)
    released, waited = list(released), list(waited)
    return pl.pallas_call(
        nothing,
        in_specs=[anywhere] * (len(released) + len(waited)),
        out_specs=[anywhere] * len(released),
        out_shape=[jax.ShapeDtypeStruct(values.shape, values.dtype) for values in released],
        input_output_aliases={i: i for i in range(len(released))},
        name="fence",
    )(*released, *waited)


class Grid:
    def __init__(self, depth):
        self.depth = depth
        dp_at = lax.axis_index("dp")
        self.y = lax.axis_index("tensor")
        self.c = dp_at % 2
        self.x = dp_at // 2 % 2
        self.z = dp_at // 4

    def move(self, values, where):
        pairs = []
        for z in range(self.depth):
            for x in range(2):
                for c in range(2):
                    for y in range(2):
                        to_z, to_x, to_c, to_y = where(z, x, c, y)
                        pairs.append(
                            (
                                ((z * 2 + x) * 2 + c) * 2 + y,
                                ((to_z * 2 + to_x) * 2 + to_c) * 2 + to_y,
                            )
                        )
        return lax.ppermute(values, AXES, pairs)

    def over_x(self, values):
        return self.move(values, lambda z, x, c, y: (z, 1 - x, c, y))

    def over_y(self, values):
        return self.move(values, lambda z, x, c, y: (z, x, c, 1 - y))

    def over_both(self, values):
        return self.move(values, lambda z, x, c, y: (z, 1 - x, c, 1 - y))

    def over_core(self, values):
        return self.move(values, lambda z, x, c, y: (z, x, 1 - c, y))

    def along_z(self, values, hops):
        return self.move(values, lambda z, x, c, y: ((z + hops) % self.depth, x, c, y))

    def across_z(self, values, bit):
        return self.move(values, lambda z, x, c, y: (z ^ bit, x, c, y))

    def spread(self, block):
        width = block.shape[1] // 2
        mine = lax.dynamic_slice_in_dim(block, self.c * width, width, 1)
        theirs = self.over_core(
            lax.dynamic_slice_in_dim(block, (1 - self.c) * width, width, 1)
        )
        first = jnp.where(self.c == 0, mine, theirs)
        second = jnp.where(self.c == 0, theirs, mine)
        return jnp.concatenate([first, second])

    def depth_groups(self):
        return [
            [(z * 2 + x) * 2 + c for z in range(self.depth)] for x in range(2) for c in range(2)
        ]

    def gather_depth(self, block):
        return lax.all_gather(block, "dp", axis_index_groups=self.depth_groups())

    def scatter_depth(self, total):
        return lax.psum_scatter(total, "dp", axis_index_groups=self.depth_groups())

    def scatter_core(self, result):
        result = result.astype(jnp.float32)
        shard = result.shape[0] // 2
        mine = lax.dynamic_slice_in_dim(result, self.c * shard, shard)
        theirs = self.over_core(
            lax.dynamic_slice_in_dim(result, (1 - self.c) * shard, shard)
        )
        first = jnp.where(self.c == 0, mine, theirs)
        second = jnp.where(self.c == 0, theirs, mine)
        return jnp.stack([first, second])

    def sum_depth(self, values):
        terms = [values] + [self.across_z(values, mask) for mask in range(1, self.depth)]
        while len(terms) > 1:
            terms = [terms[i] + terms[i + 1] for i in range(0, len(terms), 2)]
        return terms[0]

    def gather_small(self, values):
        count, shard = values.shape
        parts = jnp.zeros((self.depth, 2, 2, count, shard), values.dtype)
        parts = lax.dynamic_update_slice(
            parts, values[None, None, None], (self.z, self.x, self.c, 0, 0)
        )
        parts = parts + self.over_core(parts)
        parts = parts + self.over_x(parts)
        bit = 1
        while bit < self.depth:
            parts = parts + self.across_z(parts, bit)
            bit *= 2
        return parts.transpose(3, 0, 1, 2, 4).reshape(count, -1)


def image_shards(
    depth,
    layer_input,
    token_image,
    cotangent,
    ln1_gain,
    ln1_bias,
    w_qkv,
    qv_bias,
    w_out,
    out_bias,
    ln2_gain,
    ln2_bias,
    w_fc1,
    fc1_bias,
    w_fc2,
    fc2_bias,
):
    low = jnp.bfloat16
    wide = jnp.float32
    grid = Grid(depth)
    rows, full_width = layer_input.shape
    shard = ln1_gain.shape[0]
    head_width = qv_bias.shape[1]
    ff_width = fc1_bias.shape[0]
    padded = -(-(rows + 1) // 256) * 256

    quarter = head_width // 2
    group_width = 4 * quarter
    ff_padding = 2 * group_width - ff_width
    sources = [w_qkv[0], w_qkv[1], w_qkv[2], w_out.T]
    first_block = jnp.concatenate(
        [values[:, i * quarter : (i + 1) * quarter] for i in range(2) for values in sources],
        axis=1,
    )
    second_block = jnp.pad(w_fc1, ((0, 0), (0, ff_padding)))
    third_block = jnp.pad(w_fc2.T, ((0, 0), (0, ff_padding)))
    half = depth // 2
    blocks = [grid.spread(first_block), grid.spread(second_block), grid.spread(third_block)]
    vectors = jnp.stack([ln1_gain, ln1_bias, out_bias, ln2_gain, ln2_bias, fc2_bias])
    (vectors,) = fence([vectors], [blocks[0]])
    vectors = grid.gather_small(vectors)
    own_one = grid.gather_depth(blocks[0])

    here = grid.y
    mine = lax.dynamic_slice_in_dim(token_image, here * rows, rows)
    theirs = lax.dynamic_slice_in_dim(token_image, (1 - here) * rows, rows)
    mine, theirs = fence([mine, theirs], [blocks[0]])
    places = lax.iota(jnp.int32, rows)
    stray = mine == 1 - here
    stray_here = jnp.any(stray)
    stray_there = jnp.any(theirs == here)
    blank = mine == IMAGES
    first_blank = jnp.min(jnp.where(blank, places, rows - 1))
    last_blank = jnp.max(jnp.where(blank, places, 0))
    swap_at = jnp.where(stray_here, jnp.max(jnp.where(stray, places, 0)), first_blank)
    swapped = stray_here | stray_there
    blank_at = jnp.where(stray_here, swap_at, last_blank)

    def one_row(values, at):
        return lax.dynamic_slice_in_dim(values, at, 1)

    sent = jnp.concatenate(
        [one_row(layer_input, swap_at), one_row(cotangent, swap_at), one_row(layer_input, last_blank)]
    )
    came = grid.over_y(sent)
    biases = jnp.concatenate([qv_bias.reshape(-1), fc1_bias])
    biases = jnp.pad(biases, (0, -biases.shape[0] % 128)).reshape(-1, 128)
    (biases,) = fence([biases], [blocks[0]])
    other_biases = grid.over_y(biases)

    def sides_of(own):
        return [grid.over_x(own), grid.over_y(own)]

    beside_three, across_three = sides_of(blocks[2])
    quad = [blocks[2], beside_three, across_three, grid.over_both(blocks[2])]
    (block_two,) = fence([blocks[1]], [vectors, came])
    own_two = grid.gather_depth(block_two)
    own_one, vectors, came, other_biases, *quad = fence(
        [own_one, vectors, came, other_biases] + quad
    )
    vectors = vectors.astype(wide)
    other_biases = other_biases.reshape(-1)
    other_blank = jnp.where(stray_there, sent[0:1], came[2:3])
    spread_rows = lax.broadcasted_iota(jnp.int32, (padded, 1), 0)
    at_swap = (spread_rows == swap_at) & swapped

    def stretch(values):
        return jnp.pad(values, ((0, padded - rows), (0, 0)))

    input_rows = jnp.where(at_swap, came[0:1], stretch(layer_input))
    input_rows = jnp.where(spread_rows == rows, other_blank, input_rows)
    grad_low = jnp.where(at_swap, came[1:2], stretch(cotangent))
    grad_low = jnp.where(spread_rows == blank_at, 0, grad_low).astype(low)
    kind = jnp.where(spread_rows > rows, 3, jnp.where(spread_rows == rows, 2, 0))
    kind = jnp.where(spread_rows == blank_at, 1, kind)
    input_rows, grad_low = lax.optimization_barrier((input_rows, grad_low))

    def ordered(first, second):
        return jnp.where(grid.c == 0, first, second), jnp.where(grid.c == 0, second, first)

    spot = grid.x.reshape(1)
    inner = -(-3 * quarter // 128) * 128
    qv_groups, fc1_groups = [], []
    for flat in (biases.reshape(-1), other_biases):
        flat = flat.astype(wide)
        pair = flat[: 2 * head_width].reshape(2, 2, quarter)
        none = jnp.zeros((quarter,), wide)
        rest = jnp.zeros((inner - 3 * quarter,), wide)
        qv_groups += ordered(
            *[jnp.concatenate([pair[0, i], none, pair[1, i], rest]) for i in range(2)]
        )
        hidden_bias = flat[2 * head_width : 2 * head_width + ff_width]
        hidden_bias = jnp.pad(hidden_bias, (0, ff_padding))
        fc1_groups += ordered(hidden_bias[:group_width], hidden_bias[group_width:])

    def stacked(rows_of, picked):
        return jnp.stack([rows_of[i] for i in picked])[:, None]

    qv_stacks = [stacked(qv_groups, picked) for picked in ((0, 1), (2, 3))]
    fc1_stacks = [stacked(fc1_groups, picked) for picked in ((1, 3), (0, 2))]

    def corners_of(beside, across):
        first, second = take_halves(beside, across)
        return [grid.over_y(first), grid.over_x(second)]

    def cores_of(*values):
        return [grid.over_core(value) for value in values]

    def near_groups(own, beside, there):
        return [
            [(own, 0, 0), (beside, 0, 1)],
            [(there[0], 0, 0), (there[1], 0, 1)],
        ]

    def far_groups(across, corner, there):
        return [
            [(across, 0, 0), (corner[0], 0, 1), (corner[1], half, 1)],
            [(there[0], 0, 0), (there[1], 0, 1), (there[2], half, 1)],
        ]

    quad = jnp.stack(quad)
    gain_one, shift_one, out_shift, gain_two, shift_two, fc2_shift = [
        vectors[i : i + 1] for i in range(6)
    ]
    beside_one, across_one = sides_of(own_one)
    unit_one, _ = unit_rows(input_rows.astype(wide))
    normed = (unit_one * gain_one + shift_one).astype(low)
    own_two, beside_one, across_one, normed, quad, grad_there, kind, *stacks = fence(
        [own_two, beside_one, across_one, normed, quad, grid.over_core(grad_low), kind]
        + qv_stacks
        + fc1_stacks
    )
    qv_stacks, fc1_stacks = stacks[:2], stacks[2:]
    corner_one = corners_of(beside_one, across_one)
    there = cores_of(own_one, beside_one)
    own_two_there = grid.over_core(own_two)
    across_there = grid.over_core(across_one)
    sides_two = sides_of(own_two)
    quads = grid.gather_depth(quad)

    def heads(stack, groups, waits=()):
        return heads_forward_call(spot, kind, normed, stack, groups, waits)

    attn_weights = near_groups(own_one, beside_one, there)
    first_qkv, first_probs, *mixed = heads(qv_stacks[0], attn_weights, [own_two_there])
    *corner_one, across_there, first_qkv = fence(corner_one + [across_there, first_qkv])
    there = [across_there] + cores_of(*corner_one)
    attn_weights = attn_weights + far_groups(across_one, corner_one, there)
    second_qkv, second_probs, *more = heads(qv_stacks[1], attn_weights[2:])
    mixed = mixed + more
    beside_two, across_two, second_qkv = fence(sides_two + [second_qkv])
    corner_two = corners_of(beside_two, across_two)
    beside_there, across_there = cores_of(beside_two, across_two)
    resid, normed_two = out_project(
        spot,
        mixed,
        input_rows,
        out_shift,
        gain_two,
        shift_two,
        attn_weights,
        [beside_there, across_there],
    )
    normed_there = grid.over_core(normed)
    *corner_two, normed_two, normed_there = fence(corner_two + [normed_two, normed_there])
    up_weights = near_groups(own_two, beside_two, [own_two_there, beside_there])
    there = [across_there] + cores_of(*corner_two)
    up_weights = up_weights + far_groups(across_two, corner_two, there)
    classes = ((1, 3), (0, 2))

    def up(at, waits):
        picked = [up_weights[i] for i in classes[at]]
        return up_project(spot, normed_two, fc1_stacks[at], picked, waits)

    other_active, other_slope = up(0, [])
    (other_active,) = fence([other_active])
    active_there = grid.over_core(other_active)
    own_active, own_slope = up(1, [other_active])
    normed_two_there = grid.over_core(normed_two)
    near_mixed, far_mixed = grid.over_core(mixed[1]), grid.over_core(mixed[3])
    own_active, active_there, normed_two_there, near_mixed, far_mixed, quads = fence(
        [own_active, active_there, normed_two_there, near_mixed, far_mixed, quads]
    )
    quads_there = grid.over_core(quads)
    fc2_sums = weight_grad(spot, (grad_low, grad_there), (own_active, active_there), depth)
    fc2_near, quads_there = fence([fc2_sums[0], quads_there])
    down_weights = [
        [(source, 0, 0, at), (source, 0, 1, at + 1)]
        for at in (0, 2)
        for source in (quads, quads_there)
    ]

    def move_first(sums):
        _, beside_lo, _, _, across_hi, corner_lo, corner_hi = sums
        return [
            grid.over_x(corner_lo),
            grid.over_y(corner_hi),
            grid.over_x(beside_lo),
            grid.over_y(across_hi),
        ]

    def move_second(sums, corner_lo, corner_hi):
        beside_hi, across_lo = add_pairs(sums[2], corner_hi, sums[3], corner_lo)
        return [grid.over_x(beside_hi), grid.over_y(across_lo)]

    def join(own, first, second):
        return add_square(own, first[0], second[0], second[1], first[1])

    fc2_moved = move_first(fc2_sums)
    order = (0, 2, 1, 3)
    own_hidden, other_hidden, resid_low, sums_two, fc1_bias_sums = mlp_back(
        spot,
        grad_low,
        own_slope,
        other_slope,
        resid,
        gain_two,
        [down_weights[i] for i in order],
        [up_weights[i] for i in order],
        [fc2_near],
    )
    resid_low, other_hidden, *fc2_moved = fence([resid_low, other_hidden] + fc2_moved)
    fc2_second = move_second(fc2_sums, *fc2_moved[:2])
    hidden_there = grid.over_core(other_hidden)
    resid_there = grid.over_core(resid_low)

    def heads_back(qkv, probs, side, waits):
        order = [1 + 2 * side, 2 * side]
        return heads_backward_call(
            spot,
            resid_low,
            qkv,
            probs,
            [mixed[i] for i in order],
            [attn_weights[i] for i in order],
            (1, 0),
            waits,
        )

    far_other, far_own, far_sums = heads_back(second_qkv, second_probs, 1, [])
    *fc2_second, far_other, hidden_there, resid_there = fence(
        fc2_second + [far_other, hidden_there, resid_there]
    )
    far_there = grid.over_core(far_other)
    fc2_total = join(fc2_near, fc2_moved[2:], fc2_second)
    fc1_sums = weight_grad(
        spot, (normed_two, normed_two_there), (own_hidden, hidden_there), depth, waits=[fc2_total]
    )
    far_there, fc2_total, fc1_near = fence([far_there, fc2_total, fc1_sums[0]])
    fc2_piece = grid.scatter_depth(fc2_total)
    fc1_moved = move_first(fc1_sums)
    near_other, near_own, near_sums_qkv = heads_back(first_qkv, first_probs, 0, [fc1_near])
    near_other, *fc1_moved = fence([near_other] + fc1_moved)
    fc1_second = move_second(fc1_sums, *fc1_moved[:2])
    near_there = grid.over_core(near_other)

    def attn_grad(side, own_part, there_part, own_mixed, there_mixed, waits):
        return weight_grad(
            spot,
            (normed, normed_there),
            (own_part, there_part),
            depth,
            (side,),
            (resid_low, own_mixed, resid_there, there_mixed),
            waits,
        )

    across_lo, across_hi, corner_lo, corner_hi = attn_grad(
        2, far_own, far_there, mixed[2], far_mixed, [near_other]
    )
    across_lo, across_hi, corner_lo, corner_hi, near_there = fence(
        [across_lo, across_hi, corner_lo, corner_hi, near_there]
    )
    corners = [grid.over_x(corner_lo), grid.over_y(corner_hi)]
    attn_first = grid.over_y(across_hi)
    near_sums, beside_lo, beside_hi = attn_grad(
        0, near_own, near_there, mixed[0], near_mixed, [across_lo]
    )
    *fc1_second, beside_lo, beside_hi, fc2_piece = fence(
        fc1_second + [beside_lo, beside_hi, fc2_piece]
    )
    beside_first = grid.over_x(beside_lo)
    fc1_total = join(fc1_near, fc1_moved[2:], fc1_second)
    *corners, fc1_total = fence(corners + [fc1_total])
    fc1_piece = grid.scatter_depth(fc1_total)
    beside_hi, across_lo = add_pairs(beside_hi, corners[1], across_lo, corners[0])
    moved = [grid.over_x(beside_hi), grid.over_y(across_lo)]
    by_class = [attn_weights[i] for i in (1, 3, 0, 2)]
    input_grad, sums_one = norm_back(
        spot,
        [near_other, far_other, near_own, far_own],
        input_rows,
        resid_low,
        gain_one,
        by_class,
        [beside_hi],
    )

    def column_sum(values):
        return jnp.sum(values.astype(wide), axis=0)

    def absolute(near_other, near_own, far_other, far_own):
        near = ordered(near_own, near_other)
        far = ordered(far_own, far_other)
        return [
            (jnp.where(here == 0, one, two), jnp.where(here == 0, two, one))
            for one, two in zip(near, far)
        ]

    qkv_totals = absolute(near_sums_qkv[0], near_sums_qkv[1], far_sums[0], far_sums[1])
    query_and_value = [
        qkv_totals[half_at][side][0, at : at + quarter]
        for side in range(2)
        for at in (0, 2 * quarter)
        for half_at in range(2)
    ]
    fc1_totals = absolute(*[fc1_bias_sums[i] for i in (2, 0, 3, 1)])
    fc1_rows = []
    for side in range(2):
        fc1_rows += [fc1_totals[0][side][0], fc1_totals[1][side][0, : ff_width - group_width]]
    flat = jnp.concatenate(
        [
            sums_one[0],
            sums_one[1],
            sums_two[2],
            sums_two[0],
            sums_two[1],
            column_sum(grad_low),
            *query_and_value,
            *fc1_rows,
        ]
    )
    length = flat.shape[0]
    lines = -(-length // 1024) * 8
    flat = jnp.pad(flat, (0, lines * 128 - length)).reshape(lines, 128)
    *moved, beside_first, attn_first, flat, fc1_piece = fence(
        moved + [beside_first, attn_first, flat, fc1_piece]
    )
    total = join(near_sums, [beside_first, attn_first], moved)
    attn_piece = grid.scatter_depth(total)
    (flat, fc1_piece, fc2_piece) = fence([flat, fc1_piece, fc2_piece], [total])
    by_class = [down_weights[i] for i in classes[0] + classes[1]]
    layer_rows = down_project(
        spot, other_active, own_active, resid, fc2_shift, by_class, [total]
    )
    flat = flat + grid.over_core(flat)
    moved = [grid.over_x(flat), grid.over_y(flat), grid.over_both(flat)]
    flat = (flat + moved[0]) + (moved[1] + moved[2])
    flat = grid.sum_depth(flat)
    flat = flat.reshape(-1)
    fc1_piece = grid.scatter_core(fc1_piece)
    fc2_piece = grid.scatter_core(fc2_piece)
    swap_from = fence([one_row(layer_rows, swap_at), one_row(input_grad, swap_at)], [total])
    returned = [grid.over_y(values) for values in swap_from]
    kept = [jnp.where(swapped, one, two) for one, two in zip(returned, swap_from)]
    layer_output = lax.dynamic_update_slice(layer_rows[:rows], kept[0], (swap_at, 0))
    input_grad = lax.dynamic_update_slice(input_grad[:rows], kept[1], (swap_at, 0))
    attn_piece = grid.scatter_core(attn_piece)
    row_total = flat[: 6 * full_width].reshape(6, full_width)
    row_piece = lax.dynamic_slice_in_dim(row_total, lax.axis_index("dp") * shard, shard, 1)
    start = 6 * full_width
    qv_piece = lax.dynamic_slice_in_dim(flat, start + here * 2 * head_width, 2 * head_width)
    start = start + 4 * head_width
    fc1_bias_piece = lax.dynamic_slice_in_dim(flat, start + here * ff_width, ff_width)
    heads_piece = attn_piece.reshape(2, shard, 4, quarter).transpose(2, 1, 0, 3)
    heads_piece = heads_piece.reshape(4, shard, head_width)

    def whole_columns(pair):
        return jnp.concatenate([pair[0], pair[1][:, : group_width - ff_padding]], axis=1)

    return (
        layer_output,
        input_grad,
        row_piece[0],
        row_piece[1],
        heads_piece[:3],
        qv_piece.reshape(2, head_width),
        heads_piece[3].T,
        row_piece[2],
        row_piece[3],
        row_piece[4],
        whole_columns(fc1_piece),
        fc1_bias_piece,
        whole_columns(fc2_piece).T,
        row_piece[5],
    )


def fits_images(mesh):
    groups = mesh.shape["dp"] // 4
    return (
        mesh.shape["tensor"] == IMAGES
        and mesh.shape["dp"] % 4 == 0
        and groups >= 2
        and groups & (groups - 1) == 0
    )


def solution(mesh):
    in_specs = (
        P(("dp", "tensor"), None),
        P("dp"),
        P(("dp", "tensor"), None),
        P("dp"),
        P("dp"),
        P(None, "dp", "tensor"),
        P(None, "tensor"),
        P("tensor", "dp"),
        P("dp"),
        P("dp"),
        P("dp"),
        P("dp", "tensor"),
        P("tensor"),
        P("tensor", "dp"),
        P("dp"),
    )
    out_specs = (
        P(("dp", "tensor"), None),
        P(("dp", "tensor"), None),
        P("dp"),
        P("dp"),
        P(None, "dp", "tensor"),
        P(None, "tensor"),
        P("tensor", "dp"),
        P("dp"),
        P("dp"),
        P("dp"),
        P("dp", "tensor"),
        P("tensor"),
        P("tensor", "dp"),
        P("dp"),
    )

    def body(*arrays):
        slots = arrays[1].shape[0]
        if fits_images(mesh) and slots == IMAGES * (PATCHES + 1):
            return image_shards(mesh.shape["dp"] // 4, *arrays)
        return shards(*arrays)

    return jax.shard_map(body, mesh=mesh, in_specs=in_specs, out_specs=out_specs, check_vma=False)
```
